32 devices in a mesh: ctx: 32 (over z, y, x, core), grp: 1.
Axes of the slice: x: 2, y: 2, z: 4, core: 2. Of those that a mesh axis runs over, the one named last changes fastest.
Arguments:
- query_in: bfloat16 [4096, 8192], P('ctx', 'grp'), may hold values from -6 to 6
- key_in: bfloat16 [4096, 8192], P('ctx', 'grp'), may hold values from -6 to 6
- value_in: bfloat16 [4096, 8192], P('ctx', 'grp'), may hold values from -6 to 6
- short_taps: float32 [3, 3, 8192], P(None, None, 'grp'), may hold values from -3 to 3
- decay_rate: float32 [16, 8192], P(None, 'grp'), may hold values from 0 to 1, as said below
- residues: float32 [16, 8192], P(None, 'grp'), may hold values from -2.5 to 2.5
- doc_lengths: int32 [16], replicated, may hold values from 1 to 1024, 4096 in all
- residual: bfloat16 [4096, 8192], P('ctx', 'grp'), may hold values from -6 to 6
- norm_gain: float32 [8192], P('grp'), may hold values from 0.5 to 1.5
Outputs:
- hidden_out: bfloat16 [4096, 8192], P('ctx', 'grp')
- normed: bfloat16 [4096, 8192], P('ctx', 'grp')
The draws below stay inside these ranges and needn't reach their ends.
Inputs may be any that keep to these rules, and one draw needn't show every extreme that they name: `doc_lengths`: the lengths are positive, sum to 4096, and the largest is exactly 1024. `decay_rate`: positive decay rates.
All inputs are finite; a program needn't handle non-finite values.
Results may differ from the reference program's by a relative error of at most 0.0045.
Values may be sent and summed in bfloat16 or wider, within the bound.
No kernel may reach another device: no remote copies, remote signals or barrier semaphores. Data moves between devices by JAX's collectives and lax.ppermute only.
A program may use at most 128 MiB of HBM per device.

```python
import math
import jax
import jax.numpy as jnp
import numpy as np
from jax import lax

D = 8192
STATE = 16
KS = 3
TOKENS = 4096
NDOC = 16
MAXDOC = 1024


def draw_decay_rate(key, part):
    key_rate = jax.random.fold_in(key, 23)
    spread = jax.random.uniform(key_rate, (STATE, D), jnp.float32)
    low_end = jnp.log(jnp.float32(0.5) / MAXDOC)
    high_end = jnp.log(jnp.float32(1.0 / 40.0))
    rate_vals = jnp.exp(high_end + spread * (low_end - high_end))
    return rate_vals


def levels(key, shape, split, smallest, top_value):
    def one(dim, shards_of):
        steps = jax.random.uniform(jax.random.fold_in(jax.random.fold_in(key, 6), dim), (shards_of,), jnp.float32, smallest / len(split), top_value / len(split))
        return jnp.repeat(jnp.exp(steps), shape[dim] // shards_of).reshape((-1,) + (1,) * (len(shape) - dim - 1))

    factor_of = one(*split[0])
    for cut in split[1:]:
        factor_of = factor_of * one(*cut)
    return factor_of


def split_up(number_of, total, most, lean):
    portions = [(1 << 20) // math.isqrt(grade ** lean) + 1 for grade in range(2, number_of + 1)]
    spare, counts = total - most - (number_of - 1), [1] * (number_of - 1)
    while spare > 0:
        free = [i for i in range(number_of - 1) if counts[i] < most]
        whole, remaining = sum([portions[i] for i in free]), spare
        for i in free:
            more = min(most - counts[i], max(1, remaining * portions[i] // whole), spare)
            counts[i] = counts[i] + more
            spare = spare - more
    return np.array([most] + counts)


def uneven(own_key, number_of, total, reach, skew):
    if number_of == 2:
        one = jax.random.randint(own_key, (), max(1, total - reach), min(reach, total - 1) + 1)
        return jnp.stack([one, total - one])
    sizes = jnp.asarray(split_up(number_of, total, reach, skew), jnp.int32)
    twos = (number_of - 1) // 2
    source_of, receiver = sizes[1:1 + 2 * twos:2], sizes[2:2 + 2 * twos:2]
    room = jnp.minimum(source_of - 1, reach - receiver)
    shifted = jax.random.randint(jax.random.fold_in(own_key, 1), (twos,), 0, 1 << 20) % (room + 1)
    sizes = sizes.at[1:1 + 2 * twos:2].set(source_of - shifted).at[2:2 + 2 * twos:2].set(receiver + shifted)
    return sizes[jax.random.permutation(jax.random.fold_in(own_key, 2), number_of)]


def centred(stream_key, shape, scale, limit, split=(), kind=jnp.bfloat16):
    entries = scale * jax.random.normal(stream_key, shape, jnp.float32)
    if split:
        entries = entries * levels(stream_key, shape, split, -0.22, 0.18)
    return jnp.clip(entries, -limit, limit).astype(kind)


def setup_inputs(seed: int = 0) -> dict:
    streams_of = jax.random.split(jax.random.key(seed), 10)
    query_in = centred(streams_of[0], (TOKENS, D), 1.0, 6.0, ((0, 32),))
    key_in = centred(streams_of[1], (TOKENS, D), 1.0, 6.0, ((0, 32),))
    value_in = centred(streams_of[2], (TOKENS, D), 1.0, 6.0, ((0, 32),))
    short_taps = centred(streams_of[3], (3, KS, D), 0.6, 3.0, (), jnp.float32)
    decay_rate = draw_decay_rate(jax.random.fold_in(streams_of[9], 71), 0)
    residues = centred(streams_of[5], (STATE, D), 0.25, 2.5, (), jnp.float32)
    doc_lengths = uneven(streams_of[6], NDOC, TOKENS, MAXDOC, 2).astype(jnp.int32)
    residual = centred(streams_of[7], (TOKENS, D), 1.0, 6.0, ((0, 32),))
    norm_gain = jnp.clip(1.0 + 0.1 * jax.random.normal(streams_of[8], (D,), jnp.float32), 0.5, 1.5)
    return dict(query_in=query_in, key_in=key_in, value_in=value_in, short_taps=short_taps, decay_rate=decay_rate, residues=residues, doc_lengths=doc_lengths, residual=residual, norm_gain=norm_gain)


def short_conv(signal, taps, keep_one, keep_two):
    padded = jnp.pad(signal, ((2, 0), (0, 0)))
    return taps[0] * signal + taps[1] * padded[1:-1] * keep_one[:, None] + taps[2] * padded[:-2] * keep_two[:, None]

def segment_conv(gate_val, rate_blk, weight_blk, fresh_flags):
    decay_step = jnp.exp(-rate_blk)

    def advance(carried, inputs):
        gate_row, restart = inputs
        carried = decay_step * carried * (1.0 - restart) + gate_row[None, :]
        return (carried, lax.optimization_barrier(jnp.sum(weight_blk * carried, axis=0)))
    _, conv_full = lax.scan(advance, jnp.zeros(rate_blk.shape, jnp.float32), (gate_val, fresh_flags))
    return conv_full

def reference(query_in, key_in, value_in, short_taps, decay_rate, residues, doc_lengths, residual, norm_gain):
    lengths = doc_lengths.astype(jnp.int32)
    starts = (jnp.cumsum(lengths) - lengths).astype(jnp.int32)
    positions = jnp.arange(TOKENS, dtype=jnp.int32)
    flag_here = jnp.any(positions[:, None] == starts[None, :], axis=1)
    flag_prev = jnp.any((positions - 1)[:, None] == starts[None, :], axis=1)
    keep_one = jnp.logical_not(flag_here).astype(jnp.float32)
    keep_two = jnp.logical_not(jnp.logical_or(flag_here, flag_prev)).astype(jnp.float32)
    fresh_flags = flag_here.astype(jnp.float32)
    weight = residues * jnp.sqrt(-jnp.expm1(-2.0 * decay_rate))
    blocks = D // 512

    def split_cols(array):
        return array.reshape(TOKENS, blocks, 512).transpose(1, 0, 2)

    def split_modes(array):
        return array.reshape(STATE, blocks, 512).transpose(1, 0, 2)
    taps_blocks = short_taps.reshape(3, KS, blocks, 512).transpose(2, 0, 1, 3)

    def branch_block(packed):
        query_blk, key_blk, value_blk, taps_blk, rate_blk, weight_blk = packed
        q_short = short_conv(query_blk.astype(jnp.float32), taps_blk[0], keep_one, keep_two)
        k_short = short_conv(key_blk.astype(jnp.float32), taps_blk[1], keep_one, keep_two)
        v_short = short_conv(value_blk.astype(jnp.float32), taps_blk[2], keep_one, keep_two)
        gate_in = lax.optimization_barrier((k_short * v_short).astype(jnp.bfloat16))
        conv_full = segment_conv(gate_in.astype(jnp.float32), rate_blk, weight_blk, fresh_flags)
        conv_out = lax.optimization_barrier(conv_full.astype(jnp.bfloat16))
        return q_short * conv_out.astype(jnp.float32)
    branch = lax.map(branch_block, (split_cols(query_in), split_cols(key_in), split_cols(value_in), taps_blocks, split_modes(decay_rate), split_modes(weight)))
    branch = branch.transpose(1, 0, 2).reshape(TOKENS, D)
    hidden = residual.astype(jnp.float32) + branch
    hidden_out = hidden.astype(jnp.bfloat16)
    inverse_rms = lax.rsqrt(lax.optimization_barrier(jnp.mean(hidden * hidden, axis=1, keepdims=True)) + 1e-06)
    normed = (hidden * inverse_rms * norm_gain[None, :]).astype(jnp.bfloat16)
    return (hidden_out, normed)
```

```python
import functools

import jax
import jax.numpy as jnp
from jax import lax
from jax.experimental import pallas as pl
from jax.experimental.pallas import tpu as pltpu
from jax.sharding import PartitionSpec as P

SUBS = 8
LANES = 128
VMEM_LIMIT = 48 * 1024 * 1024
f32 = jnp.float32
bf16 = jnp.bfloat16


def from_behind(shard, axis, by):
    count = lax.axis_size(axis)
    pairs = [(i, i + by) for i in range(count) if 0 <= i + by < count]
    return lax.ppermute(shard, axis, pairs)


def doc_start_rows(len_ref, base, span):
    rows = lax.broadcasted_iota(jnp.int32, (SUBS, LANES), 0) * span + base
    starts = [jnp.int32(0)]
    for d in range(len_ref.shape[0] - 1):
        starts.append(starts[-1] + len_ref[d])
    out = []
    for j in range(span):
        pos = rows + j
        best = jnp.zeros((SUBS, LANES), jnp.int32)
        for start in starts[1:]:
            best = jnp.where(pos >= start, start, best)
        out.append(best)
    return rows, out


def flag(cond):
    return jnp.where(cond, 1.0, 0.0).astype(f32)


def row_of(ref, index):
    return jnp.broadcast_to(ref[pl.ds(index, 1), :], (SUBS, LANES))


def spread(x, scratch, span):
    scratch[...] = x.astype(f32)
    return [scratch[pl.ds(j, SUBS, stride=span), :] for j in range(span)]


def short_conv(steps, rim, taps, keep_one, keep_two):
    top = lax.broadcasted_iota(jnp.int32, (SUBS, LANES), 0) == 0
    rim = rim.astype(f32)
    behind_one = jnp.where(top, jnp.broadcast_to(rim[1:2], (SUBS, LANES)), pltpu.roll(steps[-1], 1, 0))
    behind_two = jnp.where(top, jnp.broadcast_to(rim[0:1], (SUBS, LANES)), pltpu.roll(steps[-2], 1, 0))
    padded = [behind_two, behind_one] + steps
    taps = [jnp.broadcast_to(taps[m : m + 1], (SUBS, LANES)) for m in range(3)]
    return [
        taps[0] * padded[j + 2]
        + (taps[1] * padded[j + 1]) * keep_one[j]
        + (taps[2] * padded[j]) * keep_two[j]
        for j in range(len(steps))
    ]


def state_kernel(
    base_ref, len_ref, key_ref, value_ref, rim_ref, taps_ref, rate_ref, weight_ref,
    gate_ref, state_ref, end_ref,
    masks, wide_k, wide_v, tables, ends,
    *, span, modes, width,
):
    @pl.when(pl.program_id(0) == 0)
    def _():
        rows, starts = doc_start_rows(len_ref, base_ref[0], span)
        for j in range(span):
            masks[0, j] = flag(starts[j] < rows + j)
            masks[1, j] = flag(starts[j] < rows + (j - 1))
            masks[2, j] = flag(starts[span - 1] <= rows + j)
        sub = lax.broadcasted_iota(jnp.int32, (SUBS, LANES), 0)
        through = flag(starts[span - 1] < rows)
        one = through * flag(sub >= 1)
        two = one * pltpu.roll(one, 1, 0) * flag(sub >= 2)
        four = two * pltpu.roll(two, 2, 0) * flag(sub >= 4)
        masks[3, 0] = one
        masks[3, 1] = two
        masks[3, 2] = four
        masks[3, 3] = flag(sub >= 1)

    def tile(i, carry):
        lane = pl.multiple_of(i * LANES, LANES)
        cols = pl.ds(lane, LANES)
        keep_one = [masks[0, j] for j in range(span)]
        keep_two = [masks[1, j] for j in range(span)]
        k_steps = spread(key_ref[:, cols], wide_k, span)
        v_steps = spread(value_ref[:, cols], wide_v, span)
        k_short = short_conv(k_steps, rim_ref[1, :, cols], taps_ref[1, :, cols], keep_one, keep_two)
        v_short = short_conv(v_steps, rim_ref[2, :, cols], taps_ref[2, :, cols], keep_one, keep_two)
        gates = []
        for j in range(0, span, 2):
            pair = jnp.concatenate([k_short[j] * v_short[j], k_short[j + 1] * v_short[j + 1]], axis=0).astype(bf16)
            gate_ref[pl.ds(j * SUBS, 2 * SUBS), cols] = pair
            pair = pair.astype(f32)
            gates += [pair[:SUBS] * masks[2, j], pair[SUBS:] * masks[2, j + 1]]
        rate = rate_ref[:, cols]
        tables[0] = jnp.exp(-rate)
        tables[1] = jnp.exp(-float(span) * rate)
        tables[2] = jnp.exp(-float(2 * span) * rate)
        tables[3] = jnp.exp(-float(4 * span) * rate)
        tables[4] = weight_ref[:, cols]
        decay = [row_of(tables.at[0], n) for n in range(modes)]
        state = [gates[0]] * modes
        for j in range(1, span):
            state = [decay[n] * state[n] + gates[j] for n in range(modes)]
        for n in range(modes):
            x = state[n]
            x = x + (row_of(tables.at[1], n) * masks[3, 0]) * pltpu.roll(x, 1, 0)
            x = x + (row_of(tables.at[2], n) * masks[3, 1]) * pltpu.roll(x, 2, 0)
            x = x + (row_of(tables.at[3], n) * masks[3, 2]) * pltpu.roll(x, 4, 0)
            ends[pl.ds(n, 1), :] = x[SUBS - 1 :]
            state_ref[pl.ds(n * SUBS, SUBS), cols] = (row_of(tables.at[4], n) * masks[3, 3]) * pltpu.roll(x, 1, 0)
        if width:
            end_ref[lax.div(lane, width), :, pl.ds(pl.multiple_of(lax.rem(lane, width), LANES), LANES)] = ends[...].astype(bf16)
        else:
            end_ref[:, cols] = ends[...].astype(bf16)
        return carry

    lax.fori_loop(0, key_ref.shape[1] // LANES, tile, 0)


def local_kernel(
    base_ref, len_ref, gate_ref, query_ref, rim_ref, taps_ref, rate_ref, weight_ref,
    near_ref, short_ref,
    masks, wide_q,
    *, span, modes,
):
    @pl.when(pl.program_id(0) == 0)
    def _():
        rows, starts = doc_start_rows(len_ref, base_ref[0], span)
        for j in range(span):
            masks[0, j] = flag(starts[j] < rows + j)
            masks[1, j] = flag(starts[j] < rows + (j - 1))

    def tile(i, carry):
        cols = pl.ds(pl.multiple_of(i * LANES, LANES), LANES)
        keep_one = [masks[0, j] for j in range(span)]
        keep_two = [masks[1, j] for j in range(span)]
        q_steps = spread(query_ref[:, cols], wide_q, span)
        q_short = short_conv(q_steps, rim_ref[0, :, cols], taps_ref[0, :, cols], keep_one, keep_two)
        for j in range(span):
            short_ref[pl.ds(j * SUBS, SUBS), cols] = q_short[j]
        decay = jnp.exp(-rate_ref[:, cols])
        term = weight_ref[:, cols]
        taps = []
        for lag in range(span):
            part = term[:SUBS]
            for n in range(SUBS, modes, SUBS):
                part = part + term[n : n + SUBS]
            for shift in (1, 2, 4):
                part = part + pltpu.roll(part, shift, 0)
            taps.append(part)
            term = term * decay
        live = []
        for j in range(span):
            if j % 2 == 0:
                pair = gate_ref[pl.ds(j * SUBS, 2 * SUBS), cols].astype(f32)
            live = [g * keep_one[j] for g in live]
            live.append(pair[(j % 2) * SUBS : (j % 2 + 1) * SUBS])
            total = taps[0] * live[j]
            for lag in range(1, j + 1):
                total = total + taps[lag] * live[j - lag]
            near_ref[pl.ds(j * SUBS, SUBS), cols] = total
        return carry

    lax.fori_loop(0, gate_ref.shape[1] // LANES, tile, 0)


def prefix_kernel(len_ref, end_ref, rate_ref, enter_ref, through, *, span):
    blocks = end_ref.shape[0]
    for i in range(blocks):
        through[i] = jnp.float32(1.0)
    start = jnp.int32(0)
    through[0] = jnp.float32(0.0)
    for d in range(len_ref.shape[0] - 1):
        start = start + len_ref[d]
        through[lax.div(start, jnp.int32(span))] = jnp.float32(0.0)
    decay = jnp.exp(-float(span) * rate_ref[...])
    state = jnp.zeros(decay.shape, f32)
    for i in range(blocks):
        enter_ref[i] = state.astype(bf16)
        state = end_ref[i].astype(f32) + (decay * through[i]) * state


def final_kernel(
    base_ref, len_ref, state_ref, enter_ref, near_ref, short_ref, resid_ref, rate_ref, weight_ref, gain_ref,
    *refs,
    span, modes, width, channels,
):
    if channels:
        hidden_ref, normed_ref, masks, tables, sums, whole = refs
    else:
        hidden_ref, wide_ref, sum_ref, masks, tables, sums, whole = refs
    step = pl.program_id(0)
    tiles = resid_ref.shape[1] // LANES

    @pl.when(step == 0)
    def _():
        rows, starts = doc_start_rows(len_ref, base_ref[0], span)
        for j in range(span):
            masks[0, j] = flag(starts[j] < rows)
        masks[1, 0] = flag(starts[0] < base_ref[0])
        sums[...] = jnp.zeros(sums.shape, f32)

    def tile(i, carry):
        lane = pl.multiple_of(i * LANES, LANES)
        cols = pl.ds(lane, LANES)
        if width:
            enter = enter_ref[lax.div(lane, width), :, pl.ds(pl.multiple_of(lax.rem(lane, width), LANES), LANES)]
        else:
            enter = enter_ref[:, cols]
        rate = rate_ref[:, cols]
        tables[0] = jnp.exp(-rate)
        tables[1] = weight_ref[:, cols] * enter.astype(f32)
        tables[2] = rate
        sub = lax.broadcasted_iota(jnp.int32, (SUBS, LANES), 0).astype(f32) * (-float(span))
        through = masks[1, 0]
        decay = [row_of(tables.at[0], n) for n in range(modes)]
        part = [
            state_ref[pl.ds(n * SUBS, SUBS), cols]
            + (row_of(tables.at[1], n) * through) * jnp.exp(row_of(tables.at[2], n) * sub)
            for n in range(modes)
        ]
        tile_at = step * tiles + i
        for j in range(span):
            part = [part[n] * decay[n] for n in range(modes)]
            total = part
            while len(total) > 1:
                total = [total[m] + total[m + 1] for m in range(0, len(total), 2)]
            conv = near_ref[pl.ds(j * SUBS, SUBS), cols] + total[0] * masks[0, j]
            conv = conv.astype(bf16).astype(f32)
            whole[tile_at, pl.ds(j, SUBS, stride=span), :] = short_ref[pl.ds(j * SUBS, SUBS), cols] * conv
        hidden = whole[tile_at] + resid_ref[:, cols].astype(f32)
        whole[tile_at] = hidden
        hidden_ref[:, cols] = hidden.astype(bf16)
        if not channels:
            wide_ref[:, cols] = hidden
        sums[...] = sums[...] + hidden * hidden
        return carry

    lax.fori_loop(0, tiles, tile, 0)

    @pl.when(step == pl.num_programs(0) - 1)
    def _():
        if channels:
            inverse = lax.rsqrt(jnp.sum(sums[...], axis=1, keepdims=True) / channels + 1e-06)
            inverse = jnp.broadcast_to(inverse, sums.shape)
            sums[...] = inverse

            def scale(i, carry):
                cols = pl.ds(pl.multiple_of(i * LANES, LANES), LANES)
                normed_ref[:, cols] = (whole[i] * sums[...] * gain_ref[:, cols]).astype(bf16)
                return carry

            lax.fori_loop(0, normed_ref.shape[1] // LANES, scale, 0)
        else:
            sum_ref[...] = sums[...]


def shards(
    query_in, key_in, value_in, short_taps, decay_rate, residues, doc_lengths, residual, norm_gain
):
    tok_rows, chans = query_in.shape
    modes = decay_rate.shape[0]
    span = tok_rows // SUBS
    blocks = lax.axis_size("ctx")
    grp = lax.axis_size("grp")
    few = chans // blocks
    width = few if few % LANES == 0 else 0
    chunk = min(chans, max(1024, width))
    steps = chans // chunk
    ctx_index = lax.axis_index("ctx")
    base = (ctx_index * tok_rows).astype(jnp.int32).reshape(1)
    tails = jnp.stack([query_in[tok_rows - 2 :], key_in[tok_rows - 2 :], value_in[tok_rows - 2 :]])
    rim_rows = from_behind(tails, "ctx", 1)
    weight = residues * jnp.sqrt(-jnp.expm1(-2.0 * decay_rate))

    smem = pl.BlockSpec(memory_space=pltpu.SMEM)

    def rows_spec(rows):
        return pl.BlockSpec((rows, chunk), lambda i: (0, i))

    rim_spec = pl.BlockSpec((3, 2, chunk), lambda i: (0, 0, i))
    taps_spec = pl.BlockSpec((3, 3, chunk), lambda i: (0, 0, i))
    if width:
        end_spec = pl.BlockSpec((chunk // width, modes, width), lambda i: (i, 0, 0))
        end_shape = (blocks, modes, width)
    else:
        end_spec = rows_spec(modes)
        end_shape = (modes, chans)
    params = pltpu.CompilerParams(vmem_limit_bytes=VMEM_LIMIT)
    tile_shape = (SUBS, LANES)

    def cost(per_tile, moved):
        return pl.CostEstimate(flops=per_tile * (chans // LANES) * SUBS * LANES, bytes_accessed=moved, transcendentals=0)

    gates, states, ends = pl.pallas_call(
        functools.partial(state_kernel, span=span, modes=modes, width=width),
        grid=(steps,),
        in_specs=[smem, smem, rows_spec(tok_rows), rows_spec(tok_rows), rim_spec, taps_spec, rows_spec(modes), rows_spec(modes)],
        out_specs=[rows_spec(tok_rows), rows_spec(modes * SUBS), end_spec],
        out_shape=[
            jax.ShapeDtypeStruct((tok_rows, chans), bf16),
            jax.ShapeDtypeStruct((modes * SUBS, chans), f32),
            jax.ShapeDtypeStruct(end_shape, bf16),
        ],
        scratch_shapes=[
            pltpu.VMEM((4, span) + tile_shape, f32),
            pltpu.VMEM((tok_rows, LANES), f32),
            pltpu.VMEM((tok_rows, LANES), f32),
            pltpu.VMEM((5, modes, LANES), f32),
            pltpu.VMEM((modes, LANES), f32),
        ],
        compiler_params=params,
        cost_estimate=cost(1000, 12 * tok_rows * chans),
        name="block_states",
    )(base, doc_lengths, key_in, value_in, rim_rows, short_taps, decay_rate, weight)

    near, q_short = pl.pallas_call(
        functools.partial(local_kernel, span=span, modes=modes),
        grid=(steps,),
        in_specs=[smem, smem, rows_spec(tok_rows), rows_spec(tok_rows), rim_spec, taps_spec, rows_spec(modes), rows_spec(modes)],
        out_specs=[rows_spec(tok_rows), rows_spec(tok_rows)],
        out_shape=[jax.ShapeDtypeStruct((tok_rows, chans), f32), jax.ShapeDtypeStruct((tok_rows, chans), f32)],
        scratch_shapes=[pltpu.VMEM((2, span) + tile_shape, f32), pltpu.VMEM((tok_rows, LANES), f32)],
        compiler_params=params,
        cost_estimate=cost(700, 12 * tok_rows * chans),
        name="near_part",
    )(base, doc_lengths, gates, query_in, rim_rows, short_taps, decay_rate, weight)

    if not width:
        ends = ends.reshape(modes, blocks, few).transpose(1, 0, 2)
    moved = lax.all_to_all(ends, "ctx", split_axis=0, concat_axis=0, tiled=True)
    rate_few = lax.dynamic_slice_in_dim(decay_rate, ctx_index * few, few, 1)
    enter_few = pl.pallas_call(
        functools.partial(prefix_kernel, span=tok_rows),
        in_specs=[smem, pl.BlockSpec(memory_space=pltpu.VMEM), pl.BlockSpec(memory_space=pltpu.VMEM)],
        out_specs=pl.BlockSpec(memory_space=pltpu.VMEM),
        out_shape=jax.ShapeDtypeStruct((blocks, modes, few), bf16),
        scratch_shapes=[pltpu.SMEM((blocks,), f32)],
        name="block_prefix",
    )(doc_lengths, moved, rate_few)
    enter = lax.all_to_all(enter_few, "ctx", split_axis=0, concat_axis=0, tiled=True)
    if not width:
        enter = enter.transpose(1, 0, 2).reshape(modes, chans)

    alone = grp == 1
    out_specs = [rows_spec(tok_rows)]
    out_shape = [jax.ShapeDtypeStruct((tok_rows, chans), bf16)]
    if alone:
        out_specs.append(pl.BlockSpec((tok_rows, chans), lambda i: (0, 0)))
        out_shape.append(jax.ShapeDtypeStruct((tok_rows, chans), bf16))
    else:
        out_specs += [rows_spec(tok_rows), pl.BlockSpec((tok_rows, LANES), lambda i: (0, 0))]
        out_shape += [jax.ShapeDtypeStruct((tok_rows, chans), f32), jax.ShapeDtypeStruct((tok_rows, LANES), f32)]
    outs = pl.pallas_call(
        functools.partial(final_kernel, span=span, modes=modes, width=width, channels=chans if alone else 0),
        grid=(steps,),
        in_specs=[
            smem, smem, rows_spec(modes * SUBS), end_spec, rows_spec(tok_rows), rows_spec(tok_rows), rows_spec(tok_rows),
            rows_spec(modes), rows_spec(modes), pl.BlockSpec((1, chans), lambda i: (0, 0)),
        ],
        out_specs=out_specs,
        out_shape=out_shape,
        scratch_shapes=[
            pltpu.VMEM((2, span) + tile_shape, f32),
            pltpu.VMEM((3, modes, LANES), f32),
            pltpu.VMEM((tok_rows, LANES), f32),
            pltpu.VMEM((chans // LANES, tok_rows, LANES), f32),
        ],
        compiler_params=params,
        cost_estimate=cost(900, 18 * tok_rows * chans),
        name="far_part",
    )(base, doc_lengths, states, enter, near, q_short, residual, decay_rate, weight, norm_gain.reshape(1, chans))
    if alone:
        return tuple(outs)
    hidden_out, hidden, sums = outs
    square_sum = lax.psum(jnp.sum(sums, axis=1), "grp")
    inverse_rms = lax.rsqrt(square_sum / (chans * grp) + 1e-06)
    normed = (hidden * inverse_rms[:, None] * norm_gain[None, :]).astype(bf16)
    return (hidden_out, normed)


def solution(mesh):
    return jax.shard_map(
        shards,
        mesh=mesh,
        in_specs=(
            P("ctx", "grp"),
            P("ctx", "grp"),
            P("ctx", "grp"),
            P(None, None, "grp"),
            P(None, "grp"),
            P(None, "grp"),
            P(),
            P("ctx", "grp"),
            P("grp"),
        ),
        out_specs=(P("ctx", "grp"), P("ctx", "grp")),
        check_vma=False,
    )
```

```python
import functools

import jax
import jax.numpy as jnp
from jax import lax
from jax.experimental import pallas as pl
from jax.experimental.pallas import tpu as pltpu
from jax.sharding import PartitionSpec as P

SUBS = 8
LANES = 128
VMEM_LIMIT = 60 * 1024 * 1024
UNROLL = 2
f32 = jnp.float32
bf16 = jnp.bfloat16


def from_behind(shard, axis, by):
    count = lax.axis_size(axis)
    pairs = [(i, i + by) for i in range(count) if 0 <= i + by < count]
    return lax.ppermute(shard, axis, pairs)


def doc_start_rows(len_ref, base, span):
    rows = lax.broadcasted_iota(jnp.int32, (SUBS, LANES), 0) * span + base
    starts = [jnp.int32(0)]
    for d in range(len_ref.shape[0] - 1):
        starts.append(starts[-1] + len_ref[d])
    out = []
    for j in range(span):
        pos = rows + j
        best = jnp.zeros((SUBS, LANES), jnp.int32)
        for start in starts[1:]:
            best = jnp.where(pos >= start, start, best)
        out.append(best)
    return rows, out


def flag(cond):
    return jnp.where(cond, 1.0, 0.0).astype(f32)


def each_tile(count, tile):
    def group(i, carry):
        for slot in range(UNROLL):
            tile(i * UNROLL + slot, slot)
        return carry

    lax.fori_loop(0, count // UNROLL, group, 0)


def row_of(ref, index):
    return jnp.broadcast_to(ref[pl.ds(index, 1), :], (SUBS, LANES))


def spread(x, scratch, span):
    scratch[...] = x.astype(f32)
    return [scratch[pl.ds(j, SUBS, stride=span), :] for j in range(span)]


def short_conv(steps, rim, taps, keep_one, keep_two):
    top = lax.broadcasted_iota(jnp.int32, (SUBS, LANES), 0) == 0
    rim = rim.astype(f32)
    behind_one = jnp.where(top, jnp.broadcast_to(rim[1:2], (SUBS, LANES)), pltpu.roll(steps[-1], 1, 0))
    behind_two = jnp.where(top, jnp.broadcast_to(rim[0:1], (SUBS, LANES)), pltpu.roll(steps[-2], 1, 0))
    padded = [behind_two, behind_one] + steps
    taps = [jnp.broadcast_to(taps[m : m + 1], (SUBS, LANES)) for m in range(3)]
    return [
        taps[0] * padded[j + 2]
        + (taps[1] * padded[j + 1]) * keep_one[j]
        + (taps[2] * padded[j]) * keep_two[j]
        for j in range(len(steps))
    ]


def state_kernel(
    base_ref, len_ref, key_ref, value_ref, rim_ref, taps_ref, rate_ref, weight_ref,
    gate_ref, state_ref, end_ref,
    masks, wide_k, wide_v, all_tables, all_ends,
    *, span, modes, width,
):
    @pl.when(pl.program_id(0) == 0)
    def _():
        rows, starts = doc_start_rows(len_ref, base_ref[0], span)
        for j in range(span):
            masks[0, j] = flag(starts[j] < rows + j)
            masks[1, j] = flag(starts[j] < rows + (j - 1))
            masks[2, j] = flag(starts[span - 1] <= rows + j)
        sub = lax.broadcasted_iota(jnp.int32, (SUBS, LANES), 0)
        through = flag(starts[span - 1] < rows)
        one = through * flag(sub >= 1)
        two = one * pltpu.roll(one, 1, 0) * flag(sub >= 2)
        four = two * pltpu.roll(two, 2, 0) * flag(sub >= 4)
        masks[3, 0] = one
        masks[3, 1] = two
        masks[3, 2] = four
        masks[3, 3] = flag(sub >= 1)

    def tile(i, slot):
        lane = pl.multiple_of(i * LANES, LANES)
        cols = pl.ds(lane, LANES)
        tables, ends = all_tables.at[slot], all_ends.at[slot]
        keep_one = [masks[0, j] for j in range(span)]
        keep_two = [masks[1, j] for j in range(span)]
        k_steps = spread(key_ref[:, cols], wide_k.at[slot], span)
        v_steps = spread(value_ref[:, cols], wide_v.at[slot], span)
        k_short = short_conv(k_steps, rim_ref[1, :, cols], taps_ref[1, :, cols], keep_one, keep_two)
        v_short = short_conv(v_steps, rim_ref[2, :, cols], taps_ref[2, :, cols], keep_one, keep_two)
        gates = []
        for j in range(0, span, 2):
            pair = jnp.concatenate([k_short[j] * v_short[j], k_short[j + 1] * v_short[j + 1]], axis=0).astype(bf16)
            gate_ref[pl.ds(j * SUBS, 2 * SUBS), cols] = pair
            pair = pair.astype(f32)
            gates += [pair[:SUBS] * masks[2, j], pair[SUBS:] * masks[2, j + 1]]
        rate = rate_ref[:, cols]
        tables[0] = jnp.exp(-rate)
        tables[1] = jnp.exp(-float(span) * rate)
        tables[2] = jnp.exp(-float(2 * span) * rate)
        tables[3] = jnp.exp(-float(4 * span) * rate)
        tables[4] = weight_ref[:, cols]
        decay = [row_of(tables.at[0], n) for n in range(modes)]
        state = [gates[0]] * modes
        for j in range(1, span):
            state = [decay[n] * state[n] + gates[j] for n in range(modes)]
        for n in range(modes):
            x = state[n]
            x = x + (row_of(tables.at[1], n) * masks[3, 0]) * pltpu.roll(x, 1, 0)
            x = x + (row_of(tables.at[2], n) * masks[3, 1]) * pltpu.roll(x, 2, 0)
            x = x + (row_of(tables.at[3], n) * masks[3, 2]) * pltpu.roll(x, 4, 0)
            ends[pl.ds(n, 1), :] = x[SUBS - 1 :]
            state_ref[pl.ds(n * SUBS, SUBS), cols] = (row_of(tables.at[4], n) * masks[3, 3]) * pltpu.roll(x, 1, 0)
        if width:
            end_ref[lax.div(lane, width), :, pl.ds(pl.multiple_of(lax.rem(lane, width), LANES), LANES)] = ends[...].astype(bf16)
        else:
            end_ref[:, cols] = ends[...].astype(bf16)

    each_tile(key_ref.shape[1] // LANES, tile)


def keep_masks(base_ref, len_ref, masks, span):
    rows, starts = doc_start_rows(len_ref, base_ref[0], span)
    for j in range(span):
        masks[0, j] = flag(starts[j] < rows + j)
        masks[1, j] = flag(starts[j] < rows + (j - 1))


def near_kernel(base_ref, len_ref, gate_ref, rate_ref, weight_ref, near_ref, masks, *, span, modes):
    @pl.when(pl.program_id(0) == 0)
    def _():
        keep_masks(base_ref, len_ref, masks, span)

    def tile(i, slot):
        cols = pl.ds(pl.multiple_of(i * LANES, LANES), LANES)
        decay = jnp.exp(-rate_ref[:, cols])
        term = weight_ref[:, cols]
        taps = []
        for lag in range(span):
            part = term[:SUBS]
            for n in range(SUBS, modes, SUBS):
                part = part + term[n : n + SUBS]
            for shift in (1, 2, 4):
                part = part + pltpu.roll(part, shift, 0)
            taps.append(part)
            term = term * decay
        live = []
        for j in range(span):
            if j % 2 == 0:
                pair = gate_ref[pl.ds(j * SUBS, 2 * SUBS), cols].astype(f32)
            keep = masks[0, j]
            live = [g * keep for g in live]
            live.append(pair[(j % 2) * SUBS : (j % 2 + 1) * SUBS])
            total = taps[0] * live[j]
            for lag in range(1, j + 1):
                total = total + taps[lag] * live[j - lag]
            near_ref[pl.ds(j * SUBS, SUBS), cols] = total

    each_tile(gate_ref.shape[1] // LANES, tile)


def query_kernel(base_ref, len_ref, query_ref, rim_ref, taps_ref, short_ref, masks, wide_q, *, span):
    @pl.when(pl.program_id(0) == 0)
    def _():
        keep_masks(base_ref, len_ref, masks, span)

    def tile(i, slot):
        cols = pl.ds(pl.multiple_of(i * LANES, LANES), LANES)
        keep_one = [masks[0, j] for j in range(span)]
        keep_two = [masks[1, j] for j in range(span)]
        q_steps = spread(query_ref[:, cols], wide_q.at[slot], span)
        q_short = short_conv(q_steps, rim_ref[0, :, cols], taps_ref[0, :, cols], keep_one, keep_two)
        for j in range(span):
            short_ref[pl.ds(j * SUBS, SUBS), cols] = q_short[j]

    each_tile(query_ref.shape[1] // LANES, tile)


def prefix_kernel(len_ref, end_ref, rate_ref, enter_ref, through, *, span):
    blocks = end_ref.shape[0]
    for i in range(blocks):
        through[i] = jnp.float32(1.0)
    start = jnp.int32(0)
    through[0] = jnp.float32(0.0)
    for d in range(len_ref.shape[0] - 1):
        start = start + len_ref[d]
        through[lax.div(start, jnp.int32(span))] = jnp.float32(0.0)
    decay = jnp.exp(-float(span) * rate_ref[...])
    state = jnp.zeros(decay.shape, f32)
    for i in range(blocks):
        enter_ref[i] = state.astype(bf16)
        state = end_ref[i].astype(f32) + (decay * through[i]) * state


def final_kernel(
    base_ref, len_ref, state_ref, enter_ref, near_ref, short_ref, resid_ref, rate_ref, weight_ref, gain_ref,
    *refs,
    span, modes, width, channels,
):
    if channels:
        hidden_ref, normed_ref, masks, all_tables, sums, whole = refs
    else:
        hidden_ref, wide_ref, sum_ref, masks, all_tables, sums, whole = refs
    step = pl.program_id(0)
    tiles = resid_ref.shape[1] // LANES

    @pl.when(step == 0)
    def _():
        rows, starts = doc_start_rows(len_ref, base_ref[0], span)
        for j in range(span):
            masks[0, j] = flag(starts[j] < rows)
        masks[1, 0] = flag(starts[0] < base_ref[0])
        sums[...] = jnp.zeros(sums.shape, f32)

    def tile(i, slot):
        lane = pl.multiple_of(i * LANES, LANES)
        cols = pl.ds(lane, LANES)
        tables = all_tables.at[slot]
        if width:
            enter = enter_ref[lax.div(lane, width), :, pl.ds(pl.multiple_of(lax.rem(lane, width), LANES), LANES)]
        else:
            enter = enter_ref[:, cols]
        rate = rate_ref[:, cols]
        tables[0] = jnp.exp(-rate)
        tables[1] = weight_ref[:, cols] * enter.astype(f32)
        tables[2] = rate
        sub = lax.broadcasted_iota(jnp.int32, (SUBS, LANES), 0).astype(f32) * (-float(span))
        through = masks[1, 0]
        decay = [row_of(tables.at[0], n) for n in range(modes)]
        part = [
            state_ref[pl.ds(n * SUBS, SUBS), cols]
            + (row_of(tables.at[1], n) * through) * jnp.exp(row_of(tables.at[2], n) * sub)
            for n in range(modes)
        ]
        tile_at = step * tiles + i
        for j in range(span):
            part = [part[n] * decay[n] for n in range(modes)]
            total = part
            while len(total) > 1:
                total = [total[m] + total[m + 1] for m in range(0, len(total), 2)]
            conv = near_ref[pl.ds(j * SUBS, SUBS), cols] + total[0] * masks[0, j]
            conv = conv.astype(bf16).astype(f32)
            whole[tile_at, pl.ds(j, SUBS, stride=span), :] = short_ref[pl.ds(j * SUBS, SUBS), cols] * conv
        hidden = whole[tile_at] + resid_ref[:, cols].astype(f32)
        whole[tile_at] = hidden
        hidden_ref[:, cols] = hidden.astype(bf16)
        if not channels:
            wide_ref[:, cols] = hidden
        sums[...] = sums[...] + hidden * hidden

    each_tile(tiles, tile)

    @pl.when(step == pl.num_programs(0) - 1)
    def _():
        if channels:
            inverse = lax.rsqrt(jnp.sum(sums[...], axis=1, keepdims=True) / channels + 1e-06)
            inverse = jnp.broadcast_to(inverse, sums.shape)
            sums[...] = inverse

            def scale(i, carry):
                cols = pl.ds(pl.multiple_of(i * LANES, LANES), LANES)
                normed_ref[:, cols] = (whole[i] * sums[...] * gain_ref[:, cols]).astype(bf16)
                return carry

            lax.fori_loop(0, normed_ref.shape[1] // LANES, scale, 0)
        else:
            sum_ref[...] = sums[...]


def shards(
    query_in, key_in, value_in, short_taps, decay_rate, residues, doc_lengths, residual, norm_gain
):
    tok_rows, chans = query_in.shape
    modes = decay_rate.shape[0]
    span = tok_rows // SUBS
    blocks = lax.axis_size("ctx")
    grp = lax.axis_size("grp")
    few = chans // blocks
    width = few if few % LANES == 0 else 0
    chunk = min(chans, max(1024, width))
    steps = chans // chunk
    ctx_index = lax.axis_index("ctx")
    base = (ctx_index * tok_rows).astype(jnp.int32).reshape(1)
    tails = jnp.stack([query_in[tok_rows - 2 :], key_in[tok_rows - 2 :], value_in[tok_rows - 2 :]])
    rim_rows = from_behind(tails, "ctx", 1)
    weight = residues * jnp.sqrt(-jnp.expm1(-2.0 * decay_rate))

    smem = pl.BlockSpec(memory_space=pltpu.SMEM)

    def rows_spec(rows):
        return pl.BlockSpec((rows, chunk), lambda i: (0, i))

    rim_spec = pl.BlockSpec((3, 2, chunk), lambda i: (0, 0, i))
    taps_spec = pl.BlockSpec((3, 3, chunk), lambda i: (0, 0, i))
    if width:
        end_spec = pl.BlockSpec((chunk // width, modes, width), lambda i: (i, 0, 0))
        end_shape = (blocks, modes, width)
    else:
        end_spec = rows_spec(modes)
        end_shape = (modes, chans)
    params = pltpu.CompilerParams(vmem_limit_bytes=VMEM_LIMIT)
    tile_shape = (SUBS, LANES)

    def cost(per_tile, moved):
        return pl.CostEstimate(flops=per_tile * (chans // LANES) * SUBS * LANES, bytes_accessed=moved, transcendentals=0)

    gates, states, ends = pl.pallas_call(
        functools.partial(state_kernel, span=span, modes=modes, width=width),
        grid=(steps,),
        in_specs=[smem, smem, rows_spec(tok_rows), rows_spec(tok_rows), rim_spec, taps_spec, rows_spec(modes), rows_spec(modes)],
        out_specs=[rows_spec(tok_rows), rows_spec(modes * SUBS), end_spec],
        out_shape=[
            jax.ShapeDtypeStruct((tok_rows, chans), bf16),
            jax.ShapeDtypeStruct((modes * SUBS, chans), f32),
            jax.ShapeDtypeStruct(end_shape, bf16),
        ],
        scratch_shapes=[
            pltpu.VMEM((4, span) + tile_shape, f32),
            pltpu.VMEM((UNROLL, tok_rows, LANES), f32),
            pltpu.VMEM((UNROLL, tok_rows, LANES), f32),
            pltpu.VMEM((UNROLL, 5, modes, LANES), f32),
            pltpu.VMEM((UNROLL, modes, LANES), f32),
        ],
        compiler_params=params,
        cost_estimate=cost(1000, 12 * tok_rows * chans),
        name="block_states",
    )(base, doc_lengths, key_in, value_in, rim_rows, short_taps, decay_rate, weight)

    near = pl.pallas_call(
        functools.partial(near_kernel, span=span, modes=modes),
        grid=(steps,),
        in_specs=[smem, smem, rows_spec(tok_rows), rows_spec(modes), rows_spec(modes)],
        out_specs=rows_spec(tok_rows),
        out_shape=jax.ShapeDtypeStruct((tok_rows, chans), f32),
        scratch_shapes=[pltpu.VMEM((2, span) + tile_shape, f32)],
        compiler_params=params,
        cost_estimate=cost(600, 7 * tok_rows * chans),
        name="near_part",
    )(base, doc_lengths, gates, decay_rate, weight)

    q_short = pl.pallas_call(
        functools.partial(query_kernel, span=span),
        grid=(steps,),
        in_specs=[smem, smem, rows_spec(tok_rows), rim_spec, taps_spec],
        out_specs=rows_spec(tok_rows),
        out_shape=jax.ShapeDtypeStruct((tok_rows, chans), f32),
        scratch_shapes=[pltpu.VMEM((2, span) + tile_shape, f32), pltpu.VMEM((UNROLL, tok_rows, LANES), f32)],
        compiler_params=params,
        cost_estimate=cost(200, 6 * tok_rows * chans),
        name="query_part",
    )(base, doc_lengths, query_in, rim_rows, short_taps)

    if not width:
        ends = ends.reshape(modes, blocks, few).transpose(1, 0, 2)
    moved = lax.all_to_all(ends, "ctx", split_axis=0, concat_axis=0, tiled=True)
    moved, near = lax.optimization_barrier((moved, near))
    rate_few = lax.dynamic_slice_in_dim(decay_rate, ctx_index * few, few, 1)
    enter_few = pl.pallas_call(
        functools.partial(prefix_kernel, span=tok_rows),
        in_specs=[smem, pl.BlockSpec(memory_space=pltpu.VMEM), pl.BlockSpec(memory_space=pltpu.VMEM)],
        out_specs=pl.BlockSpec(memory_space=pltpu.VMEM),
        out_shape=jax.ShapeDtypeStruct((blocks, modes, few), bf16),
        scratch_shapes=[pltpu.SMEM((blocks,), f32)],
        name="block_prefix",
    )(doc_lengths, moved, rate_few)
    enter = lax.all_to_all(enter_few, "ctx", split_axis=0, concat_axis=0, tiled=True)
    if not width:
        enter = enter.transpose(1, 0, 2).reshape(modes, chans)

    alone = grp == 1
    out_specs = [rows_spec(tok_rows)]
    out_shape = [jax.ShapeDtypeStruct((tok_rows, chans), bf16)]
    if alone:
        out_specs.append(pl.BlockSpec((tok_rows, chans), lambda i: (0, 0)))
        out_shape.append(jax.ShapeDtypeStruct((tok_rows, chans), bf16))
    else:
        out_specs += [rows_spec(tok_rows), pl.BlockSpec((tok_rows, LANES), lambda i: (0, 0))]
        out_shape += [jax.ShapeDtypeStruct((tok_rows, chans), f32), jax.ShapeDtypeStruct((tok_rows, LANES), f32)]
    outs = pl.pallas_call(
        functools.partial(final_kernel, span=span, modes=modes, width=width, channels=chans if alone else 0),
        grid=(steps,),
        in_specs=[
            smem, smem, rows_spec(modes * SUBS), end_spec, rows_spec(tok_rows), rows_spec(tok_rows), rows_spec(tok_rows),
            rows_spec(modes), rows_spec(modes), pl.BlockSpec((1, chans), lambda i: (0, 0)),
        ],
        out_specs=out_specs,
        out_shape=out_shape,
        scratch_shapes=[
            pltpu.VMEM((2, span) + tile_shape, f32),
            pltpu.VMEM((UNROLL, 3, modes, LANES), f32),
            pltpu.VMEM((tok_rows, LANES), f32),
            pltpu.VMEM((chans // LANES, tok_rows, LANES), f32),
        ],
        compiler_params=params,
        cost_estimate=cost(900, 18 * tok_rows * chans),
        name="far_part",
    )(base, doc_lengths, states, enter, near, q_short, residual, decay_rate, weight, norm_gain.reshape(1, chans))
    if alone:
        return tuple(outs)
    hidden_out, hidden, sums = outs
    square_sum = lax.psum(jnp.sum(sums, axis=1), "grp")
    inverse_rms = lax.rsqrt(square_sum / (chans * grp) + 1e-06)
    normed = (hidden * inverse_rms[:, None] * norm_gain[None, :]).astype(bf16)
    return (hidden_out, normed)


def solution(mesh):
    return jax.shard_map(
        shards,
        mesh=mesh,
        in_specs=(
            P("ctx", "grp"),
            P("ctx", "grp"),
            P("ctx", "grp"),
            P(None, None, "grp"),
            P(None, "grp"),
            P(None, "grp"),
            P(),
            P("ctx", "grp"),
            P("grp"),
        ),
        out_specs=(P("ctx", "grp"), P("ctx", "grp")),
        check_vma=False,
    )
```

```python
import functools

import jax
import jax.numpy as jnp
from jax import lax
from jax.experimental import pallas as pl
from jax.experimental.pallas import tpu as pltpu
from jax.sharding import PartitionSpec as P

SUBS = 8
LANES = 128
VMEM_LIMIT = 63 * 1024 * 1024
PAIR = 2
f32 = jnp.float32
bf16 = jnp.bfloat16


def from_behind(shard, axis, by):
    count = lax.axis_size(axis)
    pairs = [(i, i + by) for i in range(count) if 0 <= i + by < count]
    return lax.ppermute(shard, axis, pairs)


def doc_start_rows(len_ref, base, span):
    rows = lax.broadcasted_iota(jnp.int32, (SUBS, LANES), 0) * span + base
    starts = [jnp.int32(0)]
    for d in range(len_ref.shape[0] - 1):
        starts.append(starts[-1] + len_ref[d])
    out = []
    for j in range(span):
        pos = rows + j
        best = jnp.zeros((SUBS, LANES), jnp.int32)
        for start in starts[1:]:
            best = jnp.where(pos >= start, start, best)
        out.append(best)
    return rows, out


def flag(cond):
    return jnp.where(cond, 1.0, 0.0).astype(f32)


def each_pair(count, pair):
    def group(i, carry):
        pair(i)
        return carry

    lax.fori_loop(0, count // PAIR, group, 0)


def order_matrix(span, back):
    size = SUBS * span
    rows = lax.broadcasted_iota(jnp.int32, (size, size), 1 if back else 0)
    cols = lax.broadcasted_iota(jnp.int32, (size, size), 0 if back else 1)
    source = (rows % SUBS) * span + rows // SUBS
    return flag(cols == source).astype(bf16)


def reorder(order, x):
    return jnp.dot(order[...], x, preferred_element_type=f32)


def step_rows(x, slot, span):
    return [x[j * SUBS : (j + 1) * SUBS, slot * LANES : (slot + 1) * LANES] for j in range(span)]


def row_of(ref, index):
    return jnp.broadcast_to(ref[pl.ds(index, 1), :], (SUBS, LANES))


def short_conv(steps, rim, taps, keep_one, keep_two):
    top = lax.broadcasted_iota(jnp.int32, (SUBS, LANES), 0) == 0
    rim = rim.astype(f32)
    behind_one = jnp.where(top, jnp.broadcast_to(rim[1:2], (SUBS, LANES)), pltpu.roll(steps[-1], 1, 0))
    behind_two = jnp.where(top, jnp.broadcast_to(rim[0:1], (SUBS, LANES)), pltpu.roll(steps[-2], 1, 0))
    padded = [behind_two, behind_one] + steps
    taps = [jnp.broadcast_to(taps[m : m + 1], (SUBS, LANES)) for m in range(3)]
    return [
        taps[0] * padded[j + 2]
        + (taps[1] * padded[j + 1]) * keep_one[j]
        + (taps[2] * padded[j]) * keep_two[j]
        for j in range(len(steps))
    ]


def state_kernel(
    base_ref, len_ref, key_ref, value_ref, rim_ref, taps_ref, rate_ref, weight_ref,
    gate_ref, state_ref, end_ref,
    masks, order, all_tables, all_ends,
    *, span, modes, width,
):
    @pl.when(pl.program_id(0) == 0)
    def _():
        order[...] = order_matrix(span, False)
        rows, starts = doc_start_rows(len_ref, base_ref[0], span)
        for j in range(span):
            masks[0, j] = flag(starts[j] < rows + j)
            masks[1, j] = flag(starts[j] < rows + (j - 1))
            masks[2, j] = flag(starts[span - 1] <= rows + j)
        sub = lax.broadcasted_iota(jnp.int32, (SUBS, LANES), 0)
        through = flag(starts[span - 1] < rows)
        one = through * flag(sub >= 1)
        two = one * pltpu.roll(one, 1, 0) * flag(sub >= 2)
        four = two * pltpu.roll(two, 2, 0) * flag(sub >= 4)
        masks[3, 0] = one
        masks[3, 1] = two
        masks[3, 2] = four
        masks[3, 3] = flag(sub >= 1)

    def pair(i):
        both = pl.ds(pl.multiple_of(i * (PAIR * LANES), PAIR * LANES), PAIR * LANES)
        k_rows = reorder(order, key_ref[:, both])
        v_rows = reorder(order, value_ref[:, both])
        for slot in range(PAIR):
            tile(i * PAIR + slot, slot, k_rows, v_rows)

    def tile(i, slot, k_rows, v_rows):
        lane = pl.multiple_of(i * LANES, LANES)
        cols = pl.ds(lane, LANES)
        tables, ends = all_tables.at[slot], all_ends.at[slot]
        keep_one = [masks[0, j] for j in range(span)]
        keep_two = [masks[1, j] for j in range(span)]
        k_steps = step_rows(k_rows, slot, span)
        v_steps = step_rows(v_rows, slot, span)
        k_short = short_conv(k_steps, rim_ref[1, :, cols], taps_ref[1, :, cols], keep_one, keep_two)
        v_short = short_conv(v_steps, rim_ref[2, :, cols], taps_ref[2, :, cols], keep_one, keep_two)
        gates = []
        for j in range(0, span, 2):
            pair = jnp.concatenate([k_short[j] * v_short[j], k_short[j + 1] * v_short[j + 1]], axis=0).astype(bf16)
            gate_ref[pl.ds(j * SUBS, 2 * SUBS), cols] = pair
            pair = pair.astype(f32)
            gates += [pair[:SUBS] * masks[2, j], pair[SUBS:] * masks[2, j + 1]]
        rate = rate_ref[:, cols]
        tables[0] = jnp.exp(-rate)
        tables[1] = jnp.exp(-float(span) * rate)
        tables[2] = jnp.exp(-float(2 * span) * rate)
        tables[3] = jnp.exp(-float(4 * span) * rate)
        tables[4] = weight_ref[:, cols]
        decay = [row_of(tables.at[0], n) for n in range(modes)]
        state = [gates[0]] * modes
        for j in range(1, span):
            state = [decay[n] * state[n] + gates[j] for n in range(modes)]
        for n in range(modes):
            x = state[n]
            x = x + (row_of(tables.at[1], n) * masks[3, 0]) * pltpu.roll(x, 1, 0)
            x = x + (row_of(tables.at[2], n) * masks[3, 1]) * pltpu.roll(x, 2, 0)
            x = x + (row_of(tables.at[3], n) * masks[3, 2]) * pltpu.roll(x, 4, 0)
            ends[pl.ds(n, 1), :] = x[SUBS - 1 :]
            state_ref[pl.ds(n * SUBS, SUBS), cols] = (row_of(tables.at[4], n) * masks[3, 3]) * pltpu.roll(x, 1, 0)
        if width:
            end_ref[lax.div(lane, width), :, pl.ds(pl.multiple_of(lax.rem(lane, width), LANES), LANES)] = ends[...].astype(bf16)
        else:
            end_ref[:, cols] = ends[...].astype(bf16)

    each_pair(key_ref.shape[1] // LANES, pair)


def tail_kernel(query_ref, key_ref, value_ref, tail_ref):
    for i, ref in enumerate((query_ref, key_ref, value_ref)):
        rows = ref[...].astype(f32)
        tail_ref[i] = rows[rows.shape[0] - 2 :].astype(bf16)


def keep_masks(base_ref, len_ref, masks, span):
    rows, starts = doc_start_rows(len_ref, base_ref[0], span)
    for j in range(span):
        masks[0, j] = flag(starts[j] < rows + j)
        masks[1, j] = flag(starts[j] < rows + (j - 1))


def near_kernel(base_ref, len_ref, gate_ref, rate_ref, weight_ref, near_ref, masks, *, span, modes):
    @pl.when(pl.program_id(0) == 0)
    def _():
        keep_masks(base_ref, len_ref, masks, span)

    def tile(i):
        cols = pl.ds(pl.multiple_of(i * LANES, LANES), LANES)
        decay = jnp.exp(-rate_ref[:, cols])
        term = weight_ref[:, cols]
        taps = []
        for lag in range(span):
            part = term[:SUBS]
            for n in range(SUBS, modes, SUBS):
                part = part + term[n : n + SUBS]
            for shift in (1, 2, 4):
                part = part + pltpu.roll(part, shift, 0)
            taps.append(part)
            term = term * decay
        live = []
        for j in range(span):
            if j % 2 == 0:
                pair = gate_ref[pl.ds(j * SUBS, 2 * SUBS), cols].astype(f32)
            keep = masks[0, j]
            live = [g * keep for g in live]
            live.append(pair[(j % 2) * SUBS : (j % 2 + 1) * SUBS])
            total = taps[0] * live[j]
            for lag in range(1, j + 1):
                total = total + taps[lag] * live[j - lag]
            near_ref[pl.ds(j * SUBS, SUBS), cols] = total

    def pair(i):
        for slot in range(PAIR):
            tile(i * PAIR + slot)

    each_pair(gate_ref.shape[1] // LANES, pair)


def query_kernel(base_ref, len_ref, query_ref, rim_ref, taps_ref, short_ref, masks, order, *, span):
    @pl.when(pl.program_id(0) == 0)
    def _():
        order[...] = order_matrix(span, False)
        keep_masks(base_ref, len_ref, masks, span)

    def pair(i):
        both = pl.ds(pl.multiple_of(i * (PAIR * LANES), PAIR * LANES), PAIR * LANES)
        q_rows = reorder(order, query_ref[:, both])
        for slot in range(PAIR):
            tile(i * PAIR + slot, slot, q_rows)

    def tile(i, slot, q_rows):
        cols = pl.ds(pl.multiple_of(i * LANES, LANES), LANES)
        keep_one = [masks[0, j] for j in range(span)]
        keep_two = [masks[1, j] for j in range(span)]
        q_steps = step_rows(q_rows, slot, span)
        q_short = short_conv(q_steps, rim_ref[0, :, cols], taps_ref[0, :, cols], keep_one, keep_two)
        for j in range(span):
            short_ref[pl.ds(j * SUBS, SUBS), cols] = q_short[j]

    each_pair(query_ref.shape[1] // LANES, pair)


def prefix_kernel(len_ref, end_ref, rate_ref, enter_ref, through, *, span):
    blocks = end_ref.shape[0]
    for i in range(blocks):
        through[i] = jnp.float32(1.0)
    start = jnp.int32(0)
    through[0] = jnp.float32(0.0)
    for d in range(len_ref.shape[0] - 1):
        start = start + len_ref[d]
        through[lax.div(start, jnp.int32(span))] = jnp.float32(0.0)
    decay = jnp.exp(-float(span) * rate_ref[...])
    state = jnp.zeros(decay.shape, f32)
    for i in range(blocks):
        enter_ref[i] = state.astype(bf16)
        state = end_ref[i].astype(f32) + (decay * through[i]) * state


def final_kernel(
    base_ref, len_ref, state_ref, enter_ref, near_ref, short_ref, resid_ref, rate_ref, weight_ref, gain_ref,
    *refs,
    span, modes, width, channels,
):
    if channels:
        hidden_ref, normed_ref, masks, order, order_back, rounded, all_tables, sums, whole = refs
    else:
        hidden_ref, wide_ref, sum_ref, masks, order, order_back, rounded, all_tables, sums, whole = refs
    step = pl.program_id(0)
    tiles = resid_ref.shape[1] // LANES

    @pl.when(step == 0)
    def _():
        order[...] = order_matrix(span, False)
        order_back[...] = order_matrix(span, True)
        rows, starts = doc_start_rows(len_ref, base_ref[0], span)
        for j in range(span):
            masks[0, j] = flag(starts[j] < rows)
        masks[1, 0] = flag(starts[0] < base_ref[0])
        sums[...] = jnp.zeros(sums.shape, f32)

    def pair(i):
        both = pl.ds(pl.multiple_of(i * (PAIR * LANES), PAIR * LANES), PAIR * LANES)
        resid_rows = reorder(order, resid_ref[:, both])
        squares = [None] * span
        for slot in range(PAIR):
            squares = tile(i * PAIR + slot, slot, resid_rows, squares)
        for j in range(span):
            sums[pl.ds(j * SUBS, SUBS), :] += squares[j]
        hidden_ref[:, both] = reorder(order_back, rounded[...]).astype(bf16)

    def tile(i, slot, resid_rows, squares):
        lane = pl.multiple_of(i * LANES, LANES)
        cols = pl.ds(lane, LANES)
        tables = all_tables.at[slot]
        resid_steps = step_rows(resid_rows, slot, span)
        if width:
            enter = enter_ref[lax.div(lane, width), :, pl.ds(pl.multiple_of(lax.rem(lane, width), LANES), LANES)]
        else:
            enter = enter_ref[:, cols]
        rate = rate_ref[:, cols]
        tables[0] = jnp.exp(-rate)
        tables[1] = weight_ref[:, cols] * enter.astype(f32)
        tables[2] = rate
        sub = lax.broadcasted_iota(jnp.int32, (SUBS, LANES), 0).astype(f32) * (-float(span))
        through = masks[1, 0]
        decay = [row_of(tables.at[0], n) for n in range(modes)]
        part = [
            state_ref[pl.ds(n * SUBS, SUBS), cols]
            + (row_of(tables.at[1], n) * through) * jnp.exp(row_of(tables.at[2], n) * sub)
            for n in range(modes)
        ]
        tile_at = step * tiles + i
        for j in range(span):
            part = [part[n] * decay[n] for n in range(modes)]
            total = part
            while len(total) > 1:
                total = [total[m] + total[m + 1] for m in range(0, len(total), 2)]
            conv = near_ref[pl.ds(j * SUBS, SUBS), cols] + total[0] * masks[0, j]
            conv = conv.astype(bf16).astype(f32)
            hidden = resid_steps[j] + short_ref[pl.ds(j * SUBS, SUBS), cols] * conv
            if channels:
                whole[tile_at, pl.ds(j * SUBS, SUBS), :] = hidden
            else:
                wide_ref[pl.ds(j * SUBS, SUBS), cols] = hidden
            squares[j] = hidden * hidden if slot == 0 else squares[j] + hidden * hidden
            if j % 2 == 1:
                couple = jnp.concatenate([last, hidden], axis=0).astype(bf16)
                rounded[pl.ds((j - 1) * SUBS, 2 * SUBS), pl.ds(slot * LANES, LANES)] = couple
            last = hidden
        return squares

    each_pair(tiles, pair)

    @pl.when(step == pl.num_programs(0) - 1)
    def _():
        if channels:
            inverse = lax.rsqrt(jnp.sum(sums[...], axis=1, keepdims=True) / channels + 1e-06)
            sums[...] = jnp.broadcast_to(inverse, sums.shape)

            def scale(i):
                both = pl.ds(pl.multiple_of(i * (PAIR * LANES), PAIR * LANES), PAIR * LANES)
                for slot in range(PAIR):
                    cols = pl.ds(pl.multiple_of((i * PAIR + slot) * LANES, LANES), LANES)
                    normed = whole[i * PAIR + slot] * sums[...] * gain_ref[:, cols]
                    rounded[:, pl.ds(slot * LANES, LANES)] = normed.astype(bf16)
                normed_ref[:, both] = reorder(order_back, rounded[...]).astype(bf16)

            each_pair(normed_ref.shape[1] // LANES, scale)
        else:
            sum_ref[...] = sums[...]


def shards(
    query_in, key_in, value_in, short_taps, decay_rate, residues, doc_lengths, residual, norm_gain
):
    tok_rows, chans = query_in.shape
    modes = decay_rate.shape[0]
    span = tok_rows // SUBS
    blocks = lax.axis_size("ctx")
    grp = lax.axis_size("grp")
    few = chans // blocks
    width = few if few % LANES == 0 else 0
    chunk = min(chans, max(1024, width))
    steps = chans // chunk
    ctx_index = lax.axis_index("ctx")
    base = (ctx_index * tok_rows).astype(jnp.int32).reshape(1)
    params = pltpu.CompilerParams(vmem_limit_bytes=VMEM_LIMIT)
    last_rows = pl.BlockSpec((16, chans), lambda i: (tok_rows // 16 - 1, 0))
    tails = pl.pallas_call(
        tail_kernel,
        grid=(1,),
        in_specs=[last_rows] * 3,
        out_specs=pl.BlockSpec((3, 2, chans), lambda i: (0, 0, 0)),
        out_shape=jax.ShapeDtypeStruct((3, 2, chans), bf16),
        compiler_params=params,
        name="tails",
    )(query_in, key_in, value_in)
    rim_rows = from_behind(tails, "ctx", 1)
    weight = residues * jnp.sqrt(-jnp.expm1(-2.0 * decay_rate))

    smem = pl.BlockSpec(memory_space=pltpu.SMEM)

    def rows_spec(rows):
        return pl.BlockSpec((rows, chunk), lambda i: (0, i))

    rim_spec = pl.BlockSpec((3, 2, chunk), lambda i: (0, 0, i))
    taps_spec = pl.BlockSpec((3, 3, chunk), lambda i: (0, 0, i))
    if width:
        end_spec = pl.BlockSpec((chunk // width, modes, width), lambda i: (i, 0, 0))
        end_shape = (blocks, modes, width)
    else:
        end_spec = rows_spec(modes)
        end_shape = (modes, chans)
    params = pltpu.CompilerParams(vmem_limit_bytes=VMEM_LIMIT)
    tile_shape = (SUBS, LANES)

    def cost(per_tile, moved):
        return pl.CostEstimate(flops=per_tile * (chans // LANES) * SUBS * LANES, bytes_accessed=moved, transcendentals=0)

    gates, states, ends = pl.pallas_call(
        functools.partial(state_kernel, span=span, modes=modes, width=width),
        grid=(steps,),
        in_specs=[smem, smem, rows_spec(tok_rows), rows_spec(tok_rows), rim_spec, taps_spec, rows_spec(modes), rows_spec(modes)],
        out_specs=[rows_spec(tok_rows), rows_spec(modes * SUBS), end_spec],
        out_shape=[
            jax.ShapeDtypeStruct((tok_rows, chans), bf16),
            jax.ShapeDtypeStruct((modes * SUBS, chans), f32),
            jax.ShapeDtypeStruct(end_shape, bf16),
        ],
        scratch_shapes=[
            pltpu.VMEM((4, span) + tile_shape, f32),
            pltpu.VMEM((tok_rows, tok_rows), bf16),
            pltpu.VMEM((PAIR, 5, modes, LANES), f32),
            pltpu.VMEM((PAIR, modes, LANES), f32),
        ],
        compiler_params=params,
        cost_estimate=cost(1000, 12 * tok_rows * chans),
        name="block_states",
    )(base, doc_lengths, key_in, value_in, rim_rows, short_taps, decay_rate, weight)

    near = pl.pallas_call(
        functools.partial(near_kernel, span=span, modes=modes),
        grid=(steps,),
        in_specs=[smem, smem, rows_spec(tok_rows), rows_spec(modes), rows_spec(modes)],
        out_specs=rows_spec(tok_rows),
        out_shape=jax.ShapeDtypeStruct((tok_rows, chans), f32),
        scratch_shapes=[pltpu.VMEM((2, span) + tile_shape, f32)],
        compiler_params=params,
        cost_estimate=cost(600, 7 * tok_rows * chans),
        name="near_part",
    )(base, doc_lengths, gates, decay_rate, weight)

    q_short = pl.pallas_call(
        functools.partial(query_kernel, span=span),
        grid=(steps,),
        in_specs=[smem, smem, rows_spec(tok_rows), rim_spec, taps_spec],
        out_specs=rows_spec(tok_rows),
        out_shape=jax.ShapeDtypeStruct((tok_rows, chans), f32),
        scratch_shapes=[pltpu.VMEM((2, span) + tile_shape, f32), pltpu.VMEM((tok_rows, tok_rows), bf16)],
        compiler_params=params,
        cost_estimate=cost(200, 6 * tok_rows * chans),
        name="query_part",
    )(base, doc_lengths, query_in, rim_rows, short_taps)

    if not width:
        ends = ends.reshape(modes, blocks, few).transpose(1, 0, 2)
    moved = lax.all_to_all(ends, "ctx", split_axis=0, concat_axis=0, tiled=True)
    moved, near = lax.optimization_barrier((moved, near))
    rate_few = lax.dynamic_slice_in_dim(decay_rate, ctx_index * few, few, 1)
    enter_few = pl.pallas_call(
        functools.partial(prefix_kernel, span=tok_rows),
        in_specs=[smem, pl.BlockSpec(memory_space=pltpu.VMEM), pl.BlockSpec(memory_space=pltpu.VMEM)],
        out_specs=pl.BlockSpec(memory_space=pltpu.VMEM),
        out_shape=jax.ShapeDtypeStruct((blocks, modes, few), bf16),
        scratch_shapes=[pltpu.SMEM((blocks,), f32)],
        compiler_params=params,
        name="block_prefix",
    )(doc_lengths, moved, rate_few)
    enter = lax.all_to_all(enter_few, "ctx", split_axis=0, concat_axis=0, tiled=True)
    if not width:
        enter = enter.transpose(1, 0, 2).reshape(modes, chans)

    alone = grp == 1
    out_specs = [rows_spec(tok_rows)]
    out_shape = [jax.ShapeDtypeStruct((tok_rows, chans), bf16)]
    if alone:
        out_specs.append(pl.BlockSpec((tok_rows, chans), lambda i: (0, 0)))
        out_shape.append(jax.ShapeDtypeStruct((tok_rows, chans), bf16))
    else:
        out_specs += [rows_spec(tok_rows), pl.BlockSpec((tok_rows, LANES), lambda i: (0, 0))]
        out_shape += [jax.ShapeDtypeStruct((tok_rows, chans), f32), jax.ShapeDtypeStruct((tok_rows, LANES), f32)]
    outs = pl.pallas_call(
        functools.partial(final_kernel, span=span, modes=modes, width=width, channels=chans if alone else 0),
        grid=(steps,),
        in_specs=[
            smem, smem, rows_spec(modes * SUBS), end_spec, rows_spec(tok_rows), rows_spec(tok_rows), rows_spec(tok_rows),
            rows_spec(modes), rows_spec(modes), pl.BlockSpec((1, chans), lambda i: (0, 0)),
        ],
        out_specs=out_specs,
        out_shape=out_shape,
        scratch_shapes=[
            pltpu.VMEM((2, span) + tile_shape, f32),
            pltpu.VMEM((tok_rows, tok_rows), bf16),
            pltpu.VMEM((tok_rows, tok_rows), bf16),
            pltpu.VMEM((tok_rows, PAIR * LANES), bf16),
            pltpu.VMEM((PAIR, 3, modes, LANES), f32),
            pltpu.VMEM((tok_rows, LANES), f32),
            pltpu.VMEM((chans // LANES, tok_rows, LANES), f32),
        ],
        compiler_params=params,
        cost_estimate=cost(900, 18 * tok_rows * chans),
        name="far_part",
    )(base, doc_lengths, states, enter, near, q_short, residual, decay_rate, weight, norm_gain.reshape(1, chans))
    if alone:
        return tuple(outs)
    hidden_out, hidden, sums = outs
    square_sum = lax.psum(jnp.sum(sums, axis=1), "grp")
    inverse_rms = lax.rsqrt(square_sum / (chans * grp) + 1e-06)
    normed = (hidden * inverse_rms[:, None] * norm_gain[None, :]).astype(bf16)
    normed = normed.reshape(span, SUBS, chans).transpose(1, 0, 2).reshape(tok_rows, chans)
    return (hidden_out, normed)


def solution(mesh):
    return jax.shard_map(
        shards,
        mesh=mesh,
        in_specs=(
            P("ctx", "grp"),
            P("ctx", "grp"),
            P("ctx", "grp"),
            P(None, None, "grp"),
            P(None, "grp"),
            P(None, "grp"),
            P(),
            P("ctx", "grp"),
            P("grp"),
        ),
        out_specs=(P("ctx", "grp"), P("ctx", "grp")),
        check_vma=False,
    )
```

```python
import functools
import math

import jax
import jax.numpy as jnp
from jax import lax
from jax.experimental import pallas as pl
from jax.experimental.pallas import tpu as pltpu
from jax.sharding import PartitionSpec as P

SUBS = 8
LANES = 128
VMEM_LIMIT = 63 * 1024 * 1024
f32 = jnp.float32
bf16 = jnp.bfloat16


def from_behind(shard, axis, by):
    count = lax.axis_size(axis)
    pairs = [(i, i + by) for i in range(count) if 0 <= i + by < count]
    return lax.ppermute(shard, axis, pairs)


def doc_start_rows(len_ref, base, span):
    rows = lax.broadcasted_iota(jnp.int32, (SUBS, LANES), 0) * span + base
    starts = [jnp.int32(0)]
    for d in range(len_ref.shape[0] - 1):
        starts.append(starts[-1] + len_ref[d])
    out = []
    for j in range(span):
        pos = rows + j
        best = jnp.zeros((SUBS, LANES), jnp.int32)
        for start in starts[1:]:
            best = jnp.where(pos >= start, start, best)
        out.append(best)
    return rows, out


def flag(cond):
    return jnp.where(cond, 1.0, 0.0).astype(f32)


def each_group(count, most, group):
    size = math.gcd(count, most)

    def step(i, carry):
        group([pl.multiple_of((i * size + m) * LANES, LANES) for m in range(size)])
        return carry

    lax.fori_loop(0, count // size, step, 0)


def cols_of(lane):
    return pl.ds(lane, LANES)


def row_of(ref, index):
    return jnp.broadcast_to(ref[pl.ds(index, 1), :], (SUBS, LANES))


def spread(x, wide, span):
    x = x.astype(f32)
    for b in range(SUBS):
        wide[pl.ds(b * (span + 1), span), :] = x[b * span : (b + 1) * span]


def steps_of(wide, span):
    return [wide[pl.ds(j, SUBS, stride=span + 1), :] for j in range(span)]


def short_conv(steps, rim, taps, keep_one, keep_two):
    top = lax.broadcasted_iota(jnp.int32, (SUBS, LANES), 0) == 0
    rim = rim.astype(f32)
    behind_one = jnp.where(top, jnp.broadcast_to(rim[1:2], (SUBS, LANES)), pltpu.roll(steps[-1], 1, 0))
    behind_two = jnp.where(top, jnp.broadcast_to(rim[0:1], (SUBS, LANES)), pltpu.roll(steps[-2], 1, 0))
    padded = [behind_two, behind_one] + steps
    taps = [jnp.broadcast_to(taps[m : m + 1], (SUBS, LANES)) for m in range(3)]
    return [
        taps[0] * padded[j + 2]
        + (taps[1] * padded[j + 1]) * keep_one[j]
        + (taps[2] * padded[j]) * keep_two[j]
        for j in range(len(steps))
    ]


def state_kernel(
    base_ref, len_ref, key_ref, value_ref, rim_ref, taps_ref, rate_ref, weight_ref,
    gate_ref, state_ref, end_ref,
    masks, wide_k, wide_v, tables, ends, held,
    *, span, modes, width, most,
):
    @pl.when(pl.program_id(0) == 0)
    def _():
        rows, starts = doc_start_rows(len_ref, base_ref[0], span)
        for j in range(span):
            masks[0, j] = flag(starts[j] < rows + j)
            masks[1, j] = flag(starts[j] < rows + (j - 1))
            masks[2, j] = flag(starts[span - 1] <= rows + j)
        sub = lax.broadcasted_iota(jnp.int32, (SUBS, LANES), 0)
        through = flag(starts[span - 1] < rows)
        one = through * flag(sub >= 1)
        two = one * pltpu.roll(one, 1, 0) * flag(sub >= 2)
        four = two * pltpu.roll(two, 2, 0) * flag(sub >= 4)
        masks[3, 0] = one
        masks[3, 1] = two
        masks[3, 2] = four
        masks[3, 3] = flag(sub >= 1)

    def group(lanes):
        for slot, lane in enumerate(lanes):
            spread(key_ref[:, cols_of(lane)], wide_k.at[slot], span)
            spread(value_ref[:, cols_of(lane)], wide_v.at[slot], span)
            rate = rate_ref[:, cols_of(lane)]
            for m, by in enumerate((1, span, 2 * span, 4 * span)):
                tables[slot, m] = jnp.exp(-float(by) * rate)
            tables[slot, 4] = weight_ref[:, cols_of(lane)]
        for slot, lane in enumerate(lanes):
            cols = cols_of(lane)
            keep_one = [masks[0, j] for j in range(span)]
            keep_two = [masks[1, j] for j in range(span)]
            k_short = short_conv(steps_of(wide_k.at[slot], span), rim_ref[1, :, cols], taps_ref[1, :, cols], keep_one, keep_two)
            v_short = short_conv(steps_of(wide_v.at[slot], span), rim_ref[2, :, cols], taps_ref[2, :, cols], keep_one, keep_two)
            for j in range(0, span, 2):
                pair = jnp.concatenate([k_short[j] * v_short[j], k_short[j + 1] * v_short[j + 1]], axis=0).astype(bf16)
                gate_ref[pl.ds(j * SUBS, 2 * SUBS), cols] = pair
                pair = pair.astype(f32)
                held[slot, j] = pair[:SUBS] * masks[2, j]
                held[slot, j + 1] = pair[SUBS:] * masks[2, j + 1]
        states = []
        for slot, lane in enumerate(lanes):
            decay = [row_of(tables.at[slot, 0], n) for n in range(modes)]
            state = [held[slot, 0]] * modes
            for j in range(1, span):
                gate = held[slot, j]
                state = [decay[n] * state[n] + gate for n in range(modes)]
            states.append(state)
        for m, shift in enumerate((1, 2, 4)):
            for slot in range(len(lanes)):
                states[slot] = [
                    x + (row_of(tables.at[slot, m + 1], n) * masks[3, m]) * pltpu.roll(x, shift, 0)
                    for n, x in enumerate(states[slot])
                ]
        for slot, lane in enumerate(lanes):
            for n, x in enumerate(states[slot]):
                ends[slot, pl.ds(n, 1), :] = x[SUBS - 1 :]
                state_ref[pl.ds(n * SUBS, SUBS), cols_of(lane)] = (
                    row_of(tables.at[slot, 4], n) * masks[3, 3]
                ) * pltpu.roll(x, 1, 0)
        for slot, lane in enumerate(lanes):
            end = ends[slot].astype(bf16)
            if width:
                end_ref[lax.div(lane, width), :, cols_of(pl.multiple_of(lax.rem(lane, width), LANES))] = end
            else:
                end_ref[:, cols_of(lane)] = end

    each_group(key_ref.shape[1] // LANES, most, group)


def keep_masks(base_ref, len_ref, masks, span):
    rows, starts = doc_start_rows(len_ref, base_ref[0], span)
    for j in range(span):
        masks[0, j] = flag(starts[j] < rows + j)
        masks[1, j] = flag(starts[j] < rows + (j - 1))


def near_kernel(base_ref, len_ref, gate_ref, rate_ref, weight_ref, near_ref, masks, *, span, modes, most):
    @pl.when(pl.program_id(0) == 0)
    def _():
        keep_masks(base_ref, len_ref, masks, span)

    def group(lanes):
        taps = []
        for lane in lanes:
            decay = jnp.exp(-rate_ref[:, cols_of(lane)])
            term = weight_ref[:, cols_of(lane)]
            parts = []
            for lag in range(span):
                part = term[:SUBS]
                for n in range(SUBS, modes, SUBS):
                    part = part + term[n : n + SUBS]
                parts.append(part)
                term = term * decay
            taps.append(parts)
        for shift in (1, 2, 4):
            taps = [[part + pltpu.roll(part, shift, 0) for part in parts] for parts in taps]
        for parts, lane in zip(taps, lanes):
            live = []
            for j in range(span):
                if j % 2 == 0:
                    pair = gate_ref[pl.ds(j * SUBS, 2 * SUBS), cols_of(lane)].astype(f32)
                keep = masks[0, j]
                live = [g * keep for g in live]
                live.append(pair[(j % 2) * SUBS : (j % 2 + 1) * SUBS])
                total = parts[0] * live[j]
                for lag in range(1, j + 1):
                    total = total + parts[lag] * live[j - lag]
                near_ref[pl.ds(j * SUBS, SUBS), cols_of(lane)] = total

    each_group(gate_ref.shape[1] // LANES, most, group)


def query_kernel(base_ref, len_ref, query_ref, rim_ref, taps_ref, short_ref, masks, wide_q, *, span, most):
    @pl.when(pl.program_id(0) == 0)
    def _():
        keep_masks(base_ref, len_ref, masks, span)

    def group(lanes):
        for slot, lane in enumerate(lanes):
            spread(query_ref[:, cols_of(lane)], wide_q.at[slot], span)
        for slot, lane in enumerate(lanes):
            cols = cols_of(lane)
            keep_one = [masks[0, j] for j in range(span)]
            keep_two = [masks[1, j] for j in range(span)]
            q_short = short_conv(steps_of(wide_q.at[slot], span), rim_ref[0, :, cols], taps_ref[0, :, cols], keep_one, keep_two)
            for j in range(span):
                short_ref[pl.ds(j * SUBS, SUBS), cols] = q_short[j]

    each_group(query_ref.shape[1] // LANES, most, group)


def prefix_kernel(len_ref, end_ref, rate_ref, enter_ref, through, *, span):
    blocks = end_ref.shape[0]
    for i in range(blocks):
        through[i] = jnp.float32(1.0)
    start = jnp.int32(0)
    through[0] = jnp.float32(0.0)
    for d in range(len_ref.shape[0] - 1):
        start = start + len_ref[d]
        through[lax.div(start, jnp.int32(span))] = jnp.float32(0.0)
    decay = jnp.exp(-float(span) * rate_ref[...])
    state = jnp.zeros(decay.shape, f32)
    for i in range(blocks):
        enter_ref[i] = state.astype(bf16)
        state = end_ref[i].astype(f32) + (decay * through[i]) * state


def final_kernel(
    base_ref, len_ref, state_ref, enter_ref, near_ref, short_ref, resid_ref, rate_ref, weight_ref, gain_ref,
    *refs,
    span, modes, width, channels, most,
):
    if channels:
        hidden_ref, normed_ref, masks, wide, tables, sums, whole = refs
    else:
        hidden_ref, wide_ref, sum_ref, masks, wide, tables, sums, whole = refs
    step = pl.program_id(0)
    tiles = resid_ref.shape[1] // LANES

    @pl.when(step == 0)
    def _():
        rows, starts = doc_start_rows(len_ref, base_ref[0], span)
        for j in range(span):
            masks[0, j] = flag(starts[j] < rows)
        masks[1, 0] = flag(starts[0] < base_ref[0])
        sums[...] = jnp.zeros(sums.shape, f32)

    def group(lanes):
        sub = lax.broadcasted_iota(jnp.int32, (SUBS, LANES), 0).astype(f32) * (-float(span))
        through = masks[1, 0]
        for slot, lane in enumerate(lanes):
            if width:
                enter = enter_ref[lax.div(lane, width), :, cols_of(pl.multiple_of(lax.rem(lane, width), LANES))]
            else:
                enter = enter_ref[:, cols_of(lane)]
            rate = rate_ref[:, cols_of(lane)]
            tables[slot, 0] = jnp.exp(-rate)
            tables[slot, 1] = weight_ref[:, cols_of(lane)] * enter.astype(f32)
            tables[slot, 2] = rate
        parts = [
            [
                state_ref[pl.ds(n * SUBS, SUBS), cols_of(lane)]
                + (row_of(tables.at[slot, 1], n) * through) * jnp.exp(row_of(tables.at[slot, 2], n) * sub)
                for n in range(modes)
            ]
            for slot, lane in enumerate(lanes)
        ]
        for slot, lane in enumerate(lanes):
            part = parts[slot]
            decay = [row_of(tables.at[slot, 0], n) for n in range(modes)]
            for j in range(span):
                part = [part[n] * decay[n] for n in range(modes)]
                total = part
                while len(total) > 1:
                    total = [total[m] + total[m + 1] for m in range(0, len(total), 2)]
                conv = near_ref[pl.ds(j * SUBS, SUBS), cols_of(lane)] + total[0] * masks[0, j]
                conv = conv.astype(bf16).astype(f32)
                wide[slot, pl.ds(j, SUBS, stride=span + 1), :] = short_ref[pl.ds(j * SUBS, SUBS), cols_of(lane)] * conv
        for b in range(SUBS):
            rows = pl.ds(b * span, span)
            squares = sums[rows, :]
            for slot, lane in enumerate(lanes):
                hidden = wide[slot, pl.ds(b * (span + 1), span), :] + resid_ref[rows, cols_of(lane)].astype(f32)
                if channels:
                    whole[lax.div(lane, LANES) + step * tiles, rows, :] = hidden
                else:
                    wide_ref[rows, cols_of(lane)] = hidden
                hidden_ref[rows, cols_of(lane)] = hidden.astype(bf16)
                squares = squares + hidden * hidden
            sums[rows, :] = squares

    each_group(tiles, most, group)

    @pl.when(step == pl.num_programs(0) - 1)
    def _():
        if channels:
            inverse = lax.rsqrt(jnp.sum(sums[...], axis=1, keepdims=True) / channels + 1e-06)
            sums[...] = jnp.broadcast_to(inverse, sums.shape)

            def scale(lanes):
                for lane in lanes:
                    normed = whole[lax.div(lane, LANES)] * sums[...] * gain_ref[:, cols_of(lane)]
                    normed_ref[:, cols_of(lane)] = normed.astype(bf16)

            each_group(normed_ref.shape[1] // LANES, 4, scale)
        else:
            sum_ref[...] = sums[...]


def shards(
    query_in, key_in, value_in, short_taps, decay_rate, residues, doc_lengths, residual, norm_gain
):
    tok_rows, chans = query_in.shape
    modes = decay_rate.shape[0]
    span = tok_rows // SUBS
    blocks = lax.axis_size("ctx")
    grp = lax.axis_size("grp")
    few = chans // blocks
    width = few if few % LANES == 0 else 0
    chunk = min(chans, max(1024, width))
    steps = chans // chunk
    ctx_index = lax.axis_index("ctx")
    base = (ctx_index * tok_rows).astype(jnp.int32).reshape(1)
    tails = jnp.stack([query_in[tok_rows - 2 :], key_in[tok_rows - 2 :], value_in[tok_rows - 2 :]])
    rim_rows = from_behind(tails, "ctx", 1)
    weight = residues * jnp.sqrt(-jnp.expm1(-2.0 * decay_rate))

    smem = pl.BlockSpec(memory_space=pltpu.SMEM)

    def rows_spec(rows):
        return pl.BlockSpec((rows, chunk), lambda i: (0, i))

    rim_spec = pl.BlockSpec((3, 2, chunk), lambda i: (0, 0, i))
    taps_spec = pl.BlockSpec((3, 3, chunk), lambda i: (0, 0, i))
    if width:
        end_spec = pl.BlockSpec((chunk // width, modes, width), lambda i: (i, 0, 0))
        end_shape = (blocks, modes, width)
    else:
        end_spec = rows_spec(modes)
        end_shape = (modes, chans)
    params = pltpu.CompilerParams(vmem_limit_bytes=VMEM_LIMIT)
    tile_shape = (SUBS, LANES)
    wide_rows = SUBS * (span + 1)

    def cost(per_tile, moved):
        return pl.CostEstimate(flops=per_tile * (chans // LANES) * SUBS * LANES, bytes_accessed=moved, transcendentals=0)

    gates, states, ends = pl.pallas_call(
        functools.partial(state_kernel, span=span, modes=modes, width=width, most=2),
        grid=(steps,),
        in_specs=[smem, smem, rows_spec(tok_rows), rows_spec(tok_rows), rim_spec, taps_spec, rows_spec(modes), rows_spec(modes)],
        out_specs=[rows_spec(tok_rows), rows_spec(modes * SUBS), end_spec],
        out_shape=[
            jax.ShapeDtypeStruct((tok_rows, chans), bf16),
            jax.ShapeDtypeStruct((modes * SUBS, chans), f32),
            jax.ShapeDtypeStruct(end_shape, bf16),
        ],
        scratch_shapes=[
            pltpu.VMEM((4, span) + tile_shape, f32),
            pltpu.VMEM((2, wide_rows, LANES), f32),
            pltpu.VMEM((2, wide_rows, LANES), f32),
            pltpu.VMEM((2, 5, modes, LANES), f32),
            pltpu.VMEM((2, modes, LANES), f32),
            pltpu.VMEM((2, span) + tile_shape, f32),
        ],
        compiler_params=params,
        cost_estimate=cost(1000, 12 * tok_rows * chans),
        name="block_states",
    )(base, doc_lengths, key_in, value_in, rim_rows, short_taps, decay_rate, weight)

    near = pl.pallas_call(
        functools.partial(near_kernel, span=span, modes=modes, most=4),
        grid=(steps,),
        in_specs=[smem, smem, rows_spec(tok_rows), rows_spec(modes), rows_spec(modes)],
        out_specs=rows_spec(tok_rows),
        out_shape=jax.ShapeDtypeStruct((tok_rows, chans), f32),
        scratch_shapes=[pltpu.VMEM((2, span) + tile_shape, f32)],
        compiler_params=params,
        cost_estimate=cost(600, 7 * tok_rows * chans),
        name="near_part",
    )(base, doc_lengths, gates, decay_rate, weight)

    q_short = pl.pallas_call(
        functools.partial(query_kernel, span=span, most=4),
        grid=(steps,),
        in_specs=[smem, smem, rows_spec(tok_rows), rim_spec, taps_spec],
        out_specs=rows_spec(tok_rows),
        out_shape=jax.ShapeDtypeStruct((tok_rows, chans), f32),
        scratch_shapes=[pltpu.VMEM((2, span) + tile_shape, f32), pltpu.VMEM((4, wide_rows, LANES), f32)],
        compiler_params=params,
        cost_estimate=cost(200, 6 * tok_rows * chans),
        name="query_part",
    )(base, doc_lengths, query_in, rim_rows, short_taps)

    if not width:
        ends = ends.reshape(modes, blocks, few).transpose(1, 0, 2)
    moved = lax.all_to_all(ends, "ctx", split_axis=0, concat_axis=0, tiled=True)
    moved, near = lax.optimization_barrier((moved, near))
    rate_few = lax.dynamic_slice_in_dim(decay_rate, ctx_index * few, few, 1)
    enter_few = pl.pallas_call(
        functools.partial(prefix_kernel, span=tok_rows),
        in_specs=[smem, pl.BlockSpec(memory_space=pltpu.VMEM), pl.BlockSpec(memory_space=pltpu.VMEM)],
        out_specs=pl.BlockSpec(memory_space=pltpu.VMEM),
        out_shape=jax.ShapeDtypeStruct((blocks, modes, few), bf16),
        scratch_shapes=[pltpu.SMEM((blocks,), f32)],
        compiler_params=params,
        name="block_prefix",
    )(doc_lengths, moved, rate_few)
    enter = lax.all_to_all(enter_few, "ctx", split_axis=0, concat_axis=0, tiled=True)
    if not width:
        enter = enter.transpose(1, 0, 2).reshape(modes, chans)

    alone = grp == 1
    out_specs = [rows_spec(tok_rows)]
    out_shape = [jax.ShapeDtypeStruct((tok_rows, chans), bf16)]
    if alone:
        out_specs.append(pl.BlockSpec((tok_rows, chans), lambda i: (0, 0)))
        out_shape.append(jax.ShapeDtypeStruct((tok_rows, chans), bf16))
    else:
        out_specs += [rows_spec(tok_rows), pl.BlockSpec((tok_rows, LANES), lambda i: (0, 0))]
        out_shape += [jax.ShapeDtypeStruct((tok_rows, chans), f32), jax.ShapeDtypeStruct((tok_rows, LANES), f32)]
    outs = pl.pallas_call(
        functools.partial(final_kernel, span=span, modes=modes, width=width, channels=chans if alone else 0, most=2),
        grid=(steps,),
        in_specs=[
            smem, smem, rows_spec(modes * SUBS), end_spec, rows_spec(tok_rows), rows_spec(tok_rows), rows_spec(tok_rows),
            rows_spec(modes), rows_spec(modes), pl.BlockSpec((1, chans), lambda i: (0, 0)),
        ],
        out_specs=out_specs,
        out_shape=out_shape,
        scratch_shapes=[
            pltpu.VMEM((2, span) + tile_shape, f32),
            pltpu.VMEM((2, wide_rows, LANES), f32),
            pltpu.VMEM((2, 3, modes, LANES), f32),
            pltpu.VMEM((tok_rows, LANES), f32),
            pltpu.VMEM((chans // LANES, tok_rows, LANES), f32),
        ],
        compiler_params=params,
        cost_estimate=cost(900, 18 * tok_rows * chans),
        name="far_part",
    )(base, doc_lengths, states, enter, near, q_short, residual, decay_rate, weight, norm_gain.reshape(1, chans))
    if alone:
        return tuple(outs)
    hidden_out, hidden, sums = outs
    square_sum = lax.psum(jnp.sum(sums, axis=1), "grp")
    inverse_rms = lax.rsqrt(square_sum / (chans * grp) + 1e-06)
    normed = (hidden * inverse_rms[:, None] * norm_gain[None, :]).astype(bf16)
    return (hidden_out, normed)


def solution(mesh):
    return jax.shard_map(
        shards,
        mesh=mesh,
        in_specs=(
            P("ctx", "grp"),
            P("ctx", "grp"),
            P("ctx", "grp"),
            P(None, None, "grp"),
            P(None, "grp"),
            P(None, "grp"),
            P(),
            P("ctx", "grp"),
            P("grp"),
        ),
        out_specs=(P("ctx", "grp"), P("ctx", "grp")),
        check_vma=False,
    )
```

```python
import functools
import math

import jax
import jax.numpy as jnp
from jax import lax
from jax.experimental import pallas as pl
from jax.experimental.pallas import tpu as pltpu
from jax.sharding import PartitionSpec as P

SUBS = 8
LANES = 128
MIB = 1024 * 1024
f32 = jnp.float32
bf16 = jnp.bfloat16


def from_behind(shard, axis, by):
    count = lax.axis_size(axis)
    pairs = [(i, i + by) for i in range(count) if 0 <= i + by < count]
    return lax.ppermute(shard, axis, pairs)


def doc_start_rows(len_ref, base, span):
    rows = lax.broadcasted_iota(jnp.int32, (SUBS, LANES), 0) * span + base
    starts = [jnp.int32(0)]
    for d in range(len_ref.shape[0] - 1):
        starts.append(starts[-1] + len_ref[d])
    out = []
    for j in range(span):
        pos = rows + j
        best = jnp.zeros((SUBS, LANES), jnp.int32)
        for start in starts[1:]:
            best = jnp.where(pos >= start, start, best)
        out.append(best)
    return rows, out


def flag(cond):
    return jnp.where(cond, 1.0, 0.0).astype(f32)


def each_group(count, most, group):
    size = math.gcd(count, most)

    def step(i, carry):
        group([pl.multiple_of((i * size + m) * LANES, LANES) for m in range(size)])
        return carry

    lax.fori_loop(0, count // size, step, 0)


def each_chunk(chans, chunk, before, group, after, most):
    def step(c, carry):
        before(c)

        def inner(lanes):
            group([pl.multiple_of(c * chunk + lane, LANES) for lane in lanes])

        each_group(chunk // LANES, most, inner)
        after(c)
        return carry

    lax.fori_loop(0, chans // chunk, step, 0)


def cols_copy(src, dst, sem, c, chunk):
    cols = pl.ds(pl.multiple_of(c * chunk, chunk), chunk)
    return pltpu.make_async_copy(src.at[:, cols], dst.at[:, cols], sem.at[c])


def end_copy(src, dst, sem, c, chunk, width):
    if not width:
        return cols_copy(src, dst, sem, c, chunk)
    rows = pl.ds(c * (chunk // width), chunk // width)
    return pltpu.make_async_copy(src.at[rows], dst.at[rows], sem.at[c])


def cols_of(lane):
    return pl.ds(lane, LANES)


def row_of(ref, index):
    return jnp.broadcast_to(ref[pl.ds(index, 1), :], (SUBS, LANES))


def spread(x, wide, span):
    x = x.astype(f32)
    for b in range(SUBS):
        wide[pl.ds(b * (span + 1), span), :] = x[b * span : (b + 1) * span]


def steps_of(wide, span):
    return [wide[pl.ds(j, SUBS, stride=span + 1), :] for j in range(span)]


def short_conv(steps, rim, taps, keep_one, keep_two):
    top = lax.broadcasted_iota(jnp.int32, (SUBS, LANES), 0) == 0
    rim = rim.astype(f32)
    behind_one = jnp.where(top, jnp.broadcast_to(rim[1:2], (SUBS, LANES)), pltpu.roll(steps[-1], 1, 0))
    behind_two = jnp.where(top, jnp.broadcast_to(rim[0:1], (SUBS, LANES)), pltpu.roll(steps[-2], 1, 0))
    padded = [behind_two, behind_one] + steps
    taps = [jnp.broadcast_to(taps[m : m + 1], (SUBS, LANES)) for m in range(3)]
    return [
        taps[0] * padded[j + 2]
        + (taps[1] * padded[j + 1]) * keep_one[j]
        + (taps[2] * padded[j]) * keep_two[j]
        for j in range(len(steps))
    ]


def state_kernel(
    base_ref, len_ref, key_ref, value_ref, rim_ref, taps_ref, rate_ref, weight_ref,
    gate_ref, state_ref, end_out,
    key_buf, value_buf, end_ref, sems, masks, wide_k, wide_v, tables, ends, held,
    *, span, modes, width, most, chunk,
):
    chans = key_buf.shape[1]

    def fetches(c):
        return [cols_copy(key_ref, key_buf, sems.at[0], c, chunk), cols_copy(value_ref, value_buf, sems.at[1], c, chunk)]

    def store(c):
        return end_copy(end_ref, end_out, sems.at[2], c, chunk, width)

    for c in range(chans // chunk):
        for copy in fetches(c):
            copy.start()

    def prepare():
        rows, starts = doc_start_rows(len_ref, base_ref[0], span)
        for j in range(span):
            masks[0, j] = flag(starts[j] < rows + j)
            masks[1, j] = flag(starts[j] < rows + (j - 1))
            masks[2, j] = flag(starts[span - 1] <= rows + j)
        sub = lax.broadcasted_iota(jnp.int32, (SUBS, LANES), 0)
        through = flag(starts[span - 1] < rows)
        one = through * flag(sub >= 1)
        two = one * pltpu.roll(one, 1, 0) * flag(sub >= 2)
        four = two * pltpu.roll(two, 2, 0) * flag(sub >= 4)
        masks[3, 0] = one
        masks[3, 1] = two
        masks[3, 2] = four
        masks[3, 3] = flag(sub >= 1)

    prepare()

    def group(lanes):
        for slot, lane in enumerate(lanes):
            spread(key_buf[:, cols_of(lane)], wide_k.at[slot], span)
            spread(value_buf[:, cols_of(lane)], wide_v.at[slot], span)
            rate = rate_ref[:, cols_of(lane)]
            for m, by in enumerate((1, span, 2 * span, 4 * span)):
                tables[slot, m] = jnp.exp(-float(by) * rate)
            tables[slot, 4] = weight_ref[:, cols_of(lane)]
        for slot, lane in enumerate(lanes):
            cols = cols_of(lane)
            keep_one = [masks[0, j] for j in range(span)]
            keep_two = [masks[1, j] for j in range(span)]
            k_short = short_conv(steps_of(wide_k.at[slot], span), rim_ref[1, :, cols], taps_ref[1, :, cols], keep_one, keep_two)
            v_short = short_conv(steps_of(wide_v.at[slot], span), rim_ref[2, :, cols], taps_ref[2, :, cols], keep_one, keep_two)
            for j in range(0, span, 2):
                pair = jnp.concatenate([k_short[j] * v_short[j], k_short[j + 1] * v_short[j + 1]], axis=0).astype(bf16)
                gate_ref[pl.ds(j * SUBS, 2 * SUBS), cols] = pair
                pair = pair.astype(f32)
                held[slot, j] = pair[:SUBS] * masks[2, j]
                held[slot, j + 1] = pair[SUBS:] * masks[2, j + 1]
        states = []
        for slot, lane in enumerate(lanes):
            decay = [row_of(tables.at[slot, 0], n) for n in range(modes)]
            state = [held[slot, 0]] * modes
            for j in range(1, span):
                gate = held[slot, j]
                state = [decay[n] * state[n] + gate for n in range(modes)]
            states.append(state)
        for m, shift in enumerate((1, 2, 4)):
            for slot in range(len(lanes)):
                states[slot] = [
                    x + (row_of(tables.at[slot, m + 1], n) * masks[3, m]) * pltpu.roll(x, shift, 0)
                    for n, x in enumerate(states[slot])
                ]
        for slot, lane in enumerate(lanes):
            for n, x in enumerate(states[slot]):
                ends[slot, pl.ds(n, 1), :] = x[SUBS - 1 :]
                state_ref[pl.ds(n * SUBS, SUBS), cols_of(lane)] = (
                    row_of(tables.at[slot, 4], n) * masks[3, 3]
                ) * pltpu.roll(x, 1, 0)
        for slot, lane in enumerate(lanes):
            end = ends[slot].astype(bf16)
            if width:
                end_ref[lax.div(lane, width), :, cols_of(pl.multiple_of(lax.rem(lane, width), LANES))] = end
            else:
                end_ref[:, cols_of(lane)] = end

    def before(c):
        for copy in fetches(c):
            copy.wait()

    each_chunk(chans, chunk, before, group, lambda c: store(c).start(), most)
    for c in range(chans // chunk):
        store(c).wait()


def keep_masks(base_ref, len_ref, masks, span):
    rows, starts = doc_start_rows(len_ref, base_ref[0], span)
    for j in range(span):
        masks[0, j] = flag(starts[j] < rows + j)
        masks[1, j] = flag(starts[j] < rows + (j - 1))


def near_kernel(base_ref, len_ref, gate_ref, rate_ref, weight_ref, near_ref, masks, *, span, modes, most):
    keep_masks(base_ref, len_ref, masks, span)

    def group(lanes):
        taps = []
        for lane in lanes:
            decay = jnp.exp(-rate_ref[:, cols_of(lane)])
            term = weight_ref[:, cols_of(lane)]
            parts = []
            for lag in range(span):
                part = term[:SUBS]
                for n in range(SUBS, modes, SUBS):
                    part = part + term[n : n + SUBS]
                parts.append(part)
                term = term * decay
            taps.append(parts)
        for shift in (1, 2, 4):
            taps = [[part + pltpu.roll(part, shift, 0) for part in parts] for parts in taps]
        for parts, lane in zip(taps, lanes):
            live = []
            for j in range(span):
                if j % 2 == 0:
                    pair = gate_ref[pl.ds(j * SUBS, 2 * SUBS), cols_of(lane)].astype(f32)
                keep = masks[0, j]
                live = [g * keep for g in live]
                live.append(pair[(j % 2) * SUBS : (j % 2 + 1) * SUBS])
                total = parts[0] * live[j]
                for lag in range(1, j + 1):
                    total = total + parts[lag] * live[j - lag]
                near_ref[pl.ds(j * SUBS, SUBS), cols_of(lane)] = total

    each_group(gate_ref.shape[1] // LANES, most, group)


def query_kernel(base_ref, len_ref, query_ref, rim_ref, taps_ref, short_ref, query_buf, sems, masks, wide_q, *, span, most, chunk):
    chans = query_buf.shape[1]

    def fetch(c):
        return cols_copy(query_ref, query_buf, sems, c, chunk)

    for c in range(chans // chunk):
        fetch(c).start()
    keep_masks(base_ref, len_ref, masks, span)

    def group(lanes):
        for slot, lane in enumerate(lanes):
            spread(query_buf[:, cols_of(lane)], wide_q.at[slot], span)
        for slot, lane in enumerate(lanes):
            cols = cols_of(lane)
            keep_one = [masks[0, j] for j in range(span)]
            keep_two = [masks[1, j] for j in range(span)]
            q_short = short_conv(steps_of(wide_q.at[slot], span), rim_ref[0, :, cols], taps_ref[0, :, cols], keep_one, keep_two)
            for j in range(span):
                short_ref[pl.ds(j * SUBS, SUBS), cols] = q_short[j]

    each_chunk(chans, chunk, lambda c: fetch(c).wait(), group, lambda c: None, most)


def prefix_kernel(len_ref, end_in, rate_ref, enter_out, end_ref, enter_ref, sems, through, *, span):
    blocks = end_ref.shape[0]
    fetch = pltpu.make_async_copy(end_in, end_ref, sems.at[0])
    fetch.start()
    for i in range(blocks):
        through[i] = jnp.float32(1.0)
    start = jnp.int32(0)
    through[0] = jnp.float32(0.0)
    for d in range(len_ref.shape[0] - 1):
        start = start + len_ref[d]
        through[lax.div(start, jnp.int32(span))] = jnp.float32(0.0)
    decay = jnp.exp(-float(span) * rate_ref[...])
    state = jnp.zeros(decay.shape, f32)
    fetch.wait()
    for i in range(blocks):
        enter_ref[i] = state.astype(bf16)
        state = end_ref[i].astype(f32) + (decay * through[i]) * state
    store = pltpu.make_async_copy(enter_ref, enter_out, sems.at[1])
    store.start()
    store.wait()


def final_kernel(
    base_ref, len_ref, state_ref, enter_in, near_ref, short_ref, resid_in, rate_ref, weight_ref, gain_ref,
    *refs,
    span, modes, width, channels, most, chunk,
):
    if channels:
        hidden_out, normed_out, enter_ref, resid_ref, hidden_ref, sems, masks, wide, tables, sums, whole, normed_ref = refs
    else:
        hidden_out, wide_ref, sum_ref, enter_ref, resid_ref, hidden_ref, sems, masks, wide, tables, sums = refs
    chans = resid_ref.shape[1]

    def fetches(c):
        return [end_copy(enter_in, enter_ref, sems.at[0], c, chunk, width), cols_copy(resid_in, resid_ref, sems.at[1], c, chunk)]

    def store(c):
        return cols_copy(hidden_ref, hidden_out, sems.at[2], c, chunk)

    def store_normed(c):
        return cols_copy(normed_ref, normed_out, sems.at[3], c, chunk)

    for c in range(chans // chunk):
        for copy in fetches(c):
            copy.start()
    rows, starts = doc_start_rows(len_ref, base_ref[0], span)
    for j in range(span):
        masks[0, j] = flag(starts[j] < rows)
    masks[1, 0] = flag(starts[0] < base_ref[0])
    sums[...] = jnp.zeros(sums.shape, f32)

    def group(lanes):
        sub = lax.broadcasted_iota(jnp.int32, (SUBS, LANES), 0).astype(f32) * (-float(span))
        through = masks[1, 0]
        for slot, lane in enumerate(lanes):
            if width:
                enter = enter_ref[lax.div(lane, width), :, cols_of(pl.multiple_of(lax.rem(lane, width), LANES))]
            else:
                enter = enter_ref[:, cols_of(lane)]
            rate = rate_ref[:, cols_of(lane)]
            tables[slot, 0] = jnp.exp(-rate)
            tables[slot, 1] = weight_ref[:, cols_of(lane)] * enter.astype(f32)
            tables[slot, 2] = rate
        parts = [
            [
                state_ref[pl.ds(n * SUBS, SUBS), cols_of(lane)]
                + (row_of(tables.at[slot, 1], n) * through) * jnp.exp(row_of(tables.at[slot, 2], n) * sub)
                for n in range(modes)
            ]
            for slot, lane in enumerate(lanes)
        ]
        for slot, lane in enumerate(lanes):
            part = parts[slot]
            decay = [row_of(tables.at[slot, 0], n) for n in range(modes)]
            for j in range(span):
                part = [part[n] * decay[n] for n in range(modes)]
                total = part
                while len(total) > 1:
                    total = [total[m] + total[m + 1] for m in range(0, len(total), 2)]
                conv = near_ref[pl.ds(j * SUBS, SUBS), cols_of(lane)] + total[0] * masks[0, j]
                conv = conv.astype(bf16).astype(f32)
                wide[slot, pl.ds(j, SUBS, stride=span + 1), :] = short_ref[pl.ds(j * SUBS, SUBS), cols_of(lane)] * conv
        for b in range(SUBS):
            rows = pl.ds(b * span, span)
            squares = sums[rows, :]
            for slot, lane in enumerate(lanes):
                hidden = wide[slot, pl.ds(b * (span + 1), span), :] + resid_ref[rows, cols_of(lane)].astype(f32)
                if channels:
                    whole[lax.div(lane, LANES), rows, :] = hidden
                else:
                    wide_ref[rows, cols_of(lane)] = hidden
                hidden_ref[rows, cols_of(lane)] = hidden.astype(bf16)
                squares = squares + hidden * hidden
            sums[rows, :] = squares

    def before(c):
        for copy in fetches(c):
            copy.wait()

    each_chunk(chans, chunk, before, group, lambda c: store(c).start(), most)
    if channels:
        inverse = lax.rsqrt(jnp.sum(sums[...], axis=1, keepdims=True) / channels + 1e-06)
        sums[...] = jnp.broadcast_to(inverse, sums.shape)

        def scale(lanes):
            for lane in lanes:
                normed = whole[lax.div(lane, LANES)] * sums[...] * gain_ref[:, cols_of(lane)]
                normed_ref[:, cols_of(lane)] = normed.astype(bf16)

        each_chunk(chans, chunk, lambda c: None, scale, lambda c: store_normed(c).start(), 4)
        for c in range(chans // chunk):
            store_normed(c).wait()
    else:
        sum_ref[...] = sums[...]
    for c in range(chans // chunk):
        store(c).wait()


def shards(
    query_in, key_in, value_in, short_taps, decay_rate, residues, doc_lengths, residual, norm_gain
):
    tok_rows, chans = query_in.shape
    modes = decay_rate.shape[0]
    span = tok_rows // SUBS
    blocks = lax.axis_size("ctx")
    grp = lax.axis_size("grp")
    few = chans // blocks
    width = few if few % LANES == 0 else 0
    chunk = min(chans, max(1024, width))
    pieces = chans // chunk
    ctx_index = lax.axis_index("ctx")
    base = (ctx_index * tok_rows).astype(jnp.int32).reshape(1)
    tails = jnp.stack([query_in[tok_rows - 2 :], key_in[tok_rows - 2 :], value_in[tok_rows - 2 :]])
    rim_rows = from_behind(tails, "ctx", 1)
    weight = residues * jnp.sqrt(-jnp.expm1(-2.0 * decay_rate))

    smem = pl.BlockSpec(memory_space=pltpu.SMEM)
    vmem = pl.BlockSpec(memory_space=pltpu.VMEM)
    hbm = pl.BlockSpec(memory_space=pltpu.HBM)
    end_shape = (blocks, modes, few) if width else (modes, chans)
    tile_shape = (SUBS, LANES)
    wide_rows = SUBS * (span + 1)
    params = pltpu.CompilerParams(vmem_limit_bytes=16 * MIB)

    def near_by(x):
        return pltpu.with_memory_space_constraint(x, pltpu.VMEM)

    def far_off(x):
        return pltpu.with_memory_space_constraint(x, pltpu.HBM)

    def copies(kinds):
        return pltpu.SemaphoreType.DMA((kinds, pieces))

    def cost(per_tile, moved):
        return pl.CostEstimate(flops=per_tile * (chans // LANES) * SUBS * LANES, bytes_accessed=moved, transcendentals=0)

    rates, weights, taps, rims = near_by(decay_rate), near_by(weight), near_by(short_taps), near_by(rim_rows)
    gates, states, ends = pl.pallas_call(
        functools.partial(state_kernel, span=span, modes=modes, width=width, most=2, chunk=chunk),
        in_specs=[smem, smem, hbm, hbm, vmem, vmem, vmem, vmem],
        out_specs=[vmem, vmem, hbm],
        out_shape=[
            pltpu.VMEM((tok_rows, chans), bf16),
            pltpu.VMEM((modes * SUBS, chans), f32),
            jax.ShapeDtypeStruct(end_shape, bf16),
        ],
        scratch_shapes=[
            pltpu.VMEM((tok_rows, chans), bf16),
            pltpu.VMEM((tok_rows, chans), bf16),
            pltpu.VMEM(end_shape, bf16),
            copies(3),
            pltpu.VMEM((4, span) + tile_shape, f32),
            pltpu.VMEM((2, wide_rows, LANES), f32),
            pltpu.VMEM((2, wide_rows, LANES), f32),
            pltpu.VMEM((2, 5, modes, LANES), f32),
            pltpu.VMEM((2, modes, LANES), f32),
            pltpu.VMEM((2, span) + tile_shape, f32),
        ],
        compiler_params=params,
        cost_estimate=cost(1000, 12 * tok_rows * chans),
        name="block_states",
    )(base, doc_lengths, far_off(key_in), far_off(value_in), rims, taps, rates, weights)

    near = pl.pallas_call(
        functools.partial(near_kernel, span=span, modes=modes, most=4),
        in_specs=[smem, smem, vmem, vmem, vmem],
        out_specs=vmem,
        out_shape=pltpu.VMEM((tok_rows, chans), f32),
        scratch_shapes=[pltpu.VMEM((2, span) + tile_shape, f32)],
        compiler_params=params,
        cost_estimate=cost(600, 7 * tok_rows * chans),
        name="near_part",
    )(base, doc_lengths, near_by(gates), rates, weights)

    q_short = pl.pallas_call(
        functools.partial(query_kernel, span=span, most=4, chunk=chunk),
        in_specs=[smem, smem, hbm, vmem, vmem],
        out_specs=vmem,
        out_shape=pltpu.VMEM((tok_rows, chans), f32),
        scratch_shapes=[
            pltpu.VMEM((tok_rows, chans), bf16),
            pltpu.SemaphoreType.DMA((pieces,)),
            pltpu.VMEM((2, span) + tile_shape, f32),
            pltpu.VMEM((4, wide_rows, LANES), f32),
        ],
        compiler_params=params,
        cost_estimate=cost(200, 6 * tok_rows * chans),
        name="query_part",
    )(base, doc_lengths, far_off(query_in), rims, taps)

    if not width:
        ends = ends.reshape(modes, blocks, few).transpose(1, 0, 2)
    moved = lax.all_to_all(ends, "ctx", split_axis=0, concat_axis=0, tiled=True)
    moved, near = lax.optimization_barrier((moved, near))
    rate_few = lax.dynamic_slice_in_dim(decay_rate, ctx_index * few, few, 1)
    enter_few = pl.pallas_call(
        functools.partial(prefix_kernel, span=tok_rows),
        in_specs=[smem, hbm, vmem],
        out_specs=hbm,
        out_shape=jax.ShapeDtypeStruct((blocks, modes, few), bf16),
        scratch_shapes=[
            pltpu.VMEM((blocks, modes, few), bf16),
            pltpu.VMEM((blocks, modes, few), bf16),
            pltpu.SemaphoreType.DMA((2,)),
            pltpu.SMEM((blocks,), f32),
        ],
        compiler_params=params,
        name="block_prefix",
    )(doc_lengths, far_off(moved), near_by(rate_few))
    enter = lax.all_to_all(enter_few, "ctx", split_axis=0, concat_axis=0, tiled=True)
    if not width:
        enter = enter.transpose(1, 0, 2).reshape(modes, chans)

    alone = grp == 1
    out_specs = [hbm]
    out_shape = [jax.ShapeDtypeStruct((tok_rows, chans), bf16)]
    scratch = [
        pltpu.VMEM(end_shape, bf16),
        pltpu.VMEM((tok_rows, chans), bf16),
        pltpu.VMEM((tok_rows, chans), bf16),
        copies(4),
        pltpu.VMEM((2, span) + tile_shape, f32),
        pltpu.VMEM((2, wide_rows, LANES), f32),
        pltpu.VMEM((2, 3, modes, LANES), f32),
        pltpu.VMEM((tok_rows, LANES), f32),
    ]
    if alone:
        out_specs.append(hbm)
        out_shape.append(jax.ShapeDtypeStruct((tok_rows, chans), bf16))
        scratch += [pltpu.VMEM((chans // LANES, tok_rows, LANES), f32), pltpu.VMEM((tok_rows, chans), bf16)]
    else:
        out_specs += [vmem, vmem]
        out_shape += [jax.ShapeDtypeStruct((tok_rows, chans), f32), jax.ShapeDtypeStruct((tok_rows, LANES), f32)]
    outs = pl.pallas_call(
        functools.partial(
            final_kernel, span=span, modes=modes, width=width, channels=chans if alone else 0, most=2, chunk=chunk
        ),
        in_specs=[smem, smem, vmem, hbm, vmem, vmem, hbm, vmem, vmem, vmem],
        out_specs=out_specs,
        out_shape=out_shape,
        scratch_shapes=scratch,
        compiler_params=params,
        cost_estimate=cost(900, 18 * tok_rows * chans),
        name="far_part",
    )(
        base, doc_lengths, near_by(states), far_off(enter), near_by(near), near_by(q_short), far_off(residual),
        rates, weights, norm_gain.reshape(1, chans),
    )
    if alone:
        return tuple(outs)
    hidden_out, hidden, sums = outs
    square_sum = lax.psum(jnp.sum(sums, axis=1), "grp")
    inverse_rms = lax.rsqrt(square_sum / (chans * grp) + 1e-06)
    normed = (hidden * inverse_rms[:, None] * norm_gain[None, :]).astype(bf16)
    return (hidden_out, normed)


def solution(mesh):
    return jax.shard_map(
        shards,
        mesh=mesh,
        in_specs=(
            P("ctx", "grp"),
            P("ctx", "grp"),
            P("ctx", "grp"),
            P(None, None, "grp"),
            P(None, "grp"),
            P(None, "grp"),
            P(),
            P("ctx", "grp"),
            P("grp"),
        ),
        out_specs=(P("ctx", "grp"), P("ctx", "grp")),
        check_vma=False,
    )
```

```python
import functools
import math

import jax
import jax.numpy as jnp
from jax import lax
from jax.experimental import pallas as pl
from jax.experimental.pallas import tpu as pltpu
from jax.sharding import PartitionSpec as P

SUBS = 8
LANES = 128
MIB = 1024 * 1024
f32 = jnp.float32
bf16 = jnp.bfloat16


def from_behind(shard, axis, by):
    count = lax.axis_size(axis)
    pairs = [(i, i + by) for i in range(count) if 0 <= i + by < count]
    return lax.ppermute(shard, axis, pairs)


def swap(shard, axis):
    return lax.ppermute(shard, axis, [(i, i ^ 1) for i in range(lax.axis_size(axis))])


def doc_start_rows(len_ref, base, span):
    rows = lax.broadcasted_iota(jnp.int32, (SUBS, LANES), 0) * span + base
    starts = [jnp.int32(0)]
    for d in range(len_ref.shape[0] - 1):
        starts.append(starts[-1] + len_ref[d])
    out = []
    for j in range(span):
        pos = rows + j
        best = jnp.zeros((SUBS, LANES), jnp.int32)
        for start in starts[1:]:
            best = jnp.where(pos >= start, start, best)
        out.append(best)
    return rows, out


def flag(cond):
    return jnp.where(cond, 1.0, 0.0).astype(f32)


def each_group(count, most, group):
    size = math.gcd(count, most)

    def step(i, carry):
        group([pl.multiple_of((i * size + m) * LANES, LANES) for m in range(size)])
        return carry

    lax.fori_loop(0, count // size, step, 0)


def each_chunk(chans, chunk, before, group, after, most):
    def step(c, carry):
        before(c)

        def inner(lanes):
            group([pl.multiple_of(c * chunk + lane, LANES) for lane in lanes])

        each_group(chunk // LANES, most, inner)
        after(c)
        return carry

    lax.fori_loop(0, chans // chunk, step, 0)


def cols_copy(src, dst, sem, c, chunk):
    cols = pl.ds(pl.multiple_of(c * chunk, chunk), chunk)
    return pltpu.make_async_copy(src.at[:, cols], dst.at[:, cols], sem.at[c])


def cols_of(lane):
    return pl.ds(lane, LANES)


def row_of(ref, index):
    return jnp.broadcast_to(ref[pl.ds(index, 1), :], (SUBS, LANES))


def spread(x, wide, span):
    x = x.astype(f32)
    for b in range(SUBS):
        wide[pl.ds(b * (span + 1), span), :] = x[b * span : (b + 1) * span]


def steps_of(wide, span):
    return [wide[pl.ds(j, SUBS, stride=span + 1), :] for j in range(span)]


def short_conv(steps, rim, taps, keep_one, keep_two):
    top = lax.broadcasted_iota(jnp.int32, (SUBS, LANES), 0) == 0
    rim = rim.astype(f32)
    behind_one = jnp.where(top, jnp.broadcast_to(rim[1:2], (SUBS, LANES)), pltpu.roll(steps[-1], 1, 0))
    behind_two = jnp.where(top, jnp.broadcast_to(rim[0:1], (SUBS, LANES)), pltpu.roll(steps[-2], 1, 0))
    padded = [behind_two, behind_one] + steps
    taps = [jnp.broadcast_to(taps[m : m + 1], (SUBS, LANES)) for m in range(3)]
    return [
        taps[0] * padded[j + 2]
        + (taps[1] * padded[j + 1]) * keep_one[j]
        + (taps[2] * padded[j]) * keep_two[j]
        for j in range(len(steps))
    ]


def half_of(base_ref, rows, chans, lane):
    half = chans // 2
    which = lax.div(lane, half)
    mine = which == lax.rem(lax.div(base_ref[0], rows), 2)
    return mine, pl.multiple_of(lane - which * half, LANES)


def state_kernel(
    base_ref, len_ref, key_ref, value_ref, rim_ref, taps_ref, rate_ref, weight_ref,
    gate_ref, state_ref, own_ref, give_ref,
    key_buf, value_buf, sems, masks, wide_k, wide_v, tables, ends, held,
    *, span, modes, most, chunk,
):
    chans = key_buf.shape[1]

    def fetches(c):
        return [cols_copy(key_ref, key_buf, sems.at[0], c, chunk), cols_copy(value_ref, value_buf, sems.at[1], c, chunk)]

    for c in range(chans // chunk):
        for copy in fetches(c):
            copy.start()

    def prepare():
        rows, starts = doc_start_rows(len_ref, base_ref[0], span)
        for j in range(span):
            masks[0, j] = flag(starts[j] < rows + j)
            masks[1, j] = flag(starts[j] < rows + (j - 1))
            masks[2, j] = flag(starts[span - 1] <= rows + j)
        sub = lax.broadcasted_iota(jnp.int32, (SUBS, LANES), 0)
        through = flag(starts[span - 1] < rows)
        one = through * flag(sub >= 1)
        two = one * pltpu.roll(one, 1, 0) * flag(sub >= 2)
        four = two * pltpu.roll(two, 2, 0) * flag(sub >= 4)
        masks[3, 0] = one
        masks[3, 1] = two
        masks[3, 2] = four
        masks[3, 3] = flag(sub >= 1)

    prepare()

    def group(lanes):
        for slot, lane in enumerate(lanes):
            spread(key_buf[:, cols_of(lane)], wide_k.at[slot], span)
            spread(value_buf[:, cols_of(lane)], wide_v.at[slot], span)
            rate = rate_ref[:, cols_of(lane)]
            for m, by in enumerate((1, span, 2 * span, 4 * span)):
                tables[slot, m] = jnp.exp(-float(by) * rate)
            tables[slot, 4] = weight_ref[:, cols_of(lane)]
        for slot, lane in enumerate(lanes):
            cols = cols_of(lane)
            keep_one = [masks[0, j] for j in range(span)]
            keep_two = [masks[1, j] for j in range(span)]
            k_short = short_conv(steps_of(wide_k.at[slot], span), rim_ref[1, :, cols], taps_ref[1, :, cols], keep_one, keep_two)
            v_short = short_conv(steps_of(wide_v.at[slot], span), rim_ref[2, :, cols], taps_ref[2, :, cols], keep_one, keep_two)
            for j in range(0, span, 2):
                pair = jnp.concatenate([k_short[j] * v_short[j], k_short[j + 1] * v_short[j + 1]], axis=0).astype(bf16)
                gate_ref[pl.ds(j * SUBS, 2 * SUBS), cols] = pair
                pair = pair.astype(f32)
                held[slot, j] = pair[:SUBS] * masks[2, j]
                held[slot, j + 1] = pair[SUBS:] * masks[2, j + 1]
        states = []
        for slot, lane in enumerate(lanes):
            decay = [row_of(tables.at[slot, 0], n) for n in range(modes)]
            state = [held[slot, 0]] * modes
            for j in range(1, span):
                gate = held[slot, j]
                state = [decay[n] * state[n] + gate for n in range(modes)]
            states.append(state)
        for m, shift in enumerate((1, 2, 4)):
            for slot in range(len(lanes)):
                states[slot] = [
                    x + (row_of(tables.at[slot, m + 1], n) * masks[3, m]) * pltpu.roll(x, shift, 0)
                    for n, x in enumerate(states[slot])
                ]
        for slot, lane in enumerate(lanes):
            for n, x in enumerate(states[slot]):
                ends[slot, pl.ds(n, 1), :] = x[SUBS - 1 :]
                state_ref[pl.ds(n * SUBS, SUBS), cols_of(lane)] = (
                    row_of(tables.at[slot, 4], n) * masks[3, 3]
                ) * pltpu.roll(x, 1, 0)
        for slot, lane in enumerate(lanes):
            mine, here = half_of(base_ref, key_ref.shape[0], chans, lane)

            @pl.when(mine)
            def _():
                own_ref[:, cols_of(here)] = ends[slot]

            @pl.when(jnp.logical_not(mine))
            def _():
                give_ref[:, cols_of(here)] = ends[slot]

    def before(c):
        for copy in fetches(c):
            copy.wait()

    each_chunk(chans, chunk, before, group, lambda c: None, most)


def keep_masks(base_ref, len_ref, masks, span):
    rows, starts = doc_start_rows(len_ref, base_ref[0], span)
    for j in range(span):
        masks[0, j] = flag(starts[j] < rows + j)
        masks[1, j] = flag(starts[j] < rows + (j - 1))


def near_kernel(base_ref, len_ref, gate_ref, rate_ref, weight_ref, near_ref, masks, *, span, modes, most):
    keep_masks(base_ref, len_ref, masks, span)

    def group(lanes):
        taps = []
        for lane in lanes:
            decay = jnp.exp(-rate_ref[:, cols_of(lane)])
            term = weight_ref[:, cols_of(lane)]
            parts = []
            for lag in range(span):
                part = term[:SUBS]
                for n in range(SUBS, modes, SUBS):
                    part = part + term[n : n + SUBS]
                parts.append(part)
                term = term * decay
            taps.append(parts)
        for shift in (1, 2, 4):
            taps = [[part + pltpu.roll(part, shift, 0) for part in parts] for parts in taps]
        for parts, lane in zip(taps, lanes):
            live = []
            for j in range(span):
                if j % 2 == 0:
                    pair = gate_ref[pl.ds(j * SUBS, 2 * SUBS), cols_of(lane)].astype(f32)
                keep = masks[0, j]
                live = [g * keep for g in live]
                live.append(pair[(j % 2) * SUBS : (j % 2 + 1) * SUBS])
                total = parts[0] * live[j]
                for lag in range(1, j + 1):
                    total = total + parts[lag] * live[j - lag]
                near_ref[pl.ds(j * SUBS, SUBS), cols_of(lane)] = total

    each_group(gate_ref.shape[1] // LANES, most, group)


def query_kernel(base_ref, len_ref, query_ref, rim_ref, taps_ref, short_ref, query_buf, sems, masks, wide_q, *, span, most, chunk):
    chans = query_buf.shape[1]

    def fetch(c):
        return cols_copy(query_ref, query_buf, sems, c, chunk)

    for c in range(chans // chunk):
        fetch(c).start()
    keep_masks(base_ref, len_ref, masks, span)

    def group(lanes):
        for slot, lane in enumerate(lanes):
            spread(query_buf[:, cols_of(lane)], wide_q.at[slot], span)
        for slot, lane in enumerate(lanes):
            cols = cols_of(lane)
            keep_one = [masks[0, j] for j in range(span)]
            keep_two = [masks[1, j] for j in range(span)]
            q_short = short_conv(steps_of(wide_q.at[slot], span), rim_ref[0, :, cols], taps_ref[0, :, cols], keep_one, keep_two)
            for j in range(span):
                short_ref[pl.ds(j * SUBS, SUBS), cols] = q_short[j]

    each_chunk(chans, chunk, lambda c: fetch(c).wait(), group, lambda c: None, most)


def unbroken(len_ref, first, count):
    start = jnp.int32(0)
    whole = jnp.where((first <= 0) & (first + count > 0), 0.0, 1.0)
    for d in range(len_ref.shape[0] - 1):
        start = start + len_ref[d]
        whole = jnp.where((start >= first) & (start < first + count), 0.0, whole)
    return whole.astype(f32)


def pair_rates(base_ref, rate_ref, rows, shape):
    parity = lax.rem(lax.div(base_ref[0], rows), 2)
    return parity, rate_ref[:, pl.ds(pl.multiple_of(parity * shape[1], LANES), shape[1])]


def early_late(parity, own, got):
    odd = jnp.full(own.shape, parity, jnp.int32) == 1
    return jnp.where(odd, got, own), jnp.where(odd, own, got)


def pair_kernel(base_ref, len_ref, own_ref, got_ref, rate_ref, end_ref, *, rows):
    parity, rate = pair_rates(base_ref, rate_ref, rows, own_ref.shape)
    early, late = early_late(parity, own_ref[...], got_ref[...])
    through = unbroken(len_ref, base_ref[0] + (1 - parity) * rows, rows)
    end_ref[...] = (late + (jnp.exp(-float(rows) * rate) * through) * early).astype(bf16)


def reach_kernel(base_ref, len_ref, near_ref, far_ref, rate_ref, enter_ref, *, rows, reach):
    parity, rate = pair_rates(base_ref, rate_ref, rows, near_ref.shape)
    span = 2 * rows * reach
    through = unbroken(len_ref, base_ref[0] - parity * rows - span, span)
    enter_ref[...] = (
        near_ref[...].astype(f32) + (jnp.exp(-float(span) * rate) * through) * far_ref[...].astype(f32)
    ).astype(enter_ref.dtype)


def enter_kernel(base_ref, len_ref, enter_ref, own_ref, got_ref, rate_ref, mine_ref, give_ref, *, rows):
    parity, rate = pair_rates(base_ref, rate_ref, rows, own_ref.shape)
    early, _ = early_late(parity, own_ref[...], got_ref[...])
    through = unbroken(len_ref, base_ref[0] - parity * rows, rows)
    first = enter_ref[...].astype(f32)
    second = early + (jnp.exp(-float(rows) * rate) * through) * first
    give, mine = early_late(parity, second, first)
    mine_ref[...] = mine
    give_ref[...] = give


def final_kernel(
    base_ref, len_ref, state_ref, mine_ref, got_ref, near_ref, short_ref, resid_in, rate_ref, weight_ref, gain_ref,
    *refs,
    span, modes, channels, most, chunk,
):
    if channels:
        hidden_out, normed_out, resid_ref, hidden_ref, sems, masks, wide, tables, sums, whole, normed_ref = refs
    else:
        hidden_out, wide_ref, sum_ref, resid_ref, hidden_ref, sems, masks, wide, tables, sums = refs
    chans = resid_ref.shape[1]

    def fetch(c):
        return cols_copy(resid_in, resid_ref, sems.at[0], c, chunk)

    def store(c):
        return cols_copy(hidden_ref, hidden_out, sems.at[1], c, chunk)

    def store_normed(c):
        return cols_copy(normed_ref, normed_out, sems.at[2], c, chunk)

    for c in range(chans // chunk):
        fetch(c).start()
    rows, starts = doc_start_rows(len_ref, base_ref[0], span)
    for j in range(span):
        masks[0, j] = flag(starts[j] < rows)
    masks[1, 0] = flag(starts[0] < base_ref[0])
    sums[...] = jnp.zeros(sums.shape, f32)

    def group(lanes):
        sub = lax.broadcasted_iota(jnp.int32, (SUBS, LANES), 0).astype(f32) * (-float(span))
        through = masks[1, 0]
        for slot, lane in enumerate(lanes):
            mine, here = half_of(base_ref, resid_ref.shape[0], chans, lane)
            mine = jnp.full((modes, LANES), mine.astype(jnp.int32), jnp.int32) == 1
            enter = jnp.where(mine, mine_ref[:, cols_of(here)], got_ref[:, cols_of(here)])
            rate = rate_ref[:, cols_of(lane)]
            tables[slot, 0] = jnp.exp(-rate)
            tables[slot, 1] = weight_ref[:, cols_of(lane)] * enter
            tables[slot, 2] = rate
        parts = [
            [
                state_ref[pl.ds(n * SUBS, SUBS), cols_of(lane)]
                + (row_of(tables.at[slot, 1], n) * through) * jnp.exp(row_of(tables.at[slot, 2], n) * sub)
                for n in range(modes)
            ]
            for slot, lane in enumerate(lanes)
        ]
        for slot, lane in enumerate(lanes):
            part = parts[slot]
            decay = [row_of(tables.at[slot, 0], n) for n in range(modes)]
            for j in range(span):
                part = [part[n] * decay[n] for n in range(modes)]
                total = part
                while len(total) > 1:
                    total = [total[m] + total[m + 1] for m in range(0, len(total), 2)]
                conv = near_ref[pl.ds(j * SUBS, SUBS), cols_of(lane)] + total[0] * masks[0, j]
                conv = conv.astype(bf16).astype(f32)
                wide[slot, pl.ds(j, SUBS, stride=span + 1), :] = short_ref[pl.ds(j * SUBS, SUBS), cols_of(lane)] * conv
        for b in range(SUBS):
            rows = pl.ds(b * span, span)
            squares = sums[rows, :]
            for slot, lane in enumerate(lanes):
                hidden = wide[slot, pl.ds(b * (span + 1), span), :] + resid_ref[rows, cols_of(lane)].astype(f32)
                if channels:
                    whole[lax.div(lane, LANES), rows, :] = hidden
                else:
                    wide_ref[rows, cols_of(lane)] = hidden
                hidden_ref[rows, cols_of(lane)] = hidden.astype(bf16)
                squares = squares + hidden * hidden
            sums[rows, :] = squares

    each_chunk(chans, chunk, lambda c: fetch(c).wait(), group, lambda c: store(c).start(), most)
    if channels:
        inverse = lax.rsqrt(jnp.sum(sums[...], axis=1, keepdims=True) / channels + 1e-06)
        sums[...] = jnp.broadcast_to(inverse, sums.shape)

        def scale(lanes):
            for lane in lanes:
                normed = whole[lax.div(lane, LANES)] * sums[...] * gain_ref[:, cols_of(lane)]
                normed_ref[:, cols_of(lane)] = normed.astype(bf16)

        each_chunk(chans, chunk, lambda c: None, scale, lambda c: store_normed(c).start(), 4)
        for c in range(chans // chunk):
            store_normed(c).wait()
    else:
        sum_ref[...] = sums[...]
    for c in range(chans // chunk):
        store(c).wait()


def shards(
    query_in, key_in, value_in, short_taps, decay_rate, residues, doc_lengths, residual, norm_gain
):
    tok_rows, chans = query_in.shape
    modes = decay_rate.shape[0]
    span = tok_rows // SUBS
    blocks = lax.axis_size("ctx")
    grp = lax.axis_size("grp")
    chunk = min(chans, 1024)
    pieces = chans // chunk
    ctx_index = lax.axis_index("ctx")
    base = (ctx_index * tok_rows).astype(jnp.int32).reshape(1)
    tails = jnp.stack([query_in[tok_rows - 2 :], key_in[tok_rows - 2 :], value_in[tok_rows - 2 :]])
    rim_rows = from_behind(tails, "ctx", 1)
    weight = residues * jnp.sqrt(-jnp.expm1(-2.0 * decay_rate))

    smem = pl.BlockSpec(memory_space=pltpu.SMEM)
    vmem = pl.BlockSpec(memory_space=pltpu.VMEM)
    hbm = pl.BlockSpec(memory_space=pltpu.HBM)
    half = jax.ShapeDtypeStruct((modes, chans // 2), f32)
    tile_shape = (SUBS, LANES)
    wide_rows = SUBS * (span + 1)
    params = pltpu.CompilerParams(vmem_limit_bytes=16 * MIB)

    def near_by(x):
        return pltpu.with_memory_space_constraint(x, pltpu.VMEM)

    def far_off(x):
        return pltpu.with_memory_space_constraint(x, pltpu.HBM)

    def copies(kinds):
        return pltpu.SemaphoreType.DMA((kinds, pieces))

    def cost(per_tile, moved):
        return pl.CostEstimate(flops=per_tile * (chans // LANES) * SUBS * LANES, bytes_accessed=moved, transcendentals=0)

    rates, weights, taps, rims = near_by(decay_rate), near_by(weight), near_by(short_taps), near_by(rim_rows)
    gates, states, own, give = pl.pallas_call(
        functools.partial(state_kernel, span=span, modes=modes, most=2, chunk=chunk),
        in_specs=[smem, smem, hbm, hbm, vmem, vmem, vmem, vmem],
        out_specs=[vmem, vmem, vmem, vmem],
        out_shape=[
            pltpu.VMEM((tok_rows, chans), bf16),
            pltpu.VMEM((modes * SUBS, chans), f32),
            pltpu.VMEM(half.shape, f32),
            pltpu.VMEM(half.shape, f32),
        ],
        scratch_shapes=[
            pltpu.VMEM((tok_rows, chans), bf16),
            pltpu.VMEM((tok_rows, chans), bf16),
            copies(2),
            pltpu.VMEM((4, span) + tile_shape, f32),
            pltpu.VMEM((2, wide_rows, LANES), f32),
            pltpu.VMEM((2, wide_rows, LANES), f32),
            pltpu.VMEM((2, 5, modes, LANES), f32),
            pltpu.VMEM((2, modes, LANES), f32),
            pltpu.VMEM((2, span) + tile_shape, f32),
        ],
        compiler_params=params,
        cost_estimate=cost(1000, 12 * tok_rows * chans),
        name="block_states",
    )(base, doc_lengths, far_off(key_in), far_off(value_in), rims, taps, rates, weights)

    near = pl.pallas_call(
        functools.partial(near_kernel, span=span, modes=modes, most=4),
        in_specs=[smem, smem, vmem, vmem, vmem],
        out_specs=vmem,
        out_shape=pltpu.VMEM((tok_rows, chans), f32),
        scratch_shapes=[pltpu.VMEM((2, span) + tile_shape, f32)],
        compiler_params=params,
        cost_estimate=cost(600, 7 * tok_rows * chans),
        name="near_part",
    )(base, doc_lengths, near_by(gates), rates, weights)

    q_short = pl.pallas_call(
        functools.partial(query_kernel, span=span, most=4, chunk=chunk),
        in_specs=[smem, smem, hbm, vmem, vmem],
        out_specs=vmem,
        out_shape=pltpu.VMEM((tok_rows, chans), f32),
        scratch_shapes=[
            pltpu.VMEM((tok_rows, chans), bf16),
            pltpu.SemaphoreType.DMA((pieces,)),
            pltpu.VMEM((2, span) + tile_shape, f32),
            pltpu.VMEM((4, wide_rows, LANES), f32),
        ],
        compiler_params=params,
        cost_estimate=cost(200, 6 * tok_rows * chans),
        name="query_part",
    )(base, doc_lengths, far_off(query_in), rims, taps)

    got = swap(give, "ctx")

    def pair_call(kernel, operands, out_shape, name, **static):
        count = len(operands) + 1
        return pl.pallas_call(
            functools.partial(kernel, rows=tok_rows, **static),
            in_specs=[smem, smem] + [vmem] * count,
            out_specs=[vmem] * len(out_shape),
            out_shape=out_shape,
            compiler_params=params,
            name=name,
        )(base, doc_lengths, *[near_by(x) for x in operands], rates)

    sent = pltpu.VMEM(half.shape, bf16)
    ends = pair_call(pair_kernel, [own, got], [sent], "pair_ends")[0]
    one_on, two_on = from_behind(ends, "ctx", 2), from_behind(ends, "ctx", 4)
    one_on, two_on, near = lax.optimization_barrier((one_on, two_on, near))
    enter = pair_call(reach_kernel, [one_on, two_on], [sent], "reach_2", reach=1)[0]
    reach = 2
    while reach < blocks // 8:
        on = from_behind(enter, "ctx", 2 * reach)
        on, q_short = lax.optimization_barrier((on, q_short))
        enter = pair_call(reach_kernel, [enter, on], [sent], "reach_%d" % (2 * reach), reach=reach)[0]
        reach *= 2
    mine, give_back = pair_call(
        enter_kernel, [enter, own, got], [pltpu.VMEM(half.shape, f32), pltpu.VMEM(half.shape, f32)], "pair_enter"
    )
    got_back = swap(give_back, "ctx")

    alone = grp == 1
    out_specs = [hbm]
    out_shape = [jax.ShapeDtypeStruct((tok_rows, chans), bf16)]
    scratch = [
        pltpu.VMEM((tok_rows, chans), bf16),
        pltpu.VMEM((tok_rows, chans), bf16),
        copies(3),
        pltpu.VMEM((2, span) + tile_shape, f32),
        pltpu.VMEM((2, wide_rows, LANES), f32),
        pltpu.VMEM((2, 3, modes, LANES), f32),
        pltpu.VMEM((tok_rows, LANES), f32),
    ]
    if alone:
        out_specs.append(hbm)
        out_shape.append(jax.ShapeDtypeStruct((tok_rows, chans), bf16))
        scratch += [pltpu.VMEM((chans // LANES, tok_rows, LANES), f32), pltpu.VMEM((tok_rows, chans), bf16)]
    else:
        out_specs += [vmem, vmem]
        out_shape += [jax.ShapeDtypeStruct((tok_rows, chans), f32), jax.ShapeDtypeStruct((tok_rows, LANES), f32)]
    outs = pl.pallas_call(
        functools.partial(
            final_kernel, span=span, modes=modes, channels=chans if alone else 0, most=2, chunk=chunk
        ),
        in_specs=[smem, smem, vmem, vmem, vmem, vmem, vmem, hbm, vmem, vmem, vmem],
        out_specs=out_specs,
        out_shape=out_shape,
        scratch_shapes=scratch,
        compiler_params=params,
        cost_estimate=cost(900, 18 * tok_rows * chans),
        name="far_part",
    )(
        base, doc_lengths, near_by(states), near_by(mine), near_by(got_back), near_by(near), near_by(q_short), far_off(residual),
        rates, weights, norm_gain.reshape(1, chans),
    )
    if alone:
        return tuple(outs)
    hidden_out, hidden, sums = outs
    square_sum = lax.psum(jnp.sum(sums, axis=1), "grp")
    inverse_rms = lax.rsqrt(square_sum / (chans * grp) + 1e-06)
    normed = (hidden * inverse_rms[:, None] * norm_gain[None, :]).astype(bf16)
    return (hidden_out, normed)


def solution(mesh):
    return jax.shard_map(
        shards,
        mesh=mesh,
        in_specs=(
            P("ctx", "grp"),
            P("ctx", "grp"),
            P("ctx", "grp"),
            P(None, None, "grp"),
            P(None, "grp"),
            P(None, "grp"),
            P(),
            P("ctx", "grp"),
            P("grp"),
        ),
        out_specs=(P("ctx", "grp"), P("ctx", "grp")),
        check_vma=False,
    )
```

```python
import functools
import math

import jax
import jax.numpy as jnp
from jax import lax
from jax.experimental import pallas as pl
from jax.experimental.pallas import tpu as pltpu
from jax.sharding import PartitionSpec as P

SUBS = 8
LANES = 128
MIB = 1024 * 1024
A_TILES, N_TILES, Q_TILES, F_TILES = 4, 2, 8, 4
f32 = jnp.float32
bf16 = jnp.bfloat16


def from_behind(shard, axis, by):
    count = lax.axis_size(axis)
    pairs = [(i, i + by) for i in range(count) if 0 <= i + by < count]
    return lax.ppermute(shard, axis, pairs)


def swap(shard, axis):
    return lax.ppermute(shard, axis, [(i, i ^ 1) for i in range(lax.axis_size(axis))])


def doc_start_rows(len_ref, base, span):
    rows = lax.broadcasted_iota(jnp.int32, (SUBS, LANES), 0) * span + base
    starts = [jnp.int32(0)]
    for d in range(len_ref.shape[0] - 1):
        starts.append(starts[-1] + len_ref[d])
    out = []
    for j in range(span):
        pos = rows + j
        best = jnp.zeros((SUBS, LANES), jnp.int32)
        for start in starts[1:]:
            best = jnp.where(pos >= start, start, best)
        out.append(best)
    return rows, out


def flag(cond):
    return jnp.where(cond, 1.0, 0.0).astype(f32)


def each_group(count, most, group):
    size = math.gcd(count, most)

    def step(i, carry):
        group([pl.multiple_of((i * size + m) * LANES, LANES) for m in range(size)])
        return carry

    lax.fori_loop(0, count // size, step, 0)


def each_chunk(chans, chunk, before, group, after, most):
    def step(c, carry):
        before(c)

        def inner(lanes):
            group([pl.multiple_of(c * chunk + lane, LANES) for lane in lanes])

        each_group(chunk // LANES, most, inner)
        after(c)
        return carry

    lax.fori_loop(0, chans // chunk, step, 0)


def cols_copy(src, dst, sem, c, chunk):
    cols = pl.ds(pl.multiple_of(c * chunk, chunk), chunk)
    return pltpu.make_async_copy(src.at[:, cols], dst.at[:, cols], sem.at[c])


def cols_of(lane):
    return pl.ds(lane, LANES)


def row_of(ref, index):
    return jnp.broadcast_to(ref[pl.ds(index, 1), :], (SUBS, LANES))


def spread(x, wide, span):
    x = x.astype(f32)
    for b in range(SUBS):
        wide[pl.ds(b * (span + 1), span), :] = x[b * span : (b + 1) * span]


def steps_of(wide, span):
    return [wide[pl.ds(j, SUBS, stride=span + 1), :] for j in range(span)]


def short_conv(steps, rim, taps, keep_one, keep_two):
    top = lax.broadcasted_iota(jnp.int32, (SUBS, LANES), 0) == 0
    rim = rim.astype(f32)
    behind_one = jnp.where(top, jnp.broadcast_to(rim[1:2], (SUBS, LANES)), pltpu.roll(steps[-1], 1, 0))
    behind_two = jnp.where(top, jnp.broadcast_to(rim[0:1], (SUBS, LANES)), pltpu.roll(steps[-2], 1, 0))
    padded = [behind_two, behind_one] + steps
    taps = [jnp.broadcast_to(taps[m : m + 1], (SUBS, LANES)) for m in range(3)]
    return [
        taps[0] * padded[j + 2]
        + (taps[1] * padded[j + 1]) * keep_one[j]
        + (taps[2] * padded[j]) * keep_two[j]
        for j in range(len(steps))
    ]


def half_of(base_ref, rows, chans, lane):
    half = chans // 2
    which = lax.div(lane, half)
    mine = which == lax.rem(lax.div(base_ref[0], rows), 2)
    return mine, pl.multiple_of(lane - which * half, LANES)


def state_kernel(
    base_ref, len_ref, key_ref, value_ref, rim_ref, taps_ref, rate_ref, weight_ref,
    gate_ref, state_ref, own_ref, give_ref,
    key_buf, value_buf, sems, masks, wide_k, wide_v, tables, ends, held,
    *, span, modes, most, chunk,
):
    chans = key_buf.shape[1]

    def fetches(c):
        return [cols_copy(key_ref, key_buf, sems.at[0], c, chunk), cols_copy(value_ref, value_buf, sems.at[1], c, chunk)]

    for c in range(chans // chunk):
        for copy in fetches(c):
            copy.start()

    def prepare():
        rows, starts = doc_start_rows(len_ref, base_ref[0], span)
        for j in range(span):
            masks[0, j] = flag(starts[j] < rows + j)
            masks[1, j] = flag(starts[j] < rows + (j - 1))
            masks[2, j] = flag(starts[span - 1] <= rows + j)
        sub = lax.broadcasted_iota(jnp.int32, (SUBS, LANES), 0)
        through = flag(starts[span - 1] < rows)
        one = through * flag(sub >= 1)
        two = one * pltpu.roll(one, 1, 0) * flag(sub >= 2)
        four = two * pltpu.roll(two, 2, 0) * flag(sub >= 4)
        masks[3, 0] = one
        masks[3, 1] = two
        masks[3, 2] = four
        masks[3, 3] = flag(sub >= 1)

    prepare()

    def group(lanes):
        for slot, lane in enumerate(lanes):
            spread(key_buf[:, cols_of(lane)], wide_k.at[slot], span)
            spread(value_buf[:, cols_of(lane)], wide_v.at[slot], span)
            rate = rate_ref[:, cols_of(lane)]
            for m, by in enumerate((1, span, 2 * span, 4 * span)):
                tables[slot, m] = jnp.exp(-float(by) * rate)
            tables[slot, 4] = weight_ref[:, cols_of(lane)]
        for slot, lane in enumerate(lanes):
            cols = cols_of(lane)
            keep_one = [masks[0, j] for j in range(span)]
            keep_two = [masks[1, j] for j in range(span)]
            k_short = short_conv(steps_of(wide_k.at[slot], span), rim_ref[1, :, cols], taps_ref[1, :, cols], keep_one, keep_two)
            v_short = short_conv(steps_of(wide_v.at[slot], span), rim_ref[2, :, cols], taps_ref[2, :, cols], keep_one, keep_two)
            for j in range(0, span, 2):
                pair = jnp.concatenate([k_short[j] * v_short[j], k_short[j + 1] * v_short[j + 1]], axis=0).astype(bf16)
                gate_ref[pl.ds(j * SUBS, 2 * SUBS), cols] = pair
                pair = pair.astype(f32)
                held[slot, j] = pair[:SUBS] * masks[2, j]
                held[slot, j + 1] = pair[SUBS:] * masks[2, j + 1]
        states = []
        for slot, lane in enumerate(lanes):
            decay = [row_of(tables.at[slot, 0], n) for n in range(modes)]
            state = [held[slot, 0]] * modes
            for j in range(1, span):
                gate = held[slot, j]
                state = [decay[n] * state[n] + gate for n in range(modes)]
            states.append(state)
        for m, shift in enumerate((1, 2, 4)):
            for slot in range(len(lanes)):
                states[slot] = [
                    x + (row_of(tables.at[slot, m + 1], n) * masks[3, m]) * pltpu.roll(x, shift, 0)
                    for n, x in enumerate(states[slot])
                ]
        for slot, lane in enumerate(lanes):
            for n, x in enumerate(states[slot]):
                ends[slot, pl.ds(n, 1), :] = x[SUBS - 1 :]
                state_ref[pl.ds(n * SUBS, SUBS), cols_of(lane)] = (
                    row_of(tables.at[slot, 4], n) * masks[3, 3]
                ) * pltpu.roll(x, 1, 0)
        for slot, lane in enumerate(lanes):
            mine, here = half_of(base_ref, key_ref.shape[0], chans, lane)

            @pl.when(mine)
            def _():
                own_ref[:, cols_of(here)] = ends[slot]

            @pl.when(jnp.logical_not(mine))
            def _():
                give_ref[:, cols_of(here)] = ends[slot]

    def before(c):
        for copy in fetches(c):
            copy.wait()

    each_chunk(chans, chunk, before, group, lambda c: None, most)


def tail_kernel(query_ref, key_ref, value_ref, tail_ref, bufs, sems):
    rows, count = query_ref.shape[0], bufs.shape[1]
    copies = [
        pltpu.make_async_copy(ref.at[pl.ds(rows - count, count)], bufs.at[i], sems.at[i])
        for i, ref in enumerate((query_ref, key_ref, value_ref))
    ]
    for copy in copies:
        copy.start()
    for i, copy in enumerate(copies):
        copy.wait()
        tail_ref[i] = bufs[i].astype(f32)[count - 2 :].astype(bf16)


def keep_masks(base_ref, len_ref, masks, span):
    rows, starts = doc_start_rows(len_ref, base_ref[0], span)
    for j in range(span):
        masks[0, j] = flag(starts[j] < rows + j)
        masks[1, j] = flag(starts[j] < rows + (j - 1))


def near_kernel(base_ref, len_ref, gate_ref, rate_ref, weight_ref, near_ref, masks, *, span, modes, most):
    keep_masks(base_ref, len_ref, masks, span)

    def group(lanes):
        taps = []
        for lane in lanes:
            decay = jnp.exp(-rate_ref[:, cols_of(lane)])
            term = weight_ref[:, cols_of(lane)]
            parts = []
            for lag in range(span):
                part = term[:SUBS]
                for n in range(SUBS, modes, SUBS):
                    part = part + term[n : n + SUBS]
                parts.append(part)
                term = term * decay
            taps.append(parts)
        for shift in (1, 2, 4):
            taps = [[part + pltpu.roll(part, shift, 0) for part in parts] for parts in taps]
        for parts, lane in zip(taps, lanes):
            live = []
            for j in range(span):
                if j % 2 == 0:
                    pair = gate_ref[pl.ds(j * SUBS, 2 * SUBS), cols_of(lane)].astype(f32)
                keep = masks[0, j]
                live = [g * keep for g in live]
                live.append(pair[(j % 2) * SUBS : (j % 2 + 1) * SUBS])
                total = parts[0] * live[j]
                for lag in range(1, j + 1):
                    total = total + parts[lag] * live[j - lag]
                near_ref[pl.ds(j * SUBS, SUBS), cols_of(lane)] = total

    each_group(gate_ref.shape[1] // LANES, most, group)


def query_kernel(base_ref, len_ref, query_ref, rim_ref, taps_ref, short_ref, query_buf, sems, masks, wide_q, *, span, most, chunk):
    chans = query_buf.shape[1]

    def fetch(c):
        return cols_copy(query_ref, query_buf, sems, c, chunk)

    for c in range(chans // chunk):
        fetch(c).start()
    keep_masks(base_ref, len_ref, masks, span)

    def group(lanes):
        for slot, lane in enumerate(lanes):
            spread(query_buf[:, cols_of(lane)], wide_q.at[slot], span)
        for slot, lane in enumerate(lanes):
            cols = cols_of(lane)
            keep_one = [masks[0, j] for j in range(span)]
            keep_two = [masks[1, j] for j in range(span)]
            q_short = short_conv(steps_of(wide_q.at[slot], span), rim_ref[0, :, cols], taps_ref[0, :, cols], keep_one, keep_two)
            for j in range(span):
                short_ref[pl.ds(j * SUBS, SUBS), cols] = q_short[j]

    each_chunk(chans, chunk, lambda c: fetch(c).wait(), group, lambda c: None, most)


def unbroken(len_ref, first, count):
    start = jnp.int32(0)
    whole = jnp.where((first <= 0) & (first + count > 0), 0.0, 1.0)
    for d in range(len_ref.shape[0] - 1):
        start = start + len_ref[d]
        whole = jnp.where((start >= first) & (start < first + count), 0.0, whole)
    return whole.astype(f32)


def pair_rates(base_ref, rate_ref, rows, shape):
    parity = lax.rem(lax.div(base_ref[0], rows), 2)
    return parity, rate_ref[:, pl.ds(pl.multiple_of(parity * shape[1], LANES), shape[1])]


def early_late(parity, own, got):
    odd = jnp.full(own.shape, parity, jnp.int32) == 1
    return jnp.where(odd, got, own), jnp.where(odd, own, got)


def pair_kernel(base_ref, len_ref, own_ref, got_ref, rate_ref, end_ref, *, rows):
    parity, rate = pair_rates(base_ref, rate_ref, rows, own_ref.shape)
    early, late = early_late(parity, own_ref[...], got_ref[...])
    through = unbroken(len_ref, base_ref[0] + (1 - parity) * rows, rows)
    end_ref[...] = (late + (jnp.exp(-float(rows) * rate) * through) * early).astype(bf16)


def reached(base_ref, len_ref, near_ref, far_ref, rate_ref, rows, reach):
    parity, rate = pair_rates(base_ref, rate_ref, rows, near_ref.shape)
    span = 2 * rows * reach
    through = unbroken(len_ref, base_ref[0] - parity * rows - span, span)
    return near_ref[...].astype(f32) + (jnp.exp(-float(span) * rate) * through) * far_ref[...].astype(f32)


def reach_kernel(base_ref, len_ref, near_ref, far_ref, rate_ref, enter_ref, *, rows, reach):
    enter_ref[...] = reached(base_ref, len_ref, near_ref, far_ref, rate_ref, rows, reach).astype(bf16)


def enter_kernel(base_ref, len_ref, near_ref, far_ref, own_ref, got_ref, rate_ref, mine_ref, give_ref, *, rows, reach):
    first = reached(base_ref, len_ref, near_ref, far_ref, rate_ref, rows, reach)
    parity, rate = pair_rates(base_ref, rate_ref, rows, own_ref.shape)
    early, _ = early_late(parity, own_ref[...], got_ref[...])
    through = unbroken(len_ref, base_ref[0] - parity * rows, rows)
    second = early + (jnp.exp(-float(rows) * rate) * through) * first
    give, mine = early_late(parity, second, first)
    mine_ref[...] = mine
    give_ref[...] = give


def final_kernel(
    base_ref, len_ref, state_ref, mine_ref, got_ref, near_ref, short_ref, resid_in, rate_ref, weight_ref, gain_ref,
    *refs,
    span, modes, channels, most, chunk,
):
    if channels:
        hidden_out, normed_out, resid_ref, hidden_ref, sems, masks, wide, tables, sums, whole, normed_ref = refs
    else:
        hidden_out, wide_ref, sum_ref, resid_ref, hidden_ref, sems, masks, wide, tables, sums = refs
    chans = resid_ref.shape[1]

    def fetch(c):
        return cols_copy(resid_in, resid_ref, sems.at[0], c, chunk)

    def store(c):
        return cols_copy(hidden_ref, hidden_out, sems.at[1], c, chunk)

    def store_normed(c):
        return cols_copy(normed_ref, normed_out, sems.at[2], c, chunk)

    for c in range(chans // chunk):
        fetch(c).start()
    rows, starts = doc_start_rows(len_ref, base_ref[0], span)
    for j in range(span):
        masks[0, j] = flag(starts[j] < rows)
    masks[1, 0] = flag(starts[0] < base_ref[0])
    sums[...] = jnp.zeros(sums.shape, f32)

    def group(lanes):
        sub = lax.broadcasted_iota(jnp.int32, (SUBS, LANES), 0).astype(f32) * (-float(span))
        through = masks[1, 0]
        for slot, lane in enumerate(lanes):
            mine, here = half_of(base_ref, resid_ref.shape[0], chans, lane)
            mine = jnp.full((modes, LANES), mine.astype(jnp.int32), jnp.int32) == 1
            enter = jnp.where(mine, mine_ref[:, cols_of(here)], got_ref[:, cols_of(here)])
            rate = rate_ref[:, cols_of(lane)]
            tables[slot, 0] = jnp.exp(-rate)
            tables[slot, 1] = weight_ref[:, cols_of(lane)] * enter
            tables[slot, 2] = rate
        parts = [
            [
                state_ref[pl.ds(n * SUBS, SUBS), cols_of(lane)]
                + (row_of(tables.at[slot, 1], n) * through) * jnp.exp(row_of(tables.at[slot, 2], n) * sub)
                for n in range(modes)
            ]
            for slot, lane in enumerate(lanes)
        ]
        for slot, lane in enumerate(lanes):
            part = parts[slot]
            decay = [row_of(tables.at[slot, 0], n) for n in range(modes)]
            for j in range(span):
                part = [part[n] * decay[n] for n in range(modes)]
                total = part
                while len(total) > 1:
                    total = [total[m] + total[m + 1] for m in range(0, len(total), 2)]
                conv = near_ref[pl.ds(j * SUBS, SUBS), cols_of(lane)] + total[0] * masks[0, j]
                conv = conv.astype(bf16).astype(f32)
                wide[slot, pl.ds(j, SUBS, stride=span + 1), :] = short_ref[pl.ds(j * SUBS, SUBS), cols_of(lane)] * conv
        for b in range(SUBS):
            rows = pl.ds(b * span, span)
            squares = sums[rows, :]
            for slot, lane in enumerate(lanes):
                hidden = wide[slot, pl.ds(b * (span + 1), span), :] + resid_ref[rows, cols_of(lane)].astype(f32)
                if channels:
                    whole[lax.div(lane, LANES), rows, :] = hidden
                else:
                    wide_ref[rows, cols_of(lane)] = hidden
                hidden_ref[rows, cols_of(lane)] = hidden.astype(bf16)
                squares = squares + hidden * hidden
            sums[rows, :] = squares

    each_chunk(chans, chunk, lambda c: fetch(c).wait(), group, lambda c: store(c).start(), most)
    if channels:
        inverse = lax.rsqrt(jnp.sum(sums[...], axis=1, keepdims=True) / channels + 1e-06)
        sums[...] = jnp.broadcast_to(inverse, sums.shape)

        def scale(lanes):
            for lane in lanes:
                normed = whole[lax.div(lane, LANES)] * sums[...] * gain_ref[:, cols_of(lane)]
                normed_ref[:, cols_of(lane)] = normed.astype(bf16)

        each_chunk(chans, chunk, lambda c: None, scale, lambda c: store_normed(c).start(), 4)
        for c in range(chans // chunk):
            store_normed(c).wait()
    else:
        sum_ref[...] = sums[...]
    for c in range(chans // chunk):
        store(c).wait()


def shards(
    query_in, key_in, value_in, short_taps, decay_rate, residues, doc_lengths, residual, norm_gain
):
    tok_rows, chans = query_in.shape
    modes = decay_rate.shape[0]
    span = tok_rows // SUBS
    blocks = lax.axis_size("ctx")
    grp = lax.axis_size("grp")
    chunk = min(chans, 1024)
    pieces = chans // chunk
    ctx_index = lax.axis_index("ctx")
    base = (ctx_index * tok_rows).astype(jnp.int32).reshape(1)
    weight = residues * jnp.sqrt(-jnp.expm1(-2.0 * decay_rate))

    smem = pl.BlockSpec(memory_space=pltpu.SMEM)
    vmem = pl.BlockSpec(memory_space=pltpu.VMEM)
    hbm = pl.BlockSpec(memory_space=pltpu.HBM)
    half = jax.ShapeDtypeStruct((modes, chans // 2), f32)
    tile_shape = (SUBS, LANES)
    wide_rows = SUBS * (span + 1)
    params = pltpu.CompilerParams(vmem_limit_bytes=16 * MIB)

    lengths = pltpu.with_memory_space_constraint(doc_lengths, pltpu.HBM)

    def near_by(x):
        return pltpu.with_memory_space_constraint(x, pltpu.VMEM)

    def far_off(x):
        return pltpu.with_memory_space_constraint(x, pltpu.HBM)

    def copies(kinds):
        return pltpu.SemaphoreType.DMA((kinds, pieces))

    def cost(per_tile, moved):
        return pl.CostEstimate(flops=per_tile * (chans // LANES) * SUBS * LANES, bytes_accessed=moved, transcendentals=0)

    tails = pl.pallas_call(
        tail_kernel,
        in_specs=[hbm, hbm, hbm],
        out_specs=vmem,
        out_shape=pltpu.VMEM((3, 2, chans), bf16),
        scratch_shapes=[pltpu.VMEM((3, 16, chans), bf16), pltpu.SemaphoreType.DMA((3,))],
        compiler_params=params,
        name="tails",
    )(far_off(query_in), far_off(key_in), far_off(value_in))
    rim_rows = from_behind(tails, "ctx", 1)
    rates, weights, taps, rims = near_by(decay_rate), near_by(weight), near_by(short_taps), near_by(rim_rows)
    gates, states, own, give = pl.pallas_call(
        functools.partial(state_kernel, span=span, modes=modes, most=A_TILES, chunk=chunk),
        in_specs=[smem, smem, hbm, hbm, vmem, vmem, vmem, vmem],
        out_specs=[vmem, vmem, vmem, vmem],
        out_shape=[
            pltpu.VMEM((tok_rows, chans), bf16),
            pltpu.VMEM((modes * SUBS, chans), f32),
            pltpu.VMEM(half.shape, f32),
            pltpu.VMEM(half.shape, f32),
        ],
        scratch_shapes=[
            pltpu.VMEM((tok_rows, chans), bf16),
            pltpu.VMEM((tok_rows, chans), bf16),
            copies(2),
            pltpu.VMEM((4, span) + tile_shape, f32),
            pltpu.VMEM((A_TILES, wide_rows, LANES), f32),
            pltpu.VMEM((A_TILES, wide_rows, LANES), f32),
            pltpu.VMEM((A_TILES, 5, modes, LANES), f32),
            pltpu.VMEM((A_TILES, modes, LANES), f32),
            pltpu.VMEM((A_TILES, span) + tile_shape, f32),
        ],
        compiler_params=params,
        cost_estimate=cost(1000, 12 * tok_rows * chans),
        name="block_states",
    )(base, lengths, far_off(key_in), far_off(value_in), rims, taps, rates, weights)

    near = pl.pallas_call(
        functools.partial(near_kernel, span=span, modes=modes, most=N_TILES),
        in_specs=[smem, smem, vmem, vmem, vmem],
        out_specs=vmem,
        out_shape=pltpu.VMEM((tok_rows, chans), f32),
        scratch_shapes=[pltpu.VMEM((2, span) + tile_shape, f32)],
        compiler_params=params,
        cost_estimate=cost(600, 7 * tok_rows * chans),
        name="near_part",
    )(base, lengths, near_by(gates), rates, weights)

    q_short = pl.pallas_call(
        functools.partial(query_kernel, span=span, most=Q_TILES, chunk=chunk),
        in_specs=[smem, smem, hbm, vmem, vmem],
        out_specs=vmem,
        out_shape=pltpu.VMEM((tok_rows, chans), f32),
        scratch_shapes=[
            pltpu.VMEM((tok_rows, chans), bf16),
            pltpu.SemaphoreType.DMA((pieces,)),
            pltpu.VMEM((2, span) + tile_shape, f32),
            pltpu.VMEM((Q_TILES, wide_rows, LANES), f32),
        ],
        compiler_params=params,
        cost_estimate=cost(200, 6 * tok_rows * chans),
        name="query_part",
    )(base, lengths, far_off(query_in), rims, taps)

    got = swap(give, "ctx")

    def pair_call(kernel, operands, out_shape, name, **static):
        count = len(operands) + 1
        return pl.pallas_call(
            functools.partial(kernel, rows=tok_rows, **static),
            in_specs=[smem, smem] + [vmem] * count,
            out_specs=[vmem] * len(out_shape),
            out_shape=out_shape,
            compiler_params=params,
            name=name,
        )(base, lengths, *[near_by(x) for x in operands], rates)

    sent = pltpu.VMEM(half.shape, bf16)
    ends = pair_call(pair_kernel, [own, got], [sent], "pair_ends")[0]
    one_on, two_on = from_behind(ends, "ctx", 2), from_behind(ends, "ctx", 4)
    one_on, two_on, near = lax.optimization_barrier((one_on, two_on, near))
    enter, on, reach = one_on, two_on, 1
    while 2 * reach < blocks // 8:
        enter = pair_call(reach_kernel, [enter, on], [sent], "reach_%d" % (2 * reach), reach=reach)[0]
        reach *= 2
        on = from_behind(enter, "ctx", 2 * reach)
    on, q_short = lax.optimization_barrier((on, q_short))
    mine, give_back = pair_call(
        enter_kernel,
        [enter, on, own, got],
        [pltpu.VMEM(half.shape, f32), pltpu.VMEM(half.shape, f32)],
        "pair_enter",
        reach=reach,
    )
    got_back = swap(give_back, "ctx")

    alone = grp == 1
    out_specs = [hbm]
    out_shape = [jax.ShapeDtypeStruct((tok_rows, chans), bf16)]
    scratch = [
        pltpu.VMEM((tok_rows, chans), bf16),
        pltpu.VMEM((tok_rows, chans), bf16),
        copies(3),
        pltpu.VMEM((2, span) + tile_shape, f32),
        pltpu.VMEM((F_TILES, wide_rows, LANES), f32),
        pltpu.VMEM((F_TILES, 3, modes, LANES), f32),
        pltpu.VMEM((tok_rows, LANES), f32),
    ]
    if alone:
        out_specs.append(hbm)
        out_shape.append(jax.ShapeDtypeStruct((tok_rows, chans), bf16))
        scratch += [pltpu.VMEM((chans // LANES, tok_rows, LANES), f32), pltpu.VMEM((tok_rows, chans), bf16)]
    else:
        out_specs += [vmem, vmem]
        out_shape += [jax.ShapeDtypeStruct((tok_rows, chans), f32), jax.ShapeDtypeStruct((tok_rows, LANES), f32)]
    outs = pl.pallas_call(
        functools.partial(
            final_kernel, span=span, modes=modes, channels=chans if alone else 0, most=F_TILES, chunk=chunk
        ),
        in_specs=[smem, smem, vmem, vmem, vmem, vmem, vmem, hbm, vmem, vmem, vmem],
        out_specs=out_specs,
        out_shape=out_shape,
        scratch_shapes=scratch,
        compiler_params=params,
        cost_estimate=cost(900, 18 * tok_rows * chans),
        name="far_part",
    )(
        base, lengths, near_by(states), near_by(mine), near_by(got_back), near_by(near), near_by(q_short), far_off(residual),
        rates, weights, norm_gain.reshape(1, chans),
    )
    if alone:
        return tuple(outs)
    hidden_out, hidden, sums = outs
    square_sum = lax.psum(jnp.sum(sums, axis=1), "grp")
    inverse_rms = lax.rsqrt(square_sum / (chans * grp) + 1e-06)
    normed = (hidden * inverse_rms[:, None] * norm_gain[None, :]).astype(bf16)
    return (hidden_out, normed)


def solution(mesh):
    return jax.shard_map(
        shards,
        mesh=mesh,
        in_specs=(
            P("ctx", "grp"),
            P("ctx", "grp"),
            P("ctx", "grp"),
            P(None, None, "grp"),
            P(None, "grp"),
            P(None, "grp"),
            P(),
            P("ctx", "grp"),
            P("grp"),
        ),
        out_specs=(P("ctx", "grp"), P("ctx", "grp")),
        check_vma=False,
    )
```

```python
import functools
import math

import jax
import jax.numpy as jnp
from jax import lax
from jax.experimental import pallas as pl
from jax.experimental.pallas import tpu as pltpu
from jax.sharding import PartitionSpec as P

SUBS = 8
LANES = 128
MIB = 1024 * 1024
A_TILES, N_TILES, Q_TILES, F_TILES = 2, 2, 4, 4
NEAR_PARTS = 4
f32 = jnp.float32
bf16 = jnp.bfloat16


def from_behind(shard, axis, by):
    count = lax.axis_size(axis)
    pairs = [(i, i + by) for i in range(count) if 0 <= i + by < count]
    return lax.ppermute(shard, axis, pairs)


def swap(shard, axis):
    return lax.ppermute(shard, axis, [(i, i ^ 1) for i in range(lax.axis_size(axis))])


def doc_start_rows(len_ref, base, span):
    rows = lax.broadcasted_iota(jnp.int32, (SUBS, LANES), 0) * span + base
    starts = [jnp.int32(0)]
    for d in range(len_ref.shape[0] - 1):
        starts.append(starts[-1] + len_ref[d])
    out = []
    for j in range(span):
        pos = rows + j
        best = jnp.zeros((SUBS, LANES), jnp.int32)
        for start in starts[1:]:
            best = jnp.where(pos >= start, start, best)
        out.append(best)
    return rows, out


def flag(cond):
    return jnp.where(cond, 1.0, 0.0).astype(f32)


def each_group(count, most, group):
    size = math.gcd(count, most)

    def step(i, carry):
        group([pl.multiple_of((i * size + m) * LANES, LANES) for m in range(size)])
        return carry

    lax.fori_loop(0, count // size, step, 0)


def each_chunk(chans, chunk, before, group, after, most):
    def step(c, carry):
        before(c)

        def inner(lanes):
            group([pl.multiple_of(c * chunk + lane, LANES) for lane in lanes])

        each_group(chunk // LANES, most, inner)
        after(c)
        return carry

    lax.fori_loop(0, chans // chunk, step, 0)


def cols_copy(src, dst, sem, c, chunk):
    cols = pl.ds(pl.multiple_of(c * chunk, chunk), chunk)
    return pltpu.make_async_copy(src.at[:, cols], dst.at[:, cols], sem.at[c])


def cols_of(lane):
    return pl.ds(lane, LANES)


def row_of(ref, index):
    return jnp.broadcast_to(ref[pl.ds(index, 1), :], (SUBS, LANES))


def spread(x, wide, span, pad=1):
    x = x.astype(f32)
    for b in range(SUBS):
        wide[pl.ds(b * (span + pad), span), :] = x[b * span : (b + 1) * span]


def steps_of(wide, span, pad=1):
    return [wide[pl.ds(j, SUBS, stride=span + pad), :] for j in range(span)]


def short_conv(steps, rim, taps, keep_one, keep_two):
    top = lax.broadcasted_iota(jnp.int32, (SUBS, LANES), 0) == 0
    ahead = [0.0, 0.0] if rim is None else [jnp.broadcast_to(rim[m : m + 1].astype(f32), (SUBS, LANES)) for m in range(2)]
    behind_one = jnp.where(top, ahead[1], pltpu.roll(steps[-1], 1, 0))
    behind_two = jnp.where(top, ahead[0], pltpu.roll(steps[-2], 1, 0))
    padded = [behind_two, behind_one] + steps
    taps = [jnp.broadcast_to(taps[m : m + 1], (SUBS, LANES)) for m in range(3)]
    return [
        taps[0] * padded[j + 2]
        + (taps[1] * padded[j + 1]) * keep_one[j]
        + (taps[2] * padded[j]) * keep_two[j]
        for j in range(len(steps))
    ]


def half_of(base_ref, rows, chans, lane):
    half = chans // 2
    which = lax.div(lane, half)
    mine = which == lax.rem(lax.div(base_ref[0], rows), 2)
    return mine, pl.multiple_of(lane - which * half, LANES)


def state_kernel(
    base_ref, len_ref, key_ref, value_ref, rim_ref, taps_ref, rate_ref, weight_ref,
    gate_ref, state_ref, own_ref, give_ref,
    key_buf, value_buf, sems, masks, wide_k, wide_v, tables, ends, held,
    *, span, modes, most, chunk,
):
    chans = key_buf.shape[1]

    def fetches(c):
        return [cols_copy(key_ref, key_buf, sems.at[0], c, chunk), cols_copy(value_ref, value_buf, sems.at[1], c, chunk)]

    for c in range(chans // chunk):
        for copy in fetches(c):
            copy.start()

    def prepare():
        rows, starts = doc_start_rows(len_ref, base_ref[0], span)
        for j in range(span):
            masks[0, j] = flag(starts[j] < rows + j)
            masks[1, j] = flag(starts[j] < rows + (j - 1))
            masks[2, j] = flag(starts[span - 1] <= rows + j)
        sub = lax.broadcasted_iota(jnp.int32, (SUBS, LANES), 0)
        through = flag(starts[span - 1] < rows)
        one = through * flag(sub >= 1)
        two = one * pltpu.roll(one, 1, 0) * flag(sub >= 2)
        four = two * pltpu.roll(two, 2, 0) * flag(sub >= 4)
        masks[3, 0] = one
        masks[3, 1] = two
        masks[3, 2] = four
        masks[3, 3] = flag(sub >= 1)

    prepare()

    def group(lanes):
        for slot, lane in enumerate(lanes):
            spread(key_buf[:, cols_of(lane)], wide_k.at[slot], span)
            spread(value_buf[:, cols_of(lane)], wide_v.at[slot], span)
            rate = rate_ref[:, cols_of(lane)]
            for m, by in enumerate((1, span, 2 * span, 4 * span)):
                tables[slot, m] = jnp.exp(-float(by) * rate)
            tables[slot, 4] = weight_ref[:, cols_of(lane)]
        for slot, lane in enumerate(lanes):
            cols = cols_of(lane)
            keep_one = [masks[0, j] for j in range(span)]
            keep_two = [masks[1, j] for j in range(span)]
            k_short = short_conv(steps_of(wide_k.at[slot], span), rim_ref[1, :, cols], taps_ref[1, :, cols], keep_one, keep_two)
            v_short = short_conv(steps_of(wide_v.at[slot], span), rim_ref[2, :, cols], taps_ref[2, :, cols], keep_one, keep_two)
            for j in range(0, span, 2):
                pair = jnp.concatenate([k_short[j] * v_short[j], k_short[j + 1] * v_short[j + 1]], axis=0).astype(bf16)
                gate_ref[pl.ds(j * SUBS, 2 * SUBS), cols] = pair
                pair = pair.astype(f32)
                held[slot, j] = pair[:SUBS] * masks[2, j]
                held[slot, j + 1] = pair[SUBS:] * masks[2, j + 1]
        states = []
        for slot, lane in enumerate(lanes):
            decay = [row_of(tables.at[slot, 0], n) for n in range(modes)]
            state = [held[slot, 0]] * modes
            for j in range(1, span):
                gate = held[slot, j]
                state = [decay[n] * state[n] + gate for n in range(modes)]
            states.append(state)
        for m, shift in enumerate((1, 2, 4)):
            for slot in range(len(lanes)):
                states[slot] = [
                    x + (row_of(tables.at[slot, m + 1], n) * masks[3, m]) * pltpu.roll(x, shift, 0)
                    for n, x in enumerate(states[slot])
                ]
        for slot, lane in enumerate(lanes):
            for n, x in enumerate(states[slot]):
                ends[slot, pl.ds(n, 1), :] = x[SUBS - 1 :]
                state_ref[pl.ds(n * SUBS, SUBS), cols_of(lane)] = (
                    row_of(tables.at[slot, 4], n) * masks[3, 3]
                ) * pltpu.roll(x, 1, 0)
        for slot, lane in enumerate(lanes):
            mine, here = half_of(base_ref, key_ref.shape[0], chans, lane)

            @pl.when(mine)
            def _():
                own_ref[:, cols_of(here)] = ends[slot]

            @pl.when(jnp.logical_not(mine))
            def _():
                give_ref[:, cols_of(here)] = ends[slot]

    def before(c):
        for copy in fetches(c):
            copy.wait()

    each_chunk(chans, chunk, before, group, lambda c: None, most)


def tail_kernel(query_ref, key_ref, value_ref, tail_ref, bufs, sems):
    rows, count = query_ref.shape[0], bufs.shape[1]
    copies = [
        pltpu.make_async_copy(ref.at[pl.ds(rows - count, count)], bufs.at[i], sems.at[i])
        for i, ref in enumerate((query_ref, key_ref, value_ref))
    ]
    for copy in copies:
        copy.start()
    for i, copy in enumerate(copies):
        copy.wait()
        tail_ref[i] = bufs[i].astype(f32)[count - 2 :].astype(bf16)


def keep_masks(base_ref, len_ref, masks, span):
    rows, starts = doc_start_rows(len_ref, base_ref[0], span)
    for j in range(span):
        masks[0, j] = flag(starts[j] < rows + j)
        masks[1, j] = flag(starts[j] < rows + (j - 1))


def near_kernel(base_ref, len_ref, gate_ref, rate_ref, weight_ref, *refs, span, modes, most, first, count):
    near_ref, masks = refs[-2:]
    keep_masks(base_ref, len_ref, masks, span)

    def group(lanes):
        taps = []
        for lane in lanes:
            decay = jnp.exp(-rate_ref[:, cols_of(lane)])
            term = weight_ref[:, cols_of(lane)]
            parts = []
            for lag in range(span):
                part = term[:SUBS]
                for n in range(SUBS, modes, SUBS):
                    part = part + term[n : n + SUBS]
                parts.append(part)
                term = term * decay
            taps.append(parts)
        for shift in (1, 2, 4):
            taps = [[part + pltpu.roll(part, shift, 0) for part in parts] for parts in taps]
        for parts, lane in zip(taps, lanes):
            live = []
            for j in range(span):
                if j % 2 == 0:
                    pair = gate_ref[pl.ds(j * SUBS, 2 * SUBS), cols_of(lane)].astype(f32)
                keep = masks[0, j]
                live = [g * keep for g in live]
                live.append(pair[(j % 2) * SUBS : (j % 2 + 1) * SUBS])
                total = parts[0] * live[j]
                for lag in range(1, j + 1):
                    total = total + parts[lag] * live[j - lag]
                near_ref[pl.ds(j * SUBS, SUBS), cols_of(lane)] = total

    each_group(count // LANES, most, lambda lanes: group([pl.multiple_of(first + lane, LANES) for lane in lanes]))


def query_kernel(base_ref, len_ref, query_ref, taps_ref, short_ref, query_buf, sems, masks, wide_q, *, span, most, chunk):
    chans = query_buf.shape[1]

    def fetch(c):
        return cols_copy(query_ref, query_buf, sems, c, chunk)

    for c in range(chans // chunk):
        fetch(c).start()
    keep_masks(base_ref, len_ref, masks, span)

    def group(lanes):
        for slot, lane in enumerate(lanes):
            spread(query_buf[:, cols_of(lane)], wide_q.at[slot], span, 0)
        for slot, lane in enumerate(lanes):
            cols = cols_of(lane)
            keep_one = [masks[0, j] for j in range(span)]
            keep_two = [masks[1, j] for j in range(span)]
            q_short = short_conv(steps_of(wide_q.at[slot], span, 0), None, taps_ref[0, :, cols], keep_one, keep_two)
            for j in range(span):
                short_ref[pl.ds(j * SUBS, SUBS), cols] = q_short[j]

    each_chunk(chans, chunk, lambda c: fetch(c).wait(), group, lambda c: None, most)


def unbroken(len_ref, first, count):
    start = jnp.int32(0)
    whole = jnp.where((first <= 0) & (first + count > 0), 0.0, 1.0)
    for d in range(len_ref.shape[0] - 1):
        start = start + len_ref[d]
        whole = jnp.where((start >= first) & (start < first + count), 0.0, whole)
    return whole.astype(f32)


def pair_rates(base_ref, rate_ref, rows, shape):
    parity = lax.rem(lax.div(base_ref[0], rows), 2)
    return parity, rate_ref[:, pl.ds(pl.multiple_of(parity * shape[1], LANES), shape[1])]


def early_late(parity, own, got):
    odd = jnp.full(own.shape, parity, jnp.int32) == 1
    return jnp.where(odd, got, own), jnp.where(odd, own, got)


def pair_kernel(base_ref, len_ref, own_ref, got_ref, rate_ref, end_ref, *, rows):
    parity, rate = pair_rates(base_ref, rate_ref, rows, own_ref.shape)
    early, late = early_late(parity, own_ref[...], got_ref[...])
    through = unbroken(len_ref, base_ref[0] + (1 - parity) * rows, rows)
    end_ref[...] = (late + (jnp.exp(-float(rows) * rate) * through) * early).astype(bf16)


def reached(base_ref, len_ref, near_ref, far_ref, rate_ref, rows, reach):
    parity, rate = pair_rates(base_ref, rate_ref, rows, near_ref.shape)
    span = 2 * rows * reach
    through = unbroken(len_ref, base_ref[0] - parity * rows - span, span)
    return near_ref[...].astype(f32) + (jnp.exp(-float(span) * rate) * through) * far_ref[...].astype(f32)


def reach_kernel(base_ref, len_ref, near_ref, far_ref, rate_ref, enter_ref, *, rows, reach):
    enter_ref[...] = reached(base_ref, len_ref, near_ref, far_ref, rate_ref, rows, reach).astype(bf16)


def enter_kernel(base_ref, len_ref, near_ref, far_ref, own_ref, got_ref, rate_ref, mine_ref, give_ref, *, rows, reach):
    first = reached(base_ref, len_ref, near_ref, far_ref, rate_ref, rows, reach)
    parity, rate = pair_rates(base_ref, rate_ref, rows, own_ref.shape)
    early, _ = early_late(parity, own_ref[...], got_ref[...])
    through = unbroken(len_ref, base_ref[0] - parity * rows, rows)
    second = early + (jnp.exp(-float(rows) * rate) * through) * first
    give, mine = early_late(parity, second, first)
    mine_ref[...] = mine
    give_ref[...] = give


def final_kernel(
    base_ref, len_ref, state_ref, mine_ref, got_ref, near_ref, short_ref, resid_in, rim_ref, taps_ref, rate_ref, weight_ref, gain_ref,
    *refs,
    span, modes, channels, most, chunk,
):
    if channels:
        hidden_out, normed_out, resid_ref, hidden_ref, sems, masks, wide, tables, sums, whole, normed_ref = refs
    else:
        hidden_out, wide_ref, sum_ref, resid_ref, hidden_ref, sems, masks, wide, tables, sums = refs
    chans = resid_ref.shape[1]

    def fetch(c):
        return cols_copy(resid_in, resid_ref, sems.at[0], c, chunk)

    def store(c):
        return cols_copy(hidden_ref, hidden_out, sems.at[1], c, chunk)

    def store_normed(c):
        return cols_copy(normed_ref, normed_out, sems.at[2], c, chunk)

    for c in range(chans // chunk):
        fetch(c).start()
    rows, starts = doc_start_rows(len_ref, base_ref[0], span)
    for j in range(span):
        masks[0, j] = flag(starts[j] < rows)
    masks[1, 0] = flag(starts[0] < base_ref[0])
    top = flag(lax.broadcasted_iota(jnp.int32, (SUBS, LANES), 0) == 0)
    masks[1, 1] = top * flag(starts[0] < rows)
    masks[1, 2] = top * flag(starts[0] < rows - 1)
    masks[1, 3] = top * flag(starts[1] < rows)
    sums[...] = jnp.zeros(sums.shape, f32)

    def group(lanes):
        sub = lax.broadcasted_iota(jnp.int32, (SUBS, LANES), 0).astype(f32) * (-float(span))
        through = masks[1, 0]
        for slot, lane in enumerate(lanes):
            mine, here = half_of(base_ref, resid_ref.shape[0], chans, lane)
            mine = jnp.full((modes, LANES), mine.astype(jnp.int32), jnp.int32) == 1
            enter = jnp.where(mine, mine_ref[:, cols_of(here)], got_ref[:, cols_of(here)])
            rate = rate_ref[:, cols_of(lane)]
            tables[slot, 0] = jnp.exp(-rate)
            tables[slot, 1] = weight_ref[:, cols_of(lane)] * enter
            tables[slot, 2] = rate
        parts = [
            [
                state_ref[pl.ds(n * SUBS, SUBS), cols_of(lane)]
                + (row_of(tables.at[slot, 1], n) * through) * jnp.exp(row_of(tables.at[slot, 2], n) * sub)
                for n in range(modes)
            ]
            for slot, lane in enumerate(lanes)
        ]
        for slot, lane in enumerate(lanes):
            part = parts[slot]
            decay = [row_of(tables.at[slot, 0], n) for n in range(modes)]
            rim = rim_ref[0, :, cols_of(lane)].astype(f32)
            tap = taps_ref[0, :, cols_of(lane)]
            edge = [
                (tap[1:2] * rim[1:2]) * masks[1, 1] + (tap[2:3] * rim[0:1]) * masks[1, 2],
                (tap[2:3] * rim[1:2]) * masks[1, 3],
            ]
            for j in range(span):
                part = [part[n] * decay[n] for n in range(modes)]
                total = part
                while len(total) > 1:
                    total = [total[m] + total[m + 1] for m in range(0, len(total), 2)]
                conv = near_ref[pl.ds(j * SUBS, SUBS), cols_of(lane)] + total[0] * masks[0, j]
                conv = conv.astype(bf16).astype(f32)
                short = short_ref[pl.ds(j * SUBS, SUBS), cols_of(lane)]
                if j < 2:
                    short = short + edge[j]
                wide[slot, pl.ds(j, SUBS, stride=span + 1), :] = short * conv
        for b in range(SUBS):
            rows = pl.ds(b * span, span)
            squares = sums[rows, :]
            for slot, lane in enumerate(lanes):
                hidden = wide[slot, pl.ds(b * (span + 1), span), :] + resid_ref[rows, cols_of(lane)].astype(f32)
                if channels:
                    whole[lax.div(lane, LANES), rows, :] = hidden
                else:
                    wide_ref[rows, cols_of(lane)] = hidden
                hidden_ref[rows, cols_of(lane)] = hidden.astype(bf16)
                squares = squares + hidden * hidden
            sums[rows, :] = squares

    each_chunk(chans, chunk, lambda c: fetch(c).wait(), group, lambda c: store(c).start(), most)
    if channels:
        inverse = lax.rsqrt(jnp.sum(sums[...], axis=1, keepdims=True) / channels + 1e-06)
        sums[...] = jnp.broadcast_to(inverse, sums.shape)

        def scale(lanes):
            for lane in lanes:
                normed = whole[lax.div(lane, LANES)] * sums[...] * gain_ref[:, cols_of(lane)]
                normed_ref[:, cols_of(lane)] = normed.astype(bf16)

        each_chunk(chans, chunk, lambda c: None, scale, lambda c: store_normed(c).start(), 4)
        for c in range(chans // chunk):
            store_normed(c).wait()
    else:
        sum_ref[...] = sums[...]
    for c in range(chans // chunk):
        store(c).wait()


def shards(
    query_in, key_in, value_in, short_taps, decay_rate, residues, doc_lengths, residual, norm_gain
):
    tok_rows, chans = query_in.shape
    modes = decay_rate.shape[0]
    span = tok_rows // SUBS
    blocks = lax.axis_size("ctx")
    grp = lax.axis_size("grp")
    chunk = min(chans, 1024)
    pieces = chans // chunk
    ctx_index = lax.axis_index("ctx")
    base = (ctx_index * tok_rows).astype(jnp.int32).reshape(1)
    weight = residues * jnp.sqrt(-jnp.expm1(-2.0 * decay_rate))

    smem = pl.BlockSpec(memory_space=pltpu.SMEM)
    vmem = pl.BlockSpec(memory_space=pltpu.VMEM)
    hbm = pl.BlockSpec(memory_space=pltpu.HBM)
    half = jax.ShapeDtypeStruct((modes, chans // 2), f32)
    tile_shape = (SUBS, LANES)
    wide_rows = SUBS * (span + 1)
    params = pltpu.CompilerParams(vmem_limit_bytes=16 * MIB)

    lengths = pltpu.with_memory_space_constraint(doc_lengths, pltpu.HBM)

    def near_by(x):
        return pltpu.with_memory_space_constraint(x, pltpu.VMEM)

    def far_off(x):
        return pltpu.with_memory_space_constraint(x, pltpu.HBM)

    def copies(kinds):
        return pltpu.SemaphoreType.DMA((kinds, pieces))

    def cost(per_tile, moved):
        return pl.CostEstimate(flops=per_tile * (chans // LANES) * SUBS * LANES, bytes_accessed=moved, transcendentals=0)

    tails = pl.pallas_call(
        tail_kernel,
        in_specs=[hbm, hbm, hbm],
        out_specs=vmem,
        out_shape=pltpu.VMEM((3, 2, chans), bf16),
        scratch_shapes=[pltpu.VMEM((3, 16, chans), bf16), pltpu.SemaphoreType.DMA((3,))],
        compiler_params=params,
        name="tails",
    )(far_off(query_in), far_off(key_in), far_off(value_in))
    rim_rows = from_behind(tails, "ctx", 1)
    q_short = pl.pallas_call(
        functools.partial(query_kernel, span=span, most=Q_TILES, chunk=chunk),
        in_specs=[smem, smem, hbm, vmem],
        out_specs=vmem,
        out_shape=pltpu.VMEM((tok_rows, chans), f32),
        scratch_shapes=[
            pltpu.VMEM((tok_rows, chans), bf16),
            pltpu.SemaphoreType.DMA((pieces,)),
            pltpu.VMEM((2, span) + tile_shape, f32),
            pltpu.VMEM((Q_TILES, wide_rows, LANES), f32),
        ],
        compiler_params=params,
        cost_estimate=cost(200, 6 * tok_rows * chans),
        name="query_part",
    )(base, lengths, far_off(query_in), near_by(short_taps))
    rim_rows, q_short = lax.optimization_barrier((rim_rows, q_short))
    rates, weights, taps, rims = near_by(decay_rate), near_by(weight), near_by(short_taps), near_by(rim_rows)
    gates, states, own, give = pl.pallas_call(
        functools.partial(state_kernel, span=span, modes=modes, most=A_TILES, chunk=chunk),
        in_specs=[smem, smem, hbm, hbm, vmem, vmem, vmem, vmem],
        out_specs=[vmem, vmem, vmem, vmem],
        out_shape=[
            pltpu.VMEM((tok_rows, chans), bf16),
            pltpu.VMEM((modes * SUBS, chans), f32),
            pltpu.VMEM(half.shape, f32),
            pltpu.VMEM(half.shape, f32),
        ],
        scratch_shapes=[
            pltpu.VMEM((tok_rows, chans), bf16),
            pltpu.VMEM((tok_rows, chans), bf16),
            copies(2),
            pltpu.VMEM((4, span) + tile_shape, f32),
            pltpu.VMEM((A_TILES, wide_rows, LANES), f32),
            pltpu.VMEM((A_TILES, wide_rows, LANES), f32),
            pltpu.VMEM((A_TILES, 5, modes, LANES), f32),
            pltpu.VMEM((A_TILES, modes, LANES), f32),
            pltpu.VMEM((A_TILES, span) + tile_shape, f32),
        ],
        compiler_params=params,
        cost_estimate=cost(1000, 12 * tok_rows * chans),
        name="block_states",
    )(base, lengths, far_off(key_in), far_off(value_in), rims, taps, rates, weights)

    def near_piece(part, near):
        count = chans // NEAR_PARTS
        before = [] if near is None else [near_by(near)]
        return pl.pallas_call(
            functools.partial(
                near_kernel, span=span, modes=modes, most=N_TILES, first=part * count, count=count
            ),
            in_specs=[smem, smem, vmem, vmem, vmem] + [vmem] * len(before),
            out_specs=vmem,
            out_shape=pltpu.VMEM((tok_rows, chans), f32),
            scratch_shapes=[pltpu.VMEM((2, span) + tile_shape, f32)],
            compiler_params=params,
            input_output_aliases={5: 0} if before else {},
            cost_estimate=cost(600 // NEAR_PARTS, 7 * tok_rows * count),
            name="near_part_%d" % part,
        )(base, lengths, near_by(gates), rates, weights, *before)

    got = swap(give, "ctx")
    near = near_piece(0, None)
    got, near = lax.optimization_barrier((got, near))

    def pair_call(kernel, operands, out_shape, name, **static):
        count = len(operands) + 1
        return pl.pallas_call(
            functools.partial(kernel, rows=tok_rows, **static),
            in_specs=[smem, smem] + [vmem] * count,
            out_specs=[vmem] * len(out_shape),
            out_shape=out_shape,
            compiler_params=params,
            name=name,
        )(base, lengths, *[near_by(x) for x in operands], rates)

    sent = pltpu.VMEM(half.shape, bf16)
    ends = pair_call(pair_kernel, [own, got], [sent], "pair_ends")[0]
    one_on, two_on = from_behind(ends, "ctx", 2), from_behind(ends, "ctx", 4)
    near = near_piece(1, near)
    one_on, two_on, near = lax.optimization_barrier((one_on, two_on, near))
    enter, on, reach = one_on, two_on, 1
    while 2 * reach < blocks // 8:
        enter = pair_call(reach_kernel, [enter, on], [sent], "reach_%d" % (2 * reach), reach=reach)[0]
        reach *= 2
        on = from_behind(enter, "ctx", 2 * reach)
    near = near_piece(2, near)
    on, near = lax.optimization_barrier((on, near))
    mine, give_back = pair_call(
        enter_kernel,
        [enter, on, own, got],
        [pltpu.VMEM(half.shape, f32), pltpu.VMEM(half.shape, f32)],
        "pair_enter",
        reach=reach,
    )
    got_back = swap(give_back, "ctx")
    near = near_piece(3, near)

    alone = grp == 1
    out_specs = [hbm]
    out_shape = [jax.ShapeDtypeStruct((tok_rows, chans), bf16)]
    scratch = [
        pltpu.VMEM((tok_rows, chans), bf16),
        pltpu.VMEM((tok_rows, chans), bf16),
        copies(3),
        pltpu.VMEM((2, span) + tile_shape, f32),
        pltpu.VMEM((F_TILES, wide_rows, LANES), f32),
        pltpu.VMEM((F_TILES, 3, modes, LANES), f32),
        pltpu.VMEM((tok_rows, LANES), f32),
    ]
    if alone:
        out_specs.append(hbm)
        out_shape.append(jax.ShapeDtypeStruct((tok_rows, chans), bf16))
        scratch += [pltpu.VMEM((chans // LANES, tok_rows, LANES), f32), pltpu.VMEM((tok_rows, chans), bf16)]
    else:
        out_specs += [vmem, vmem]
        out_shape += [jax.ShapeDtypeStruct((tok_rows, chans), f32), jax.ShapeDtypeStruct((tok_rows, LANES), f32)]
    outs = pl.pallas_call(
        functools.partial(
            final_kernel, span=span, modes=modes, channels=chans if alone else 0, most=F_TILES, chunk=chunk
        ),
        in_specs=[smem, smem, vmem, vmem, vmem, vmem, vmem, hbm, vmem, vmem, vmem, vmem, vmem],
        out_specs=out_specs,
        out_shape=out_shape,
        scratch_shapes=scratch,
        compiler_params=params,
        cost_estimate=cost(900, 18 * tok_rows * chans),
        name="far_part",
    )(
        base, lengths, near_by(states), near_by(mine), near_by(got_back), near_by(near), near_by(q_short), far_off(residual),
        rims, taps, rates, weights, norm_gain.reshape(1, chans),
    )
    if alone:
        return tuple(outs)
    hidden_out, hidden, sums = outs
    square_sum = lax.psum(jnp.sum(sums, axis=1), "grp")
    inverse_rms = lax.rsqrt(square_sum / (chans * grp) + 1e-06)
    normed = (hidden * inverse_rms[:, None] * norm_gain[None, :]).astype(bf16)
    return (hidden_out, normed)


def solution(mesh):
    return jax.shard_map(
        shards,
        mesh=mesh,
        in_specs=(
            P("ctx", "grp"),
            P("ctx", "grp"),
            P("ctx", "grp"),
            P(None, None, "grp"),
            P(None, "grp"),
            P(None, "grp"),
            P(),
            P("ctx", "grp"),
            P("grp"),
        ),
        out_specs=(P("ctx", "grp"), P("ctx", "grp")),
        check_vma=False,
    )
```

```python
import functools
import math

import jax
import jax.numpy as jnp
from jax import lax
from jax.experimental import pallas as pl
from jax.experimental.pallas import tpu as pltpu
from jax.sharding import PartitionSpec as P

SUBS = 8
LANES = 128
MIB = 1024 * 1024
A_TILES, N_TILES, Q_TILES, F_TILES = 2, 2, 4, 4
NEAR_PARTS = 2
f32 = jnp.float32
bf16 = jnp.bfloat16


def from_behind(shard, axis, by):
    count = lax.axis_size(axis)
    pairs = [(i, i + by) for i in range(count) if 0 <= i + by < count]
    return lax.ppermute(shard, axis, pairs)


def swap(shard, axis):
    return lax.ppermute(shard, axis, [(i, i ^ 1) for i in range(lax.axis_size(axis))])


def doc_start_rows(len_ref, base, span):
    rows = lax.broadcasted_iota(jnp.int32, (SUBS, LANES), 0) * span + base
    starts = [jnp.int32(0)]
    for d in range(len_ref.shape[0] - 1):
        starts.append(starts[-1] + len_ref[d])
    out = []
    for j in range(span):
        pos = rows + j
        best = jnp.zeros((SUBS, LANES), jnp.int32)
        for start in starts[1:]:
            best = jnp.where(pos >= start, start, best)
        out.append(best)
    return rows, out


def flag(cond):
    return jnp.where(cond, 1.0, 0.0).astype(f32)


def each_group(count, most, group):
    size = math.gcd(count, most)

    def step(i, carry):
        group([pl.multiple_of((i * size + m) * LANES, LANES) for m in range(size)])
        return carry

    lax.fori_loop(0, count // size, step, 0)


def each_chunk(chans, chunk, before, group, after, most):
    def step(c, carry):
        before(c)

        def inner(lanes):
            group([pl.multiple_of(c * chunk + lane, LANES) for lane in lanes])

        each_group(chunk // LANES, most, inner)
        after(c)
        return carry

    lax.fori_loop(0, chans // chunk, step, 0)


def cols_copy(src, dst, sem, c, chunk):
    cols = pl.ds(pl.multiple_of(c * chunk, chunk), chunk)
    return pltpu.make_async_copy(src.at[:, cols], dst.at[:, cols], sem.at[c])


def cols_of(lane):
    return pl.ds(lane, LANES)


def row_of(ref, index):
    return jnp.broadcast_to(ref[pl.ds(index, 1), :], (SUBS, LANES))


def spread(x, wide, span):
    x = x.astype(f32)
    for b in range(SUBS):
        wide[pl.ds(b * (span + 1), span), :] = x[b * span : (b + 1) * span]


class Conv:
    def __init__(self, wide, rim, taps, span):
        self.wide, self.span = wide, span
        self.taps = [jnp.broadcast_to(taps[m : m + 1], (SUBS, LANES)) for m in range(3)]
        top = lax.broadcasted_iota(jnp.int32, (SUBS, LANES), 0) == 0
        ahead = [0.0, 0.0] if rim is None else [jnp.broadcast_to(rim[m : m + 1].astype(f32), (SUBS, LANES)) for m in range(2)]
        self.behind = [jnp.where(top, ahead[m], pltpu.roll(self.row(span - 2 + m), 1, 0)) for m in range(2)]

    def row(self, j):
        return self.wide[pl.ds(j, SUBS, stride=self.span + 1), :]

    def step(self, j, keep_one, keep_two):
        here = self.row(j)
        two, one = self.behind
        self.behind = [one, here]
        return self.taps[0] * here + (self.taps[1] * one) * keep_one + (self.taps[2] * two) * keep_two


def half_of(base_ref, rows, chans, lane):
    half = chans // 2
    which = lax.div(lane, half)
    mine = which == lax.rem(lax.div(base_ref[0], rows), 2)
    return mine, pl.multiple_of(lane - which * half, LANES)


def state_kernel(
    base_ref, len_ref, key_ref, value_ref, rim_ref, taps_ref, rate_ref, weight_ref,
    gate_ref, state_ref, own_ref, give_ref,
    key_buf, value_buf, sems, masks, wide_k, wide_v, tables, ends, held,
    *, span, modes, most, chunk,
):
    chans = key_buf.shape[1]

    def fetches(c):
        return [cols_copy(key_ref, key_buf, sems.at[0], c, chunk), cols_copy(value_ref, value_buf, sems.at[1], c, chunk)]

    for c in range(chans // chunk):
        for copy in fetches(c):
            copy.start()

    def prepare():
        rows, starts = doc_start_rows(len_ref, base_ref[0], span)
        for j in range(span):
            masks[0, j] = flag(starts[j] < rows + j)
            masks[1, j] = flag(starts[j] < rows + (j - 1))
            masks[2, j] = flag(starts[span - 1] <= rows + j)
        sub = lax.broadcasted_iota(jnp.int32, (SUBS, LANES), 0)
        through = flag(starts[span - 1] < rows)
        one = through * flag(sub >= 1)
        two = one * pltpu.roll(one, 1, 0) * flag(sub >= 2)
        four = two * pltpu.roll(two, 2, 0) * flag(sub >= 4)
        masks[3, 0] = one
        masks[3, 1] = two
        masks[3, 2] = four
        masks[3, 3] = flag(sub >= 1)

    prepare()

    def group(lanes):
        for slot, lane in enumerate(lanes):
            spread(key_buf[:, cols_of(lane)], wide_k.at[slot], span)
            spread(value_buf[:, cols_of(lane)], wide_v.at[slot], span)
            rate = rate_ref[:, cols_of(lane)]
            for m, by in enumerate((1, span, 2 * span, 4 * span)):
                tables[slot, m] = jnp.exp(-float(by) * rate)
            tables[slot, 4] = weight_ref[:, cols_of(lane)]
        convs = [
            [
                Conv(wide.at[slot], rim_ref[i, :, cols_of(lane)], taps_ref[i, :, cols_of(lane)], span)
                for i, wide in ((1, wide_k), (2, wide_v))
            ]
            for slot, lane in enumerate(lanes)
        ]
        last = [None] * len(lanes)
        for j in range(span):
            keep_one, keep_two = masks[0, j], masks[1, j]
            for slot, lane in enumerate(lanes):
                k_short, v_short = [conv.step(j, keep_one, keep_two) for conv in convs[slot]]
                if j % 2 == 0:
                    last[slot] = k_short * v_short
                    continue
                pair = jnp.concatenate([last[slot], k_short * v_short], axis=0).astype(bf16)
                gate_ref[pl.ds((j - 1) * SUBS, 2 * SUBS), cols_of(lane)] = pair
                pair = pair.astype(f32)
                held[slot, j - 1] = pair[:SUBS] * masks[2, j - 1]
                held[slot, j] = pair[SUBS:] * masks[2, j]
        states = []
        for slot, lane in enumerate(lanes):
            decay = [row_of(tables.at[slot, 0], n) for n in range(modes)]
            state = [held[slot, 0]] * modes
            for j in range(1, span):
                gate = held[slot, j]
                state = [decay[n] * state[n] + gate for n in range(modes)]
            states.append(state)
        for m, shift in enumerate((1, 2, 4)):
            joined = masks[3, m] > 0.0
            for slot in range(len(lanes)):
                states[slot] = [
                    x + jnp.where(joined, row_of(tables.at[slot, m + 1], n) * pltpu.roll(x, shift, 0), 0.0)
                    for n, x in enumerate(states[slot])
                ]
        inner = masks[3, 3] > 0.0
        for slot, lane in enumerate(lanes):
            for n, x in enumerate(states[slot]):
                ends[slot, pl.ds(n, 1), :] = x[SUBS - 1 :]
                state_ref[pl.ds(n * SUBS, SUBS), cols_of(lane)] = jnp.where(
                    inner, row_of(tables.at[slot, 4], n) * pltpu.roll(x, 1, 0), 0.0
                )
        for slot, lane in enumerate(lanes):
            mine, here = half_of(base_ref, key_ref.shape[0], chans, lane)

            @pl.when(mine)
            def _():
                own_ref[:, cols_of(here)] = ends[slot]

            @pl.when(jnp.logical_not(mine))
            def _():
                give_ref[:, cols_of(here)] = ends[slot]

    def before(c):
        for copy in fetches(c):
            copy.wait()

    each_chunk(chans, chunk, before, group, lambda c: None, most)


def tail_kernel(query_ref, key_ref, value_ref, tail_ref, bufs, sems):
    rows, count = query_ref.shape[0], bufs.shape[1]
    copies = [
        pltpu.make_async_copy(ref.at[pl.ds(rows - count, count)], bufs.at[i], sems.at[i])
        for i, ref in enumerate((query_ref, key_ref, value_ref))
    ]
    for copy in copies:
        copy.start()
    for i, copy in enumerate(copies):
        copy.wait()
        tail_ref[i] = bufs[i].astype(f32)[count - 2 :].astype(bf16)


def keep_masks(base_ref, len_ref, masks, span):
    rows, starts = doc_start_rows(len_ref, base_ref[0], span)
    for j in range(span):
        masks[0, j] = flag(starts[j] < rows + j)
        masks[1, j] = flag(starts[j] < rows + (j - 1))


def near_kernel(base_ref, len_ref, gate_ref, rate_ref, weight_ref, *refs, span, modes, most, first, count):
    near_ref, masks = refs[-2:]
    keep_masks(base_ref, len_ref, masks, span)

    def group(lanes):
        taps = []
        for lane in lanes:
            decay = jnp.exp(-rate_ref[:, cols_of(lane)])
            term = weight_ref[:, cols_of(lane)]
            parts = []
            for lag in range(span):
                part = term[:SUBS]
                for n in range(SUBS, modes, SUBS):
                    part = part + term[n : n + SUBS]
                parts.append(part)
                term = term * decay
            taps.append(parts)
        for shift in (1, 2, 4):
            taps = [[part + pltpu.roll(part, shift, 0) for part in parts] for parts in taps]
        for parts, lane in zip(taps, lanes):
            live = []
            for j in range(span):
                if j % 2 == 0:
                    pair = gate_ref[pl.ds(j * SUBS, 2 * SUBS), cols_of(lane)].astype(f32)
                keep = masks[0, j]
                live = [g * keep for g in live]
                live.append(pair[(j % 2) * SUBS : (j % 2 + 1) * SUBS])
                total = parts[0] * live[j]
                for lag in range(1, j + 1):
                    total = total + parts[lag] * live[j - lag]
                near_ref[pl.ds(j * SUBS, SUBS), cols_of(lane)] = total

    each_group(count // LANES, most, lambda lanes: group([pl.multiple_of(first + lane, LANES) for lane in lanes]))


def query_kernel(base_ref, len_ref, query_ref, taps_ref, short_ref, query_buf, sems, masks, wide_q, *, span, most, chunk):
    chans = query_buf.shape[1]

    def fetch(c):
        return cols_copy(query_ref, query_buf, sems, c, chunk)

    for c in range(chans // chunk):
        fetch(c).start()
    keep_masks(base_ref, len_ref, masks, span)

    def group(lanes):
        for slot, lane in enumerate(lanes):
            spread(query_buf[:, cols_of(lane)], wide_q.at[slot], span)
        convs = [Conv(wide_q.at[slot], None, taps_ref[0, :, cols_of(lane)], span) for slot, lane in enumerate(lanes)]
        for j in range(span):
            keep_one, keep_two = masks[0, j], masks[1, j]
            for slot, lane in enumerate(lanes):
                short_ref[pl.ds(j * SUBS, SUBS), cols_of(lane)] = convs[slot].step(j, keep_one, keep_two)

    each_chunk(chans, chunk, lambda c: fetch(c).wait(), group, lambda c: None, most)


def unbroken(len_ref, first, count):
    start = jnp.int32(0)
    whole = jnp.where((first <= 0) & (first + count > 0), 0.0, 1.0)
    for d in range(len_ref.shape[0] - 1):
        start = start + len_ref[d]
        whole = jnp.where((start >= first) & (start < first + count), 0.0, whole)
    return whole.astype(f32)


def pair_rates(base_ref, rate_ref, rows, shape):
    parity = lax.rem(lax.div(base_ref[0], rows), 2)
    return parity, rate_ref[:, pl.ds(pl.multiple_of(parity * shape[1], LANES), shape[1])]


def early_late(parity, own, got):
    odd = jnp.full(own.shape, parity, jnp.int32) == 1
    return jnp.where(odd, got, own), jnp.where(odd, own, got)


def pair_kernel(base_ref, len_ref, own_ref, got_ref, rate_ref, end_ref, *, rows):
    parity, rate = pair_rates(base_ref, rate_ref, rows, own_ref.shape)
    early, late = early_late(parity, own_ref[...], got_ref[...])
    through = unbroken(len_ref, base_ref[0] + (1 - parity) * rows, rows)
    end_ref[...] = (late + (jnp.exp(-float(rows) * rate) * through) * early).astype(bf16)


def reached(base_ref, len_ref, near_ref, far_ref, rate_ref, rows, reach):
    parity, rate = pair_rates(base_ref, rate_ref, rows, near_ref.shape)
    span = 2 * rows * reach
    through = unbroken(len_ref, base_ref[0] - parity * rows - span, span)
    return near_ref[...].astype(f32) + (jnp.exp(-float(span) * rate) * through) * far_ref[...].astype(f32)


def reach_kernel(base_ref, len_ref, near_ref, far_ref, rate_ref, enter_ref, *, rows, reach):
    enter_ref[...] = reached(base_ref, len_ref, near_ref, far_ref, rate_ref, rows, reach).astype(bf16)


def enter_kernel(base_ref, len_ref, near_ref, far_ref, own_ref, got_ref, rate_ref, mine_ref, give_ref, *, rows, reach):
    first = reached(base_ref, len_ref, near_ref, far_ref, rate_ref, rows, reach)
    parity, rate = pair_rates(base_ref, rate_ref, rows, own_ref.shape)
    early, _ = early_late(parity, own_ref[...], got_ref[...])
    through = unbroken(len_ref, base_ref[0] - parity * rows, rows)
    second = early + (jnp.exp(-float(rows) * rate) * through) * first
    give, mine = early_late(parity, second, first)
    mine_ref[...] = mine
    give_ref[...] = give


def final_kernel(
    base_ref, len_ref, state_ref, mine_ref, got_ref, near_ref, short_ref, resid_in, rim_ref, taps_ref, rate_ref, weight_ref, gain_ref,
    *refs,
    span, modes, channels, most, chunk,
):
    if channels:
        hidden_out, normed_out, resid_ref, hidden_ref, sems, masks, wide, tables, sums, whole, normed_ref = refs
    else:
        hidden_out, wide_ref, sum_ref, resid_ref, hidden_ref, sems, masks, wide, tables, sums = refs
    chans = resid_ref.shape[1]

    def fetch(c):
        return cols_copy(resid_in, resid_ref, sems.at[0], c, chunk)

    def store(c):
        return cols_copy(hidden_ref, hidden_out, sems.at[1], c, chunk)

    def store_normed(c):
        return cols_copy(normed_ref, normed_out, sems.at[2], c, chunk)

    for c in range(chans // chunk):
        fetch(c).start()
    rows, starts = doc_start_rows(len_ref, base_ref[0], span)
    for j in range(span):
        masks[0, j] = flag(starts[j] < rows)
    masks[1, 0] = flag(starts[0] < base_ref[0])
    top = flag(lax.broadcasted_iota(jnp.int32, (SUBS, LANES), 0) == 0)
    masks[1, 1] = top * flag(starts[0] < rows)
    masks[1, 2] = top * flag(starts[0] < rows - 1)
    masks[1, 3] = top * flag(starts[1] < rows)
    sums[...] = jnp.zeros(sums.shape, f32)

    def group(lanes):
        sub = lax.broadcasted_iota(jnp.int32, (SUBS, LANES), 0).astype(f32) * (-float(span))
        through = masks[1, 0]
        for slot, lane in enumerate(lanes):
            mine, here = half_of(base_ref, resid_ref.shape[0], chans, lane)
            mine = jnp.full((modes, LANES), mine.astype(jnp.int32), jnp.int32) == 1
            enter = jnp.where(mine, mine_ref[:, cols_of(here)], got_ref[:, cols_of(here)])
            rate = rate_ref[:, cols_of(lane)]
            tables[slot, 0] = jnp.exp(-rate)
            tables[slot, 1] = weight_ref[:, cols_of(lane)] * enter
            tables[slot, 2] = rate
        parts = [
            [
                state_ref[pl.ds(n * SUBS, SUBS), cols_of(lane)]
                + (row_of(tables.at[slot, 1], n) * through) * jnp.exp(row_of(tables.at[slot, 2], n) * sub)
                for n in range(modes)
            ]
            for slot, lane in enumerate(lanes)
        ]
        for slot, lane in enumerate(lanes):
            part = parts[slot]
            decay = [row_of(tables.at[slot, 0], n) for n in range(modes)]
            rim = rim_ref[0, :, cols_of(lane)].astype(f32)
            tap = taps_ref[0, :, cols_of(lane)]
            edge = [
                (tap[1:2] * rim[1:2]) * masks[1, 1] + (tap[2:3] * rim[0:1]) * masks[1, 2],
                (tap[2:3] * rim[1:2]) * masks[1, 3],
            ]
            for j in range(span):
                part = [part[n] * decay[n] for n in range(modes)]
                total = part
                while len(total) > 1:
                    total = [total[m] + total[m + 1] for m in range(0, len(total), 2)]
                conv = near_ref[pl.ds(j * SUBS, SUBS), cols_of(lane)] + total[0] * masks[0, j]
                conv = conv.astype(bf16).astype(f32)
                short = short_ref[pl.ds(j * SUBS, SUBS), cols_of(lane)]
                if j < 2:
                    short = short + edge[j]
                wide[slot, pl.ds(j, SUBS, stride=span + 1), :] = short * conv
        for b in range(SUBS):
            rows = pl.ds(b * span, span)
            squares = sums[rows, :]
            for slot, lane in enumerate(lanes):
                hidden = wide[slot, pl.ds(b * (span + 1), span), :] + resid_ref[rows, cols_of(lane)].astype(f32)
                if channels:
                    whole[lax.div(lane, LANES), rows, :] = hidden
                else:
                    wide_ref[rows, cols_of(lane)] = hidden
                hidden_ref[rows, cols_of(lane)] = hidden.astype(bf16)
                squares = squares + hidden * hidden
            sums[rows, :] = squares

    each_chunk(chans, chunk, lambda c: fetch(c).wait(), group, lambda c: store(c).start(), most)
    if channels:
        inverse = lax.rsqrt(jnp.sum(sums[...], axis=1, keepdims=True) / channels + 1e-06)
        sums[...] = jnp.broadcast_to(inverse, sums.shape)

        def scale(lanes):
            for lane in lanes:
                normed = whole[lax.div(lane, LANES)] * sums[...] * gain_ref[:, cols_of(lane)]
                normed_ref[:, cols_of(lane)] = normed.astype(bf16)

        each_chunk(chans, chunk, lambda c: None, scale, lambda c: store_normed(c).start(), 4)
        for c in range(chans // chunk):
            store_normed(c).wait()
    else:
        sum_ref[...] = sums[...]
    for c in range(chans // chunk):
        store(c).wait()


def shards(
    query_in, key_in, value_in, short_taps, decay_rate, residues, doc_lengths, residual, norm_gain
):
    tok_rows, chans = query_in.shape
    modes = decay_rate.shape[0]
    span = tok_rows // SUBS
    blocks = lax.axis_size("ctx")
    grp = lax.axis_size("grp")
    chunk = min(chans, 1024)
    pieces = chans // chunk
    ctx_index = lax.axis_index("ctx")
    base = (ctx_index * tok_rows).astype(jnp.int32).reshape(1)
    weight = residues * jnp.sqrt(-jnp.expm1(-2.0 * decay_rate))

    smem = pl.BlockSpec(memory_space=pltpu.SMEM)
    vmem = pl.BlockSpec(memory_space=pltpu.VMEM)
    hbm = pl.BlockSpec(memory_space=pltpu.HBM)
    half = jax.ShapeDtypeStruct((modes, chans // 2), f32)
    tile_shape = (SUBS, LANES)
    wide_rows = SUBS * (span + 1)
    params = pltpu.CompilerParams(vmem_limit_bytes=16 * MIB)

    lengths = pltpu.with_memory_space_constraint(doc_lengths, pltpu.HBM)

    def near_by(x):
        return pltpu.with_memory_space_constraint(x, pltpu.VMEM)

    def far_off(x):
        return pltpu.with_memory_space_constraint(x, pltpu.HBM)

    def copies(kinds):
        return pltpu.SemaphoreType.DMA((kinds, pieces))

    def cost(per_tile, moved):
        return pl.CostEstimate(flops=per_tile * (chans // LANES) * SUBS * LANES, bytes_accessed=moved, transcendentals=0)

    tails = pl.pallas_call(
        tail_kernel,
        in_specs=[hbm, hbm, hbm],
        out_specs=vmem,
        out_shape=pltpu.VMEM((3, 2, chans), bf16),
        scratch_shapes=[pltpu.VMEM((3, 16, chans), bf16), pltpu.SemaphoreType.DMA((3,))],
        compiler_params=params,
        name="tails",
    )(far_off(query_in), far_off(key_in), far_off(value_in))
    rim_rows = from_behind(tails, "ctx", 1)
    q_short = pl.pallas_call(
        functools.partial(query_kernel, span=span, most=Q_TILES, chunk=chunk),
        in_specs=[smem, smem, hbm, vmem],
        out_specs=vmem,
        out_shape=pltpu.VMEM((tok_rows, chans), f32),
        scratch_shapes=[
            pltpu.VMEM((tok_rows, chans), bf16),
            pltpu.SemaphoreType.DMA((pieces,)),
            pltpu.VMEM((2, span) + tile_shape, f32),
            pltpu.VMEM((Q_TILES, wide_rows, LANES), f32),
        ],
        compiler_params=params,
        cost_estimate=cost(200, 6 * tok_rows * chans),
        name="query_part",
    )(base, lengths, far_off(query_in), near_by(short_taps))
    rim_rows, q_short = lax.optimization_barrier((rim_rows, q_short))
    rates, weights, taps, rims = near_by(decay_rate), near_by(weight), near_by(short_taps), near_by(rim_rows)
    gates, states, own, give = pl.pallas_call(
        functools.partial(state_kernel, span=span, modes=modes, most=A_TILES, chunk=chunk),
        in_specs=[smem, smem, hbm, hbm, vmem, vmem, vmem, vmem],
        out_specs=[vmem, vmem, vmem, vmem],
        out_shape=[
            pltpu.VMEM((tok_rows, chans), bf16),
            pltpu.VMEM((modes * SUBS, chans), f32),
            pltpu.VMEM(half.shape, f32),
            pltpu.VMEM(half.shape, f32),
        ],
        scratch_shapes=[
            pltpu.VMEM((tok_rows, chans), bf16),
            pltpu.VMEM((tok_rows, chans), bf16),
            copies(2),
            pltpu.VMEM((4, span) + tile_shape, f32),
            pltpu.VMEM((A_TILES, wide_rows, LANES), f32),
            pltpu.VMEM((A_TILES, wide_rows, LANES), f32),
            pltpu.VMEM((A_TILES, 5, modes, LANES), f32),
            pltpu.VMEM((A_TILES, modes, LANES), f32),
            pltpu.VMEM((A_TILES, span) + tile_shape, f32),
        ],
        compiler_params=params,
        cost_estimate=cost(1000, 12 * tok_rows * chans),
        name="block_states",
    )(base, lengths, far_off(key_in), far_off(value_in), rims, taps, rates, weights)

    def near_piece(part, near):
        count = chans // NEAR_PARTS
        before = [] if near is None else [near_by(near)]
        return pl.pallas_call(
            functools.partial(
                near_kernel, span=span, modes=modes, most=N_TILES, first=part * count, count=count
            ),
            in_specs=[smem, smem, vmem, vmem, vmem] + [vmem] * len(before),
            out_specs=vmem,
            out_shape=pltpu.VMEM((tok_rows, chans), f32),
            scratch_shapes=[pltpu.VMEM((2, span) + tile_shape, f32)],
            compiler_params=params,
            input_output_aliases={5: 0} if before else {},
            cost_estimate=cost(600 // NEAR_PARTS, 7 * tok_rows * count),
            name="near_part_%d" % part,
        )(base, lengths, near_by(gates), rates, weights, *before)

    got = swap(give, "ctx")

    def pair_call(kernel, operands, out_shape, name, **static):
        count = len(operands) + 1
        return pl.pallas_call(
            functools.partial(kernel, rows=tok_rows, **static),
            in_specs=[smem, smem] + [vmem] * count,
            out_specs=[vmem] * len(out_shape),
            out_shape=out_shape,
            compiler_params=params,
            name=name,
        )(base, lengths, *[near_by(x) for x in operands], rates)

    sent = pltpu.VMEM(half.shape, bf16)
    ends = pair_call(pair_kernel, [own, got], [sent], "pair_ends")[0]
    one_on, two_on = from_behind(ends, "ctx", 2), from_behind(ends, "ctx", 4)
    near = near_piece(0, None)
    one_on, two_on, near = lax.optimization_barrier((one_on, two_on, near))
    enter, on, reach = one_on, two_on, 1
    while 2 * reach < blocks // 8:
        enter = pair_call(reach_kernel, [enter, on], [sent], "reach_%d" % (2 * reach), reach=reach)[0]
        reach *= 2
        on = from_behind(enter, "ctx", 2 * reach)
    near = near_piece(1, near)
    on, near = lax.optimization_barrier((on, near))
    mine, give_back = pair_call(
        enter_kernel,
        [enter, on, own, got],
        [pltpu.VMEM(half.shape, f32), pltpu.VMEM(half.shape, f32)],
        "pair_enter",
        reach=reach,
    )
    got_back = swap(give_back, "ctx")

    alone = grp == 1
    out_specs = [hbm]
    out_shape = [jax.ShapeDtypeStruct((tok_rows, chans), bf16)]
    scratch = [
        pltpu.VMEM((tok_rows, chans), bf16),
        pltpu.VMEM((tok_rows, chans), bf16),
        copies(3),
        pltpu.VMEM((2, span) + tile_shape, f32),
        pltpu.VMEM((F_TILES, wide_rows, LANES), f32),
        pltpu.VMEM((F_TILES, 3, modes, LANES), f32),
        pltpu.VMEM((tok_rows, LANES), f32),
    ]
    if alone:
        out_specs.append(hbm)
        out_shape.append(jax.ShapeDtypeStruct((tok_rows, chans), bf16))
        scratch += [pltpu.VMEM((chans // LANES, tok_rows, LANES), f32), pltpu.VMEM((tok_rows, chans), bf16)]
    else:
        out_specs += [vmem, vmem]
        out_shape += [jax.ShapeDtypeStruct((tok_rows, chans), f32), jax.ShapeDtypeStruct((tok_rows, LANES), f32)]
    outs = pl.pallas_call(
        functools.partial(
            final_kernel, span=span, modes=modes, channels=chans if alone else 0, most=F_TILES, chunk=chunk
        ),
        in_specs=[smem, smem, vmem, vmem, vmem, vmem, vmem, hbm, vmem, vmem, vmem, vmem, vmem],
        out_specs=out_specs,
        out_shape=out_shape,
        scratch_shapes=scratch,
        compiler_params=params,
        cost_estimate=cost(900, 18 * tok_rows * chans),
        name="far_part",
    )(
        base, lengths, near_by(states), near_by(mine), near_by(got_back), near_by(near), near_by(q_short), far_off(residual),
        rims, taps, rates, weights, norm_gain.reshape(1, chans),
    )
    if alone:
        return tuple(outs)
    hidden_out, hidden, sums = outs
    square_sum = lax.psum(jnp.sum(sums, axis=1), "grp")
    inverse_rms = lax.rsqrt(square_sum / (chans * grp) + 1e-06)
    normed = (hidden * inverse_rms[:, None] * norm_gain[None, :]).astype(bf16)
    return (hidden_out, normed)


def solution(mesh):
    return jax.shard_map(
        shards,
        mesh=mesh,
        in_specs=(
            P("ctx", "grp"),
            P("ctx", "grp"),
            P("ctx", "grp"),
            P(None, None, "grp"),
            P(None, "grp"),
            P(None, "grp"),
            P(),
            P("ctx", "grp"),
            P("grp"),
        ),
        out_specs=(P("ctx", "grp"), P("ctx", "grp")),
        check_vma=False,
    )
```

```python
import functools
import math

import jax
import jax.numpy as jnp
from jax import lax
from jax.experimental import pallas as pl
from jax.experimental.pallas import tpu as pltpu
from jax.sharding import PartitionSpec as P

SUBS = 8
LANES = 128
MIB = 1024 * 1024
A_TILES, N_TILES, Q_TILES, F_TILES = 2, 2, 4, 4
NEAR_PARTS = 2
f32 = jnp.float32
bf16 = jnp.bfloat16


def from_behind(shard, axis, by):
    count = lax.axis_size(axis)
    pairs = [(i, i + by) for i in range(count) if 0 <= i + by < count]
    return lax.ppermute(shard, axis, pairs)


def swap(shard, axis):
    return lax.ppermute(shard, axis, [(i, i ^ 1) for i in range(lax.axis_size(axis))])


def doc_start_rows(len_ref, base, span):
    rows = lax.broadcasted_iota(jnp.int32, (SUBS, LANES), 0) * span + base
    starts = [jnp.int32(0)]
    for d in range(len_ref.shape[0] - 1):
        starts.append(starts[-1] + len_ref[d])
    out = []
    for j in range(span):
        pos = rows + j
        best = jnp.zeros((SUBS, LANES), jnp.int32)
        for start in starts[1:]:
            best = jnp.where(pos >= start, start, best)
        out.append(best)
    return rows, out


def flag(cond):
    return jnp.where(cond, 1.0, 0.0).astype(f32)


def each_group(count, most, group):
    size = math.gcd(count, most)

    def step(i, carry):
        group([pl.multiple_of((i * size + m) * LANES, LANES) for m in range(size)])
        return carry

    lax.fori_loop(0, count // size, step, 0)


def each_chunk(chans, chunk, before, group, after, most):
    def step(c, carry):
        before(c)

        def inner(lanes):
            group([pl.multiple_of(c * chunk + lane, LANES) for lane in lanes])

        each_group(chunk // LANES, most, inner)
        after(c)
        return carry

    lax.fori_loop(0, chans // chunk, step, 0)


def cols_copy(src, dst, sem, c, chunk):
    cols = pl.ds(pl.multiple_of(c * chunk, chunk), chunk)
    return pltpu.make_async_copy(src.at[:, cols], dst.at[:, cols], sem.at[c])


def cols_of(lane):
    return pl.ds(lane, LANES)


def row_of(ref, index):
    return ref[pl.ds(index, SUBS, stride=0), :]


def spread(x, wide, span):
    x = x.astype(f32)
    for b in range(SUBS):
        wide[pl.ds(b * (span + 1), span), :] = x[b * span : (b + 1) * span]


class Conv:
    def __init__(self, wide, rim, taps, span):
        self.wide, self.span = wide, span
        self.taps = [jnp.broadcast_to(taps[m : m + 1], (SUBS, LANES)) for m in range(3)]
        top = lax.broadcasted_iota(jnp.int32, (SUBS, LANES), 0) == 0
        ahead = [0.0, 0.0] if rim is None else [jnp.broadcast_to(rim[m : m + 1].astype(f32), (SUBS, LANES)) for m in range(2)]
        self.behind = [jnp.where(top, ahead[m], pltpu.roll(self.row(span - 2 + m), 1, 0)) for m in range(2)]

    def row(self, j):
        return self.wide[pl.ds(j, SUBS, stride=self.span + 1), :]

    def step(self, j, keep_one, keep_two):
        here = self.row(j)
        two, one = self.behind
        self.behind = [one, here]
        return self.taps[0] * here + (self.taps[1] * one) * keep_one + (self.taps[2] * two) * keep_two


def sub_passes(base_ref, len_ref, passes, span):
    for b in range(SUBS):
        passes[b] = jnp.float32(1.0)
    start = jnp.int32(0)
    for d in range(len_ref.shape[0]):
        at = start - base_ref[0]

        @pl.when((at >= 0) & (at < SUBS * span))
        def _():
            passes[lax.div(at, jnp.int32(span))] = jnp.float32(0.0)

        start = start + len_ref[d]


def half_of(base_ref, rows, chans, lane):
    half = chans // 2
    which = lax.div(lane, half)
    mine = which == lax.rem(lax.div(base_ref[0], rows), 2)
    return mine, pl.multiple_of(lane - which * half, LANES)


def sub_state(state_ref, lane, b, modes):
    return state_ref[lax.div(lane, LANES), pl.ds(b * (modes + 1), modes), :]


def state_kernel(
    base_ref, len_ref, key_ref, value_ref, rim_ref, taps_ref, rate_ref,
    gate_ref, state_ref, own_ref, give_ref,
    key_buf, value_buf, sems, masks, passes, wide_k, wide_v, tables, held,
    *, span, modes, most, chunk,
):
    chans = key_buf.shape[1]

    def fetches(c):
        return [cols_copy(key_ref, key_buf, sems.at[0], c, chunk), cols_copy(value_ref, value_buf, sems.at[1], c, chunk)]

    for c in range(chans // chunk):
        for copy in fetches(c):
            copy.start()

    def prepare():
        rows, starts = doc_start_rows(len_ref, base_ref[0], span)
        for j in range(span):
            masks[0, j] = flag(starts[j] < rows + j)
            masks[1, j] = flag(starts[j] < rows + (j - 1))
            masks[2, j] = flag(starts[span - 1] <= rows + j)
        sub_passes(base_ref, len_ref, passes, span)

    prepare()

    def group(lanes):
        for slot, lane in enumerate(lanes):
            spread(key_buf[:, cols_of(lane)], wide_k.at[slot], span)
            spread(value_buf[:, cols_of(lane)], wide_v.at[slot], span)
            rate = rate_ref[:, cols_of(lane)]
            tables[slot] = jnp.exp(-rate)
        convs = [
            [
                Conv(wide.at[slot], rim_ref[i, :, cols_of(lane)], taps_ref[i, :, cols_of(lane)], span)
                for i, wide in ((1, wide_k), (2, wide_v))
            ]
            for slot, lane in enumerate(lanes)
        ]
        last = [None] * len(lanes)
        for j in range(span):
            keep_one, keep_two = masks[0, j], masks[1, j]
            for slot, lane in enumerate(lanes):
                k_short, v_short = [conv.step(j, keep_one, keep_two) for conv in convs[slot]]
                if j % 2 == 0:
                    last[slot] = k_short * v_short
                    continue
                pair = jnp.concatenate([last[slot], k_short * v_short], axis=0).astype(bf16)
                gate_ref[pl.ds((j - 1) * SUBS, 2 * SUBS), cols_of(lane)] = pair
                pair = pair.astype(f32)
                held[slot, j - 1] = pair[:SUBS] * masks[2, j - 1]
                held[slot, j] = pair[SUBS:] * masks[2, j]
        for slot, lane in enumerate(lanes):
            decay = [row_of(tables.at[slot], n) for n in range(modes)]
            state = [held[slot, 0]] * modes
            for j in range(1, span):
                gate = held[slot, j]
                state = [decay[n] * state[n] + gate for n in range(modes)]
            for n in range(modes):
                state_ref[lax.div(lane, LANES), pl.ds(n, SUBS, stride=modes + 1), :] = state[n]
        for slot, lane in enumerate(lanes):
            leap = jnp.exp(-float(span) * rate_ref[:, cols_of(lane)])
            end = sub_state(state_ref, lane, 0, modes)
            for b in range(1, SUBS):
                end = (leap * passes[b]) * end + sub_state(state_ref, lane, b, modes)
            mine, here = half_of(base_ref, key_ref.shape[0], chans, lane)

            @pl.when(mine)
            def _():
                own_ref[:, cols_of(here)] = end

            @pl.when(jnp.logical_not(mine))
            def _():
                give_ref[:, cols_of(here)] = end

    def before(c):
        for copy in fetches(c):
            copy.wait()

    each_chunk(chans, chunk, before, group, lambda c: None, most)


def tail_kernel(query_ref, key_ref, value_ref, tail_ref, bufs, sems):
    rows, count = query_ref.shape[0], bufs.shape[1]
    copies = [
        pltpu.make_async_copy(ref.at[pl.ds(rows - count, count)], bufs.at[i], sems.at[i])
        for i, ref in enumerate((query_ref, key_ref, value_ref))
    ]
    for copy in copies:
        copy.start()
    for i, copy in enumerate(copies):
        copy.wait()
        tail_ref[i] = bufs[i].astype(f32)[count - 2 :].astype(bf16)


def keep_masks(base_ref, len_ref, masks, span):
    rows, starts = doc_start_rows(len_ref, base_ref[0], span)
    for j in range(span):
        masks[0, j] = flag(starts[j] < rows + j)
        masks[1, j] = flag(starts[j] < rows + (j - 1))


def near_kernel(base_ref, len_ref, gate_ref, rate_ref, weight_ref, *refs, span, modes, most, first, count):
    near_ref, masks, sums, tap_rows = refs[-4:]
    keep_masks(base_ref, len_ref, masks, span)

    def group(lanes):
        for slot, lane in enumerate(lanes):
            decay = jnp.exp(-rate_ref[:, cols_of(lane)])
            term = weight_ref[:, cols_of(lane)]
            for lag in range(span):
                part = term[:SUBS]
                for n in range(SUBS, modes, SUBS):
                    part = part + term[n : n + SUBS]
                sums[slot, pl.ds(lag * (SUBS + 1), SUBS), :] = part
                term = term * decay
        for slot in range(len(lanes)):
            for first_lag in range(0, span, SUBS):
                total = [
                    sums[slot, pl.ds(first_lag * (SUBS + 1) + m, SUBS, stride=SUBS + 1), :] for m in range(SUBS)
                ]
                while len(total) > 1:
                    total = [total[m] + total[m + 1] for m in range(0, len(total), 2)]
                tap_rows[slot, pl.ds(first_lag, SUBS), :] = total[0]
        taps = [[row_of(tap_rows.at[slot], lag) for lag in range(span)] for slot in range(len(lanes))]
        for parts, lane in zip(taps, lanes):
            live = []
            for j in range(span):
                if j % 2 == 0:
                    pair = gate_ref[pl.ds(j * SUBS, 2 * SUBS), cols_of(lane)].astype(f32)
                keep = masks[0, j]
                live = [g * keep for g in live]
                live.append(pair[(j % 2) * SUBS : (j % 2 + 1) * SUBS])
                total = parts[0] * live[j]
                for lag in range(1, j + 1):
                    total = total + parts[lag] * live[j - lag]
                near_ref[pl.ds(j * SUBS, SUBS), cols_of(lane)] = total

    each_group(count // LANES, most, lambda lanes: group([pl.multiple_of(first + lane, LANES) for lane in lanes]))


def query_kernel(base_ref, len_ref, query_ref, taps_ref, short_ref, query_buf, sems, masks, wide_q, *, span, most, chunk):
    chans = query_buf.shape[1]

    def fetch(c):
        return cols_copy(query_ref, query_buf, sems, c, chunk)

    for c in range(chans // chunk):
        fetch(c).start()
    keep_masks(base_ref, len_ref, masks, span)

    def group(lanes):
        for slot, lane in enumerate(lanes):
            spread(query_buf[:, cols_of(lane)], wide_q.at[slot], span)
        convs = [Conv(wide_q.at[slot], None, taps_ref[0, :, cols_of(lane)], span) for slot, lane in enumerate(lanes)]
        for j in range(span):
            keep_one, keep_two = masks[0, j], masks[1, j]
            for slot, lane in enumerate(lanes):
                short_ref[pl.ds(j * SUBS, SUBS), cols_of(lane)] = convs[slot].step(j, keep_one, keep_two)

    each_chunk(chans, chunk, lambda c: fetch(c).wait(), group, lambda c: None, most)


def unbroken(len_ref, first, count):
    start = jnp.int32(0)
    whole = jnp.where((first <= 0) & (first + count > 0), 0.0, 1.0)
    for d in range(len_ref.shape[0] - 1):
        start = start + len_ref[d]
        whole = jnp.where((start >= first) & (start < first + count), 0.0, whole)
    return whole.astype(f32)


def pair_rates(base_ref, rate_ref, rows, shape):
    parity = lax.rem(lax.div(base_ref[0], rows), 2)
    return parity, rate_ref[:, pl.ds(pl.multiple_of(parity * shape[1], LANES), shape[1])]


def early_late(parity, own, got):
    odd = jnp.full(own.shape, parity, jnp.int32) == 1
    return jnp.where(odd, got, own), jnp.where(odd, own, got)


def pair_kernel(base_ref, len_ref, own_ref, got_ref, rate_ref, end_ref, *, rows):
    parity, rate = pair_rates(base_ref, rate_ref, rows, own_ref.shape)
    early, late = early_late(parity, own_ref[...], got_ref[...])
    through = unbroken(len_ref, base_ref[0] + (1 - parity) * rows, rows)
    end_ref[...] = (late + (jnp.exp(-float(rows) * rate) * through) * early).astype(bf16)


def reached(base_ref, len_ref, near_ref, far_ref, rate_ref, rows, reach):
    parity, rate = pair_rates(base_ref, rate_ref, rows, near_ref.shape)
    span = 2 * rows * reach
    through = unbroken(len_ref, base_ref[0] - parity * rows - span, span)
    return near_ref[...].astype(f32) + (jnp.exp(-float(span) * rate) * through) * far_ref[...].astype(f32)


def reach_kernel(base_ref, len_ref, near_ref, far_ref, rate_ref, enter_ref, *, rows, reach):
    enter_ref[...] = reached(base_ref, len_ref, near_ref, far_ref, rate_ref, rows, reach).astype(bf16)


def enter_kernel(base_ref, len_ref, near_ref, far_ref, own_ref, got_ref, rate_ref, mine_ref, give_ref, *, rows, reach):
    first = reached(base_ref, len_ref, near_ref, far_ref, rate_ref, rows, reach)
    parity, rate = pair_rates(base_ref, rate_ref, rows, own_ref.shape)
    early, _ = early_late(parity, own_ref[...], got_ref[...])
    through = unbroken(len_ref, base_ref[0] - parity * rows, rows)
    second = early + (jnp.exp(-float(rows) * rate) * through) * first
    give, mine = early_late(parity, second, first)
    mine_ref[...] = mine
    give_ref[...] = give


def final_kernel(
    base_ref, len_ref, state_ref, mine_ref, got_ref, near_ref, short_ref, resid_in, rim_ref, taps_ref, rate_ref, weight_ref, gain_ref,
    *refs,
    span, modes, channels, most, chunk,
):
    if channels:
        hidden_out, normed_out, resid_ref, hidden_ref, sems, masks, passes, wide, tables, starts_at, sums, whole, normed_ref = refs
    else:
        hidden_out, wide_ref, sum_ref, resid_ref, hidden_ref, sems, masks, passes, wide, tables, starts_at, sums = refs
    chans = resid_ref.shape[1]

    def fetch(c):
        return cols_copy(resid_in, resid_ref, sems.at[0], c, chunk)

    def store(c):
        return cols_copy(hidden_ref, hidden_out, sems.at[1], c, chunk)

    def store_normed(c):
        return cols_copy(normed_ref, normed_out, sems.at[2], c, chunk)

    for c in range(chans // chunk):
        fetch(c).start()
    rows, starts = doc_start_rows(len_ref, base_ref[0], span)
    for j in range(span):
        masks[0, j] = flag(starts[j] < rows)
    sub_passes(base_ref, len_ref, passes, span)
    top = flag(lax.broadcasted_iota(jnp.int32, (SUBS, LANES), 0) == 0)
    masks[1, 1] = top * flag(starts[0] < rows)
    masks[1, 2] = top * flag(starts[0] < rows - 1)
    masks[1, 3] = top * flag(starts[1] < rows)
    sums[...] = jnp.zeros(sums.shape, f32)

    def group(lanes):
        for slot, lane in enumerate(lanes):
            mine, here = half_of(base_ref, resid_ref.shape[0], chans, lane)
            mine = jnp.full((modes, LANES), mine.astype(jnp.int32), jnp.int32) == 1
            state = jnp.where(mine, mine_ref[:, cols_of(here)], got_ref[:, cols_of(here)])
            rate = rate_ref[:, cols_of(lane)]
            weight = weight_ref[:, cols_of(lane)]
            tables[slot] = jnp.exp(-rate)
            leap = jnp.exp(-float(span) * rate)
            for b in range(SUBS):
                starts_at[slot, pl.ds(b * (modes + 1), modes), :] = weight * state
                if b < SUBS - 1:
                    state = (leap * passes[b]) * state + sub_state(state_ref, lane, b, modes)
        for slot, lane in enumerate(lanes):
            part = [starts_at[slot, pl.ds(n, SUBS, stride=modes + 1), :] for n in range(modes)]
            decay = [row_of(tables.at[slot], n) for n in range(modes)]
            rim = rim_ref[0, :, cols_of(lane)].astype(f32)
            tap = taps_ref[0, :, cols_of(lane)]
            edge = [
                (tap[1:2] * rim[1:2]) * masks[1, 1] + (tap[2:3] * rim[0:1]) * masks[1, 2],
                (tap[2:3] * rim[1:2]) * masks[1, 3],
            ]
            for j in range(span):
                part = [part[n] * decay[n] for n in range(modes)]
                total = part
                while len(total) > 1:
                    total = [total[m] + total[m + 1] for m in range(0, len(total), 2)]
                conv = near_ref[pl.ds(j * SUBS, SUBS), cols_of(lane)] + total[0] * masks[0, j]
                conv = conv.astype(bf16).astype(f32)
                short = short_ref[pl.ds(j * SUBS, SUBS), cols_of(lane)]
                if j < 2:
                    short = short + edge[j]
                wide[slot, pl.ds(j, SUBS, stride=span + 1), :] = short * conv
        for b in range(SUBS):
            rows = pl.ds(b * span, span)
            squares = sums[rows, :]
            for slot, lane in enumerate(lanes):
                hidden = wide[slot, pl.ds(b * (span + 1), span), :] + resid_ref[rows, cols_of(lane)].astype(f32)
                if channels:
                    whole[lax.div(lane, LANES), rows, :] = hidden
                else:
                    wide_ref[rows, cols_of(lane)] = hidden
                hidden_ref[rows, cols_of(lane)] = hidden.astype(bf16)
                squares = squares + hidden * hidden
            sums[rows, :] = squares

    each_chunk(chans, chunk, lambda c: fetch(c).wait(), group, lambda c: store(c).start(), most)
    if channels:
        inverse = lax.rsqrt(jnp.sum(sums[...], axis=1, keepdims=True) / channels + 1e-06)
        sums[...] = jnp.broadcast_to(inverse, sums.shape)

        def scale(lanes):
            for lane in lanes:
                normed = whole[lax.div(lane, LANES)] * sums[...] * gain_ref[:, cols_of(lane)]
                normed_ref[:, cols_of(lane)] = normed.astype(bf16)

        each_chunk(chans, chunk, lambda c: None, scale, lambda c: store_normed(c).start(), 4)
        for c in range(chans // chunk):
            store_normed(c).wait()
    else:
        sum_ref[...] = sums[...]
    for c in range(chans // chunk):
        store(c).wait()


def shards(
    query_in, key_in, value_in, short_taps, decay_rate, residues, doc_lengths, residual, norm_gain
):
    tok_rows, chans = query_in.shape
    modes = decay_rate.shape[0]
    span = tok_rows // SUBS
    blocks = lax.axis_size("ctx")
    grp = lax.axis_size("grp")
    chunk = min(chans, 1024)
    pieces = chans // chunk
    ctx_index = lax.axis_index("ctx")
    base = (ctx_index * tok_rows).astype(jnp.int32).reshape(1)
    weight = residues * jnp.sqrt(-jnp.expm1(-2.0 * decay_rate))

    smem = pl.BlockSpec(memory_space=pltpu.SMEM)
    vmem = pl.BlockSpec(memory_space=pltpu.VMEM)
    hbm = pl.BlockSpec(memory_space=pltpu.HBM)
    half = jax.ShapeDtypeStruct((modes, chans // 2), f32)
    tile_shape = (SUBS, LANES)
    wide_rows = SUBS * (span + 1)
    params = pltpu.CompilerParams(vmem_limit_bytes=16 * MIB)

    lengths = pltpu.with_memory_space_constraint(doc_lengths, pltpu.HBM)

    def near_by(x):
        return pltpu.with_memory_space_constraint(x, pltpu.VMEM)

    def far_off(x):
        return pltpu.with_memory_space_constraint(x, pltpu.HBM)

    def copies(kinds):
        return pltpu.SemaphoreType.DMA((kinds, pieces))

    def cost(per_tile, moved):
        return pl.CostEstimate(flops=per_tile * (chans // LANES) * SUBS * LANES, bytes_accessed=moved, transcendentals=0)

    tails = pl.pallas_call(
        tail_kernel,
        in_specs=[hbm, hbm, hbm],
        out_specs=vmem,
        out_shape=pltpu.VMEM((3, 2, chans), bf16),
        scratch_shapes=[pltpu.VMEM((3, 16, chans), bf16), pltpu.SemaphoreType.DMA((3,))],
        compiler_params=params,
        name="tails",
    )(far_off(query_in), far_off(key_in), far_off(value_in))
    rim_rows = from_behind(tails, "ctx", 1)
    q_short = pl.pallas_call(
        functools.partial(query_kernel, span=span, most=Q_TILES, chunk=chunk),
        in_specs=[smem, smem, hbm, vmem],
        out_specs=vmem,
        out_shape=pltpu.VMEM((tok_rows, chans), f32),
        scratch_shapes=[
            pltpu.VMEM((tok_rows, chans), bf16),
            pltpu.SemaphoreType.DMA((pieces,)),
            pltpu.VMEM((2, span) + tile_shape, f32),
            pltpu.VMEM((Q_TILES, wide_rows, LANES), f32),
        ],
        compiler_params=params,
        cost_estimate=cost(200, 6 * tok_rows * chans),
        name="query_part",
    )(base, lengths, far_off(query_in), near_by(short_taps))
    rim_rows, q_short = lax.optimization_barrier((rim_rows, q_short))
    rates, weights, taps, rims = near_by(decay_rate), near_by(weight), near_by(short_taps), near_by(rim_rows)
    gates, states, own, give = pl.pallas_call(
        functools.partial(state_kernel, span=span, modes=modes, most=A_TILES, chunk=chunk),
        in_specs=[smem, smem, hbm, hbm, vmem, vmem, vmem],
        out_specs=[vmem, vmem, vmem, vmem],
        out_shape=[
            pltpu.VMEM((tok_rows, chans), bf16),
            pltpu.VMEM((chans // LANES, SUBS * (modes + 1), LANES), f32),
            pltpu.VMEM(half.shape, f32),
            pltpu.VMEM(half.shape, f32),
        ],
        scratch_shapes=[
            pltpu.VMEM((tok_rows, chans), bf16),
            pltpu.VMEM((tok_rows, chans), bf16),
            copies(2),
            pltpu.VMEM((3, span) + tile_shape, f32),
            pltpu.SMEM((SUBS,), f32),
            pltpu.VMEM((A_TILES, wide_rows, LANES), f32),
            pltpu.VMEM((A_TILES, wide_rows, LANES), f32),
            pltpu.VMEM((A_TILES, modes, LANES), f32),
            pltpu.VMEM((A_TILES, span) + tile_shape, f32),
        ],
        compiler_params=params,
        cost_estimate=cost(1000, 12 * tok_rows * chans),
        name="block_states",
    )(base, lengths, far_off(key_in), far_off(value_in), rims, taps, rates)

    def near_piece(part, near):
        count = chans // NEAR_PARTS
        before = [] if near is None else [near_by(near)]
        return pl.pallas_call(
            functools.partial(
                near_kernel, span=span, modes=modes, most=N_TILES, first=part * count, count=count
            ),
            in_specs=[smem, smem, vmem, vmem, vmem] + [vmem] * len(before),
            out_specs=vmem,
            out_shape=pltpu.VMEM((tok_rows, chans), f32),
            scratch_shapes=[
                pltpu.VMEM((2, span) + tile_shape, f32),
                pltpu.VMEM((N_TILES, span * (SUBS + 1), LANES), f32),
                pltpu.VMEM((N_TILES, span, LANES), f32),
            ],
            compiler_params=params,
            input_output_aliases={5: 0} if before else {},
            cost_estimate=cost(600 // NEAR_PARTS, 7 * tok_rows * count),
            name="near_part_%d" % part,
        )(base, lengths, near_by(gates), rates, weights, *before)

    got = swap(give, "ctx")

    def pair_call(kernel, operands, out_shape, name, **static):
        count = len(operands) + 1
        return pl.pallas_call(
            functools.partial(kernel, rows=tok_rows, **static),
            in_specs=[smem, smem] + [vmem] * count,
            out_specs=[vmem] * len(out_shape),
            out_shape=out_shape,
            compiler_params=params,
            name=name,
        )(base, lengths, *[near_by(x) for x in operands], rates)

    sent = pltpu.VMEM(half.shape, bf16)
    ends = pair_call(pair_kernel, [own, got], [sent], "pair_ends")[0]
    one_on, two_on = from_behind(ends, "ctx", 2), from_behind(ends, "ctx", 4)
    near = near_piece(0, None)
    one_on, two_on, near = lax.optimization_barrier((one_on, two_on, near))
    enter, on, reach = one_on, two_on, 1
    while 2 * reach < blocks // 8:
        enter = pair_call(reach_kernel, [enter, on], [sent], "reach_%d" % (2 * reach), reach=reach)[0]
        reach *= 2
        on = from_behind(enter, "ctx", 2 * reach)
    near = near_piece(1, near)
    on, near = lax.optimization_barrier((on, near))
    mine, give_back = pair_call(
        enter_kernel,
        [enter, on, own, got],
        [pltpu.VMEM(half.shape, f32), pltpu.VMEM(half.shape, f32)],
        "pair_enter",
        reach=reach,
    )
    got_back = swap(give_back, "ctx")

    alone = grp == 1
    out_specs = [hbm]
    out_shape = [jax.ShapeDtypeStruct((tok_rows, chans), bf16)]
    scratch = [
        pltpu.VMEM((tok_rows, chans), bf16),
        pltpu.VMEM((tok_rows, chans), bf16),
        copies(3),
        pltpu.VMEM((2, span) + tile_shape, f32),
        pltpu.SMEM((SUBS,), f32),
        pltpu.VMEM((F_TILES, wide_rows, LANES), f32),
        pltpu.VMEM((F_TILES, modes, LANES), f32),
        pltpu.VMEM((F_TILES, SUBS * (modes + 1), LANES), f32),
        pltpu.VMEM((tok_rows, LANES), f32),
    ]
    if alone:
        out_specs.append(hbm)
        out_shape.append(jax.ShapeDtypeStruct((tok_rows, chans), bf16))
        scratch += [pltpu.VMEM((chans // LANES, tok_rows, LANES), f32), pltpu.VMEM((tok_rows, chans), bf16)]
    else:
        out_specs += [vmem, vmem]
        out_shape += [jax.ShapeDtypeStruct((tok_rows, chans), f32), jax.ShapeDtypeStruct((tok_rows, LANES), f32)]
    outs = pl.pallas_call(
        functools.partial(
            final_kernel, span=span, modes=modes, channels=chans if alone else 0, most=F_TILES, chunk=chunk
        ),
        in_specs=[smem, smem, vmem, vmem, vmem, vmem, vmem, hbm, vmem, vmem, vmem, vmem, vmem],
        out_specs=out_specs,
        out_shape=out_shape,
        scratch_shapes=scratch,
        compiler_params=params,
        cost_estimate=cost(900, 18 * tok_rows * chans),
        name="far_part",
    )(
        base, lengths, near_by(states), near_by(mine), near_by(got_back), near_by(near), near_by(q_short), far_off(residual),
        rims, taps, rates, weights, norm_gain.reshape(1, chans),
    )
    if alone:
        return tuple(outs)
    hidden_out, hidden, sums = outs
    square_sum = lax.psum(jnp.sum(sums, axis=1), "grp")
    inverse_rms = lax.rsqrt(square_sum / (chans * grp) + 1e-06)
    normed = (hidden * inverse_rms[:, None] * norm_gain[None, :]).astype(bf16)
    return (hidden_out, normed)


def solution(mesh):
    return jax.shard_map(
        shards,
        mesh=mesh,
        in_specs=(
            P("ctx", "grp"),
            P("ctx", "grp"),
            P("ctx", "grp"),
            P(None, None, "grp"),
            P(None, "grp"),
            P(None, "grp"),
            P(),
            P("ctx", "grp"),
            P("grp"),
        ),
        out_specs=(P("ctx", "grp"), P("ctx", "grp")),
        check_vma=False,
    )
```

```python
import functools
import math

import jax
import jax.numpy as jnp
from jax import lax
from jax.experimental import pallas as pl
from jax.experimental.pallas import tpu as pltpu
from jax.sharding import PartitionSpec as P

SUBS = 8
LANES = 128
MIB = 1024 * 1024
A_TILES, N_TILES, Q_TILES, F_TILES = 2, 2, 4, 4
NEAR_PARTS = 2
f32 = jnp.float32
bf16 = jnp.bfloat16


def from_behind(shard, axis, by):
    count = lax.axis_size(axis)
    pairs = [(i, i + by) for i in range(count) if 0 <= i + by < count]
    return lax.ppermute(shard, axis, pairs)


def swap(shard, axis):
    return lax.ppermute(shard, axis, [(i, i ^ 1) for i in range(lax.axis_size(axis))])


def doc_start_rows(len_ref, base, span):
    rows = lax.broadcasted_iota(jnp.int32, (SUBS, LANES), 0) * span + base
    starts = [jnp.int32(0)]
    for d in range(len_ref.shape[0] - 1):
        starts.append(starts[-1] + len_ref[d])
    out = []
    for j in range(span):
        pos = rows + j
        best = jnp.zeros((SUBS, LANES), jnp.int32)
        for start in starts[1:]:
            best = jnp.where(pos >= start, start, best)
        out.append(best)
    return rows, out


def flag(cond):
    return jnp.where(cond, 1.0, 0.0).astype(f32)


def each_group(count, most, group):
    size = math.gcd(count, most)

    def step(i, carry):
        group([pl.multiple_of((i * size + m) * LANES, LANES) for m in range(size)])
        return carry

    lax.fori_loop(0, count // size, step, 0)


def each_chunk(chans, chunk, before, group, after, most):
    def step(c, carry):
        before(c)

        def inner(lanes):
            group([pl.multiple_of(c * chunk + lane, LANES) for lane in lanes])

        each_group(chunk // LANES, most, inner)
        after(c)
        return carry

    lax.fori_loop(0, chans // chunk, step, 0)


def cols_copy(src, dst, sem, c, chunk):
    cols = pl.ds(pl.multiple_of(c * chunk, chunk), chunk)
    return pltpu.make_async_copy(src.at[:, cols], dst.at[:, cols], sem.at[c])


def cols_of(lane):
    return pl.ds(lane, LANES)


def row_of(ref, index):
    return ref[pl.ds(index, SUBS, stride=0), :]


def spread(x, wide, span):
    x = x.astype(f32)
    for b in range(SUBS):
        wide[pl.ds(b * (span + 1), span), :] = x[b * span : (b + 1) * span]


class Conv:
    def __init__(self, wide, rim, taps, span):
        self.wide, self.span = wide, span
        self.taps = [jnp.broadcast_to(taps[m : m + 1], (SUBS, LANES)) for m in range(3)]
        top = lax.broadcasted_iota(jnp.int32, (SUBS, LANES), 0) == 0
        ahead = [0.0, 0.0] if rim is None else [jnp.broadcast_to(rim[m : m + 1].astype(f32), (SUBS, LANES)) for m in range(2)]
        self.behind = [jnp.where(top, ahead[m], pltpu.roll(self.row(span - 2 + m), 1, 0)) for m in range(2)]

    def row(self, j):
        return self.wide[pl.ds(j, SUBS, stride=self.span + 1), :]

    def step(self, j, keep_one, keep_two):
        here = self.row(j)
        two, one = self.behind
        self.behind = [one, here]
        return self.taps[0] * here + (self.taps[1] * one) * keep_one + (self.taps[2] * two) * keep_two


def half_of(chans, lane):
    half = chans // 2
    which = lax.div(lane, half)
    mine = which == lax.rem(lax.axis_index("ctx"), 2)
    return mine, pl.multiple_of(lane - which * half, LANES)


def twice(mask, modes):
    return jnp.concatenate([mask] * (modes // SUBS), axis=0)


def sub_state(state_ref, lane, b, modes):
    return state_ref[lax.div(lane, LANES), pl.ds(b * (modes + 1), modes), :]


def state_kernel(
    masks, key_ref, value_ref, rim_ref, taps_ref, rate_ref,
    gate_ref, state_ref, own_ref, give_ref,
    key_buf, value_buf, sems, wide_k, wide_v, tables, held,
    *, span, modes, most, chunk,
):
    chans = key_buf.shape[1]

    def fetches(c):
        return [cols_copy(key_ref, key_buf, sems.at[0], c, chunk), cols_copy(value_ref, value_buf, sems.at[1], c, chunk)]

    for c in range(chans // chunk):
        for copy in fetches(c):
            copy.start()

    at = Masks(span)

    def group(lanes):
        for slot, lane in enumerate(lanes):
            spread(key_buf[:, cols_of(lane)], wide_k.at[slot], span)
            spread(value_buf[:, cols_of(lane)], wide_v.at[slot], span)
            rate = rate_ref[:, cols_of(lane)]
            tables[slot] = jnp.exp(-rate)
        convs = [
            [
                Conv(wide.at[slot], rim_ref[i, :, cols_of(lane)], taps_ref[i, :, cols_of(lane)], span)
                for i, wide in ((1, wide_k), (2, wide_v))
            ]
            for slot, lane in enumerate(lanes)
        ]
        last = [None] * len(lanes)
        for j in range(span):
            keep_one, keep_two = masks[at.one + j], masks[at.two + j]
            for slot, lane in enumerate(lanes):
                k_short, v_short = [conv.step(j, keep_one, keep_two) for conv in convs[slot]]
                if j % 2 == 0:
                    last[slot] = k_short * v_short
                    continue
                pair = jnp.concatenate([last[slot], k_short * v_short], axis=0).astype(bf16)
                gate_ref[pl.ds((j - 1) * SUBS, 2 * SUBS), cols_of(lane)] = pair
                pair = pair.astype(f32)
                held[slot, j - 1] = pair[:SUBS] * masks[at.last + j - 1]
                held[slot, j] = pair[SUBS:] * masks[at.last + j]
        for slot, lane in enumerate(lanes):
            decay = [row_of(tables.at[slot], n) for n in range(modes)]
            state = [held[slot, 0]] * modes
            for j in range(1, span):
                gate = held[slot, j]
                state = [decay[n] * state[n] + gate for n in range(modes)]
            for n in range(modes):
                state_ref[lax.div(lane, LANES), pl.ds(n, SUBS, stride=modes + 1), :] = state[n]
        for slot, lane in enumerate(lanes):
            leap = jnp.exp(-float(span) * rate_ref[:, cols_of(lane)])
            end = sub_state(state_ref, lane, 0, modes)
            for b in range(1, SUBS):
                end = (leap * twice(masks[at.passes + b], modes)) * end + sub_state(state_ref, lane, b, modes)
            mine, here = half_of(chans, lane)

            @pl.when(mine)
            def _():
                own_ref[:, cols_of(here)] = end

            @pl.when(jnp.logical_not(mine))
            def _():
                give_ref[:, cols_of(here)] = end

    def before(c):
        for copy in fetches(c):
            copy.wait()

    each_chunk(chans, chunk, before, group, lambda c: None, most)


def tail_kernel(query_ref, key_ref, value_ref, tail_ref, bufs, sems):
    rows, count = query_ref.shape[0], bufs.shape[1]
    copies = [
        pltpu.make_async_copy(ref.at[pl.ds(rows - count, count)], bufs.at[i], sems.at[i])
        for i, ref in enumerate((query_ref, key_ref, value_ref))
    ]
    for copy in copies:
        copy.start()
    for i, copy in enumerate(copies):
        copy.wait()
        tail_ref[i] = bufs[i].astype(f32)[count - 2 :].astype(bf16)


def unbroken(len_ref, first, count):
    start = jnp.int32(0)
    whole = jnp.where((first <= 0) & (first + count > 0), 0.0, 1.0)
    for d in range(len_ref.shape[0] - 1):
        start = start + len_ref[d]
        whole = jnp.where((start >= first) & (start < first + count), 0.0, whole)
    return whole.astype(f32)


class Masks:
    def __init__(self, span):
        self.one, self.two, self.last, self.enter = 0, span, 2 * span, 3 * span
        self.passes = 4 * span
        self.edges = self.passes + SUBS
        self.late = self.edges + 3
        self.early = self.late + 1
        self.reach = self.late + 2

    def count(self, reaches):
        return self.reach + reaches


def write_masks(base_ref, len_ref, masks, span, reaches):
    at = Masks(span)
    rows, starts = doc_start_rows(len_ref, base_ref[0], span)
    for j in range(span):
        masks[at.one + j] = flag(starts[j] < rows + j)
        masks[at.two + j] = flag(starts[j] < rows + (j - 1))
        masks[at.last + j] = flag(starts[span - 1] <= rows + j)
        masks[at.enter + j] = flag(starts[j] < rows)
    top = flag(lax.broadcasted_iota(jnp.int32, (SUBS, LANES), 0) == 0)
    masks[at.edges] = top * masks[at.one]
    masks[at.edges + 1] = top * masks[at.two]
    masks[at.edges + 2] = top * masks[at.two + 1]
    size = SUBS * span
    parity = lax.rem(lax.div(base_ref[0], size), 2)
    pair_at = base_ref[0] - parity * size
    ranges = [(base_ref[0] + b * span, span) for b in range(SUBS)]
    flags = [at.passes + b for b in range(SUBS)]
    ranges += [(pair_at + size, size), (pair_at, size)]
    flags += [at.late, at.early]
    for m in range(reaches):
        ranges.append((pair_at - (2 * size << m), 2 * size << m))
        flags.append(at.reach + m)
    for index, (first, count) in zip(flags, ranges):
        masks[index] = jnp.full((SUBS, LANES), unbroken(len_ref, first, count), f32)


def near_kernel(masks, gate_ref, rate_ref, weight_ref, *refs, span, modes, most, first, count):
    near_ref, sums, tap_rows = refs[-3:]
    at = Masks(span)

    def group(lanes):
        for slot, lane in enumerate(lanes):
            decay = jnp.exp(-rate_ref[:, cols_of(lane)])
            term = weight_ref[:, cols_of(lane)]
            for lag in range(span):
                part = term[:SUBS]
                for n in range(SUBS, modes, SUBS):
                    part = part + term[n : n + SUBS]
                sums[slot, pl.ds(lag * (SUBS + 1), SUBS), :] = part
                term = term * decay
        for slot in range(len(lanes)):
            for first_lag in range(0, span, SUBS):
                total = [
                    sums[slot, pl.ds(first_lag * (SUBS + 1) + m, SUBS, stride=SUBS + 1), :] for m in range(SUBS)
                ]
                while len(total) > 1:
                    total = [total[m] + total[m + 1] for m in range(0, len(total), 2)]
                tap_rows[slot, pl.ds(first_lag, SUBS), :] = total[0]
        taps = [[row_of(tap_rows.at[slot], lag) for lag in range(span)] for slot in range(len(lanes))]
        for parts, lane in zip(taps, lanes):
            live = []
            for j in range(span):
                if j % 2 == 0:
                    pair = gate_ref[pl.ds(j * SUBS, 2 * SUBS), cols_of(lane)].astype(f32)
                keep = masks[at.one + j]
                live = [g * keep for g in live]
                live.append(pair[(j % 2) * SUBS : (j % 2 + 1) * SUBS])
                total = parts[0] * live[j]
                for lag in range(1, j + 1):
                    total = total + parts[lag] * live[j - lag]
                near_ref[pl.ds(j * SUBS, SUBS), cols_of(lane)] = total

    each_group(count // LANES, most, lambda lanes: group([pl.multiple_of(first + lane, LANES) for lane in lanes]))


def query_kernel(base_ref, len_ref, query_ref, taps_ref, short_ref, masks, query_buf, sems, wide_q, *, span, most, chunk, reaches):
    chans = query_buf.shape[1]

    def fetch(c):
        return cols_copy(query_ref, query_buf, sems, c, chunk)

    for c in range(chans // chunk):
        fetch(c).start()
    write_masks(base_ref, len_ref, masks, span, reaches)
    at = Masks(span)

    def group(lanes):
        for slot, lane in enumerate(lanes):
            spread(query_buf[:, cols_of(lane)], wide_q.at[slot], span)
        convs = [Conv(wide_q.at[slot], None, taps_ref[0, :, cols_of(lane)], span) for slot, lane in enumerate(lanes)]
        for j in range(span):
            keep_one, keep_two = masks[at.one + j], masks[at.two + j]
            for slot, lane in enumerate(lanes):
                short_ref[pl.ds(j * SUBS, SUBS), cols_of(lane)] = convs[slot].step(j, keep_one, keep_two)

    each_chunk(chans, chunk, lambda c: fetch(c).wait(), group, lambda c: None, most)


def final_kernel(
    masks, state_ref, mine_ref, got_ref, near_ref, short_ref, resid_in, rim_ref, taps_ref, rate_ref, weight_ref, gain_ref,
    *refs,
    span, modes, channels, most, chunk,
):
    if channels:
        hidden_out, normed_out, resid_ref, hidden_ref, sems, wide, tables, starts_at, sums, whole, normed_ref = refs
    else:
        hidden_out, wide_ref, sum_ref, resid_ref, hidden_ref, sems, wide, tables, starts_at, sums = refs
    chans = resid_ref.shape[1]

    def fetch(c):
        return cols_copy(resid_in, resid_ref, sems.at[0], c, chunk)

    def store(c):
        return cols_copy(hidden_ref, hidden_out, sems.at[1], c, chunk)

    def store_normed(c):
        return cols_copy(normed_ref, normed_out, sems.at[2], c, chunk)

    for c in range(chans // chunk):
        fetch(c).start()
    at = Masks(span)
    sums[...] = jnp.zeros(sums.shape, f32)

    def group(lanes):
        for slot, lane in enumerate(lanes):
            mine, here = half_of(chans, lane)
            mine = jnp.full((modes, LANES), mine.astype(jnp.int32), jnp.int32) == 1
            state = jnp.where(mine, mine_ref[:, cols_of(here)], got_ref[:, cols_of(here)])
            rate = rate_ref[:, cols_of(lane)]
            weight = weight_ref[:, cols_of(lane)]
            tables[slot] = jnp.exp(-rate)
            leap = jnp.exp(-float(span) * rate)
            for b in range(SUBS):
                starts_at[slot, pl.ds(b * (modes + 1), modes), :] = weight * state
                if b < SUBS - 1:
                    state = (leap * twice(masks[at.passes + b], modes)) * state + sub_state(state_ref, lane, b, modes)
        for slot, lane in enumerate(lanes):
            part = [starts_at[slot, pl.ds(n, SUBS, stride=modes + 1), :] for n in range(modes)]
            decay = [row_of(tables.at[slot], n) for n in range(modes)]
            rim = rim_ref[0, :, cols_of(lane)].astype(f32)
            tap = taps_ref[0, :, cols_of(lane)]
            edge = [
                (tap[1:2] * rim[1:2]) * masks[at.edges] + (tap[2:3] * rim[0:1]) * masks[at.edges + 1],
                (tap[2:3] * rim[1:2]) * masks[at.edges + 2],
            ]
            for j in range(span):
                part = [part[n] * decay[n] for n in range(modes)]
                total = part
                while len(total) > 1:
                    total = [total[m] + total[m + 1] for m in range(0, len(total), 2)]
                conv = near_ref[pl.ds(j * SUBS, SUBS), cols_of(lane)] + total[0] * masks[at.enter + j]
                conv = conv.astype(bf16).astype(f32)
                short = short_ref[pl.ds(j * SUBS, SUBS), cols_of(lane)]
                if j < 2:
                    short = short + edge[j]
                wide[slot, pl.ds(j, SUBS, stride=span + 1), :] = short * conv
        for b in range(SUBS):
            rows = pl.ds(b * span, span)
            squares = sums[rows, :]
            for slot, lane in enumerate(lanes):
                hidden = wide[slot, pl.ds(b * (span + 1), span), :] + resid_ref[rows, cols_of(lane)].astype(f32)
                if channels:
                    whole[lax.div(lane, LANES), rows, :] = hidden
                else:
                    wide_ref[rows, cols_of(lane)] = hidden
                hidden_ref[rows, cols_of(lane)] = hidden.astype(bf16)
                squares = squares + hidden * hidden
            sums[rows, :] = squares

    each_chunk(chans, chunk, lambda c: fetch(c).wait(), group, lambda c: store(c).start(), most)
    if channels:
        inverse = lax.rsqrt(jnp.sum(sums[...], axis=1, keepdims=True) / channels + 1e-06)
        sums[...] = jnp.broadcast_to(inverse, sums.shape)

        def scale(lanes):
            for lane in lanes:
                normed = whole[lax.div(lane, LANES)] * sums[...] * gain_ref[:, cols_of(lane)]
                normed_ref[:, cols_of(lane)] = normed.astype(bf16)

        each_chunk(chans, chunk, lambda c: None, scale, lambda c: store_normed(c).start(), 4)
        for c in range(chans // chunk):
            store_normed(c).wait()
    else:
        sum_ref[...] = sums[...]
    for c in range(chans // chunk):
        store(c).wait()


def shards(
    query_in, key_in, value_in, short_taps, decay_rate, residues, doc_lengths, residual, norm_gain
):
    tok_rows, chans = query_in.shape
    modes = decay_rate.shape[0]
    span = tok_rows // SUBS
    blocks = lax.axis_size("ctx")
    grp = lax.axis_size("grp")
    chunk = min(chans, 1024)
    pieces = chans // chunk
    ctx_index = lax.axis_index("ctx")
    base = (ctx_index * tok_rows).astype(jnp.int32).reshape(1)
    weight = residues * jnp.sqrt(-jnp.expm1(-2.0 * decay_rate))

    smem = pl.BlockSpec(memory_space=pltpu.SMEM)
    vmem = pl.BlockSpec(memory_space=pltpu.VMEM)
    hbm = pl.BlockSpec(memory_space=pltpu.HBM)
    half = jax.ShapeDtypeStruct((modes, chans // 2), f32)
    tile_shape = (SUBS, LANES)
    wide_rows = SUBS * (span + 1)
    params = pltpu.CompilerParams(vmem_limit_bytes=16 * MIB)

    lengths = pltpu.with_memory_space_constraint(doc_lengths, pltpu.HBM)

    def near_by(x):
        return pltpu.with_memory_space_constraint(x, pltpu.VMEM)

    def far_off(x):
        return pltpu.with_memory_space_constraint(x, pltpu.HBM)

    def copies(kinds):
        return pltpu.SemaphoreType.DMA((kinds, pieces))

    def cost(per_tile, moved):
        return pl.CostEstimate(flops=per_tile * (chans // LANES) * SUBS * LANES, bytes_accessed=moved, transcendentals=0)

    tails = pl.pallas_call(
        tail_kernel,
        in_specs=[hbm, hbm, hbm],
        out_specs=vmem,
        out_shape=pltpu.VMEM((3, 2, chans), bf16),
        scratch_shapes=[pltpu.VMEM((3, 16, chans), bf16), pltpu.SemaphoreType.DMA((3,))],
        compiler_params=params,
        name="tails",
    )(far_off(query_in), far_off(key_in), far_off(value_in))
    rim_rows = from_behind(tails, "ctx", 1)
    reaches = max(1, (blocks // 8).bit_length() - 1)
    mask_shape = (Masks(span).count(reaches),) + tile_shape
    q_short, masks = pl.pallas_call(
        functools.partial(query_kernel, span=span, most=Q_TILES, chunk=chunk, reaches=reaches),
        in_specs=[smem, smem, hbm, vmem],
        out_specs=[vmem, vmem],
        out_shape=[pltpu.VMEM((tok_rows, chans), f32), pltpu.VMEM(mask_shape, f32)],
        scratch_shapes=[
            pltpu.VMEM((tok_rows, chans), bf16),
            pltpu.SemaphoreType.DMA((pieces,)),
            pltpu.VMEM((Q_TILES, wide_rows, LANES), f32),
        ],
        compiler_params=params,
        cost_estimate=cost(200, 6 * tok_rows * chans),
        name="query_part",
    )(base, lengths, far_off(query_in), near_by(short_taps))
    rim_rows, q_short = lax.optimization_barrier((rim_rows, q_short))
    rates, weights, taps, rims = near_by(decay_rate), near_by(weight), near_by(short_taps), near_by(rim_rows)
    gates, states, own, give = pl.pallas_call(
        functools.partial(state_kernel, span=span, modes=modes, most=A_TILES, chunk=chunk),
        in_specs=[vmem, hbm, hbm, vmem, vmem, vmem],
        out_specs=[vmem, vmem, vmem, vmem],
        out_shape=[
            pltpu.VMEM((tok_rows, chans), bf16),
            pltpu.VMEM((chans // LANES, SUBS * (modes + 1), LANES), f32),
            pltpu.VMEM(half.shape, f32),
            pltpu.VMEM(half.shape, f32),
        ],
        scratch_shapes=[
            pltpu.VMEM((tok_rows, chans), bf16),
            pltpu.VMEM((tok_rows, chans), bf16),
            copies(2),
            pltpu.VMEM((A_TILES, wide_rows, LANES), f32),
            pltpu.VMEM((A_TILES, wide_rows, LANES), f32),
            pltpu.VMEM((A_TILES, modes, LANES), f32),
            pltpu.VMEM((A_TILES, span) + tile_shape, f32),
        ],
        compiler_params=params,
        cost_estimate=cost(1000, 12 * tok_rows * chans),
        name="block_states",
    )(near_by(masks), far_off(key_in), far_off(value_in), rims, taps, rates)

    def near_piece(part, near):
        count = chans // NEAR_PARTS
        before = [] if near is None else [near_by(near)]
        return pl.pallas_call(
            functools.partial(
                near_kernel, span=span, modes=modes, most=N_TILES, first=part * count, count=count
            ),
            in_specs=[vmem] * (4 + len(before)),
            out_specs=vmem,
            out_shape=pltpu.VMEM((tok_rows, chans), f32),
            scratch_shapes=[
                pltpu.VMEM((N_TILES, span * (SUBS + 1), LANES), f32),
                pltpu.VMEM((N_TILES, span, LANES), f32),
            ],
            compiler_params=params,
            input_output_aliases={4: 0} if before else {},
            cost_estimate=cost(600 // NEAR_PARTS, 7 * tok_rows * count),
            name="near_part_%d" % part,
        )(near_by(masks), near_by(gates), rates, weights, *before)

    got = swap(give, "ctx")

    odd = lax.rem(ctx_index, 2) == 1
    few_rates = lax.dynamic_slice_in_dim(decay_rate, lax.rem(ctx_index, 2) * half.shape[1], half.shape[1], 1)
    at = Masks(span)

    def leap(rows, index):
        return jnp.exp(-float(rows) * few_rates) * masks[index, 0, 0]

    early, late = jnp.where(odd, got, own), jnp.where(odd, own, got)
    ends = (late + leap(tok_rows, at.late) * early).astype(bf16)
    one_on, two_on = from_behind(ends, "ctx", 2), from_behind(ends, "ctx", 4)
    near = near_piece(0, None)
    one_on, two_on, near = lax.optimization_barrier((one_on, two_on, near))
    enter, on = one_on, two_on
    for m in range(reaches - 1):
        enter = (enter.astype(f32) + leap(2 * tok_rows << m, at.reach + m) * on.astype(f32)).astype(bf16)
        on = from_behind(enter, "ctx", 4 << m)
    near = near_piece(1, near)
    on, near = lax.optimization_barrier((on, near))
    first = enter.astype(f32) + leap(2 * tok_rows << (reaches - 1), at.reach + reaches - 1) * on.astype(f32)
    second = early + leap(tok_rows, at.early) * first
    mine, give_back = jnp.where(odd, second, first), jnp.where(odd, first, second)
    got_back = swap(give_back, "ctx")

    alone = grp == 1
    out_specs = [hbm]
    out_shape = [jax.ShapeDtypeStruct((tok_rows, chans), bf16)]
    scratch = [
        pltpu.VMEM((tok_rows, chans), bf16),
        pltpu.VMEM((tok_rows, chans), bf16),
        copies(3),
        pltpu.VMEM((F_TILES, wide_rows, LANES), f32),
        pltpu.VMEM((F_TILES, modes, LANES), f32),
        pltpu.VMEM((F_TILES, SUBS * (modes + 1), LANES), f32),
        pltpu.VMEM((tok_rows, LANES), f32),
    ]
    if alone:
        out_specs.append(hbm)
        out_shape.append(jax.ShapeDtypeStruct((tok_rows, chans), bf16))
        scratch += [pltpu.VMEM((chans // LANES, tok_rows, LANES), f32), pltpu.VMEM((tok_rows, chans), bf16)]
    else:
        out_specs += [vmem, vmem]
        out_shape += [jax.ShapeDtypeStruct((tok_rows, chans), f32), jax.ShapeDtypeStruct((tok_rows, LANES), f32)]
    outs = pl.pallas_call(
        functools.partial(
            final_kernel, span=span, modes=modes, channels=chans if alone else 0, most=F_TILES, chunk=chunk
        ),
        in_specs=[vmem, vmem, vmem, vmem, vmem, vmem, hbm, vmem, vmem, vmem, vmem, vmem],
        out_specs=out_specs,
        out_shape=out_shape,
        scratch_shapes=scratch,
        compiler_params=params,
        cost_estimate=cost(900, 18 * tok_rows * chans),
        name="far_part",
    )(
        near_by(masks), near_by(states), near_by(mine), near_by(got_back), near_by(near), near_by(q_short), far_off(residual),
        rims, taps, rates, weights, norm_gain.reshape(1, chans),
    )
    if alone:
        return tuple(outs)
    hidden_out, hidden, sums = outs
    square_sum = lax.psum(jnp.sum(sums, axis=1), "grp")
    inverse_rms = lax.rsqrt(square_sum / (chans * grp) + 1e-06)
    normed = (hidden * inverse_rms[:, None] * norm_gain[None, :]).astype(bf16)
    return (hidden_out, normed)


def solution(mesh):
    return jax.shard_map(
        shards,
        mesh=mesh,
        in_specs=(
            P("ctx", "grp"),
            P("ctx", "grp"),
            P("ctx", "grp"),
            P(None, None, "grp"),
            P(None, "grp"),
            P(None, "grp"),
            P(),
            P("ctx", "grp"),
            P("grp"),
        ),
        out_specs=(P("ctx", "grp"), P("ctx", "grp")),
        check_vma=False,
    )
```

```python
import functools
import math

import jax
import jax.numpy as jnp
from jax import lax
from jax.experimental import pallas as pl
from jax.experimental.pallas import tpu as pltpu
from jax.sharding import PartitionSpec as P

SUBS = 8
LANES = 128
MIB = 1024 * 1024
A_TILES, N_TILES, Q_TILES, F_TILES = 2, 2, 4, 4
NEAR_PARTS = 2
f32 = jnp.float32
bf16 = jnp.bfloat16


def from_behind(shard, axis, by):
    count = lax.axis_size(axis)
    pairs = [(i, i + by) for i in range(count) if 0 <= i + by < count]
    return lax.ppermute(shard, axis, pairs)


def swap(shard, axis):
    return lax.ppermute(shard, axis, [(i, i ^ 1) for i in range(lax.axis_size(axis))])


def doc_start_rows(len_ref, base, span):
    rows = lax.broadcasted_iota(jnp.int32, (SUBS, LANES), 0) * span + base
    starts = [jnp.int32(0)]
    for d in range(len_ref.shape[0] - 1):
        starts.append(starts[-1] + len_ref[d])
    out = []
    for j in range(span):
        pos = rows + j
        best = jnp.zeros((SUBS, LANES), jnp.int32)
        for start in starts[1:]:
            best = jnp.where(pos >= start, start, best)
        out.append(best)
    return rows, out


def flag(cond):
    return jnp.where(cond, 1.0, 0.0).astype(f32)


def each_group(count, most, group):
    size = math.gcd(count, most)

    def step(i, carry):
        group([pl.multiple_of((i * size + m) * LANES, LANES) for m in range(size)])
        return carry

    lax.fori_loop(0, count // size, step, 0)


def each_chunk(chans, chunk, before, group, after, most):
    def step(c, carry):
        before(c)

        def inner(lanes):
            group([pl.multiple_of(c * chunk + lane, LANES) for lane in lanes])

        each_group(chunk // LANES, most, inner)
        after(c)
        return carry

    lax.fori_loop(0, chans // chunk, step, 0)


def cols_copy(src, dst, sem, c, chunk):
    cols = pl.ds(pl.multiple_of(c * chunk, chunk), chunk)
    return pltpu.make_async_copy(src.at[:, cols], dst.at[:, cols], sem.at[c])


def cols_of(lane):
    return pl.ds(lane, LANES)


def row_of(ref, index):
    return ref[pl.ds(index, SUBS, stride=0), :]


def spread(x, wide, span):
    x = x.astype(f32)
    for b in range(SUBS):
        wide[pl.ds(b * (span + 1), span), :] = x[b * span : (b + 1) * span]


class Conv:
    def __init__(self, wide, rim, taps, span):
        self.wide, self.span = wide, span
        self.taps = [jnp.broadcast_to(taps[m : m + 1], (SUBS, LANES)) for m in range(3)]
        top = lax.broadcasted_iota(jnp.int32, (SUBS, LANES), 0) == 0
        ahead = [0.0, 0.0] if rim is None else [jnp.broadcast_to(rim[m : m + 1].astype(f32), (SUBS, LANES)) for m in range(2)]
        self.behind = [jnp.where(top, ahead[m], pltpu.roll(self.row(span - 2 + m), 1, 0)) for m in range(2)]

    def row(self, j):
        return self.wide[pl.ds(j, SUBS, stride=self.span + 1), :]

    def step(self, j, keep_one, keep_two):
        here = self.row(j)
        two, one = self.behind
        self.behind = [one, here]
        return self.taps[0] * here + (self.taps[1] * one) * keep_one + (self.taps[2] * two) * keep_two


def half_of(chans, lane):
    half = chans // 2
    which = lax.div(lane, half)
    mine = which == lax.rem(lax.axis_index("ctx"), 2)
    return mine, pl.multiple_of(lane - which * half, LANES)


def twice(mask, modes):
    return jnp.concatenate([mask] * (modes // SUBS), axis=0)


def sub_state(state_ref, lane, b, modes):
    return state_ref[lax.div(lane, LANES), pl.ds(b * (modes + 1), modes), :]


def state_kernel(
    masks, key_ref, value_ref, rim_ref, taps_ref, rate_ref,
    gate_ref, state_ref, own_ref, give_ref,
    key_buf, value_buf, sems, wide_k, wide_v, tables, held,
    *, span, modes, most, chunk,
):
    chans = key_buf.shape[1]

    def fetches(c):
        return [cols_copy(key_ref, key_buf, sems.at[0], c, chunk), cols_copy(value_ref, value_buf, sems.at[1], c, chunk)]

    for c in range(chans // chunk):
        for copy in fetches(c):
            copy.start()

    at = Masks(span)

    def group(lanes):
        for slot, lane in enumerate(lanes):
            spread(key_buf[:, cols_of(lane)], wide_k.at[slot], span)
            spread(value_buf[:, cols_of(lane)], wide_v.at[slot], span)
            rate = rate_ref[:, cols_of(lane)]
            tables[slot] = jnp.exp(-rate)
        convs = [
            [
                Conv(wide.at[slot], rim_ref[i, :, cols_of(lane)], taps_ref[i, :, cols_of(lane)], span)
                for i, wide in ((1, wide_k), (2, wide_v))
            ]
            for slot, lane in enumerate(lanes)
        ]
        last = [None] * len(lanes)
        for j in range(span):
            keep_one, keep_two = masks[at.one + j], masks[at.two + j]
            for slot, lane in enumerate(lanes):
                k_short, v_short = [conv.step(j, keep_one, keep_two) for conv in convs[slot]]
                if j % 2 == 0:
                    last[slot] = k_short * v_short
                    continue
                pair = jnp.concatenate([last[slot], k_short * v_short], axis=0).astype(bf16)
                gate_ref[pl.ds((j - 1) * SUBS, 2 * SUBS), cols_of(lane)] = pair
                pair = pair.astype(f32)
                held[slot, j - 1] = pair[:SUBS] * masks[at.last + j - 1]
                held[slot, j] = pair[SUBS:] * masks[at.last + j]
        for slot, lane in enumerate(lanes):
            decay = [row_of(tables.at[slot], n) for n in range(modes)]
            state = [held[slot, 0]] * modes
            for j in range(1, span):
                gate = held[slot, j]
                state = [decay[n] * state[n] + gate for n in range(modes)]
            for n in range(modes):
                state_ref[lax.div(lane, LANES), pl.ds(n, SUBS, stride=modes + 1), :] = state[n]
        for slot, lane in enumerate(lanes):
            leap = jnp.exp(-float(span) * rate_ref[:, cols_of(lane)])
            end = sub_state(state_ref, lane, 0, modes)
            for b in range(1, SUBS):
                end = (leap * twice(masks[at.passes + b], modes)) * end + sub_state(state_ref, lane, b, modes)
            mine, here = half_of(chans, lane)

            @pl.when(mine)
            def _():
                own_ref[:, cols_of(here)] = end

            @pl.when(jnp.logical_not(mine))
            def _():
                give_ref[:, cols_of(here)] = end

    def before(c):
        for copy in fetches(c):
            copy.wait()

    each_chunk(chans, chunk, before, group, lambda c: None, most)


def tail_kernel(query_ref, key_ref, value_ref, tail_ref, bufs, sems):
    rows, count = query_ref.shape[0], bufs.shape[1]
    copies = [
        pltpu.make_async_copy(ref.at[pl.ds(rows - count, count)], bufs.at[i], sems.at[i])
        for i, ref in enumerate((query_ref, key_ref, value_ref))
    ]
    for copy in copies:
        copy.start()
    for i, copy in enumerate(copies):
        copy.wait()
        tail_ref[i] = bufs[i].astype(f32)[count - 2 :].astype(bf16)


def unbroken(len_ref, first, count):
    start = jnp.int32(0)
    whole = jnp.where((first <= 0) & (first + count > 0), 0.0, 1.0)
    for d in range(len_ref.shape[0] - 1):
        start = start + len_ref[d]
        whole = jnp.where((start >= first) & (start < first + count), 0.0, whole)
    return whole.astype(f32)


class Masks:
    def __init__(self, span):
        self.one, self.two, self.last, self.enter = 0, span, 2 * span, 3 * span
        self.passes = 4 * span
        self.edges = self.passes + SUBS
        self.late = self.edges + 3
        self.early = self.late + 1
        self.reach = self.late + 2

    def count(self, reaches):
        return self.reach + reaches


def write_masks(base_ref, len_ref, masks, span, reaches):
    at = Masks(span)
    rows, starts = doc_start_rows(len_ref, base_ref[0], span)
    for j in range(span):
        masks[at.one + j] = flag(starts[j] < rows + j)
        masks[at.two + j] = flag(starts[j] < rows + (j - 1))
        masks[at.last + j] = flag(starts[span - 1] <= rows + j)
        masks[at.enter + j] = flag(starts[j] < rows)
    top = flag(lax.broadcasted_iota(jnp.int32, (SUBS, LANES), 0) == 0)
    masks[at.edges] = top * masks[at.one]
    masks[at.edges + 1] = top * masks[at.two]
    masks[at.edges + 2] = top * masks[at.two + 1]
    size = SUBS * span
    parity = lax.rem(lax.div(base_ref[0], size), 2)
    pair_at = base_ref[0] - parity * size
    ranges = [(base_ref[0] + b * span, span) for b in range(SUBS)]
    flags = [at.passes + b for b in range(SUBS)]
    ranges += [(pair_at + size, size), (pair_at, size)]
    flags += [at.late, at.early]
    for m in range(reaches):
        ranges.append((pair_at - (2 * size << m), 2 * size << m))
        flags.append(at.reach + m)
    for index, (first, count) in zip(flags, ranges):
        masks[index] = jnp.full((SUBS, LANES), unbroken(len_ref, first, count), f32)


def near_kernel(masks, gate_ref, rate_ref, weight_ref, *refs, span, modes, most, first, count):
    near_ref, sums, tap_rows = refs[-3:]
    at = Masks(span)

    def group(lanes):
        for slot, lane in enumerate(lanes):
            decay = jnp.exp(-rate_ref[:, cols_of(lane)])
            term = weight_ref[:, cols_of(lane)]
            for lag in range(span):
                part = term[:SUBS]
                for n in range(SUBS, modes, SUBS):
                    part = part + term[n : n + SUBS]
                sums[slot, pl.ds(lag * (SUBS + 1), SUBS), :] = part
                term = term * decay
        for slot in range(len(lanes)):
            for first_lag in range(0, span, SUBS):
                total = [
                    sums[slot, pl.ds(first_lag * (SUBS + 1) + m, SUBS, stride=SUBS + 1), :] for m in range(SUBS)
                ]
                while len(total) > 1:
                    total = [total[m] + total[m + 1] for m in range(0, len(total), 2)]
                tap_rows[slot, pl.ds(first_lag, SUBS), :] = total[0]
        taps = [[row_of(tap_rows.at[slot], lag) for lag in range(span)] for slot in range(len(lanes))]
        for parts, lane in zip(taps, lanes):
            live = []
            for j in range(span):
                if j % 2 == 0:
                    pair = gate_ref[pl.ds(j * SUBS, 2 * SUBS), cols_of(lane)].astype(f32)
                keep = masks[at.one + j]
                live = [g * keep for g in live]
                live.append(pair[(j % 2) * SUBS : (j % 2 + 1) * SUBS])
                total = parts[0] * live[j]
                for lag in range(1, j + 1):
                    total = total + parts[lag] * live[j - lag]
                near_ref[pl.ds(j * SUBS, SUBS), cols_of(lane)] = total

    each_group(count // LANES, most, lambda lanes: group([pl.multiple_of(first + lane, LANES) for lane in lanes]))


def query_kernel(base_ref, len_ref, query_ref, taps_ref, short_ref, masks, query_buf, sems, wide_q, *, span, most, chunk, reaches):
    chans = query_buf.shape[1]

    def fetch(c):
        return cols_copy(query_ref, query_buf, sems, c, chunk)

    for c in range(chans // chunk):
        fetch(c).start()
    write_masks(base_ref, len_ref, masks, span, reaches)
    at = Masks(span)

    def group(lanes):
        for slot, lane in enumerate(lanes):
            spread(query_buf[:, cols_of(lane)], wide_q.at[slot], span)
        convs = [Conv(wide_q.at[slot], None, taps_ref[0, :, cols_of(lane)], span) for slot, lane in enumerate(lanes)]
        for j in range(span):
            keep_one, keep_two = masks[at.one + j], masks[at.two + j]
            for slot, lane in enumerate(lanes):
                short_ref[pl.ds(j * SUBS, SUBS), cols_of(lane)] = convs[slot].step(j, keep_one, keep_two)

    each_chunk(chans, chunk, lambda c: fetch(c).wait(), group, lambda c: None, most)


def pair_rates(rate_ref, count):
    parity = lax.rem(lax.axis_index("ctx"), 2)
    return parity, rate_ref[:, pl.ds(pl.multiple_of(parity * count, LANES), count)]


def early_late(parity, own, got):
    odd = jnp.full(own.shape, parity, jnp.int32) == 1
    return jnp.where(odd, got, own), jnp.where(odd, own, got)


def leap(masks, index, rate, rows):
    return jnp.exp(-float(rows) * rate) * masks[index][0:1, 0:1]


def pair_kernel(masks, own_ref, got_ref, rate_ref, end_ref, *, rows, index):
    parity, rate = pair_rates(rate_ref, own_ref.shape[1])
    early, late = early_late(parity, own_ref[...], got_ref[...])
    end_ref[...] = (late + leap(masks, index, rate, rows) * early).astype(bf16)


def reach_kernel(masks, near_ref, far_ref, rate_ref, enter_ref, *, rows, index):
    _, rate = pair_rates(rate_ref, near_ref.shape[1])
    enter_ref[...] = (near_ref[...].astype(f32) + leap(masks, index, rate, rows) * far_ref[...].astype(f32)).astype(bf16)


def enter_kernel(
    masks, near_ref, far_ref, own_ref, got_ref, rate_ref, mine_ref, give_ref, *, rows, index, block, block_index
):
    parity, rate = pair_rates(rate_ref, own_ref.shape[1])
    first = near_ref[...].astype(f32) + leap(masks, index, rate, rows) * far_ref[...].astype(f32)
    early, _ = early_late(parity, own_ref[...], got_ref[...])
    second = early + leap(masks, block_index, rate, block) * first
    give, mine = early_late(parity, second, first)
    mine_ref[...] = mine
    give_ref[...] = give


def final_kernel(
    masks, state_ref, mine_ref, got_ref, near_ref, short_ref, resid_in, rim_ref, taps_ref, rate_ref, weight_ref, gain_ref,
    *refs,
    span, modes, channels, most, chunk,
):
    if channels:
        hidden_out, normed_out, resid_ref, hidden_ref, sems, wide, tables, starts_at, sums, whole, normed_ref = refs
    else:
        hidden_out, wide_ref, sum_ref, resid_ref, hidden_ref, sems, wide, tables, starts_at, sums = refs
    chans = resid_ref.shape[1]

    def fetch(c):
        return cols_copy(resid_in, resid_ref, sems.at[0], c, chunk)

    def store(c):
        return cols_copy(hidden_ref, hidden_out, sems.at[1], c, chunk)

    def store_normed(c):
        return cols_copy(normed_ref, normed_out, sems.at[2], c, chunk)

    for c in range(chans // chunk):
        fetch(c).start()
    at = Masks(span)
    sums[...] = jnp.zeros(sums.shape, f32)

    def group(lanes):
        for slot, lane in enumerate(lanes):
            mine, here = half_of(chans, lane)
            mine = jnp.full((modes, LANES), mine.astype(jnp.int32), jnp.int32) == 1
            state = jnp.where(mine, mine_ref[:, cols_of(here)], got_ref[:, cols_of(here)])
            rate = rate_ref[:, cols_of(lane)]
            weight = weight_ref[:, cols_of(lane)]
            tables[slot] = jnp.exp(-rate)
            leap = jnp.exp(-float(span) * rate)
            for b in range(SUBS):
                starts_at[slot, pl.ds(b * (modes + 1), modes), :] = weight * state
                if b < SUBS - 1:
                    state = (leap * twice(masks[at.passes + b], modes)) * state + sub_state(state_ref, lane, b, modes)
        for slot, lane in enumerate(lanes):
            part = [starts_at[slot, pl.ds(n, SUBS, stride=modes + 1), :] for n in range(modes)]
            decay = [row_of(tables.at[slot], n) for n in range(modes)]
            rim = rim_ref[0, :, cols_of(lane)].astype(f32)
            tap = taps_ref[0, :, cols_of(lane)]
            edge = [
                (tap[1:2] * rim[1:2]) * masks[at.edges] + (tap[2:3] * rim[0:1]) * masks[at.edges + 1],
                (tap[2:3] * rim[1:2]) * masks[at.edges + 2],
            ]
            for j in range(span):
                part = [part[n] * decay[n] for n in range(modes)]
                total = part
                while len(total) > 1:
                    total = [total[m] + total[m + 1] for m in range(0, len(total), 2)]
                conv = near_ref[pl.ds(j * SUBS, SUBS), cols_of(lane)] + total[0] * masks[at.enter + j]
                conv = conv.astype(bf16).astype(f32)
                short = short_ref[pl.ds(j * SUBS, SUBS), cols_of(lane)]
                if j < 2:
                    short = short + edge[j]
                wide[slot, pl.ds(j, SUBS, stride=span + 1), :] = short * conv
        for b in range(SUBS):
            rows = pl.ds(b * span, span)
            squares = sums[rows, :]
            for slot, lane in enumerate(lanes):
                hidden = wide[slot, pl.ds(b * (span + 1), span), :] + resid_ref[rows, cols_of(lane)].astype(f32)
                if channels:
                    whole[lax.div(lane, LANES), rows, :] = hidden
                else:
                    wide_ref[rows, cols_of(lane)] = hidden
                hidden_ref[rows, cols_of(lane)] = hidden.astype(bf16)
                squares = squares + hidden * hidden
            sums[rows, :] = squares

    each_chunk(chans, chunk, lambda c: fetch(c).wait(), group, lambda c: store(c).start(), most)
    if channels:
        inverse = lax.rsqrt(jnp.sum(sums[...], axis=1, keepdims=True) / channels + 1e-06)
        sums[...] = jnp.broadcast_to(inverse, sums.shape)

        def scale(lanes):
            for lane in lanes:
                normed = whole[lax.div(lane, LANES)] * sums[...] * gain_ref[:, cols_of(lane)]
                normed_ref[:, cols_of(lane)] = normed.astype(bf16)

        each_chunk(chans, chunk, lambda c: None, scale, lambda c: store_normed(c).start(), 4)
        for c in range(chans // chunk):
            store_normed(c).wait()
    else:
        sum_ref[...] = sums[...]
    for c in range(chans // chunk):
        store(c).wait()


def shards(
    query_in, key_in, value_in, short_taps, decay_rate, residues, doc_lengths, residual, norm_gain
):
    tok_rows, chans = query_in.shape
    modes = decay_rate.shape[0]
    span = tok_rows // SUBS
    blocks = lax.axis_size("ctx")
    grp = lax.axis_size("grp")
    chunk = min(chans, 1024)
    pieces = chans // chunk
    ctx_index = lax.axis_index("ctx")
    base = (ctx_index * tok_rows).astype(jnp.int32).reshape(1)
    weight = residues * jnp.sqrt(-jnp.expm1(-2.0 * decay_rate))

    smem = pl.BlockSpec(memory_space=pltpu.SMEM)
    vmem = pl.BlockSpec(memory_space=pltpu.VMEM)
    hbm = pl.BlockSpec(memory_space=pltpu.HBM)
    half = jax.ShapeDtypeStruct((modes, chans // 2), f32)
    tile_shape = (SUBS, LANES)
    wide_rows = SUBS * (span + 1)
    params = pltpu.CompilerParams(vmem_limit_bytes=16 * MIB)

    lengths = pltpu.with_memory_space_constraint(doc_lengths, pltpu.HBM)

    def near_by(x):
        return pltpu.with_memory_space_constraint(x, pltpu.VMEM)

    def far_off(x):
        return pltpu.with_memory_space_constraint(x, pltpu.HBM)

    def copies(kinds):
        return pltpu.SemaphoreType.DMA((kinds, pieces))

    def cost(per_tile, moved):
        return pl.CostEstimate(flops=per_tile * (chans // LANES) * SUBS * LANES, bytes_accessed=moved, transcendentals=0)

    tails = pl.pallas_call(
        tail_kernel,
        in_specs=[hbm, hbm, hbm],
        out_specs=vmem,
        out_shape=pltpu.VMEM((3, 2, chans), bf16),
        scratch_shapes=[pltpu.VMEM((3, 16, chans), bf16), pltpu.SemaphoreType.DMA((3,))],
        compiler_params=params,
        name="tails",
    )(far_off(query_in), far_off(key_in), far_off(value_in))
    rim_rows = from_behind(tails, "ctx", 1)
    reaches = max(1, (blocks // 8).bit_length() - 1)
    mask_shape = (Masks(span).count(reaches),) + tile_shape
    q_short, masks = pl.pallas_call(
        functools.partial(query_kernel, span=span, most=Q_TILES, chunk=chunk, reaches=reaches),
        in_specs=[smem, smem, hbm, vmem],
        out_specs=[vmem, vmem],
        out_shape=[pltpu.VMEM((tok_rows, chans), f32), pltpu.VMEM(mask_shape, f32)],
        scratch_shapes=[
            pltpu.VMEM((tok_rows, chans), bf16),
            pltpu.SemaphoreType.DMA((pieces,)),
            pltpu.VMEM((Q_TILES, wide_rows, LANES), f32),
        ],
        compiler_params=params,
        cost_estimate=cost(200, 6 * tok_rows * chans),
        name="query_part",
    )(base, lengths, far_off(query_in), near_by(short_taps))
    rim_rows, q_short = lax.optimization_barrier((rim_rows, q_short))
    rates, weights, taps, rims = near_by(decay_rate), near_by(weight), near_by(short_taps), near_by(rim_rows)
    gates, states, own, give = pl.pallas_call(
        functools.partial(state_kernel, span=span, modes=modes, most=A_TILES, chunk=chunk),
        in_specs=[vmem, hbm, hbm, vmem, vmem, vmem],
        out_specs=[vmem, vmem, vmem, vmem],
        out_shape=[
            pltpu.VMEM((tok_rows, chans), bf16),
            pltpu.VMEM((chans // LANES, SUBS * (modes + 1), LANES), f32),
            pltpu.VMEM(half.shape, f32),
            pltpu.VMEM(half.shape, f32),
        ],
        scratch_shapes=[
            pltpu.VMEM((tok_rows, chans), bf16),
            pltpu.VMEM((tok_rows, chans), bf16),
            copies(2),
            pltpu.VMEM((A_TILES, wide_rows, LANES), f32),
            pltpu.VMEM((A_TILES, wide_rows, LANES), f32),
            pltpu.VMEM((A_TILES, modes, LANES), f32),
            pltpu.VMEM((A_TILES, span) + tile_shape, f32),
        ],
        compiler_params=params,
        cost_estimate=cost(1000, 12 * tok_rows * chans),
        name="block_states",
    )(near_by(masks), far_off(key_in), far_off(value_in), rims, taps, rates)

    def near_piece(part, near):
        count = chans // NEAR_PARTS
        before = [] if near is None else [near_by(near)]
        return pl.pallas_call(
            functools.partial(
                near_kernel, span=span, modes=modes, most=N_TILES, first=part * count, count=count
            ),
            in_specs=[vmem] * (4 + len(before)),
            out_specs=vmem,
            out_shape=pltpu.VMEM((tok_rows, chans), f32),
            scratch_shapes=[
                pltpu.VMEM((N_TILES, span * (SUBS + 1), LANES), f32),
                pltpu.VMEM((N_TILES, span, LANES), f32),
            ],
            compiler_params=params,
            input_output_aliases={4: 0} if before else {},
            cost_estimate=cost(600 // NEAR_PARTS, 7 * tok_rows * count),
            name="near_part_%d" % part,
        )(near_by(masks), near_by(gates), rates, weights, *before)

    got = swap(give, "ctx")

    at = Masks(span)

    def pair_call(kernel, operands, out_shape, name, **static):
        return pl.pallas_call(
            functools.partial(kernel, **static),
            in_specs=[vmem] * (len(operands) + 2),
            out_specs=[vmem] * len(out_shape),
            out_shape=out_shape,
            compiler_params=params,
            name=name,
        )(near_by(masks), *[near_by(x) for x in operands], rates)

    sent, kept = pltpu.VMEM(half.shape, bf16), pltpu.VMEM(half.shape, f32)
    ends = pair_call(pair_kernel, [own, got], [sent], "pair_ends", rows=tok_rows, index=at.late)[0]
    one_on, two_on = from_behind(ends, "ctx", 2), from_behind(ends, "ctx", 4)
    near = near_piece(0, None)
    one_on, two_on, near = lax.optimization_barrier((one_on, two_on, near))
    enter, on = one_on, two_on
    for m in range(reaches - 1):
        enter = pair_call(
            reach_kernel, [enter, on], [sent], "reach_%d" % m, rows=2 * tok_rows << m, index=at.reach + m
        )[0]
        on = from_behind(enter, "ctx", 4 << m)
    near = near_piece(1, near)
    on, near = lax.optimization_barrier((on, near))
    mine, give_back = pair_call(
        enter_kernel,
        [enter, on, own, got],
        [kept, kept],
        "pair_enter",
        rows=2 * tok_rows << (reaches - 1),
        index=at.reach + reaches - 1,
        block=tok_rows,
        block_index=at.early,
    )
    got_back = swap(give_back, "ctx")

    alone = grp == 1
    out_specs = [hbm]
    out_shape = [jax.ShapeDtypeStruct((tok_rows, chans), bf16)]
    scratch = [
        pltpu.VMEM((tok_rows, chans), bf16),
        pltpu.VMEM((tok_rows, chans), bf16),
        copies(3),
        pltpu.VMEM((F_TILES, wide_rows, LANES), f32),
        pltpu.VMEM((F_TILES, modes, LANES), f32),
        pltpu.VMEM((F_TILES, SUBS * (modes + 1), LANES), f32),
        pltpu.VMEM((tok_rows, LANES), f32),
    ]
    if alone:
        out_specs.append(hbm)
        out_shape.append(jax.ShapeDtypeStruct((tok_rows, chans), bf16))
        scratch += [pltpu.VMEM((chans // LANES, tok_rows, LANES), f32), pltpu.VMEM((tok_rows, chans), bf16)]
    else:
        out_specs += [vmem, vmem]
        out_shape += [jax.ShapeDtypeStruct((tok_rows, chans), f32), jax.ShapeDtypeStruct((tok_rows, LANES), f32)]
    outs = pl.pallas_call(
        functools.partial(
            final_kernel, span=span, modes=modes, channels=chans if alone else 0, most=F_TILES, chunk=chunk
        ),
        in_specs=[vmem, vmem, vmem, vmem, vmem, vmem, hbm, vmem, vmem, vmem, vmem, vmem],
        out_specs=out_specs,
        out_shape=out_shape,
        scratch_shapes=scratch,
        compiler_params=params,
        cost_estimate=cost(900, 18 * tok_rows * chans),
        name="far_part",
    )(
        near_by(masks), near_by(states), near_by(mine), near_by(got_back), near_by(near), near_by(q_short), far_off(residual),
        rims, taps, rates, weights, norm_gain.reshape(1, chans),
    )
    if alone:
        return tuple(outs)
    hidden_out, hidden, sums = outs
    square_sum = lax.psum(jnp.sum(sums, axis=1), "grp")
    inverse_rms = lax.rsqrt(square_sum / (chans * grp) + 1e-06)
    normed = (hidden * inverse_rms[:, None] * norm_gain[None, :]).astype(bf16)
    return (hidden_out, normed)


def solution(mesh):
    return jax.shard_map(
        shards,
        mesh=mesh,
        in_specs=(
            P("ctx", "grp"),
            P("ctx", "grp"),
            P("ctx", "grp"),
            P(None, None, "grp"),
            P(None, "grp"),
            P(None, "grp"),
            P(),
            P("ctx", "grp"),
            P("grp"),
        ),
        out_specs=(P("ctx", "grp"), P("ctx", "grp")),
        check_vma=False,
    )
```

```python
import functools
import math

import jax
import jax.numpy as jnp
from jax import lax
from jax.experimental import pallas as pl
from jax.experimental.pallas import tpu as pltpu
from jax.sharding import PartitionSpec as P

SUBS = 8
LANES = 128
MIB = 1024 * 1024
A_TILES, N_TILES, Q_TILES, F_TILES = 2, 2, 4, 4
NEAR_PARTS = 2
f32 = jnp.float32
bf16 = jnp.bfloat16


def from_behind(shard, axis, by):
    count = lax.axis_size(axis)
    pairs = [(i, i + by) for i in range(count) if 0 <= i + by < count]
    return lax.ppermute(shard, axis, pairs)


def swap(shard, axis):
    return lax.ppermute(shard, axis, [(i, i ^ 1) for i in range(lax.axis_size(axis))])


def doc_start_rows(len_ref, base, span):
    rows = lax.broadcasted_iota(jnp.int32, (SUBS, LANES), 0) * span + base
    starts = [jnp.int32(0)]
    for d in range(len_ref.shape[0] - 1):
        starts.append(starts[-1] + len_ref[d])
    out = []
    for j in range(span):
        pos = rows + j
        best = jnp.zeros((SUBS, LANES), jnp.int32)
        for start in starts[1:]:
            best = jnp.where(pos >= start, start, best)
        out.append(best)
    return rows, out


def flag(cond):
    return jnp.where(cond, 1.0, 0.0).astype(f32)


def each_group(count, most, group):
    size = math.gcd(count, most)

    def step(i, carry):
        group([pl.multiple_of((i * size + m) * LANES, LANES) for m in range(size)])
        return carry

    lax.fori_loop(0, count // size, step, 0)


def each_chunk(chans, chunk, before, group, after, most):
    def step(c, carry):
        before(c)

        def inner(lanes):
            group([pl.multiple_of(c * chunk + lane, LANES) for lane in lanes])

        each_group(chunk // LANES, most, inner)
        after(c)
        return carry

    lax.fori_loop(0, chans // chunk, step, 0)


def cols_copy(src, dst, sem, c, chunk):
    cols = pl.ds(pl.multiple_of(c * chunk, chunk), chunk)
    return pltpu.make_async_copy(src.at[:, cols], dst.at[:, cols], sem.at[c])


def cols_of(lane):
    return pl.ds(lane, LANES)


def row_of(ref, index):
    return ref[pl.ds(index, SUBS, stride=0), :]


def spread(x, wide, span):
    x = x.astype(f32)
    for b in range(SUBS):
        wide[pl.ds(b * (span + 1), span), :] = x[b * span : (b + 1) * span]


class Conv:
    def __init__(self, wide, rim, taps, span):
        self.wide, self.span = wide, span
        self.taps = [jnp.broadcast_to(taps[m : m + 1], (SUBS, LANES)) for m in range(3)]
        top = lax.broadcasted_iota(jnp.int32, (SUBS, LANES), 0) == 0
        ahead = [0.0, 0.0] if rim is None else [jnp.broadcast_to(rim[m : m + 1].astype(f32), (SUBS, LANES)) for m in range(2)]
        self.behind = [jnp.where(top, ahead[m], pltpu.roll(self.row(span - 2 + m), 1, 0)) for m in range(2)]

    def row(self, j):
        return self.wide[pl.ds(j, SUBS, stride=self.span + 1), :]

    def step(self, j, keep_one, keep_two):
        here = self.row(j)
        two, one = self.behind
        self.behind = [one, here]
        return self.taps[0] * here + (self.taps[1] * one) * keep_one + (self.taps[2] * two) * keep_two


def half_start(chans, own):
    parity = lax.rem(lax.axis_index("ctx"), 2)
    return pl.multiple_of((parity if own else 1 - parity) * (chans // 2), LANES)


def twice(mask, modes):
    return jnp.concatenate([mask] * (modes // SUBS), axis=0)


def sub_state(state_ref, lane, b, modes):
    return state_ref[lax.div(lane, LANES), pl.ds(b * (modes + 1), modes), :]


def state_kernel(
    masks, key_ref, value_ref, rim_ref, taps_ref, rate_ref, *refs, span, modes, most, own
):
    gate_ref, state_ref, end_ref, wide_k, wide_v, tables, held = refs[-7:]
    half = key_ref.shape[1] // 2
    first = half_start(2 * half, own)
    at = Masks(span)

    def group(lanes):
        for slot, lane in enumerate(lanes):
            spread(key_ref[:, cols_of(lane)], wide_k.at[slot], span)
            spread(value_ref[:, cols_of(lane)], wide_v.at[slot], span)
            rate = rate_ref[:, cols_of(lane)]
            tables[slot] = jnp.exp(-rate)
        convs = [
            [
                Conv(wide.at[slot], rim_ref[i, :, cols_of(lane)], taps_ref[i, :, cols_of(lane)], span)
                for i, wide in ((1, wide_k), (2, wide_v))
            ]
            for slot, lane in enumerate(lanes)
        ]
        last = [None] * len(lanes)
        for j in range(span):
            keep_one, keep_two = masks[at.one + j], masks[at.two + j]
            for slot, lane in enumerate(lanes):
                k_short, v_short = [conv.step(j, keep_one, keep_two) for conv in convs[slot]]
                if j % 2 == 0:
                    last[slot] = k_short * v_short
                    continue
                pair = jnp.concatenate([last[slot], k_short * v_short], axis=0).astype(bf16)
                gate_ref[pl.ds((j - 1) * SUBS, 2 * SUBS), cols_of(lane)] = pair
                pair = pair.astype(f32)
                held[slot, j - 1] = pair[:SUBS] * masks[at.last + j - 1]
                held[slot, j] = pair[SUBS:] * masks[at.last + j]
        for slot, lane in enumerate(lanes):
            decay = [row_of(tables.at[slot], n) for n in range(modes)]
            state = [held[slot, 0]] * modes
            for j in range(1, span):
                gate = held[slot, j]
                state = [decay[n] * state[n] + gate for n in range(modes)]
            for n in range(modes):
                state_ref[lax.div(lane, LANES), pl.ds(n, SUBS, stride=modes + 1), :] = state[n]
        for slot, lane in enumerate(lanes):
            leap = jnp.exp(-float(span) * rate_ref[:, cols_of(lane)])
            end = sub_state(state_ref, lane, 0, modes)
            for b in range(1, SUBS):
                end = (leap * twice(masks[at.passes + b], modes)) * end + sub_state(state_ref, lane, b, modes)
            end_ref[:, cols_of(pl.multiple_of(lane - first, LANES))] = end

    each_group(half // LANES, most, lambda lanes: group([pl.multiple_of(first + lane, LANES) for lane in lanes]))


def tail_kernel(query_ref, key_ref, value_ref, tail_ref, bufs, sems):
    rows, count = query_ref.shape[0], bufs.shape[1]
    copies = [
        pltpu.make_async_copy(ref.at[pl.ds(rows - count, count)], bufs.at[i], sems.at[i])
        for i, ref in enumerate((query_ref, key_ref, value_ref))
    ]
    for copy in copies:
        copy.start()
    for i, copy in enumerate(copies):
        copy.wait()
        tail_ref[i] = bufs[i].astype(f32)[count - 2 :].astype(bf16)


def unbroken(len_ref, first, count):
    start = jnp.int32(0)
    whole = jnp.where((first <= 0) & (first + count > 0), 0.0, 1.0)
    for d in range(len_ref.shape[0] - 1):
        start = start + len_ref[d]
        whole = jnp.where((start >= first) & (start < first + count), 0.0, whole)
    return whole.astype(f32)


class Masks:
    def __init__(self, span):
        self.one, self.two, self.last, self.enter = 0, span, 2 * span, 3 * span
        self.passes = 4 * span
        self.edges = self.passes + SUBS
        self.late = self.edges + 3
        self.early = self.late + 1
        self.reach = self.late + 2

    def count(self, reaches):
        return self.reach + reaches


def write_masks(base_ref, len_ref, masks, span, reaches):
    at = Masks(span)
    rows, starts = doc_start_rows(len_ref, base_ref[0], span)
    for j in range(span):
        masks[at.one + j] = flag(starts[j] < rows + j)
        masks[at.two + j] = flag(starts[j] < rows + (j - 1))
        masks[at.last + j] = flag(starts[span - 1] <= rows + j)
        masks[at.enter + j] = flag(starts[j] < rows)
    top = flag(lax.broadcasted_iota(jnp.int32, (SUBS, LANES), 0) == 0)
    masks[at.edges] = top * masks[at.one]
    masks[at.edges + 1] = top * masks[at.two]
    masks[at.edges + 2] = top * masks[at.two + 1]
    size = SUBS * span
    parity = lax.rem(lax.div(base_ref[0], size), 2)
    pair_at = base_ref[0] - parity * size
    ranges = [(base_ref[0] + b * span, span) for b in range(SUBS)]
    flags = [at.passes + b for b in range(SUBS)]
    ranges += [(pair_at + size, size), (pair_at, size)]
    flags += [at.late, at.early]
    for m in range(reaches):
        ranges.append((pair_at - (2 * size << m), 2 * size << m))
        flags.append(at.reach + m)
    for index, (first, count) in zip(flags, ranges):
        masks[index] = jnp.full((SUBS, LANES), unbroken(len_ref, first, count), f32)


def near_kernel(masks, gate_ref, rate_ref, weight_ref, *refs, span, modes, most, first, count):
    near_ref, sums, tap_rows = refs[-3:]
    at = Masks(span)

    def group(lanes):
        for slot, lane in enumerate(lanes):
            decay = jnp.exp(-rate_ref[:, cols_of(lane)])
            term = weight_ref[:, cols_of(lane)]
            for lag in range(span):
                part = term[:SUBS]
                for n in range(SUBS, modes, SUBS):
                    part = part + term[n : n + SUBS]
                sums[slot, pl.ds(lag * (SUBS + 1), SUBS), :] = part
                term = term * decay
        for slot in range(len(lanes)):
            for first_lag in range(0, span, SUBS):
                total = [
                    sums[slot, pl.ds(first_lag * (SUBS + 1) + m, SUBS, stride=SUBS + 1), :] for m in range(SUBS)
                ]
                while len(total) > 1:
                    total = [total[m] + total[m + 1] for m in range(0, len(total), 2)]
                tap_rows[slot, pl.ds(first_lag, SUBS), :] = total[0]
        taps = [[row_of(tap_rows.at[slot], lag) for lag in range(span)] for slot in range(len(lanes))]
        for parts, lane in zip(taps, lanes):
            live = []
            for j in range(span):
                if j % 2 == 0:
                    pair = gate_ref[pl.ds(j * SUBS, 2 * SUBS), cols_of(lane)].astype(f32)
                keep = masks[at.one + j]
                live = [g * keep for g in live]
                live.append(pair[(j % 2) * SUBS : (j % 2 + 1) * SUBS])
                total = parts[0] * live[j]
                for lag in range(1, j + 1):
                    total = total + parts[lag] * live[j - lag]
                near_ref[pl.ds(j * SUBS, SUBS), cols_of(lane)] = total

    each_group(count // LANES, most, lambda lanes: group([pl.multiple_of(first + lane, LANES) for lane in lanes]))


def query_kernel(base_ref, len_ref, query_ref, taps_ref, short_ref, masks, query_buf, sems, wide_q, *, span, most, chunk, reaches):
    chans = query_buf.shape[1]

    def fetch(c):
        return cols_copy(query_ref, query_buf, sems, c, chunk)

    for c in range(chans // chunk):
        fetch(c).start()
    write_masks(base_ref, len_ref, masks, span, reaches)
    at = Masks(span)

    def group(lanes):
        for slot, lane in enumerate(lanes):
            spread(query_buf[:, cols_of(lane)], wide_q.at[slot], span)
        convs = [Conv(wide_q.at[slot], None, taps_ref[0, :, cols_of(lane)], span) for slot, lane in enumerate(lanes)]
        for j in range(span):
            keep_one, keep_two = masks[at.one + j], masks[at.two + j]
            for slot, lane in enumerate(lanes):
                short_ref[pl.ds(j * SUBS, SUBS), cols_of(lane)] = convs[slot].step(j, keep_one, keep_two)

    each_chunk(chans, chunk, lambda c: fetch(c).wait(), group, lambda c: None, most)


def pair_rates(rate_ref, count):
    parity = lax.rem(lax.axis_index("ctx"), 2)
    return parity, rate_ref[:, pl.ds(pl.multiple_of(parity * count, LANES), count)]


def early_late(parity, own, got):
    odd = jnp.full(own.shape, parity, jnp.int32) == 1
    return jnp.where(odd, got, own), jnp.where(odd, own, got)


def leap(masks, index, rate, rows):
    return jnp.exp(-float(rows) * rate) * masks[index][0:1, 0:1]


def pair_kernel(masks, own_ref, got_ref, rate_ref, end_ref, *, rows, index):
    parity, rate = pair_rates(rate_ref, own_ref.shape[1])
    early, late = early_late(parity, own_ref[...], got_ref[...])
    end_ref[...] = (late + leap(masks, index, rate, rows) * early).astype(bf16)


def reach_kernel(masks, near_ref, far_ref, rate_ref, enter_ref, *, rows, index):
    _, rate = pair_rates(rate_ref, near_ref.shape[1])
    enter_ref[...] = (near_ref[...].astype(f32) + leap(masks, index, rate, rows) * far_ref[...].astype(f32)).astype(bf16)


def enter_kernel(
    masks, near_ref, far_ref, own_ref, got_ref, rate_ref, mine_ref, give_ref, *, rows, index, block, block_index
):
    parity, rate = pair_rates(rate_ref, own_ref.shape[1])
    first = near_ref[...].astype(f32) + leap(masks, index, rate, rows) * far_ref[...].astype(f32)
    early, _ = early_late(parity, own_ref[...], got_ref[...])
    second = early + leap(masks, block_index, rate, block) * first
    give, mine = early_late(parity, second, first)
    mine_ref[...] = mine
    give_ref[...] = give


def final_kernel(
    masks, state_ref, enter_ref, near_ref, short_ref, resid_ref, rim_ref, taps_ref, rate_ref, weight_ref, *refs,
    span, modes, channels, most, chunk, own,
):
    if own:
        hidden_out, whole, sums, hidden_ref, sems, wide, tables, starts_at = refs
    elif channels:
        gain_ref, _, _, _, hidden_out, whole, sums, normed_out, hidden_ref, sems, wide, tables, starts_at, normed_ref = refs
    else:
        _, _, _, hidden_out, whole, sums, hidden_ref, sems, wide, tables, starts_at = refs
    chans = resid_ref.shape[1]
    half = chans // 2
    first = half_start(chans, own)
    at = Masks(span)

    def store(c):
        here = pl.ds(pl.multiple_of(c * chunk, chunk), chunk)
        there = pl.ds(pl.multiple_of(first + c * chunk, chunk), chunk)
        return pltpu.make_async_copy(hidden_ref.at[:, here], hidden_out.at[:, there], sems.at[0, c])

    def store_normed(c):
        return cols_copy(normed_ref, normed_out, sems.at[1], c, chunk)

    if own:
        sums[...] = jnp.zeros(sums.shape, f32)

    def group(lanes):
        for slot, lane in enumerate(lanes):
            state = enter_ref[:, cols_of(pl.multiple_of(lane - first, LANES))]
            rate = rate_ref[:, cols_of(lane)]
            weight = weight_ref[:, cols_of(lane)]
            tables[slot] = jnp.exp(-rate)
            leap = jnp.exp(-float(span) * rate)
            for b in range(SUBS):
                starts_at[slot, pl.ds(b * (modes + 1), modes), :] = weight * state
                if b < SUBS - 1:
                    state = (leap * twice(masks[at.passes + b], modes)) * state + sub_state(state_ref, lane, b, modes)
        for slot, lane in enumerate(lanes):
            part = [starts_at[slot, pl.ds(n, SUBS, stride=modes + 1), :] for n in range(modes)]
            decay = [row_of(tables.at[slot], n) for n in range(modes)]
            rim = rim_ref[0, :, cols_of(lane)].astype(f32)
            tap = taps_ref[0, :, cols_of(lane)]
            edge = [
                (tap[1:2] * rim[1:2]) * masks[at.edges] + (tap[2:3] * rim[0:1]) * masks[at.edges + 1],
                (tap[2:3] * rim[1:2]) * masks[at.edges + 2],
            ]
            for j in range(span):
                part = [part[n] * decay[n] for n in range(modes)]
                total = part
                while len(total) > 1:
                    total = [total[m] + total[m + 1] for m in range(0, len(total), 2)]
                conv = near_ref[pl.ds(j * SUBS, SUBS), cols_of(lane)] + total[0] * masks[at.enter + j]
                conv = conv.astype(bf16).astype(f32)
                short = short_ref[pl.ds(j * SUBS, SUBS), cols_of(lane)]
                if j < 2:
                    short = short + edge[j]
                wide[slot, pl.ds(j, SUBS, stride=span + 1), :] = short * conv
        for b in range(SUBS):
            rows = pl.ds(b * span, span)
            squares = sums[rows, :]
            for slot, lane in enumerate(lanes):
                hidden = wide[slot, pl.ds(b * (span + 1), span), :] + resid_ref[rows, cols_of(lane)].astype(f32)
                whole[lax.div(lane, LANES), rows, :] = hidden
                hidden_ref[rows, cols_of(pl.multiple_of(lane - first, LANES))] = hidden.astype(bf16)
                squares = squares + hidden * hidden
            sums[rows, :] = squares

    each_chunk(
        half,
        chunk,
        lambda c: None,
        lambda lanes: group([pl.multiple_of(first + lane, LANES) for lane in lanes]),
        lambda c: store(c).start(),
        most,
    )
    if channels and not own:
        inverse = lax.rsqrt(jnp.sum(sums[...], axis=1, keepdims=True) / channels + 1e-06)
        sums[...] = jnp.broadcast_to(inverse, sums.shape)

        def scale(lanes):
            for lane in lanes:
                normed = whole[lax.div(lane, LANES)] * sums[...] * gain_ref[:, cols_of(lane)]
                normed_ref[:, cols_of(lane)] = normed.astype(bf16)

        each_chunk(chans, chunk, lambda c: None, scale, lambda c: store_normed(c).start(), 4)
        for c in range(chans // chunk):
            store_normed(c).wait()
    for c in range(half // chunk):
        store(c).wait()


def shards(
    query_in, key_in, value_in, short_taps, decay_rate, residues, doc_lengths, residual, norm_gain
):
    tok_rows, chans = query_in.shape
    modes = decay_rate.shape[0]
    span = tok_rows // SUBS
    blocks = lax.axis_size("ctx")
    grp = lax.axis_size("grp")
    chunk = min(chans // 2, 1024)
    pieces = chans // chunk
    ctx_index = lax.axis_index("ctx")
    base = (ctx_index * tok_rows).astype(jnp.int32).reshape(1)
    weight = residues * jnp.sqrt(-jnp.expm1(-2.0 * decay_rate))

    smem = pl.BlockSpec(memory_space=pltpu.SMEM)
    vmem = pl.BlockSpec(memory_space=pltpu.VMEM)
    hbm = pl.BlockSpec(memory_space=pltpu.HBM)
    tile_shape = (SUBS, LANES)
    wide_rows = SUBS * (span + 1)
    params = pltpu.CompilerParams(vmem_limit_bytes=16 * MIB)

    lengths = pltpu.with_memory_space_constraint(doc_lengths, pltpu.HBM)

    def near_by(x):
        return pltpu.with_memory_space_constraint(x, pltpu.VMEM)

    def far_off(x):
        return pltpu.with_memory_space_constraint(x, pltpu.HBM)

    def copies(kinds):
        return pltpu.SemaphoreType.DMA((kinds, pieces))

    def cost(per_tile, moved):
        return pl.CostEstimate(flops=per_tile * (chans // LANES) * SUBS * LANES, bytes_accessed=moved, transcendentals=0)

    tails = pl.pallas_call(
        tail_kernel,
        in_specs=[hbm, hbm, hbm],
        out_specs=vmem,
        out_shape=pltpu.VMEM((3, 2, chans), bf16),
        scratch_shapes=[pltpu.VMEM((3, 16, chans), bf16), pltpu.SemaphoreType.DMA((3,))],
        compiler_params=params,
        name="tails",
    )(far_off(query_in), far_off(key_in), far_off(value_in))
    rim_rows = from_behind(tails, "ctx", 1)
    reaches = max(1, (blocks // 8).bit_length() - 1)
    mask_shape = (Masks(span).count(reaches),) + tile_shape
    q_short, masks = pl.pallas_call(
        functools.partial(query_kernel, span=span, most=Q_TILES, chunk=chunk, reaches=reaches),
        in_specs=[smem, smem, hbm, vmem],
        out_specs=[vmem, vmem],
        out_shape=[pltpu.VMEM((tok_rows, chans), f32), pltpu.VMEM(mask_shape, f32)],
        scratch_shapes=[
            pltpu.VMEM((tok_rows, chans), bf16),
            pltpu.SemaphoreType.DMA((pieces,)),
            pltpu.VMEM((Q_TILES, wide_rows, LANES), f32),
        ],
        compiler_params=params,
        cost_estimate=cost(200, 6 * tok_rows * chans),
        name="query_part",
    )(base, lengths, far_off(query_in), near_by(short_taps))
    rim_rows, q_short = lax.optimization_barrier((rim_rows, q_short))
    rates, weights, taps, rims = near_by(decay_rate), near_by(weight), near_by(short_taps), near_by(rim_rows)
    kept = pltpu.VMEM((modes, chans // 2), f32)
    sent = pltpu.VMEM((modes, chans // 2), bf16)
    keys, values = near_by(key_in), near_by(value_in)

    def states_of(own, before):
        return pl.pallas_call(
            functools.partial(state_kernel, span=span, modes=modes, most=A_TILES, own=own),
            in_specs=[vmem] * (6 + len(before)),
            out_specs=[vmem] * 3,
            out_shape=[
                pltpu.VMEM((tok_rows, chans), bf16),
                pltpu.VMEM((chans // LANES, SUBS * (modes + 1), LANES), f32),
                kept,
            ],
            scratch_shapes=[
                pltpu.VMEM((A_TILES, wide_rows, LANES), f32),
                pltpu.VMEM((A_TILES, wide_rows, LANES), f32),
                pltpu.VMEM((A_TILES, modes, LANES), f32),
                pltpu.VMEM((A_TILES, span) + tile_shape, f32),
            ],
            input_output_aliases={6 + i: i for i in range(len(before))},
            compiler_params=params,
            cost_estimate=cost(500, 6 * tok_rows * chans),
            name="block_states_own" if own else "block_states_give",
        )(near_by(masks), keys, values, rims, taps, rates, *[near_by(x) for x in before])

    gates, states, give = states_of(False, [])
    got = swap(give, "ctx")
    gates, states, own = states_of(True, [gates, states])
    got, gates, states, own = lax.optimization_barrier((got, gates, states, own))

    def near_piece(part, near):
        count = chans // NEAR_PARTS
        before = [] if near is None else [near_by(near)]
        return pl.pallas_call(
            functools.partial(
                near_kernel, span=span, modes=modes, most=N_TILES, first=part * count, count=count
            ),
            in_specs=[vmem] * (4 + len(before)),
            out_specs=vmem,
            out_shape=pltpu.VMEM((tok_rows, chans), f32),
            scratch_shapes=[
                pltpu.VMEM((N_TILES, span * (SUBS + 1), LANES), f32),
                pltpu.VMEM((N_TILES, span, LANES), f32),
            ],
            compiler_params=params,
            input_output_aliases={4: 0} if before else {},
            cost_estimate=cost(600 // NEAR_PARTS, 7 * tok_rows * count),
            name="near_part_%d" % part,
        )(near_by(masks), near_by(gates), rates, weights, *before)

    got = swap(give, "ctx")

    at = Masks(span)

    def pair_call(kernel, operands, out_shape, name, **static):
        return pl.pallas_call(
            functools.partial(kernel, **static),
            in_specs=[vmem] * (len(operands) + 2),
            out_specs=[vmem] * len(out_shape),
            out_shape=out_shape,
            compiler_params=params,
            name=name,
        )(near_by(masks), *[near_by(x) for x in operands], rates)

    ends = pair_call(pair_kernel, [own, got], [sent], "pair_ends", rows=tok_rows, index=at.late)[0]
    one_on, two_on = from_behind(ends, "ctx", 2), from_behind(ends, "ctx", 4)
    near = near_piece(0, None)
    one_on, two_on, near = lax.optimization_barrier((one_on, two_on, near))
    enter, on = one_on, two_on
    for m in range(reaches - 1):
        enter = pair_call(
            reach_kernel, [enter, on], [sent], "reach_%d" % m, rows=2 * tok_rows << m, index=at.reach + m
        )[0]
        on = from_behind(enter, "ctx", 4 << m)
    near = near_piece(1, near)
    on, near = lax.optimization_barrier((on, near))
    mine, give_back = pair_call(
        enter_kernel,
        [enter, on, own, got],
        [kept, kept],
        "pair_enter",
        rows=2 * tok_rows << (reaches - 1),
        index=at.reach + reaches - 1,
        block=tok_rows,
        block_index=at.early,
    )
    got_back = swap(give_back, "ctx")

    alone = grp == 1
    resid = near_by(residual)

    def finish(own, enter, before):
        last = alone and not own
        out_specs = [hbm, vmem, vmem]
        out_shape = [
            jax.ShapeDtypeStruct((tok_rows, chans), bf16),
            pltpu.VMEM((chans // LANES, tok_rows, LANES), f32),
            pltpu.VMEM((tok_rows, LANES), f32),
        ]
        scratch = [
            pltpu.VMEM((tok_rows, chans // 2), bf16),
            copies(2),
            pltpu.VMEM((F_TILES, wide_rows, LANES), f32),
            pltpu.VMEM((F_TILES, modes, LANES), f32),
            pltpu.VMEM((F_TILES, SUBS * (modes + 1), LANES), f32),
        ]
        operands = [near_by(x) for x in (masks, states, enter, near, q_short)] + [resid, rims, taps, rates, weights]
        if last:
            operands.append(near_by(norm_gain.reshape(1, chans)))
            out_specs.append(hbm)
            out_shape.append(jax.ShapeDtypeStruct((tok_rows, chans), bf16))
            scratch.append(pltpu.VMEM((tok_rows, chans), bf16))
        count = len(operands)
        in_specs = [vmem] * count
        if before:
            operands += [far_off(before[0]), near_by(before[1]), near_by(before[2])]
            in_specs += [hbm, vmem, vmem]
        return pl.pallas_call(
            functools.partial(
                final_kernel, span=span, modes=modes, channels=chans if alone else 0, most=F_TILES, chunk=chunk, own=own
            ),
            in_specs=in_specs,
            out_specs=out_specs,
            out_shape=out_shape,
            scratch_shapes=scratch,
            input_output_aliases={count + i: i for i in range(len(before))},
            compiler_params=params,
            cost_estimate=cost(450, 9 * tok_rows * chans),
            name="far_part_own" if own else "far_part_other",
        )(*operands)

    before = finish(True, mine, [])
    got_back, *before = lax.optimization_barrier((got_back, *before))
    outs = finish(False, got_back, before)
    if alone:
        return (outs[0], outs[3])
    hidden_out, whole, sums = outs
    hidden = whole.transpose(1, 0, 2).reshape(tok_rows, chans)
    square_sum = lax.psum(jnp.sum(sums, axis=1), "grp")
    inverse_rms = lax.rsqrt(square_sum / (chans * grp) + 1e-06)
    normed = (hidden * inverse_rms[:, None] * norm_gain[None, :]).astype(bf16)
    return (hidden_out, normed)


def solution(mesh):
    return jax.shard_map(
        shards,
        mesh=mesh,
        in_specs=(
            P("ctx", "grp"),
            P("ctx", "grp"),
            P("ctx", "grp"),
            P(None, None, "grp"),
            P(None, "grp"),
            P(None, "grp"),
            P(),
            P("ctx", "grp"),
            P("grp"),
        ),
        out_specs=(P("ctx", "grp"), P("ctx", "grp")),
        check_vma=False,
    )
```

```python
import functools
import math

import jax
import jax.numpy as jnp
from jax import lax
from jax.experimental import pallas as pl
from jax.experimental.pallas import tpu as pltpu
from jax.sharding import PartitionSpec as P

SUBS = 8
LANES = 128
MIB = 1024 * 1024
A_TILES, N_TILES, Q_TILES, F_TILES = 2, 2, 4, 4
NEAR_PARTS = 2
f32 = jnp.float32
bf16 = jnp.bfloat16


def from_behind(shard, axis, by):
    count = lax.axis_size(axis)
    pairs = [(i, i + by) for i in range(count) if 0 <= i + by < count]
    return lax.ppermute(shard, axis, pairs)


def swap(shard, axis):
    return lax.ppermute(shard, axis, [(i, i ^ 1) for i in range(lax.axis_size(axis))])


def doc_start_rows(len_ref, base, span):
    rows = lax.broadcasted_iota(jnp.int32, (SUBS, LANES), 0) * span + base
    starts = [jnp.int32(0)]
    for d in range(len_ref.shape[0] - 1):
        starts.append(starts[-1] + len_ref[d])
    out = []
    for j in range(span):
        pos = rows + j
        best = jnp.zeros((SUBS, LANES), jnp.int32)
        for start in starts[1:]:
            best = jnp.where(pos >= start, start, best)
        out.append(best)
    return rows, out


def flag(cond):
    return jnp.where(cond, 1.0, 0.0).astype(f32)


def each_group(count, most, group):
    size = math.gcd(count, most)

    def step(i, carry):
        group([pl.multiple_of((i * size + m) * LANES, LANES) for m in range(size)])
        return carry

    lax.fori_loop(0, count // size, step, 0)


def each_chunk(chans, chunk, before, group, after, most):
    def step(c, carry):
        before(c)

        def inner(lanes):
            group([pl.multiple_of(c * chunk + lane, LANES) for lane in lanes])

        each_group(chunk // LANES, most, inner)
        after(c)
        return carry

    lax.fori_loop(0, chans // chunk, step, 0)


def cols_copy(src, dst, sem, c, chunk):
    cols = pl.ds(pl.multiple_of(c * chunk, chunk), chunk)
    return pltpu.make_async_copy(src.at[:, cols], dst.at[:, cols], sem.at[c])


def cols_of(lane):
    return pl.ds(lane, LANES)


def row_of(ref, index):
    return ref[pl.ds(index, SUBS, stride=0), :]


def spread(x, wide, span):
    x = x.astype(f32)
    for b in range(SUBS):
        wide[pl.ds(b * (span + 1), span), :] = x[b * span : (b + 1) * span]


class Conv:
    def __init__(self, wide, rim, taps, span):
        self.wide, self.span = wide, span
        self.taps = [jnp.broadcast_to(taps[m : m + 1], (SUBS, LANES)) for m in range(3)]
        top = lax.broadcasted_iota(jnp.int32, (SUBS, LANES), 0) == 0
        ahead = [0.0, 0.0] if rim is None else [jnp.broadcast_to(rim[m : m + 1].astype(f32), (SUBS, LANES)) for m in range(2)]
        self.behind = [jnp.where(top, ahead[m], pltpu.roll(self.row(span - 2 + m), 1, 0)) for m in range(2)]

    def row(self, j):
        return self.wide[pl.ds(j, SUBS, stride=self.span + 1), :]

    def step(self, j, keep_one, keep_two):
        here = self.row(j)
        two, one = self.behind
        self.behind = [one, here]
        return self.taps[0] * here + (self.taps[1] * one) * keep_one + (self.taps[2] * two) * keep_two


def half_start(chans, own):
    parity = lax.rem(lax.axis_index("ctx"), 2)
    return pl.multiple_of((parity if own else 1 - parity) * (chans // 2), LANES)


def twice(mask, modes):
    return jnp.concatenate([mask] * (modes // SUBS), axis=0)


def sub_state(state_ref, lane, b, modes):
    return state_ref[lax.div(lane, LANES), pl.ds(b * (modes + 1), modes), :]


def state_kernel(
    masks, key_ref, value_ref, rim_ref, taps_ref, rate_ref, *refs, span, modes, most, own
):
    gate_ref, state_ref, end_ref, wide_k, wide_v, tables, held = refs[-7:]
    half = key_ref.shape[1] // 2
    first = half_start(2 * half, own)
    at = Masks(span)

    def group(lanes):
        for slot, lane in enumerate(lanes):
            spread(key_ref[:, cols_of(lane)], wide_k.at[slot], span)
            spread(value_ref[:, cols_of(lane)], wide_v.at[slot], span)
            rate = rate_ref[:, cols_of(lane)]
            tables[slot] = jnp.exp(-rate)
        convs = [
            [
                Conv(wide.at[slot], rim_ref[i, :, cols_of(lane)], taps_ref[i, :, cols_of(lane)], span)
                for i, wide in ((1, wide_k), (2, wide_v))
            ]
            for slot, lane in enumerate(lanes)
        ]
        last = [None] * len(lanes)
        for j in range(span):
            keep_one, keep_two = masks[at.one + j], masks[at.two + j]
            for slot, lane in enumerate(lanes):
                k_short, v_short = [conv.step(j, keep_one, keep_two) for conv in convs[slot]]
                if j % 2 == 0:
                    last[slot] = k_short * v_short
                    continue
                pair = jnp.concatenate([last[slot], k_short * v_short], axis=0).astype(bf16)
                gate_ref[pl.ds((j - 1) * SUBS, 2 * SUBS), cols_of(lane)] = pair
                pair = pair.astype(f32)
                held[slot, j - 1] = pair[:SUBS] * masks[at.last + j - 1]
                held[slot, j] = pair[SUBS:] * masks[at.last + j]
        for slot, lane in enumerate(lanes):
            decay = [row_of(tables.at[slot], n) for n in range(modes)]
            state = [held[slot, 0]] * modes
            for j in range(1, span):
                gate = held[slot, j]
                state = [decay[n] * state[n] + gate for n in range(modes)]
            for n in range(modes):
                state_ref[lax.div(lane, LANES), pl.ds(n, SUBS, stride=modes + 1), :] = state[n]
        for slot, lane in enumerate(lanes):
            leap = jnp.exp(-float(span) * rate_ref[:, cols_of(lane)])
            end = sub_state(state_ref, lane, 0, modes)
            for b in range(1, SUBS):
                end = (leap * twice(masks[at.passes + b], modes)) * end + sub_state(state_ref, lane, b, modes)
            end_ref[:, cols_of(pl.multiple_of(lane - first, LANES))] = end

    each_group(half // LANES, most, lambda lanes: group([pl.multiple_of(first + lane, LANES) for lane in lanes]))


def tail_kernel(query_ref, key_ref, value_ref, tail_ref, bufs, sems):
    rows, count = query_ref.shape[0], bufs.shape[1]
    copies = [
        pltpu.make_async_copy(ref.at[pl.ds(rows - count, count)], bufs.at[i], sems.at[i])
        for i, ref in enumerate((query_ref, key_ref, value_ref))
    ]
    for copy in copies:
        copy.start()
    for i, copy in enumerate(copies):
        copy.wait()
        tail_ref[i] = bufs[i].astype(f32)[count - 2 :].astype(bf16)


def unbroken(len_ref, first, count):
    start = jnp.int32(0)
    whole = jnp.where((first <= 0) & (first + count > 0), 0.0, 1.0)
    for d in range(len_ref.shape[0] - 1):
        start = start + len_ref[d]
        whole = jnp.where((start >= first) & (start < first + count), 0.0, whole)
    return whole.astype(f32)


class Masks:
    def __init__(self, span):
        self.one, self.two, self.last, self.enter = 0, span, 2 * span, 3 * span
        self.passes = 4 * span
        self.edges = self.passes + SUBS
        self.late = self.edges + 3
        self.early = self.late + 1
        self.reach = self.late + 2

    def count(self, reaches):
        return self.reach + reaches


def write_masks(base_ref, len_ref, masks, span, reaches):
    at = Masks(span)
    rows, starts = doc_start_rows(len_ref, base_ref[0], span)
    for j in range(span):
        masks[at.one + j] = flag(starts[j] < rows + j)
        masks[at.two + j] = flag(starts[j] < rows + (j - 1))
        masks[at.last + j] = flag(starts[span - 1] <= rows + j)
        masks[at.enter + j] = flag(starts[j] < rows)
    top = flag(lax.broadcasted_iota(jnp.int32, (SUBS, LANES), 0) == 0)
    masks[at.edges] = top * masks[at.one]
    masks[at.edges + 1] = top * masks[at.two]
    masks[at.edges + 2] = top * masks[at.two + 1]
    size = SUBS * span
    parity = lax.rem(lax.div(base_ref[0], size), 2)
    pair_at = base_ref[0] - parity * size
    ranges = [(base_ref[0] + b * span, span) for b in range(SUBS)]
    flags = [at.passes + b for b in range(SUBS)]
    ranges += [(pair_at + size, size), (pair_at, size)]
    flags += [at.late, at.early]
    for m in range(reaches):
        ranges.append((pair_at - (2 * size << m), 2 * size << m))
        flags.append(at.reach + m)
    for index, (first, count) in zip(flags, ranges):
        masks[index] = jnp.full((SUBS, LANES), unbroken(len_ref, first, count), f32)


def near_kernel(masks, gate_ref, rate_ref, weight_ref, *refs, span, modes, most, first, count):
    near_ref, sums, tap_rows = refs[-3:]
    at = Masks(span)

    def group(lanes):
        for slot, lane in enumerate(lanes):
            decay = jnp.exp(-rate_ref[:, cols_of(lane)])
            term = weight_ref[:, cols_of(lane)]
            for lag in range(span):
                part = term[:SUBS]
                for n in range(SUBS, modes, SUBS):
                    part = part + term[n : n + SUBS]
                sums[slot, pl.ds(lag * (SUBS + 1), SUBS), :] = part
                term = term * decay
        for slot in range(len(lanes)):
            for first_lag in range(0, span, SUBS):
                total = [
                    sums[slot, pl.ds(first_lag * (SUBS + 1) + m, SUBS, stride=SUBS + 1), :] for m in range(SUBS)
                ]
                while len(total) > 1:
                    total = [total[m] + total[m + 1] for m in range(0, len(total), 2)]
                tap_rows[slot, pl.ds(first_lag, SUBS), :] = total[0]
        taps = [[row_of(tap_rows.at[slot], lag) for lag in range(span)] for slot in range(len(lanes))]
        for parts, lane in zip(taps, lanes):
            live = []
            for j in range(span):
                if j % 2 == 0:
                    pair = gate_ref[pl.ds(j * SUBS, 2 * SUBS), cols_of(lane)].astype(f32)
                keep = masks[at.one + j]
                live = [g * keep for g in live]
                live.append(pair[(j % 2) * SUBS : (j % 2 + 1) * SUBS])
                total = parts[0] * live[j]
                for lag in range(1, j + 1):
                    total = total + parts[lag] * live[j - lag]
                near_ref[pl.ds(j * SUBS, SUBS), cols_of(lane)] = total

    each_group(count // LANES, most, lambda lanes: group([pl.multiple_of(first + lane, LANES) for lane in lanes]))


def query_kernel(*refs, span, most, chunk, reaches, first, count):
    if reaches:
        base_ref, len_ref, query_ref, taps_ref, value_in, short_ref, masks, value_ref, query_buf, sems, wide_q, value_sem = refs
        value_copy = pltpu.make_async_copy(value_in, value_ref, value_sem)
    else:
        masks, query_ref, taps_ref, _, short_ref, query_buf, sems, wide_q = refs

    def fetch(c):
        there = pl.ds(first + c * chunk if isinstance(c, int) else pl.multiple_of(first + c * chunk, chunk), chunk)
        here = pl.ds(c * chunk if isinstance(c, int) else pl.multiple_of(c * chunk, chunk), chunk)
        return pltpu.make_async_copy(query_ref.at[:, there], query_buf.at[:, here], sems.at[c])

    for c in range(count // chunk):
        fetch(c).start()
    if reaches:
        value_copy.start()
        write_masks(base_ref, len_ref, masks, span, reaches)
    at = Masks(span)

    def group(lanes):
        for slot, lane in enumerate(lanes):
            spread(query_buf[:, cols_of(lane)], wide_q.at[slot], span)
        convs = [
            Conv(wide_q.at[slot], None, taps_ref[0, :, cols_of(pl.multiple_of(first + lane, LANES))], span)
            for slot, lane in enumerate(lanes)
        ]
        for j in range(span):
            keep_one, keep_two = masks[at.one + j], masks[at.two + j]
            for slot, lane in enumerate(lanes):
                short_ref[pl.ds(j * SUBS, SUBS), cols_of(pl.multiple_of(first + lane, LANES))] = convs[slot].step(j, keep_one, keep_two)

    each_chunk(count, chunk, lambda c: fetch(c).wait(), group, lambda c: None, most)
    if reaches:
        value_copy.wait()


def pair_rates(rate_ref, count):
    parity = lax.rem(lax.axis_index("ctx"), 2)
    return parity, rate_ref[:, pl.ds(pl.multiple_of(parity * count, LANES), count)]


def early_late(parity, own, got):
    odd = jnp.full(own.shape, parity, jnp.int32) == 1
    return jnp.where(odd, got, own), jnp.where(odd, own, got)


def leap(masks, index, rate, rows):
    return jnp.exp(-float(rows) * rate) * masks[index][0:1, 0:1]


def pair_kernel(masks, own_ref, got_ref, rate_ref, end_ref, *, rows, index):
    parity, rate = pair_rates(rate_ref, own_ref.shape[1])
    early, late = early_late(parity, own_ref[...], got_ref[...])
    end_ref[...] = (late + leap(masks, index, rate, rows) * early).astype(bf16)


def reach_kernel(masks, near_ref, far_ref, rate_ref, enter_ref, *, rows, index):
    _, rate = pair_rates(rate_ref, near_ref.shape[1])
    enter_ref[...] = (near_ref[...].astype(f32) + leap(masks, index, rate, rows) * far_ref[...].astype(f32)).astype(bf16)


def enter_kernel(
    masks, near_ref, far_ref, own_ref, got_ref, rate_ref, mine_ref, give_ref, *, rows, index, block, block_index
):
    parity, rate = pair_rates(rate_ref, own_ref.shape[1])
    first = near_ref[...].astype(f32) + leap(masks, index, rate, rows) * far_ref[...].astype(f32)
    early, _ = early_late(parity, own_ref[...], got_ref[...])
    second = early + leap(masks, block_index, rate, block) * first
    give, mine = early_late(parity, second, first)
    mine_ref[...] = mine
    give_ref[...] = give


def final_kernel(
    masks, state_ref, enter_ref, near_ref, short_ref, resid_ref, rim_ref, taps_ref, rate_ref, weight_ref, *refs,
    span, modes, channels, most, chunk, own,
):
    if own:
        hidden_out, whole, sums, hidden_ref, sems, wide, tables, starts_at = refs
    elif channels:
        gain_ref, _, _, _, hidden_out, whole, sums, normed_out, hidden_ref, sems, wide, tables, starts_at, normed_ref = refs
    else:
        _, _, _, hidden_out, whole, sums, hidden_ref, sems, wide, tables, starts_at = refs
    chans = resid_ref.shape[1]
    half = chans // 2
    first = half_start(chans, own)
    at = Masks(span)

    def store(c):
        here = pl.ds(pl.multiple_of(c * chunk, chunk), chunk)
        there = pl.ds(pl.multiple_of(first + c * chunk, chunk), chunk)
        return pltpu.make_async_copy(hidden_ref.at[:, here], hidden_out.at[:, there], sems.at[0, c])

    def store_normed(c):
        return cols_copy(normed_ref, normed_out, sems.at[1], c, chunk)

    if own:
        sums[...] = jnp.zeros(sums.shape, f32)

    def group(lanes):
        for slot, lane in enumerate(lanes):
            state = enter_ref[:, cols_of(pl.multiple_of(lane - first, LANES))]
            rate = rate_ref[:, cols_of(lane)]
            weight = weight_ref[:, cols_of(lane)]
            tables[slot] = jnp.exp(-rate)
            leap = jnp.exp(-float(span) * rate)
            for b in range(SUBS):
                starts_at[slot, pl.ds(b * (modes + 1), modes), :] = weight * state
                if b < SUBS - 1:
                    state = (leap * twice(masks[at.passes + b], modes)) * state + sub_state(state_ref, lane, b, modes)
        for slot, lane in enumerate(lanes):
            part = [starts_at[slot, pl.ds(n, SUBS, stride=modes + 1), :] for n in range(modes)]
            decay = [row_of(tables.at[slot], n) for n in range(modes)]
            rim = rim_ref[0, :, cols_of(lane)].astype(f32)
            tap = taps_ref[0, :, cols_of(lane)]
            edge = [
                (tap[1:2] * rim[1:2]) * masks[at.edges] + (tap[2:3] * rim[0:1]) * masks[at.edges + 1],
                (tap[2:3] * rim[1:2]) * masks[at.edges + 2],
            ]
            for j in range(span):
                part = [part[n] * decay[n] for n in range(modes)]
                total = part
                while len(total) > 1:
                    total = [total[m] + total[m + 1] for m in range(0, len(total), 2)]
                conv = near_ref[pl.ds(j * SUBS, SUBS), cols_of(lane)] + total[0] * masks[at.enter + j]
                conv = conv.astype(bf16).astype(f32)
                short = short_ref[pl.ds(j * SUBS, SUBS), cols_of(lane)]
                if j < 2:
                    short = short + edge[j]
                wide[slot, pl.ds(j, SUBS, stride=span + 1), :] = short * conv
        for b in range(SUBS):
            rows = pl.ds(b * span, span)
            squares = sums[rows, :]
            for slot, lane in enumerate(lanes):
                hidden = wide[slot, pl.ds(b * (span + 1), span), :] + resid_ref[rows, cols_of(lane)].astype(f32)
                whole[lax.div(lane, LANES), rows, :] = hidden
                hidden_ref[rows, cols_of(pl.multiple_of(lane - first, LANES))] = hidden.astype(bf16)
                squares = squares + hidden * hidden
            sums[rows, :] = squares

    each_chunk(
        half,
        chunk,
        lambda c: None,
        lambda lanes: group([pl.multiple_of(first + lane, LANES) for lane in lanes]),
        lambda c: store(c).start(),
        most,
    )
    if channels and not own:
        inverse = lax.rsqrt(jnp.sum(sums[...], axis=1, keepdims=True) / channels + 1e-06)
        sums[...] = jnp.broadcast_to(inverse, sums.shape)

        def scale(lanes):
            for lane in lanes:
                normed = whole[lax.div(lane, LANES)] * sums[...] * gain_ref[:, cols_of(lane)]
                normed_ref[:, cols_of(lane)] = normed.astype(bf16)

        each_chunk(chans, chunk, lambda c: None, scale, lambda c: store_normed(c).start(), 4)
        for c in range(chans // chunk):
            store_normed(c).wait()
    for c in range(half // chunk):
        store(c).wait()


def shards(
    query_in, key_in, value_in, short_taps, decay_rate, residues, doc_lengths, residual, norm_gain
):
    tok_rows, chans = query_in.shape
    modes = decay_rate.shape[0]
    span = tok_rows // SUBS
    blocks = lax.axis_size("ctx")
    grp = lax.axis_size("grp")
    chunk = min(chans // 2, 1024)
    pieces = chans // chunk
    ctx_index = lax.axis_index("ctx")
    base = (ctx_index * tok_rows).astype(jnp.int32).reshape(1)
    weight = residues * jnp.sqrt(-jnp.expm1(-2.0 * decay_rate))

    smem = pl.BlockSpec(memory_space=pltpu.SMEM)
    vmem = pl.BlockSpec(memory_space=pltpu.VMEM)
    hbm = pl.BlockSpec(memory_space=pltpu.HBM)
    tile_shape = (SUBS, LANES)
    wide_rows = SUBS * (span + 1)
    params = pltpu.CompilerParams(vmem_limit_bytes=16 * MIB)

    lengths = pltpu.with_memory_space_constraint(doc_lengths, pltpu.HBM)

    def near_by(x):
        return pltpu.with_memory_space_constraint(x, pltpu.VMEM)

    def far_off(x):
        return pltpu.with_memory_space_constraint(x, pltpu.HBM)

    def copies(kinds):
        return pltpu.SemaphoreType.DMA((kinds, pieces))

    def cost(per_tile, moved):
        return pl.CostEstimate(flops=per_tile * (chans // LANES) * SUBS * LANES, bytes_accessed=moved, transcendentals=0)

    tails = pl.pallas_call(
        tail_kernel,
        in_specs=[hbm, hbm, hbm],
        out_specs=vmem,
        out_shape=pltpu.VMEM((3, 2, chans), bf16),
        scratch_shapes=[pltpu.VMEM((3, 16, chans), bf16), pltpu.SemaphoreType.DMA((3,))],
        compiler_params=params,
        name="tails",
    )(far_off(query_in), far_off(key_in), far_off(value_in))
    rim_rows = from_behind(tails, "ctx", 1)
    reaches = max(1, (blocks // 8).bit_length() - 1)
    mask_shape = (Masks(span).count(reaches),) + tile_shape

    def query_piece(part, masks, before):
        count = chans // 2
        scratch = [
            pltpu.VMEM((tok_rows, count), bf16),
            pltpu.SemaphoreType.DMA((count // chunk,)),
            pltpu.VMEM((Q_TILES, wide_rows, LANES), f32),
        ]
        out_shape = [pltpu.VMEM((tok_rows, chans), f32)]
        if part == 0:
            operands = [base, lengths, far_off(query_in), near_by(short_taps), far_off(value_in)]
            in_specs = [smem, smem, hbm, vmem, hbm]
            out_shape += [pltpu.VMEM(mask_shape, f32), pltpu.VMEM((tok_rows, chans), bf16)]
            scratch.append(pltpu.SemaphoreType.DMA(()))
        else:
            operands = [near_by(masks), far_off(query_in), near_by(short_taps), near_by(before)]
            in_specs = [vmem, hbm, vmem, vmem]
        return pl.pallas_call(
            functools.partial(
                query_kernel, span=span, most=Q_TILES, chunk=chunk, reaches=0 if part else reaches,
                first=part * count, count=count,
            ),
            in_specs=in_specs,
            out_specs=[vmem] * len(out_shape),
            out_shape=out_shape,
            scratch_shapes=scratch,
            input_output_aliases={3: 0} if part else {},
            compiler_params=params,
            cost_estimate=cost(100, 3 * tok_rows * chans),
            name="query_part_%d" % part,
        )(*operands)

    q_short, masks, values = query_piece(0, None, None)
    rim_rows, q_short, values = lax.optimization_barrier((rim_rows, q_short, values))
    rates, weights, taps, rims = near_by(decay_rate), near_by(weight), near_by(short_taps), near_by(rim_rows)
    kept = pltpu.VMEM((modes, chans // 2), f32)
    sent = pltpu.VMEM((modes, chans // 2), bf16)
    keys, values = near_by(key_in), near_by(values)

    def states_of(own, before):
        return pl.pallas_call(
            functools.partial(state_kernel, span=span, modes=modes, most=A_TILES, own=own),
            in_specs=[vmem] * (6 + len(before)),
            out_specs=[vmem] * 3,
            out_shape=[
                pltpu.VMEM((tok_rows, chans), bf16),
                pltpu.VMEM((chans // LANES, SUBS * (modes + 1), LANES), f32),
                kept,
            ],
            scratch_shapes=[
                pltpu.VMEM((A_TILES, wide_rows, LANES), f32),
                pltpu.VMEM((A_TILES, wide_rows, LANES), f32),
                pltpu.VMEM((A_TILES, modes, LANES), f32),
                pltpu.VMEM((A_TILES, span) + tile_shape, f32),
            ],
            input_output_aliases={6 + i: i for i in range(len(before))},
            compiler_params=params,
            cost_estimate=cost(500, 6 * tok_rows * chans),
            name="block_states_own" if own else "block_states_give",
        )(near_by(masks), keys, values, rims, taps, rates, *[near_by(x) for x in before])

    gates, states, give = states_of(False, [])
    got = swap(give, "ctx")
    gates, states, own = states_of(True, [gates, states])
    got, gates, states, own = lax.optimization_barrier((got, gates, states, own))

    def near_piece(part, near):
        count = chans // NEAR_PARTS
        before = [] if near is None else [near_by(near)]
        return pl.pallas_call(
            functools.partial(
                near_kernel, span=span, modes=modes, most=N_TILES, first=part * count, count=count
            ),
            in_specs=[vmem] * (4 + len(before)),
            out_specs=vmem,
            out_shape=pltpu.VMEM((tok_rows, chans), f32),
            scratch_shapes=[
                pltpu.VMEM((N_TILES, span * (SUBS + 1), LANES), f32),
                pltpu.VMEM((N_TILES, span, LANES), f32),
            ],
            compiler_params=params,
            input_output_aliases={4: 0} if before else {},
            cost_estimate=cost(600 // NEAR_PARTS, 7 * tok_rows * count),
            name="near_part_%d" % part,
        )(near_by(masks), near_by(gates), rates, weights, *before)

    got = swap(give, "ctx")

    at = Masks(span)

    def pair_call(kernel, operands, out_shape, name, **static):
        return pl.pallas_call(
            functools.partial(kernel, **static),
            in_specs=[vmem] * (len(operands) + 2),
            out_specs=[vmem] * len(out_shape),
            out_shape=out_shape,
            compiler_params=params,
            name=name,
        )(near_by(masks), *[near_by(x) for x in operands], rates)

    ends = pair_call(pair_kernel, [own, got], [sent], "pair_ends", rows=tok_rows, index=at.late)[0]
    two_on = from_behind(ends, "ctx", 4)
    near = near_piece(0, None)
    ends, near = lax.optimization_barrier((ends, near))
    one_on = from_behind(ends, "ctx", 2)
    near = near_piece(1, near)
    one_on, two_on, near = lax.optimization_barrier((one_on, two_on, near))
    enter, on = one_on, two_on
    for m in range(reaches - 1):
        enter = pair_call(
            reach_kernel, [enter, on], [sent], "reach_%d" % m, rows=2 * tok_rows << m, index=at.reach + m
        )[0]
        on = from_behind(enter, "ctx", 4 << m)
    q_short = query_piece(1, masks, q_short)[0]
    on, q_short = lax.optimization_barrier((on, q_short))
    mine, give_back = pair_call(
        enter_kernel,
        [enter, on, own, got],
        [kept, kept],
        "pair_enter",
        rows=2 * tok_rows << (reaches - 1),
        index=at.reach + reaches - 1,
        block=tok_rows,
        block_index=at.early,
    )
    got_back = swap(give_back, "ctx")

    alone = grp == 1
    resid = near_by(residual)

    def finish(own, enter, before):
        last = alone and not own
        out_specs = [hbm, vmem, vmem]
        out_shape = [
            jax.ShapeDtypeStruct((tok_rows, chans), bf16),
            pltpu.VMEM((chans // LANES, tok_rows, LANES), f32),
            pltpu.VMEM((tok_rows, LANES), f32),
        ]
        scratch = [
            pltpu.VMEM((tok_rows, chans // 2), bf16),
            copies(2),
            pltpu.VMEM((F_TILES, wide_rows, LANES), f32),
            pltpu.VMEM((F_TILES, modes, LANES), f32),
            pltpu.VMEM((F_TILES, SUBS * (modes + 1), LANES), f32),
        ]
        operands = [near_by(x) for x in (masks, states, enter, near, q_short)] + [resid, rims, taps, rates, weights]
        if last:
            operands.append(near_by(norm_gain.reshape(1, chans)))
            out_specs.append(hbm)
            out_shape.append(jax.ShapeDtypeStruct((tok_rows, chans), bf16))
            scratch.append(pltpu.VMEM((tok_rows, chans), bf16))
        count = len(operands)
        in_specs = [vmem] * count
        if before:
            operands += [far_off(before[0]), near_by(before[1]), near_by(before[2])]
            in_specs += [hbm, vmem, vmem]
        return pl.pallas_call(
            functools.partial(
                final_kernel, span=span, modes=modes, channels=chans if alone else 0, most=F_TILES, chunk=chunk, own=own
            ),
            in_specs=in_specs,
            out_specs=out_specs,
            out_shape=out_shape,
            scratch_shapes=scratch,
            input_output_aliases={count + i: i for i in range(len(before))},
            compiler_params=params,
            cost_estimate=cost(450, 9 * tok_rows * chans),
            name="far_part_own" if own else "far_part_other",
        )(*operands)

    before = finish(True, mine, [])
    got_back, *before = lax.optimization_barrier((got_back, *before))
    outs = finish(False, got_back, before)
    if alone:
        return (outs[0], outs[3])
    hidden_out, whole, sums = outs
    hidden = whole.transpose(1, 0, 2).reshape(tok_rows, chans)
    square_sum = lax.psum(jnp.sum(sums, axis=1), "grp")
    inverse_rms = lax.rsqrt(square_sum / (chans * grp) + 1e-06)
    normed = (hidden * inverse_rms[:, None] * norm_gain[None, :]).astype(bf16)
    return (hidden_out, normed)


def solution(mesh):
    return jax.shard_map(
        shards,
        mesh=mesh,
        in_specs=(
            P("ctx", "grp"),
            P("ctx", "grp"),
            P("ctx", "grp"),
            P(None, None, "grp"),
            P(None, "grp"),
            P(None, "grp"),
            P(),
            P("ctx", "grp"),
            P("grp"),
        ),
        out_specs=(P("ctx", "grp"), P("ctx", "grp")),
        check_vma=False,
    )
```

```python
import functools
import math

import jax
import jax.numpy as jnp
from jax import lax
from jax.experimental import pallas as pl
from jax.experimental.pallas import tpu as pltpu
from jax.sharding import PartitionSpec as P

SUBS = 8
LANES = 128
MIB = 1024 * 1024
A_TILES, N_TILES, Q_TILES, F_TILES = 2, 2, 4, 4
NEAR_PARTS = 2
f32 = jnp.float32
bf16 = jnp.bfloat16


def from_behind(shard, axis, by):
    count = lax.axis_size(axis)
    pairs = [(i, i + by) for i in range(count) if 0 <= i + by < count]
    return lax.ppermute(shard, axis, pairs)


def swap(shard, axis):
    return lax.ppermute(shard, axis, [(i, i ^ 1) for i in range(lax.axis_size(axis))])


def doc_start_rows(len_ref, base, span):
    rows = lax.broadcasted_iota(jnp.int32, (SUBS, LANES), 0) * span + base
    starts = [jnp.int32(0)]
    for d in range(len_ref.shape[0] - 1):
        starts.append(starts[-1] + len_ref[d])
    out = []
    for j in range(span):
        pos = rows + j
        best = jnp.zeros((SUBS, LANES), jnp.int32)
        for start in starts[1:]:
            best = jnp.where(pos >= start, start, best)
        out.append(best)
    return rows, out


def flag(cond):
    return jnp.where(cond, 1.0, 0.0).astype(f32)


def each_group(count, most, group):
    size = math.gcd(count, most)

    def step(i, carry):
        group([pl.multiple_of((i * size + m) * LANES, LANES) for m in range(size)])
        return carry

    lax.fori_loop(0, count // size, step, 0)


def each_chunk(chans, chunk, before, group, after, most):
    def step(c, carry):
        before(c)

        def inner(lanes):
            group([pl.multiple_of(c * chunk + lane, LANES) for lane in lanes])

        each_group(chunk // LANES, most, inner)
        after(c)
        return carry

    lax.fori_loop(0, chans // chunk, step, 0)


def cols_copy(src, dst, sem, c, chunk):
    cols = pl.ds(pl.multiple_of(c * chunk, chunk), chunk)
    return pltpu.make_async_copy(src.at[:, cols], dst.at[:, cols], sem.at[c])


def cols_of(lane):
    return pl.ds(lane, LANES)


def row_of(ref, index):
    return ref[pl.ds(index, SUBS, stride=0), :]


def spread(x, wide, span):
    x = x.astype(f32)
    for b in range(SUBS):
        wide[pl.ds(b * (span + 1), span), :] = x[b * span : (b + 1) * span]


class Conv:
    def __init__(self, wide, rim, taps, span):
        self.wide, self.span = wide, span
        self.taps = [jnp.broadcast_to(taps[m : m + 1], (SUBS, LANES)) for m in range(3)]
        top = lax.broadcasted_iota(jnp.int32, (SUBS, LANES), 0) == 0
        ahead = [0.0, 0.0] if rim is None else [jnp.broadcast_to(rim[m : m + 1].astype(f32), (SUBS, LANES)) for m in range(2)]
        self.behind = [jnp.where(top, ahead[m], pltpu.roll(self.row(span - 2 + m), 1, 0)) for m in range(2)]

    def row(self, j):
        return self.wide[pl.ds(j, SUBS, stride=self.span + 1), :]

    def step(self, j, keep_one, keep_two):
        here = self.row(j)
        two, one = self.behind
        self.behind = [one, here]
        return self.taps[0] * here + (self.taps[1] * one) * keep_one + (self.taps[2] * two) * keep_two


def half_start(chans, own):
    parity = lax.rem(lax.axis_index("ctx"), 2)
    return pl.multiple_of((parity if own else 1 - parity) * (chans // 2), LANES)


def twice(mask, modes):
    return jnp.concatenate([mask] * (modes // SUBS), axis=0)


def sub_state(state_ref, lane, b, modes):
    return state_ref[lax.div(lane, LANES), pl.ds(b * (modes + 1), modes), :]


def state_kernel(
    masks, key_ref, value_ref, rim_ref, taps_ref, rate_ref, *refs, span, modes, most, own
):
    gate_ref, state_ref, end_ref, wide_k, wide_v, tables, held = refs[-7:]
    half = key_ref.shape[1] // 2
    first = half_start(2 * half, own)
    at = Masks(span)

    def group(lanes):
        for slot, lane in enumerate(lanes):
            spread(key_ref[:, cols_of(lane)], wide_k.at[slot], span)
            spread(value_ref[:, cols_of(lane)], wide_v.at[slot], span)
            rate = rate_ref[:, cols_of(lane)]
            tables[slot] = jnp.exp(-rate)
        convs = [
            [
                Conv(wide.at[slot], rim_ref[i, :, cols_of(lane)], taps_ref[i, :, cols_of(lane)], span)
                for i, wide in ((1, wide_k), (2, wide_v))
            ]
            for slot, lane in enumerate(lanes)
        ]
        last = [None] * len(lanes)
        for j in range(span):
            keep_one, keep_two = masks[at.one + j], masks[at.two + j]
            for slot, lane in enumerate(lanes):
                k_short, v_short = [conv.step(j, keep_one, keep_two) for conv in convs[slot]]
                if j % 2 == 0:
                    last[slot] = k_short * v_short
                    continue
                pair = jnp.concatenate([last[slot], k_short * v_short], axis=0).astype(bf16)
                gate_ref[pl.ds((j - 1) * SUBS, 2 * SUBS), cols_of(lane)] = pair
                pair = pair.astype(f32)
                held[slot, j - 1] = pair[:SUBS] * masks[at.last + j - 1]
                held[slot, j] = pair[SUBS:] * masks[at.last + j]
        for slot, lane in enumerate(lanes):
            decay = [row_of(tables.at[slot], n) for n in range(modes)]
            state = [held[slot, 0]] * modes
            for j in range(1, span):
                gate = held[slot, j]
                state = [decay[n] * state[n] + gate for n in range(modes)]
            for n in range(modes):
                state_ref[lax.div(lane, LANES), pl.ds(n, SUBS, stride=modes + 1), :] = state[n]
        for slot, lane in enumerate(lanes):
            leap = jnp.exp(-float(span) * rate_ref[:, cols_of(lane)])
            end = sub_state(state_ref, lane, 0, modes)
            for b in range(1, SUBS):
                end = (leap * twice(masks[at.passes + b], modes)) * end + sub_state(state_ref, lane, b, modes)
            end_ref[:, cols_of(pl.multiple_of(lane - first, LANES))] = end

    each_group(half // LANES, most, lambda lanes: group([pl.multiple_of(first + lane, LANES) for lane in lanes]))


def tail_kernel(query_ref, key_ref, value_ref, tail_ref, bufs, sems):
    rows, count = query_ref.shape[0], bufs.shape[1]
    copies = [
        pltpu.make_async_copy(ref.at[pl.ds(rows - count, count)], bufs.at[i], sems.at[i])
        for i, ref in enumerate((query_ref, key_ref, value_ref))
    ]
    for copy in copies:
        copy.start()
    for i, copy in enumerate(copies):
        copy.wait()
        tail_ref[i] = bufs[i].astype(f32)[count - 2 :].astype(bf16)


def unbroken(len_ref, first, count):
    start = jnp.int32(0)
    whole = jnp.where((first <= 0) & (first + count > 0), 0.0, 1.0)
    for d in range(len_ref.shape[0] - 1):
        start = start + len_ref[d]
        whole = jnp.where((start >= first) & (start < first + count), 0.0, whole)
    return whole.astype(f32)


class Masks:
    def __init__(self, span):
        self.one, self.two, self.last, self.enter = 0, span, 2 * span, 3 * span
        self.passes = 4 * span
        self.edges = self.passes + SUBS
        self.late = self.edges + 3
        self.early = self.late + 1
        self.reach = self.late + 2

    def count(self, reaches):
        return self.reach + reaches


def write_masks(base_ref, len_ref, masks, span, reaches):
    at = Masks(span)
    rows, starts = doc_start_rows(len_ref, base_ref[0], span)
    for j in range(span):
        masks[at.one + j] = flag(starts[j] < rows + j)
        masks[at.two + j] = flag(starts[j] < rows + (j - 1))
        masks[at.last + j] = flag(starts[span - 1] <= rows + j)
        masks[at.enter + j] = flag(starts[j] < rows)
    top = flag(lax.broadcasted_iota(jnp.int32, (SUBS, LANES), 0) == 0)
    masks[at.edges] = top * masks[at.one]
    masks[at.edges + 1] = top * masks[at.two]
    masks[at.edges + 2] = top * masks[at.two + 1]
    size = SUBS * span
    parity = lax.rem(lax.div(base_ref[0], size), 2)
    pair_at = base_ref[0] - parity * size
    ranges = [(base_ref[0] + b * span, span) for b in range(SUBS)]
    flags = [at.passes + b for b in range(SUBS)]
    ranges += [(pair_at + size, size), (pair_at, size)]
    flags += [at.late, at.early]
    for m in range(reaches):
        ranges.append((pair_at - (2 * size << m), 2 * size << m))
        flags.append(at.reach + m)
    for index, (first, count) in zip(flags, ranges):
        masks[index] = jnp.full((SUBS, LANES), unbroken(len_ref, first, count), f32)


def near_kernel(masks, gate_ref, rate_ref, weight_ref, *refs, span, modes, most, first, count):
    near_ref, sums, tap_rows = refs[-3:]
    at = Masks(span)

    def group(lanes):
        for slot, lane in enumerate(lanes):
            decay = jnp.exp(-rate_ref[:, cols_of(lane)])
            term = weight_ref[:, cols_of(lane)]
            for lag in range(span):
                part = term[:SUBS]
                for n in range(SUBS, modes, SUBS):
                    part = part + term[n : n + SUBS]
                sums[slot, pl.ds(lag * (SUBS + 1), SUBS), :] = part
                term = term * decay
        for slot in range(len(lanes)):
            for first_lag in range(0, span, SUBS):
                total = [
                    sums[slot, pl.ds(first_lag * (SUBS + 1) + m, SUBS, stride=SUBS + 1), :] for m in range(SUBS)
                ]
                while len(total) > 1:
                    total = [total[m] + total[m + 1] for m in range(0, len(total), 2)]
                tap_rows[slot, pl.ds(first_lag, SUBS), :] = total[0]
        taps = [[row_of(tap_rows.at[slot], lag) for lag in range(span)] for slot in range(len(lanes))]
        for parts, lane in zip(taps, lanes):
            live = []
            for j in range(span):
                if j % 2 == 0:
                    pair = gate_ref[pl.ds(j * SUBS, 2 * SUBS), cols_of(lane)].astype(f32)
                keep = masks[at.one + j]
                live = [g * keep for g in live]
                live.append(pair[(j % 2) * SUBS : (j % 2 + 1) * SUBS])
                total = parts[0] * live[j]
                for lag in range(1, j + 1):
                    total = total + parts[lag] * live[j - lag]
                near_ref[pl.ds(j * SUBS, SUBS), cols_of(lane)] = total

    each_group(count // LANES, most, lambda lanes: group([pl.multiple_of(first + lane, LANES) for lane in lanes]))


def query_kernel(*refs, span, most, chunk, reaches, first, count):
    if reaches:
        base_ref, len_ref, query_ref, taps_in, rate_in, short_ref, masks, taps_ref, rate_ref, query_buf, sems, wide_q, param_sems = refs
        taps_copy = pltpu.make_async_copy(taps_in, taps_ref, param_sems.at[0])
        rate_copy = pltpu.make_async_copy(rate_in, rate_ref, param_sems.at[1])
        taps_copy.start()
    else:
        masks, query_ref, taps_ref, _, short_ref, query_buf, sems, wide_q = refs

    def fetch(c):
        there = pl.ds(first + c * chunk if isinstance(c, int) else pl.multiple_of(first + c * chunk, chunk), chunk)
        here = pl.ds(c * chunk if isinstance(c, int) else pl.multiple_of(c * chunk, chunk), chunk)
        return pltpu.make_async_copy(query_ref.at[:, there], query_buf.at[:, here], sems.at[c])

    for c in range(count // chunk):
        fetch(c).start()
    if reaches:
        rate_copy.start()
        write_masks(base_ref, len_ref, masks, span, reaches)
        taps_copy.wait()
    at = Masks(span)

    def group(lanes):
        for slot, lane in enumerate(lanes):
            spread(query_buf[:, cols_of(lane)], wide_q.at[slot], span)
        convs = [
            Conv(wide_q.at[slot], None, taps_ref[0, :, cols_of(pl.multiple_of(first + lane, LANES))], span)
            for slot, lane in enumerate(lanes)
        ]
        for j in range(span):
            keep_one, keep_two = masks[at.one + j], masks[at.two + j]
            for slot, lane in enumerate(lanes):
                short_ref[pl.ds(j * SUBS, SUBS), cols_of(pl.multiple_of(first + lane, LANES))] = convs[slot].step(j, keep_one, keep_two)

    each_chunk(count, chunk, lambda c: fetch(c).wait(), group, lambda c: None, most)
    if reaches:
        rate_copy.wait()


def pair_rates(rate_ref, count):
    parity = lax.rem(lax.axis_index("ctx"), 2)
    return parity, rate_ref[:, pl.ds(pl.multiple_of(parity * count, LANES), count)]


def early_late(parity, own, got):
    odd = jnp.full(own.shape, parity, jnp.int32) == 1
    return jnp.where(odd, got, own), jnp.where(odd, own, got)


def leap(masks, index, rate, rows):
    return jnp.exp(-float(rows) * rate) * masks[index][0:1, 0:1]


def pair_kernel(masks, own_ref, got_ref, rate_ref, end_ref, *, rows, index):
    parity, rate = pair_rates(rate_ref, own_ref.shape[1])
    early, late = early_late(parity, own_ref[...], got_ref[...])
    end_ref[...] = (late + leap(masks, index, rate, rows) * early).astype(bf16)


def reach_kernel(masks, near_ref, far_ref, rate_ref, enter_ref, *, rows, index):
    _, rate = pair_rates(rate_ref, near_ref.shape[1])
    enter_ref[...] = (near_ref[...].astype(f32) + leap(masks, index, rate, rows) * far_ref[...].astype(f32)).astype(bf16)


def enter_kernel(
    masks, near_ref, far_ref, own_ref, got_ref, rate_ref, mine_ref, give_ref, *, rows, index, block, block_index
):
    parity, rate = pair_rates(rate_ref, own_ref.shape[1])
    first = near_ref[...].astype(f32) + leap(masks, index, rate, rows) * far_ref[...].astype(f32)
    early, _ = early_late(parity, own_ref[...], got_ref[...])
    second = early + leap(masks, block_index, rate, block) * first
    give, mine = early_late(parity, second, first)
    mine_ref[...] = mine
    give_ref[...] = give


def final_kernel(
    masks, state_ref, enter_ref, near_ref, short_ref, resid_ref, rim_ref, taps_ref, rate_ref, weight_ref, *refs,
    span, modes, channels, most, chunk, own,
):
    if own:
        hidden_out, whole, sums, hidden_ref, sems, wide, tables, starts_at = refs
    elif channels:
        gain_ref, _, _, _, hidden_out, whole, sums, normed_out, hidden_ref, sems, wide, tables, starts_at, normed_ref = refs
    else:
        _, _, _, hidden_out, whole, sums, hidden_ref, sems, wide, tables, starts_at = refs
    chans = resid_ref.shape[1]
    half = chans // 2
    first = half_start(chans, own)
    at = Masks(span)

    def store(c):
        here = pl.ds(pl.multiple_of(c * chunk, chunk), chunk)
        there = pl.ds(pl.multiple_of(first + c * chunk, chunk), chunk)
        return pltpu.make_async_copy(hidden_ref.at[:, here], hidden_out.at[:, there], sems.at[0, c])

    def store_normed(c):
        return cols_copy(normed_ref, normed_out, sems.at[1], c, chunk)

    if own:
        sums[...] = jnp.zeros(sums.shape, f32)

    def group(lanes):
        for slot, lane in enumerate(lanes):
            state = enter_ref[:, cols_of(pl.multiple_of(lane - first, LANES))]
            rate = rate_ref[:, cols_of(lane)]
            weight = weight_ref[:, cols_of(lane)]
            tables[slot] = jnp.exp(-rate)
            leap = jnp.exp(-float(span) * rate)
            for b in range(SUBS):
                starts_at[slot, pl.ds(b * (modes + 1), modes), :] = weight * state
                if b < SUBS - 1:
                    state = (leap * twice(masks[at.passes + b], modes)) * state + sub_state(state_ref, lane, b, modes)
        for slot, lane in enumerate(lanes):
            part = [starts_at[slot, pl.ds(n, SUBS, stride=modes + 1), :] for n in range(modes)]
            decay = [row_of(tables.at[slot], n) for n in range(modes)]
            rim = rim_ref[0, :, cols_of(lane)].astype(f32)
            tap = taps_ref[0, :, cols_of(lane)]
            edge = [
                (tap[1:2] * rim[1:2]) * masks[at.edges] + (tap[2:3] * rim[0:1]) * masks[at.edges + 1],
                (tap[2:3] * rim[1:2]) * masks[at.edges + 2],
            ]
            for j in range(span):
                part = [part[n] * decay[n] for n in range(modes)]
                total = part
                while len(total) > 1:
                    total = [total[m] + total[m + 1] for m in range(0, len(total), 2)]
                conv = near_ref[pl.ds(j * SUBS, SUBS), cols_of(lane)] + total[0] * masks[at.enter + j]
                conv = conv.astype(bf16).astype(f32)
                short = short_ref[pl.ds(j * SUBS, SUBS), cols_of(lane)]
                if j < 2:
                    short = short + edge[j]
                wide[slot, pl.ds(j, SUBS, stride=span + 1), :] = short * conv
        for b in range(SUBS):
            rows = pl.ds(b * span, span)
            squares = sums[rows, :]
            for slot, lane in enumerate(lanes):
                hidden = wide[slot, pl.ds(b * (span + 1), span), :] + resid_ref[rows, cols_of(lane)].astype(f32)
                whole[lax.div(lane, LANES), rows, :] = hidden
                hidden_ref[rows, cols_of(pl.multiple_of(lane - first, LANES))] = hidden.astype(bf16)
                squares = squares + hidden * hidden
            sums[rows, :] = squares

    each_chunk(
        half,
        chunk,
        lambda c: None,
        lambda lanes: group([pl.multiple_of(first + lane, LANES) for lane in lanes]),
        lambda c: store(c).start(),
        most,
    )
    if channels and not own:
        inverse = lax.rsqrt(jnp.sum(sums[...], axis=1, keepdims=True) / channels + 1e-06)
        sums[...] = jnp.broadcast_to(inverse, sums.shape)

        def scale(lanes):
            for lane in lanes:
                normed = whole[lax.div(lane, LANES)] * sums[...] * gain_ref[:, cols_of(lane)]
                normed_ref[:, cols_of(lane)] = normed.astype(bf16)

        each_chunk(chans, chunk, lambda c: None, scale, lambda c: store_normed(c).start(), 4)
        for c in range(chans // chunk):
            store_normed(c).wait()
    for c in range(half // chunk):
        store(c).wait()


def shards(
    query_in, key_in, value_in, short_taps, decay_rate, residues, doc_lengths, residual, norm_gain
):
    tok_rows, chans = query_in.shape
    modes = decay_rate.shape[0]
    span = tok_rows // SUBS
    blocks = lax.axis_size("ctx")
    grp = lax.axis_size("grp")
    chunk = min(chans // 2, 1024)
    pieces = chans // chunk
    ctx_index = lax.axis_index("ctx")
    base = (ctx_index * tok_rows).astype(jnp.int32).reshape(1)
    weight = residues * jnp.sqrt(-jnp.expm1(-2.0 * decay_rate))

    smem = pl.BlockSpec(memory_space=pltpu.SMEM)
    vmem = pl.BlockSpec(memory_space=pltpu.VMEM)
    hbm = pl.BlockSpec(memory_space=pltpu.HBM)
    tile_shape = (SUBS, LANES)
    wide_rows = SUBS * (span + 1)
    params = pltpu.CompilerParams(vmem_limit_bytes=16 * MIB)

    lengths = pltpu.with_memory_space_constraint(doc_lengths, pltpu.HBM)

    def near_by(x):
        return pltpu.with_memory_space_constraint(x, pltpu.VMEM)

    def far_off(x):
        return pltpu.with_memory_space_constraint(x, pltpu.HBM)

    def copies(kinds):
        return pltpu.SemaphoreType.DMA((kinds, pieces))

    def cost(per_tile, moved):
        return pl.CostEstimate(flops=per_tile * (chans // LANES) * SUBS * LANES, bytes_accessed=moved, transcendentals=0)

    tails = pl.pallas_call(
        tail_kernel,
        in_specs=[hbm, hbm, hbm],
        out_specs=vmem,
        out_shape=pltpu.VMEM((3, 2, chans), bf16),
        scratch_shapes=[pltpu.VMEM((3, 16, chans), bf16), pltpu.SemaphoreType.DMA((3,))],
        compiler_params=params,
        name="tails",
    )(far_off(query_in), far_off(key_in), far_off(value_in))
    rim_rows = from_behind(tails, "ctx", 1)
    reaches = max(1, (blocks // 8).bit_length() - 1)
    mask_shape = (Masks(span).count(reaches),) + tile_shape

    def query_piece(part, masks, before):
        count = chans // 2
        scratch = [
            pltpu.VMEM((tok_rows, count), bf16),
            pltpu.SemaphoreType.DMA((count // chunk,)),
            pltpu.VMEM((Q_TILES, wide_rows, LANES), f32),
        ]
        out_shape = [pltpu.VMEM((tok_rows, chans), f32)]
        if part == 0:
            operands = [base, lengths, far_off(query_in), far_off(short_taps), far_off(decay_rate)]
            in_specs = [smem, smem, hbm, hbm, hbm]
            out_shape += [
                pltpu.VMEM(mask_shape, f32), pltpu.VMEM(short_taps.shape, f32), pltpu.VMEM(decay_rate.shape, f32)
            ]
            scratch.append(pltpu.SemaphoreType.DMA((2,)))
        else:
            operands = [near_by(masks), far_off(query_in), taps, near_by(before)]
            in_specs = [vmem, hbm, vmem, vmem]
        return pl.pallas_call(
            functools.partial(
                query_kernel, span=span, most=Q_TILES, chunk=chunk, reaches=0 if part else reaches,
                first=part * count, count=count,
            ),
            in_specs=in_specs,
            out_specs=[vmem] * len(out_shape),
            out_shape=out_shape,
            scratch_shapes=scratch,
            input_output_aliases={3: 0} if part else {},
            compiler_params=params,
            cost_estimate=cost(100, 3 * tok_rows * chans),
            name="query_part_%d" % part,
        )(*operands)

    q_short, masks, taps, rates = query_piece(0, None, None)
    rim_rows, q_short = lax.optimization_barrier((rim_rows, q_short))
    rates, weights, taps, rims = near_by(rates), near_by(weight), near_by(taps), near_by(rim_rows)
    kept = pltpu.VMEM((modes, chans // 2), f32)
    sent = pltpu.VMEM((modes, chans // 2), bf16)
    keys, values = near_by(key_in), near_by(value_in)

    def states_of(own, before):
        return pl.pallas_call(
            functools.partial(state_kernel, span=span, modes=modes, most=A_TILES, own=own),
            in_specs=[vmem] * (6 + len(before)),
            out_specs=[vmem] * 3,
            out_shape=[
                pltpu.VMEM((tok_rows, chans), bf16),
                pltpu.VMEM((chans // LANES, SUBS * (modes + 1), LANES), f32),
                kept,
            ],
            scratch_shapes=[
                pltpu.VMEM((A_TILES, wide_rows, LANES), f32),
                pltpu.VMEM((A_TILES, wide_rows, LANES), f32),
                pltpu.VMEM((A_TILES, modes, LANES), f32),
                pltpu.VMEM((A_TILES, span) + tile_shape, f32),
            ],
            input_output_aliases={6 + i: i for i in range(len(before))},
            compiler_params=params,
            cost_estimate=cost(500, 6 * tok_rows * chans),
            name="block_states_own" if own else "block_states_give",
        )(near_by(masks), keys, values, rims, taps, rates, *[near_by(x) for x in before])

    gates, states, give = states_of(False, [])
    got = swap(give, "ctx")
    gates, states, own = states_of(True, [gates, states])
    got, gates, states, own = lax.optimization_barrier((got, gates, states, own))

    def near_piece(part, near):
        count = chans // NEAR_PARTS
        before = [] if near is None else [near_by(near)]
        return pl.pallas_call(
            functools.partial(
                near_kernel, span=span, modes=modes, most=N_TILES, first=part * count, count=count
            ),
            in_specs=[vmem] * (4 + len(before)),
            out_specs=vmem,
            out_shape=pltpu.VMEM((tok_rows, chans), f32),
            scratch_shapes=[
                pltpu.VMEM((N_TILES, span * (SUBS + 1), LANES), f32),
                pltpu.VMEM((N_TILES, span, LANES), f32),
            ],
            compiler_params=params,
            input_output_aliases={4: 0} if before else {},
            cost_estimate=cost(600 // NEAR_PARTS, 7 * tok_rows * count),
            name="near_part_%d" % part,
        )(near_by(masks), near_by(gates), rates, weights, *before)

    got = swap(give, "ctx")

    at = Masks(span)

    def pair_call(kernel, operands, out_shape, name, **static):
        return pl.pallas_call(
            functools.partial(kernel, **static),
            in_specs=[vmem] * (len(operands) + 2),
            out_specs=[vmem] * len(out_shape),
            out_shape=out_shape,
            compiler_params=params,
            name=name,
        )(near_by(masks), *[near_by(x) for x in operands], rates)

    ends = pair_call(pair_kernel, [own, got], [sent], "pair_ends", rows=tok_rows, index=at.late)[0]
    one_on, two_on = from_behind(ends, "ctx", 2), from_behind(ends, "ctx", 4)
    near = near_piece(0, None)
    one_on, two_on, near = lax.optimization_barrier((one_on, two_on, near))
    enter, on = one_on, two_on
    for m in range(reaches - 1):
        enter = pair_call(
            reach_kernel, [enter, on], [sent], "reach_%d" % m, rows=2 * tok_rows << m, index=at.reach + m
        )[0]
        on = from_behind(enter, "ctx", 4 << m)
    q_short, near = query_piece(1, masks, q_short)[0], near_piece(1, near)
    on, q_short, near = lax.optimization_barrier((on, q_short, near))
    mine, give_back = pair_call(
        enter_kernel,
        [enter, on, own, got],
        [kept, kept],
        "pair_enter",
        rows=2 * tok_rows << (reaches - 1),
        index=at.reach + reaches - 1,
        block=tok_rows,
        block_index=at.early,
    )
    got_back = swap(give_back, "ctx")

    alone = grp == 1
    resid = near_by(residual)

    def finish(own, enter, before):
        last = alone and not own
        out_specs = [hbm, vmem, vmem]
        out_shape = [
            jax.ShapeDtypeStruct((tok_rows, chans), bf16),
            pltpu.VMEM((chans // LANES, tok_rows, LANES), f32),
            pltpu.VMEM((tok_rows, LANES), f32),
        ]
        scratch = [
            pltpu.VMEM((tok_rows, chans // 2), bf16),
            copies(2),
            pltpu.VMEM((F_TILES, wide_rows, LANES), f32),
            pltpu.VMEM((F_TILES, modes, LANES), f32),
            pltpu.VMEM((F_TILES, SUBS * (modes + 1), LANES), f32),
        ]
        operands = [near_by(x) for x in (masks, states, enter, near, q_short)] + [resid, rims, taps, rates, weights]
        if last:
            operands.append(near_by(norm_gain.reshape(1, chans)))
            out_specs.append(hbm)
            out_shape.append(jax.ShapeDtypeStruct((tok_rows, chans), bf16))
            scratch.append(pltpu.VMEM((tok_rows, chans), bf16))
        count = len(operands)
        in_specs = [vmem] * count
        if before:
            operands += [far_off(before[0]), near_by(before[1]), near_by(before[2])]
            in_specs += [hbm, vmem, vmem]
        return pl.pallas_call(
            functools.partial(
                final_kernel, span=span, modes=modes, channels=chans if alone else 0, most=F_TILES, chunk=chunk, own=own
            ),
            in_specs=in_specs,
            out_specs=out_specs,
            out_shape=out_shape,
            scratch_shapes=scratch,
            input_output_aliases={count + i: i for i in range(len(before))},
            compiler_params=params,
            cost_estimate=cost(450, 9 * tok_rows * chans),
            name="far_part_own" if own else "far_part_other",
        )(*operands)

    before = finish(True, mine, [])
    got_back, *before = lax.optimization_barrier((got_back, *before))
    outs = finish(False, got_back, before)
    if alone:
        return (outs[0], outs[3])
    hidden_out, whole, sums = outs
    hidden = whole.transpose(1, 0, 2).reshape(tok_rows, chans)
    square_sum = lax.psum(jnp.sum(sums, axis=1), "grp")
    inverse_rms = lax.rsqrt(square_sum / (chans * grp) + 1e-06)
    normed = (hidden * inverse_rms[:, None] * norm_gain[None, :]).astype(bf16)
    return (hidden_out, normed)


def solution(mesh):
    return jax.shard_map(
        shards,
        mesh=mesh,
        in_specs=(
            P("ctx", "grp"),
            P("ctx", "grp"),
            P("ctx", "grp"),
            P(None, None, "grp"),
            P(None, "grp"),
            P(None, "grp"),
            P(),
            P("ctx", "grp"),
            P("grp"),
        ),
        out_specs=(P("ctx", "grp"), P("ctx", "grp")),
        check_vma=False,
    )
```

```python
import functools
import math

import jax
import jax.numpy as jnp
from jax import lax
from jax.experimental import pallas as pl
from jax.experimental.pallas import tpu as pltpu
from jax.sharding import PartitionSpec as P

SUBS = 8
LANES = 128
MIB = 1024 * 1024
A_TILES, N_TILES, Q_TILES, F_TILES = 2, 2, 4, 4
NEAR_PARTS = 2
f32 = jnp.float32
bf16 = jnp.bfloat16


def from_behind(shard, axis, by):
    count = lax.axis_size(axis)
    pairs = [(i, i + by) for i in range(count) if 0 <= i + by < count]
    return lax.ppermute(shard, axis, pairs)


def swap(shard, axis, bit=1):
    return lax.ppermute(shard, axis, [(i, i ^ bit) for i in range(lax.axis_size(axis))])


def doc_start_rows(len_ref, base, span):
    rows = lax.broadcasted_iota(jnp.int32, (SUBS, LANES), 0) * span + base
    starts = [jnp.int32(0)]
    for d in range(len_ref.shape[0] - 1):
        starts.append(starts[-1] + len_ref[d])
    out = []
    for j in range(span):
        pos = rows + j
        best = jnp.zeros((SUBS, LANES), jnp.int32)
        for start in starts[1:]:
            best = jnp.where(pos >= start, start, best)
        out.append(best)
    return rows, out


def flag(cond):
    return jnp.where(cond, 1.0, 0.0).astype(f32)


def each_group(count, most, group):
    size = math.gcd(count, most)

    def step(i, carry):
        group([pl.multiple_of((i * size + m) * LANES, LANES) for m in range(size)])
        return carry

    lax.fori_loop(0, count // size, step, 0)


def each_chunk(chans, chunk, before, group, after, most):
    def step(c, carry):
        before(c)

        def inner(lanes):
            group([pl.multiple_of(c * chunk + lane, LANES) for lane in lanes])

        each_group(chunk // LANES, most, inner)
        after(c)
        return carry

    lax.fori_loop(0, chans // chunk, step, 0)


def cols_copy(src, dst, sem, c, chunk):
    cols = pl.ds(pl.multiple_of(c * chunk, chunk), chunk)
    return pltpu.make_async_copy(src.at[:, cols], dst.at[:, cols], sem.at[c])


def cols_of(lane):
    return pl.ds(lane, LANES)


def row_of(ref, index):
    return ref[pl.ds(index, SUBS, stride=0), :]


def spread(x, wide, span):
    x = x.astype(f32)
    for b in range(SUBS):
        wide[pl.ds(b * (span + 1), span), :] = x[b * span : (b + 1) * span]


class Conv:
    def __init__(self, wide, rim, taps, span):
        self.wide, self.span = wide, span
        self.taps = [jnp.broadcast_to(taps[m : m + 1], (SUBS, LANES)) for m in range(3)]
        top = lax.broadcasted_iota(jnp.int32, (SUBS, LANES), 0) == 0
        ahead = [0.0, 0.0] if rim is None else [jnp.broadcast_to(rim[m : m + 1].astype(f32), (SUBS, LANES)) for m in range(2)]
        self.behind = [jnp.where(top, ahead[m], pltpu.roll(self.row(span - 2 + m), 1, 0)) for m in range(2)]

    def row(self, j):
        return self.wide[pl.ds(j, SUBS, stride=self.span + 1), :]

    def step(self, j, keep_one, keep_two):
        here = self.row(j)
        two, one = self.behind
        self.behind = [one, here]
        return self.taps[0] * here + (self.taps[1] * one) * keep_one + (self.taps[2] * two) * keep_two


def half_start(chans, own):
    parity = lax.rem(lax.axis_index("ctx"), 2)
    return pl.multiple_of((parity if own else 1 - parity) * (chans // 2), LANES)


def twice(mask, modes):
    return jnp.concatenate([mask] * (modes // SUBS), axis=0)


def sub_state(state_ref, lane, b, modes):
    return state_ref[lax.div(lane, LANES), pl.ds(b * (modes + 1), modes), :]


def state_kernel(
    masks, key_ref, value_ref, rim_ref, taps_ref, rate_ref, *refs, span, modes, most, own
):
    gate_ref, state_ref, end_ref, wide_k, wide_v, tables, held = refs[-7:]
    half = key_ref.shape[1] // 2
    first = half_start(2 * half, own)
    at = Masks(span)

    def group(lanes):
        for slot, lane in enumerate(lanes):
            spread(key_ref[:, cols_of(lane)], wide_k.at[slot], span)
            spread(value_ref[:, cols_of(lane)], wide_v.at[slot], span)
            rate = rate_ref[:, cols_of(lane)]
            tables[slot] = jnp.exp(-rate)
        convs = [
            [
                Conv(wide.at[slot], rim_ref[i, :, cols_of(lane)], taps_ref[i, :, cols_of(lane)], span)
                for i, wide in ((1, wide_k), (2, wide_v))
            ]
            for slot, lane in enumerate(lanes)
        ]
        last = [None] * len(lanes)
        for j in range(span):
            keep_one, keep_two = masks[at.one + j], masks[at.two + j]
            for slot, lane in enumerate(lanes):
                k_short, v_short = [conv.step(j, keep_one, keep_two) for conv in convs[slot]]
                if j % 2 == 0:
                    last[slot] = k_short * v_short
                    continue
                pair = jnp.concatenate([last[slot], k_short * v_short], axis=0).astype(bf16)
                gate_ref[pl.ds((j - 1) * SUBS, 2 * SUBS), cols_of(lane)] = pair
                pair = pair.astype(f32)
                held[slot, j - 1] = pair[:SUBS] * masks[at.last + j - 1]
                held[slot, j] = pair[SUBS:] * masks[at.last + j]
        for slot, lane in enumerate(lanes):
            decay = [row_of(tables.at[slot], n) for n in range(modes)]
            state = [held[slot, 0]] * modes
            for j in range(1, span):
                gate = held[slot, j]
                state = [decay[n] * state[n] + gate for n in range(modes)]
            for n in range(modes):
                state_ref[lax.div(lane, LANES), pl.ds(n, SUBS, stride=modes + 1), :] = state[n]
        for slot, lane in enumerate(lanes):
            leap = jnp.exp(-float(span) * rate_ref[:, cols_of(lane)])
            end = sub_state(state_ref, lane, 0, modes)
            for b in range(1, SUBS):
                end = (leap * twice(masks[at.passes + b], modes)) * end + sub_state(state_ref, lane, b, modes)
            end_ref[:, cols_of(pl.multiple_of(lane - first, LANES))] = end

    each_group(half // LANES, most, lambda lanes: group([pl.multiple_of(first + lane, LANES) for lane in lanes]))


def tail_kernel(query_ref, key_ref, value_ref, tail_ref, bufs, sems):
    rows, count = query_ref.shape[0], bufs.shape[1]
    copies = [
        pltpu.make_async_copy(ref.at[pl.ds(rows - count, count)], bufs.at[i], sems.at[i])
        for i, ref in enumerate((query_ref, key_ref, value_ref))
    ]
    for copy in copies:
        copy.start()
    for i, copy in enumerate(copies):
        copy.wait()
        tail_ref[i] = bufs[i].astype(f32)[count - 2 :].astype(bf16)


def unbroken(len_ref, first, count):
    start = jnp.int32(0)
    whole = jnp.where((first <= 0) & (first + count > 0), 0.0, 1.0)
    for d in range(len_ref.shape[0] - 1):
        start = start + len_ref[d]
        whole = jnp.where((start >= first) & (start < first + count), 0.0, whole)
    return whole.astype(f32)


class Masks:
    def __init__(self, span):
        self.one, self.two, self.last, self.enter = 0, span, 2 * span, 3 * span
        self.passes = 4 * span
        self.edges = self.passes + SUBS
        self.late = self.edges + 3
        self.early = self.late + 1
        self.levels = self.late + 2

    def lead(self, level):
        return self.levels + 2 * level

    def later(self, level):
        return self.levels + 2 * level + 1

    def count(self, levels):
        return self.levels + 2 * levels + 1


def write_masks(base_ref, len_ref, masks, span, levels):
    at = Masks(span)
    rows, starts = doc_start_rows(len_ref, base_ref[0], span)
    for j in range(span):
        masks[at.one + j] = flag(starts[j] < rows + j)
        masks[at.two + j] = flag(starts[j] < rows + (j - 1))
        masks[at.last + j] = flag(starts[span - 1] <= rows + j)
        masks[at.enter + j] = flag(starts[j] < rows)
    top = flag(lax.broadcasted_iota(jnp.int32, (SUBS, LANES), 0) == 0)
    masks[at.edges] = top * masks[at.one]
    masks[at.edges + 1] = top * masks[at.two]
    masks[at.edges + 2] = top * masks[at.two + 1]
    size = SUBS * span
    parity = lax.rem(lax.div(base_ref[0], size), 2)
    pair_at = base_ref[0] - parity * size
    ranges = [(base_ref[0] + b * span, span) for b in range(SUBS)]
    flags = [at.passes + b for b in range(SUBS)]
    ranges += [(pair_at + size, size), (pair_at, size)]
    flags += [at.late, at.early]
    for m in range(levels + 1):
        group = 2 * size << m
        group_at = base_ref[0] - lax.rem(base_ref[0], group)
        ranges.append((group_at, pair_at - group_at))
        flags.append(at.lead(m))
        if m < levels:
            ranges.append((group_at + group * (1 - lax.rem(lax.div(base_ref[0], group), 2)), group))
            flags.append(at.later(m))
    for index, (first, count) in zip(flags, ranges):
        masks[index] = jnp.full((SUBS, LANES), unbroken(len_ref, first, count), f32)


def near_kernel(masks, gate_ref, rate_ref, weight_ref, *refs, span, modes, most, first, count):
    near_ref, sums, tap_rows = refs[-3:]
    at = Masks(span)

    def group(lanes):
        for slot, lane in enumerate(lanes):
            decay = jnp.exp(-rate_ref[:, cols_of(lane)])
            term = weight_ref[:, cols_of(lane)]
            for lag in range(span):
                part = term[:SUBS]
                for n in range(SUBS, modes, SUBS):
                    part = part + term[n : n + SUBS]
                sums[slot, pl.ds(lag * (SUBS + 1), SUBS), :] = part
                term = term * decay
        for slot in range(len(lanes)):
            for first_lag in range(0, span, SUBS):
                total = [
                    sums[slot, pl.ds(first_lag * (SUBS + 1) + m, SUBS, stride=SUBS + 1), :] for m in range(SUBS)
                ]
                while len(total) > 1:
                    total = [total[m] + total[m + 1] for m in range(0, len(total), 2)]
                tap_rows[slot, pl.ds(first_lag, SUBS), :] = total[0]
        taps = [[row_of(tap_rows.at[slot], lag) for lag in range(span)] for slot in range(len(lanes))]
        for parts, lane in zip(taps, lanes):
            live = []
            for j in range(span):
                if j % 2 == 0:
                    pair = gate_ref[pl.ds(j * SUBS, 2 * SUBS), cols_of(lane)].astype(f32)
                keep = masks[at.one + j]
                live = [g * keep for g in live]
                live.append(pair[(j % 2) * SUBS : (j % 2 + 1) * SUBS])
                total = parts[0] * live[j]
                for lag in range(1, j + 1):
                    total = total + parts[lag] * live[j - lag]
                near_ref[pl.ds(j * SUBS, SUBS), cols_of(lane)] = total

    each_group(count // LANES, most, lambda lanes: group([pl.multiple_of(first + lane, LANES) for lane in lanes]))


def query_kernel(*refs, span, most, chunk, levels, first, count):
    if not first:
        base_ref, len_ref, query_ref, taps_ref, value_in, short_ref, masks, value_ref, query_buf, sems, wide_q, value_sem = refs
        value_copy = pltpu.make_async_copy(value_in, value_ref, value_sem)
    else:
        masks, query_ref, taps_ref, _, short_ref, query_buf, sems, wide_q = refs

    def fetch(c):
        there = pl.ds(first + c * chunk if isinstance(c, int) else pl.multiple_of(first + c * chunk, chunk), chunk)
        here = pl.ds(c * chunk if isinstance(c, int) else pl.multiple_of(c * chunk, chunk), chunk)
        return pltpu.make_async_copy(query_ref.at[:, there], query_buf.at[:, here], sems.at[c])

    for c in range(count // chunk):
        fetch(c).start()
    if not first:
        value_copy.start()
        write_masks(base_ref, len_ref, masks, span, levels)
    at = Masks(span)

    def group(lanes):
        for slot, lane in enumerate(lanes):
            spread(query_buf[:, cols_of(lane)], wide_q.at[slot], span)
        convs = [
            Conv(wide_q.at[slot], None, taps_ref[0, :, cols_of(pl.multiple_of(first + lane, LANES))], span)
            for slot, lane in enumerate(lanes)
        ]
        for j in range(span):
            keep_one, keep_two = masks[at.one + j], masks[at.two + j]
            for slot, lane in enumerate(lanes):
                short_ref[pl.ds(j * SUBS, SUBS), cols_of(pl.multiple_of(first + lane, LANES))] = convs[slot].step(j, keep_one, keep_two)

    each_chunk(count, chunk, lambda c: fetch(c).wait(), group, lambda c: None, most)
    if not first:
        value_copy.wait()


def pair_rates(rate_ref, count):
    parity = lax.rem(lax.axis_index("ctx"), 2)
    return parity, rate_ref[:, pl.ds(pl.multiple_of(parity * count, LANES), count)]


def early_late(parity, own, got):
    odd = jnp.full(own.shape, parity, jnp.int32) == 1
    return jnp.where(odd, got, own), jnp.where(odd, own, got)


def leap(masks, index, rate, rows):
    return jnp.exp(-float(rows) * rate) * masks[index][0:1, 0:1]


def pair_kernel(masks, own_ref, got_ref, rate_ref, total_ref, sent_ref, *, rows, index):
    parity, rate = pair_rates(rate_ref, own_ref.shape[1])
    early, late = early_late(parity, own_ref[...], got_ref[...])
    total = late + leap(masks, index, rate, rows) * early
    total_ref[...] = total
    sent_ref[...] = total.astype(bf16)


def lead_leap(masks, index, rate, rows, bit):
    me = lax.axis_index("ctx")
    lead = (lax.rem(me, bit) - lax.rem(me, 2)) * rows
    return jnp.exp(rate * -lead.astype(f32)) * masks[index][0:1, 0:1]


def level_kernel(masks, total_ref, got_ref, rate_ref, *refs, rows, level, lead, later):
    before_ref, (new_ref, sent_ref, enter_ref) = (refs[0] if level else None), refs[-3:]
    _, rate = pair_rates(rate_ref, total_ref.shape[1])
    bit = 2 << level
    after = lax.rem(lax.div(lax.axis_index("ctx"), bit), 2)
    got = got_ref[...].astype(f32)
    early, late = early_late(after, total_ref[...], got)
    total = late + leap(masks, later, rate, bit * rows) * early
    new_ref[...] = total
    sent_ref[...] = total.astype(bf16)
    entering = jnp.where(jnp.full(got.shape, after, jnp.int32) == 1, got, 0.0) * lead_leap(masks, lead, rate, rows, bit)
    enter_ref[...] = entering if before_ref is None else before_ref[...] + entering


def enter_kernel(
    masks, before_ref, got_ref, own_ref, other_ref, rate_ref, mine_ref, give_ref, *, rows, bit, lead, early_index
):
    parity, rate = pair_rates(rate_ref, own_ref.shape[1])
    first = before_ref[...] + lead_leap(masks, lead, rate, rows, bit) * got_ref[...].astype(f32)
    early, _ = early_late(parity, own_ref[...], other_ref[...])
    second = early + leap(masks, early_index, rate, rows) * first
    give, mine = early_late(parity, second, first)
    mine_ref[...] = mine
    give_ref[...] = give


def final_kernel(
    masks, state_ref, enter_ref, near_ref, short_ref, resid_ref, rim_ref, taps_ref, rate_ref, weight_ref, *refs,
    span, modes, channels, most, chunk, own,
):
    if own:
        hidden_out, whole, sums, hidden_ref, sems, wide, tables, starts_at = refs
    elif channels:
        gain_ref, _, _, _, hidden_out, whole, sums, normed_out, hidden_ref, sems, wide, tables, starts_at, normed_ref = refs
    else:
        _, _, _, hidden_out, whole, sums, hidden_ref, sems, wide, tables, starts_at = refs
    chans = resid_ref.shape[1]
    half = chans // 2
    first = half_start(chans, own)
    at = Masks(span)

    def store(c):
        here = pl.ds(pl.multiple_of(c * chunk, chunk), chunk)
        there = pl.ds(pl.multiple_of(first + c * chunk, chunk), chunk)
        return pltpu.make_async_copy(hidden_ref.at[:, here], hidden_out.at[:, there], sems.at[0, c])

    def store_normed(c):
        return cols_copy(normed_ref, normed_out, sems.at[1], c, chunk)

    if own:
        sums[...] = jnp.zeros(sums.shape, f32)

    def group(lanes):
        for slot, lane in enumerate(lanes):
            state = enter_ref[:, cols_of(pl.multiple_of(lane - first, LANES))]
            rate = rate_ref[:, cols_of(lane)]
            weight = weight_ref[:, cols_of(lane)]
            tables[slot] = jnp.exp(-rate)
            leap = jnp.exp(-float(span) * rate)
            for b in range(SUBS):
                starts_at[slot, pl.ds(b * (modes + 1), modes), :] = weight * state
                if b < SUBS - 1:
                    state = (leap * twice(masks[at.passes + b], modes)) * state + sub_state(state_ref, lane, b, modes)
        for slot, lane in enumerate(lanes):
            part = [starts_at[slot, pl.ds(n, SUBS, stride=modes + 1), :] for n in range(modes)]
            decay = [row_of(tables.at[slot], n) for n in range(modes)]
            rim = rim_ref[0, :, cols_of(lane)].astype(f32)
            tap = taps_ref[0, :, cols_of(lane)]
            edge = [
                (tap[1:2] * rim[1:2]) * masks[at.edges] + (tap[2:3] * rim[0:1]) * masks[at.edges + 1],
                (tap[2:3] * rim[1:2]) * masks[at.edges + 2],
            ]
            for j in range(span):
                part = [part[n] * decay[n] for n in range(modes)]
                total = part
                while len(total) > 1:
                    total = [total[m] + total[m + 1] for m in range(0, len(total), 2)]
                conv = near_ref[pl.ds(j * SUBS, SUBS), cols_of(lane)] + total[0] * masks[at.enter + j]
                conv = conv.astype(bf16).astype(f32)
                short = short_ref[pl.ds(j * SUBS, SUBS), cols_of(lane)]
                if j < 2:
                    short = short + edge[j]
                wide[slot, pl.ds(j, SUBS, stride=span + 1), :] = short * conv
        for b in range(SUBS):
            rows = pl.ds(b * span, span)
            squares = sums[rows, :]
            for slot, lane in enumerate(lanes):
                hidden = wide[slot, pl.ds(b * (span + 1), span), :] + resid_ref[rows, cols_of(lane)].astype(f32)
                whole[lax.div(lane, LANES), rows, :] = hidden
                hidden_ref[rows, cols_of(pl.multiple_of(lane - first, LANES))] = hidden.astype(bf16)
                squares = squares + hidden * hidden
            sums[rows, :] = squares

    each_chunk(
        half,
        chunk,
        lambda c: None,
        lambda lanes: group([pl.multiple_of(first + lane, LANES) for lane in lanes]),
        lambda c: store(c).start(),
        most,
    )
    if channels and not own:
        inverse = lax.rsqrt(jnp.sum(sums[...], axis=1, keepdims=True) / channels + 1e-06)
        sums[...] = jnp.broadcast_to(inverse, sums.shape)

        def scale(lanes):
            for lane in lanes:
                normed = whole[lax.div(lane, LANES)] * sums[...] * gain_ref[:, cols_of(lane)]
                normed_ref[:, cols_of(lane)] = normed.astype(bf16)

        each_chunk(chans, chunk, lambda c: None, scale, lambda c: store_normed(c).start(), 4)
        for c in range(chans // chunk):
            store_normed(c).wait()
    for c in range(half // chunk):
        store(c).wait()


def shards(
    query_in, key_in, value_in, short_taps, decay_rate, residues, doc_lengths, residual, norm_gain
):
    tok_rows, chans = query_in.shape
    modes = decay_rate.shape[0]
    span = tok_rows // SUBS
    blocks = lax.axis_size("ctx")
    grp = lax.axis_size("grp")
    chunk = min(chans // 2, 1024)
    pieces = chans // chunk
    ctx_index = lax.axis_index("ctx")
    base = (ctx_index * tok_rows).astype(jnp.int32).reshape(1)
    weight = residues * jnp.sqrt(-jnp.expm1(-2.0 * decay_rate))

    smem = pl.BlockSpec(memory_space=pltpu.SMEM)
    vmem = pl.BlockSpec(memory_space=pltpu.VMEM)
    hbm = pl.BlockSpec(memory_space=pltpu.HBM)
    tile_shape = (SUBS, LANES)
    wide_rows = SUBS * (span + 1)
    params = pltpu.CompilerParams(vmem_limit_bytes=16 * MIB)

    lengths = pltpu.with_memory_space_constraint(doc_lengths, pltpu.HBM)

    def near_by(x):
        return pltpu.with_memory_space_constraint(x, pltpu.VMEM)

    def far_off(x):
        return pltpu.with_memory_space_constraint(x, pltpu.HBM)

    def copies(kinds):
        return pltpu.SemaphoreType.DMA((kinds, pieces))

    def cost(per_tile, moved):
        return pl.CostEstimate(flops=per_tile * (chans // LANES) * SUBS * LANES, bytes_accessed=moved, transcendentals=0)

    tails = pl.pallas_call(
        tail_kernel,
        in_specs=[hbm, hbm, hbm],
        out_specs=vmem,
        out_shape=pltpu.VMEM((3, 2, chans), bf16),
        scratch_shapes=[pltpu.VMEM((3, 16, chans), bf16), pltpu.SemaphoreType.DMA((3,))],
        compiler_params=params,
        name="tails",
    )(far_off(query_in), far_off(key_in), far_off(value_in))
    rim_rows = from_behind(tails, "ctx", 1)
    levels = max(1, (blocks // 4).bit_length() - 2)
    mask_shape = (Masks(span).count(levels),) + tile_shape

    def query_piece(part, masks, before):
        count = chans // 2
        scratch = [
            pltpu.VMEM((tok_rows, count), bf16),
            pltpu.SemaphoreType.DMA((count // chunk,)),
            pltpu.VMEM((Q_TILES, wide_rows, LANES), f32),
        ]
        out_shape = [pltpu.VMEM((tok_rows, chans), f32)]
        if part == 0:
            operands = [base, lengths, far_off(query_in), near_by(short_taps), far_off(value_in)]
            in_specs = [smem, smem, hbm, vmem, hbm]
            out_shape += [pltpu.VMEM(mask_shape, f32), pltpu.VMEM((tok_rows, chans), bf16)]
            scratch.append(pltpu.SemaphoreType.DMA(()))
        else:
            operands = [near_by(masks), far_off(query_in), near_by(short_taps), near_by(before)]
            in_specs = [vmem, hbm, vmem, vmem]
        return pl.pallas_call(
            functools.partial(
                query_kernel, span=span, most=Q_TILES, chunk=chunk, levels=levels,
                first=part * count, count=count,
            ),
            in_specs=in_specs,
            out_specs=[vmem] * len(out_shape),
            out_shape=out_shape,
            scratch_shapes=scratch,
            input_output_aliases={3: 0} if part else {},
            compiler_params=params,
            cost_estimate=cost(100, 3 * tok_rows * chans),
            name="query_part_%d" % part,
        )(*operands)

    q_short, masks, values = query_piece(0, None, None)
    rim_rows, q_short, values = lax.optimization_barrier((rim_rows, q_short, values))
    rates, weights, taps, rims = near_by(decay_rate), near_by(weight), near_by(short_taps), near_by(rim_rows)
    kept = pltpu.VMEM((modes, chans // 2), f32)
    sent = pltpu.VMEM((modes, chans // 2), bf16)
    keys, values = near_by(key_in), near_by(values)

    def states_of(own, before):
        return pl.pallas_call(
            functools.partial(state_kernel, span=span, modes=modes, most=A_TILES, own=own),
            in_specs=[vmem] * (6 + len(before)),
            out_specs=[vmem] * 3,
            out_shape=[
                pltpu.VMEM((tok_rows, chans), bf16),
                pltpu.VMEM((chans // LANES, SUBS * (modes + 1), LANES), f32),
                kept,
            ],
            scratch_shapes=[
                pltpu.VMEM((A_TILES, wide_rows, LANES), f32),
                pltpu.VMEM((A_TILES, wide_rows, LANES), f32),
                pltpu.VMEM((A_TILES, modes, LANES), f32),
                pltpu.VMEM((A_TILES, span) + tile_shape, f32),
            ],
            input_output_aliases={6 + i: i for i in range(len(before))},
            compiler_params=params,
            cost_estimate=cost(500, 6 * tok_rows * chans),
            name="block_states_own" if own else "block_states_give",
        )(near_by(masks), keys, values, rims, taps, rates, *[near_by(x) for x in before])

    gates, states, give = states_of(False, [])
    got = swap(give, "ctx")
    gates, states, own = states_of(True, [gates, states])
    got, gates, states, own = lax.optimization_barrier((got, gates, states, own))

    def near_piece(part, near):
        count = chans // NEAR_PARTS
        before = [] if near is None else [near_by(near)]
        return pl.pallas_call(
            functools.partial(
                near_kernel, span=span, modes=modes, most=N_TILES, first=part * count, count=count
            ),
            in_specs=[vmem] * (4 + len(before)),
            out_specs=vmem,
            out_shape=pltpu.VMEM((tok_rows, chans), f32),
            scratch_shapes=[
                pltpu.VMEM((N_TILES, span * (SUBS + 1), LANES), f32),
                pltpu.VMEM((N_TILES, span, LANES), f32),
            ],
            compiler_params=params,
            input_output_aliases={4: 0} if before else {},
            cost_estimate=cost(600 // NEAR_PARTS, 7 * tok_rows * count),
            name="near_part_%d" % part,
        )(near_by(masks), near_by(gates), rates, weights, *before)

    got = swap(give, "ctx")

    at = Masks(span)

    def pair_call(kernel, operands, out_shape, name, extra=(), **static):
        return pl.pallas_call(
            functools.partial(kernel, **static),
            in_specs=[vmem] * (len(operands) + 2 + len(extra)),
            out_specs=[vmem] * len(out_shape),
            out_shape=out_shape,
            compiler_params=params,
            name=name,
        )(near_by(masks), *[near_by(x) for x in operands], rates, *[near_by(x) for x in extra])

    total, ends = pair_call(pair_kernel, [own, got], [kept, sent], "pair_ends", rows=tok_rows, index=at.late)
    entering, near = [], None
    for m in range(levels):
        met = swap(ends, "ctx", 2 << m)
        if m < NEAR_PARTS:
            near = near_piece(m, near)
            met, near = lax.optimization_barrier((met, near))
        total, ends, enter = pair_call(
            level_kernel,
            [total, met],
            [kept, sent, kept],
            "level_%d" % m,
            extra=entering,
            rows=tok_rows,
            level=m,
            lead=at.lead(m),
            later=at.later(m),
        )
        entering = [enter]
    on = from_behind(ends, "ctx", 2 << levels)
    for m in range(levels, NEAR_PARTS):
        near = near_piece(m, near)
    q_short = query_piece(1, masks, q_short)[0]
    on, q_short, near = lax.optimization_barrier((on, q_short, near))
    mine, give_back = pair_call(
        enter_kernel,
        entering + [on, own, got],
        [kept, kept],
        "pair_enter",
        rows=tok_rows,
        bit=2 << levels,
        lead=at.lead(levels),
        early_index=at.early,
    )
    got_back = swap(give_back, "ctx")

    alone = grp == 1
    resid = near_by(residual)

    def finish(own, enter, before):
        last = alone and not own
        out_specs = [hbm, vmem, vmem]
        out_shape = [
            jax.ShapeDtypeStruct((tok_rows, chans), bf16),
            pltpu.VMEM((chans // LANES, tok_rows, LANES), f32),
            pltpu.VMEM((tok_rows, LANES), f32),
        ]
        scratch = [
            pltpu.VMEM((tok_rows, chans // 2), bf16),
            copies(2),
            pltpu.VMEM((F_TILES, wide_rows, LANES), f32),
            pltpu.VMEM((F_TILES, modes, LANES), f32),
            pltpu.VMEM((F_TILES, SUBS * (modes + 1), LANES), f32),
        ]
        operands = [near_by(x) for x in (masks, states, enter, near, q_short)] + [resid, rims, taps, rates, weights]
        if last:
            operands.append(near_by(norm_gain.reshape(1, chans)))
            out_specs.append(hbm)
            out_shape.append(jax.ShapeDtypeStruct((tok_rows, chans), bf16))
            scratch.append(pltpu.VMEM((tok_rows, chans), bf16))
        count = len(operands)
        in_specs = [vmem] * count
        if before:
            operands += [far_off(before[0]), near_by(before[1]), near_by(before[2])]
            in_specs += [hbm, vmem, vmem]
        return pl.pallas_call(
            functools.partial(
                final_kernel, span=span, modes=modes, channels=chans if alone else 0, most=F_TILES, chunk=chunk, own=own
            ),
            in_specs=in_specs,
            out_specs=out_specs,
            out_shape=out_shape,
            scratch_shapes=scratch,
            input_output_aliases={count + i: i for i in range(len(before))},
            compiler_params=params,
            cost_estimate=cost(450, 9 * tok_rows * chans),
            name="far_part_own" if own else "far_part_other",
        )(*operands)

    before = finish(True, mine, [])
    got_back, *before = lax.optimization_barrier((got_back, *before))
    outs = finish(False, got_back, before)
    if alone:
        return (outs[0], outs[3])
    hidden_out, whole, sums = outs
    hidden = whole.transpose(1, 0, 2).reshape(tok_rows, chans)
    square_sum = lax.psum(jnp.sum(sums, axis=1), "grp")
    inverse_rms = lax.rsqrt(square_sum / (chans * grp) + 1e-06)
    normed = (hidden * inverse_rms[:, None] * norm_gain[None, :]).astype(bf16)
    return (hidden_out, normed)


def solution(mesh):
    return jax.shard_map(
        shards,
        mesh=mesh,
        in_specs=(
            P("ctx", "grp"),
            P("ctx", "grp"),
            P("ctx", "grp"),
            P(None, None, "grp"),
            P(None, "grp"),
            P(None, "grp"),
            P(),
            P("ctx", "grp"),
            P("grp"),
        ),
        out_specs=(P("ctx", "grp"), P("ctx", "grp")),
        check_vma=False,
    )
```

```python
import functools
import math

import jax
import jax.numpy as jnp
from jax import lax
from jax.experimental import pallas as pl
from jax.experimental.pallas import tpu as pltpu
from jax.sharding import PartitionSpec as P

SUBS = 8
LANES = 128
MIB = 1024 * 1024
A_TILES, N_TILES, Q_TILES, F_TILES = 2, 2, 4, 4
NEAR_PARTS = 2
f32 = jnp.float32
bf16 = jnp.bfloat16


def swap(shard, axis, bit=1):
    return lax.ppermute(shard, axis, [(i, i ^ bit) for i in range(lax.axis_size(axis))])


def swap_across(shard, axis, size):
    count = lax.axis_size(axis)
    pairs = [(i, i + size) for i in range(count - size) if (i // size) % 2 == 1]
    return lax.ppermute(shard, axis, pairs + [(j, i) for i, j in pairs])


def doc_start_rows(len_ref, base, span):
    rows = lax.broadcasted_iota(jnp.int32, (SUBS, LANES), 0) * span + base
    starts = [jnp.int32(0)]
    for d in range(len_ref.shape[0] - 1):
        starts.append(starts[-1] + len_ref[d])
    out = []
    for j in range(span):
        pos = rows + j
        best = jnp.zeros((SUBS, LANES), jnp.int32)
        for start in starts[1:]:
            best = jnp.where(pos >= start, start, best)
        out.append(best)
    return rows, out


def flag(cond):
    return jnp.where(cond, 1.0, 0.0).astype(f32)


def each_group(count, most, group):
    size = math.gcd(count, most)

    def step(i, carry):
        group([pl.multiple_of((i * size + m) * LANES, LANES) for m in range(size)])
        return carry

    lax.fori_loop(0, count // size, step, 0)


def each_chunk(chans, chunk, before, group, after, most):
    def step(c, carry):
        before(c)

        def inner(lanes):
            group([pl.multiple_of(c * chunk + lane, LANES) for lane in lanes])

        each_group(chunk // LANES, most, inner)
        after(c)
        return carry

    lax.fori_loop(0, chans // chunk, step, 0)


def cols_copy(src, dst, sem, c, chunk):
    cols = pl.ds(pl.multiple_of(c * chunk, chunk), chunk)
    return pltpu.make_async_copy(src.at[:, cols], dst.at[:, cols], sem.at[c])


def cols_of(lane):
    return pl.ds(lane, LANES)


def row_of(ref, index):
    return ref[pl.ds(index, SUBS, stride=0), :]


def spread(x, wide, span):
    x = x.astype(f32)
    for b in range(SUBS):
        wide[pl.ds(b * (span + 1), span), :] = x[b * span : (b + 1) * span]


class Conv:
    def __init__(self, wide, rim, taps, span):
        self.wide, self.span = wide, span
        self.taps = [jnp.broadcast_to(taps[m : m + 1], (SUBS, LANES)) for m in range(3)]
        top = lax.broadcasted_iota(jnp.int32, (SUBS, LANES), 0) == 0
        ahead = [0.0, 0.0] if rim is None else [jnp.broadcast_to(rim[m : m + 1], (SUBS, LANES)) for m in range(2)]
        self.behind = [jnp.where(top, ahead[m], pltpu.roll(self.row(span - 2 + m), 1, 0)) for m in range(2)]

    def row(self, j):
        return self.wide[pl.ds(j, SUBS, stride=self.span + 1), :]

    def step(self, j, keep_one, keep_two):
        here = self.row(j)
        two, one = self.behind
        self.behind = [one, here]
        return self.taps[0] * here + (self.taps[1] * one) * keep_one + (self.taps[2] * two) * keep_two


def rim_of(even_ref, odd_ref, index, cols):
    odd = jnp.full((2, LANES), lax.rem(lax.axis_index("ctx"), 2), jnp.int32) == 1
    return jnp.where(odd, odd_ref[index, :, cols].astype(f32), even_ref[index, :, cols].astype(f32))


def half_start(chans, own):
    parity = lax.rem(lax.axis_index("ctx"), 2)
    return pl.multiple_of((parity if own else 1 - parity) * (chans // 2), LANES)


def twice(mask, modes):
    return jnp.concatenate([mask] * (modes // SUBS), axis=0)


def sub_state(state_ref, lane, b, modes):
    return state_ref[lax.div(lane, LANES), pl.ds(b * (modes + 1), modes), :]


def state_kernel(
    masks, key_ref, value_ref, even_ref, odd_ref, taps_ref, rate_ref, *refs, span, modes, most, own
):
    gate_ref, state_ref, end_ref, wide_k, wide_v, tables, held = refs[-7:]
    half = key_ref.shape[1] // 2
    first = half_start(2 * half, own)
    at = Masks(span)

    def group(lanes):
        for slot, lane in enumerate(lanes):
            spread(key_ref[:, cols_of(lane)], wide_k.at[slot], span)
            spread(value_ref[:, cols_of(lane)], wide_v.at[slot], span)
            rate = rate_ref[:, cols_of(lane)]
            tables[slot] = jnp.exp(-rate)
        convs = [
            [
                Conv(wide.at[slot], rim_of(even_ref, odd_ref, i, cols_of(lane)), taps_ref[i, :, cols_of(lane)], span)
                for i, wide in ((1, wide_k), (2, wide_v))
            ]
            for slot, lane in enumerate(lanes)
        ]
        last = [None] * len(lanes)
        for j in range(span):
            keep_one, keep_two = masks[at.one + j], masks[at.two + j]
            for slot, lane in enumerate(lanes):
                k_short, v_short = [conv.step(j, keep_one, keep_two) for conv in convs[slot]]
                if j % 2 == 0:
                    last[slot] = k_short * v_short
                    continue
                pair = jnp.concatenate([last[slot], k_short * v_short], axis=0).astype(bf16)
                gate_ref[pl.ds((j - 1) * SUBS, 2 * SUBS), cols_of(lane)] = pair
                pair = pair.astype(f32)
                held[slot, j - 1] = pair[:SUBS] * masks[at.last + j - 1]
                held[slot, j] = pair[SUBS:] * masks[at.last + j]
        for slot, lane in enumerate(lanes):
            decay = [row_of(tables.at[slot], n) for n in range(modes)]
            state = [held[slot, 0]] * modes
            for j in range(1, span):
                gate = held[slot, j]
                state = [decay[n] * state[n] + gate for n in range(modes)]
            for n in range(modes):
                state_ref[lax.div(lane, LANES), pl.ds(n, SUBS, stride=modes + 1), :] = state[n]
        for slot, lane in enumerate(lanes):
            leap = jnp.exp(-float(span) * rate_ref[:, cols_of(lane)])
            end = sub_state(state_ref, lane, 0, modes)
            for b in range(1, SUBS):
                end = (leap * twice(masks[at.passes + b], modes)) * end + sub_state(state_ref, lane, b, modes)
            end_ref[:, cols_of(pl.multiple_of(lane - first, LANES))] = end

    each_group(half // LANES, most, lambda lanes: group([pl.multiple_of(first + lane, LANES) for lane in lanes]))


def tail_kernel(query_ref, key_ref, value_ref, tail_ref, bufs, sems):
    rows, count = query_ref.shape[0], bufs.shape[1]
    copies = [
        pltpu.make_async_copy(ref.at[pl.ds(rows - count, count)], bufs.at[i], sems.at[i])
        for i, ref in enumerate((query_ref, key_ref, value_ref))
    ]
    for copy in copies:
        copy.start()
    for i, copy in enumerate(copies):
        copy.wait()
        tail_ref[i] = bufs[i].astype(f32)[count - 2 :].astype(bf16)


def unbroken(len_ref, first, count):
    start = jnp.int32(0)
    whole = jnp.where((first <= 0) & (first + count > 0), 0.0, 1.0)
    for d in range(len_ref.shape[0] - 1):
        start = start + len_ref[d]
        whole = jnp.where((start >= first) & (start < first + count), 0.0, whole)
    return whole.astype(f32)


class Masks:
    def __init__(self, span):
        self.one, self.two, self.last, self.enter = 0, span, 2 * span, 3 * span
        self.passes = 4 * span
        self.edges = self.passes + SUBS
        self.late = self.edges + 3
        self.early = self.late + 1
        self.levels = self.late + 2

    def lead(self, level):
        return self.levels + 2 * level

    def later(self, level):
        return self.levels + 2 * level + 1

    def count(self, levels):
        return self.levels + 2 * levels + 1


def write_masks(base_ref, len_ref, masks, span, levels):
    at = Masks(span)
    rows, starts = doc_start_rows(len_ref, base_ref[0], span)
    for j in range(span):
        masks[at.one + j] = flag(starts[j] < rows + j)
        masks[at.two + j] = flag(starts[j] < rows + (j - 1))
        masks[at.last + j] = flag(starts[span - 1] <= rows + j)
        masks[at.enter + j] = flag(starts[j] < rows)
    top = flag(lax.broadcasted_iota(jnp.int32, (SUBS, LANES), 0) == 0)
    masks[at.edges] = top * masks[at.one]
    masks[at.edges + 1] = top * masks[at.two]
    masks[at.edges + 2] = top * masks[at.two + 1]
    size = SUBS * span
    parity = lax.rem(lax.div(base_ref[0], size), 2)
    pair_at = base_ref[0] - parity * size
    ranges = [(base_ref[0] + b * span, span) for b in range(SUBS)]
    flags = [at.passes + b for b in range(SUBS)]
    ranges += [(pair_at + size, size), (pair_at, size)]
    flags += [at.late, at.early]
    for m in range(levels + 1):
        group = 2 * size << m
        group_at = base_ref[0] - lax.rem(base_ref[0], group)
        ranges.append((group_at, pair_at - group_at))
        flags.append(at.lead(m))
        if m < levels:
            ranges.append((group_at + group * (1 - lax.rem(lax.div(base_ref[0], group), 2)), group))
            flags.append(at.later(m))
    for index, (first, count) in zip(flags, ranges):
        masks[index] = jnp.full((SUBS, LANES), unbroken(len_ref, first, count), f32)


def near_kernel(masks, gate_ref, rate_ref, weight_ref, *refs, span, modes, most, first, count):
    near_ref, sums, tap_rows = refs[-3:]
    at = Masks(span)

    def group(lanes):
        for slot, lane in enumerate(lanes):
            decay = jnp.exp(-rate_ref[:, cols_of(lane)])
            term = weight_ref[:, cols_of(lane)]
            for lag in range(span):
                part = term[:SUBS]
                for n in range(SUBS, modes, SUBS):
                    part = part + term[n : n + SUBS]
                sums[slot, pl.ds(lag * (SUBS + 1), SUBS), :] = part
                term = term * decay
        for slot in range(len(lanes)):
            for first_lag in range(0, span, SUBS):
                total = [
                    sums[slot, pl.ds(first_lag * (SUBS + 1) + m, SUBS, stride=SUBS + 1), :] for m in range(SUBS)
                ]
                while len(total) > 1:
                    total = [total[m] + total[m + 1] for m in range(0, len(total), 2)]
                tap_rows[slot, pl.ds(first_lag, SUBS), :] = total[0]
        taps = [[row_of(tap_rows.at[slot], lag) for lag in range(span)] for slot in range(len(lanes))]
        for parts, lane in zip(taps, lanes):
            live = []
            for j in range(span):
                if j % 2 == 0:
                    pair = gate_ref[pl.ds(j * SUBS, 2 * SUBS), cols_of(lane)].astype(f32)
                keep = masks[at.one + j]
                live = [g * keep for g in live]
                live.append(pair[(j % 2) * SUBS : (j % 2 + 1) * SUBS])
                total = parts[0] * live[j]
                for lag in range(1, j + 1):
                    total = total + parts[lag] * live[j - lag]
                near_ref[pl.ds(j * SUBS, SUBS), cols_of(lane)] = total

    each_group(count // LANES, most, lambda lanes: group([pl.multiple_of(first + lane, LANES) for lane in lanes]))


def query_kernel(*refs, span, most, chunk, levels, first, count):
    if not first:
        base_ref, len_ref, query_ref, taps_ref, value_in, short_ref, masks, value_ref, query_buf, sems, wide_q, value_sem = refs
        value_copy = pltpu.make_async_copy(value_in, value_ref, value_sem)
    else:
        masks, query_ref, taps_ref, _, short_ref, query_buf, sems, wide_q = refs

    def fetch(c):
        there = pl.ds(first + c * chunk if isinstance(c, int) else pl.multiple_of(first + c * chunk, chunk), chunk)
        here = pl.ds(c * chunk if isinstance(c, int) else pl.multiple_of(c * chunk, chunk), chunk)
        return pltpu.make_async_copy(query_ref.at[:, there], query_buf.at[:, here], sems.at[c])

    for c in range(count // chunk):
        fetch(c).start()
    if not first:
        value_copy.start()
        write_masks(base_ref, len_ref, masks, span, levels)
    at = Masks(span)

    def group(lanes):
        for slot, lane in enumerate(lanes):
            spread(query_buf[:, cols_of(lane)], wide_q.at[slot], span)
        convs = [
            Conv(wide_q.at[slot], None, taps_ref[0, :, cols_of(pl.multiple_of(first + lane, LANES))], span)
            for slot, lane in enumerate(lanes)
        ]
        for j in range(span):
            keep_one, keep_two = masks[at.one + j], masks[at.two + j]
            for slot, lane in enumerate(lanes):
                short_ref[pl.ds(j * SUBS, SUBS), cols_of(pl.multiple_of(first + lane, LANES))] = convs[slot].step(j, keep_one, keep_two)

    each_chunk(count, chunk, lambda c: fetch(c).wait(), group, lambda c: None, most)
    if not first:
        value_copy.wait()


def pair_rates(rate_ref, count):
    parity = lax.rem(lax.axis_index("ctx"), 2)
    return parity, rate_ref[:, pl.ds(pl.multiple_of(parity * count, LANES), count)]


def early_late(parity, own, got):
    odd = jnp.full(own.shape, parity, jnp.int32) == 1
    return jnp.where(odd, got, own), jnp.where(odd, own, got)


def leap(masks, index, rate, rows):
    return jnp.exp(-float(rows) * rate) * masks[index][0:1, 0:1]


def pair_kernel(masks, own_ref, got_ref, rate_ref, total_ref, sent_ref, *, rows, index):
    parity, rate = pair_rates(rate_ref, own_ref.shape[1])
    early, late = early_late(parity, own_ref[...], got_ref[...])
    total = late + leap(masks, index, rate, rows) * early
    total_ref[...] = total
    sent_ref[...] = total.astype(bf16)


def lead_leap(masks, index, rate, rows, bit):
    me = lax.axis_index("ctx")
    lead = (lax.rem(me, bit) - lax.rem(me, 2)) * rows
    return jnp.exp(rate * -lead.astype(f32)) * masks[index][0:1, 0:1]


def level_kernel(masks, total_ref, got_ref, rate_ref, *refs, rows, level, lead, later):
    before_ref = refs[0] if level else None
    sent_ref, enter_ref, *new_ref = refs[1 if level else 0 :]
    _, rate = pair_rates(rate_ref, total_ref.shape[1])
    bit = 2 << level
    after = lax.rem(lax.div(lax.axis_index("ctx"), bit), 2)
    got = got_ref[...].astype(f32)
    early, late = early_late(after, total_ref[...], got)
    total = late + leap(masks, later, rate, bit * rows) * early
    for ref in new_ref:
        ref[...] = total
    sent_ref[...] = total.astype(bf16)
    entering = jnp.where(jnp.full(got.shape, after, jnp.int32) == 1, got, 0.0) * lead_leap(masks, lead, rate, rows, bit)
    enter_ref[...] = entering if before_ref is None else before_ref[...] + entering


def enter_kernel(
    masks, before_ref, even_ref, odd_ref, own_ref, other_ref, rate_ref, mine_ref, give_ref, *, rows, bit, lead, early_index
):
    parity, rate = pair_rates(rate_ref, own_ref.shape[1])
    group = jnp.full(own_ref.shape, lax.div(lax.axis_index("ctx"), bit), jnp.int32)
    got = jnp.where(lax.rem(group, 2) == 1, odd_ref[...].astype(f32), even_ref[...].astype(f32))
    got = jnp.where(group == 0, 0.0, got)
    first = before_ref[...] + lead_leap(masks, lead, rate, rows, bit) * got
    early, _ = early_late(parity, own_ref[...], other_ref[...])
    second = early + leap(masks, early_index, rate, rows) * first
    give, mine = early_late(parity, second, first)
    mine_ref[...] = mine
    give_ref[...] = give


def final_kernel(
    masks, state_ref, enter_ref, near_ref, short_ref, resid_ref, even_ref, odd_ref, taps_ref, rate_ref, weight_ref, *refs,
    span, modes, channels, most, chunk, own,
):
    if own:
        hidden_out, whole, sums, hidden_ref, sems, wide, tables, starts_at = refs
    elif channels:
        gain_ref, _, _, _, hidden_out, whole, sums, normed_out, hidden_ref, sems, wide, tables, starts_at, normed_ref = refs
    else:
        _, _, _, hidden_out, whole, sums, hidden_ref, sems, wide, tables, starts_at = refs
    chans = resid_ref.shape[1]
    half = chans // 2
    first = half_start(chans, own)
    at = Masks(span)

    def store(c):
        here = pl.ds(pl.multiple_of(c * chunk, chunk), chunk)
        there = pl.ds(pl.multiple_of(first + c * chunk, chunk), chunk)
        return pltpu.make_async_copy(hidden_ref.at[:, here], hidden_out.at[:, there], sems.at[0, c])

    def store_normed(c):
        return cols_copy(normed_ref, normed_out, sems.at[1], c, chunk)

    if own:
        sums[...] = jnp.zeros(sums.shape, f32)

    def group(lanes):
        for slot, lane in enumerate(lanes):
            state = enter_ref[:, cols_of(pl.multiple_of(lane - first, LANES))]
            rate = rate_ref[:, cols_of(lane)]
            weight = weight_ref[:, cols_of(lane)]
            tables[slot] = jnp.exp(-rate)
            leap = jnp.exp(-float(span) * rate)
            for b in range(SUBS):
                starts_at[slot, pl.ds(b * (modes + 1), modes), :] = weight * state
                if b < SUBS - 1:
                    state = (leap * twice(masks[at.passes + b], modes)) * state + sub_state(state_ref, lane, b, modes)
        for slot, lane in enumerate(lanes):
            part = [starts_at[slot, pl.ds(n, SUBS, stride=modes + 1), :] for n in range(modes)]
            decay = [row_of(tables.at[slot], n) for n in range(modes)]
            rim = rim_of(even_ref, odd_ref, 0, cols_of(lane))
            tap = taps_ref[0, :, cols_of(lane)]
            edge = [
                (tap[1:2] * rim[1:2]) * masks[at.edges] + (tap[2:3] * rim[0:1]) * masks[at.edges + 1],
                (tap[2:3] * rim[1:2]) * masks[at.edges + 2],
            ]
            for j in range(span):
                part = [part[n] * decay[n] for n in range(modes)]
                total = part
                while len(total) > 1:
                    total = [total[m] + total[m + 1] for m in range(0, len(total), 2)]
                conv = near_ref[pl.ds(j * SUBS, SUBS), cols_of(lane)] + total[0] * masks[at.enter + j]
                conv = conv.astype(bf16).astype(f32)
                short = short_ref[pl.ds(j * SUBS, SUBS), cols_of(lane)]
                if j < 2:
                    short = short + edge[j]
                wide[slot, pl.ds(j, SUBS, stride=span + 1), :] = short * conv
        for b in range(SUBS):
            rows = pl.ds(b * span, span)
            squares = sums[rows, :]
            for slot, lane in enumerate(lanes):
                hidden = wide[slot, pl.ds(b * (span + 1), span), :] + resid_ref[rows, cols_of(lane)].astype(f32)
                whole[lax.div(lane, LANES), rows, :] = hidden
                hidden_ref[rows, cols_of(pl.multiple_of(lane - first, LANES))] = hidden.astype(bf16)
                squares = squares + hidden * hidden
            sums[rows, :] = squares

    each_chunk(
        half,
        chunk,
        lambda c: None,
        lambda lanes: group([pl.multiple_of(first + lane, LANES) for lane in lanes]),
        lambda c: store(c).start(),
        most,
    )
    if channels and not own:
        inverse = lax.rsqrt(jnp.sum(sums[...], axis=1, keepdims=True) / channels + 1e-06)
        sums[...] = jnp.broadcast_to(inverse, sums.shape)

        def scale(lanes):
            for lane in lanes:
                normed = whole[lax.div(lane, LANES)] * sums[...] * gain_ref[:, cols_of(lane)]
                normed_ref[:, cols_of(lane)] = normed.astype(bf16)

        each_chunk(chans, chunk, lambda c: None, scale, lambda c: store_normed(c).start(), 4)
        for c in range(chans // chunk):
            store_normed(c).wait()
    for c in range(half // chunk):
        store(c).wait()


def shards(
    query_in, key_in, value_in, short_taps, decay_rate, residues, doc_lengths, residual, norm_gain
):
    tok_rows, chans = query_in.shape
    modes = decay_rate.shape[0]
    span = tok_rows // SUBS
    blocks = lax.axis_size("ctx")
    grp = lax.axis_size("grp")
    chunk = min(chans // 2, 1024)
    pieces = chans // chunk
    ctx_index = lax.axis_index("ctx")
    base = (ctx_index * tok_rows).astype(jnp.int32).reshape(1)
    weight = residues * jnp.sqrt(-jnp.expm1(-2.0 * decay_rate))

    smem = pl.BlockSpec(memory_space=pltpu.SMEM)
    vmem = pl.BlockSpec(memory_space=pltpu.VMEM)
    hbm = pl.BlockSpec(memory_space=pltpu.HBM)
    tile_shape = (SUBS, LANES)
    wide_rows = SUBS * (span + 1)
    params = pltpu.CompilerParams(vmem_limit_bytes=16 * MIB)

    lengths = pltpu.with_memory_space_constraint(doc_lengths, pltpu.HBM)

    def near_by(x):
        return pltpu.with_memory_space_constraint(x, pltpu.VMEM)

    def far_off(x):
        return pltpu.with_memory_space_constraint(x, pltpu.HBM)

    def copies(kinds):
        return pltpu.SemaphoreType.DMA((kinds, pieces))

    def cost(per_tile, moved):
        return pl.CostEstimate(flops=per_tile * (chans // LANES) * SUBS * LANES, bytes_accessed=moved, transcendentals=0)

    tails = pl.pallas_call(
        tail_kernel,
        in_specs=[hbm, hbm, hbm],
        out_specs=vmem,
        out_shape=pltpu.VMEM((3, 2, chans), bf16),
        scratch_shapes=[pltpu.VMEM((3, 16, chans), bf16), pltpu.SemaphoreType.DMA((3,))],
        compiler_params=params,
        name="tails",
    )(far_off(query_in), far_off(key_in), far_off(value_in))
    rims = (swap_across(tails, "ctx", 1), swap(tails, "ctx"))
    levels = max(1, (blocks // 4).bit_length() - 2)
    mask_shape = (Masks(span).count(levels),) + tile_shape

    def query_piece(part, masks, before):
        count = chans // 2
        scratch = [
            pltpu.VMEM((tok_rows, count), bf16),
            pltpu.SemaphoreType.DMA((count // chunk,)),
            pltpu.VMEM((Q_TILES, wide_rows, LANES), f32),
        ]
        out_shape = [pltpu.VMEM((tok_rows, chans), f32)]
        if part == 0:
            operands = [base, lengths, far_off(query_in), near_by(short_taps), far_off(value_in)]
            in_specs = [smem, smem, hbm, vmem, hbm]
            out_shape += [pltpu.VMEM(mask_shape, f32), pltpu.VMEM((tok_rows, chans), bf16)]
            scratch.append(pltpu.SemaphoreType.DMA(()))
        else:
            operands = [near_by(masks), far_off(query_in), near_by(short_taps), near_by(before)]
            in_specs = [vmem, hbm, vmem, vmem]
        return pl.pallas_call(
            functools.partial(
                query_kernel, span=span, most=Q_TILES, chunk=chunk, levels=levels,
                first=part * count, count=count,
            ),
            in_specs=in_specs,
            out_specs=[vmem] * len(out_shape),
            out_shape=out_shape,
            scratch_shapes=scratch,
            input_output_aliases={3: 0} if part else {},
            compiler_params=params,
            cost_estimate=cost(100, 3 * tok_rows * chans),
            name="query_part_%d" % part,
        )(*operands)

    q_short, masks, values = query_piece(0, None, None)
    rims, q_short, values = lax.optimization_barrier((rims, q_short, values))
    rates, weights, taps, rims = near_by(decay_rate), near_by(weight), near_by(short_taps), [near_by(x) for x in rims]
    kept = pltpu.VMEM((modes, chans // 2), f32)
    sent = pltpu.VMEM((modes, chans // 2), bf16)
    keys, values = near_by(key_in), near_by(values)

    def states_of(own, before):
        return pl.pallas_call(
            functools.partial(state_kernel, span=span, modes=modes, most=A_TILES, own=own),
            in_specs=[vmem] * (7 + len(before)),
            out_specs=[vmem] * 3,
            out_shape=[
                pltpu.VMEM((tok_rows, chans), bf16),
                pltpu.VMEM((chans // LANES, SUBS * (modes + 1), LANES), f32),
                kept,
            ],
            scratch_shapes=[
                pltpu.VMEM((A_TILES, wide_rows, LANES), f32),
                pltpu.VMEM((A_TILES, wide_rows, LANES), f32),
                pltpu.VMEM((A_TILES, modes, LANES), f32),
                pltpu.VMEM((A_TILES, span) + tile_shape, f32),
            ],
            input_output_aliases={7 + i: i for i in range(len(before))},
            compiler_params=params,
            cost_estimate=cost(500, 6 * tok_rows * chans),
            name="block_states_own" if own else "block_states_give",
        )(near_by(masks), keys, values, *rims, taps, rates, *[near_by(x) for x in before])

    gates, states, give = states_of(False, [])
    got = swap(give, "ctx")
    gates, states, own = states_of(True, [gates, states])
    got, gates, states, own = lax.optimization_barrier((got, gates, states, own))

    def near_piece(part, near):
        count = chans // NEAR_PARTS
        before = [] if near is None else [near_by(near)]
        return pl.pallas_call(
            functools.partial(
                near_kernel, span=span, modes=modes, most=N_TILES, first=part * count, count=count
            ),
            in_specs=[vmem] * (4 + len(before)),
            out_specs=vmem,
            out_shape=pltpu.VMEM((tok_rows, chans), f32),
            scratch_shapes=[
                pltpu.VMEM((N_TILES, span * (SUBS + 1), LANES), f32),
                pltpu.VMEM((N_TILES, span, LANES), f32),
            ],
            compiler_params=params,
            input_output_aliases={4: 0} if before else {},
            cost_estimate=cost(600 // NEAR_PARTS, 7 * tok_rows * count),
            name="near_part_%d" % part,
        )(near_by(masks), near_by(gates), rates, weights, *before)

    got = swap(give, "ctx")

    at = Masks(span)

    def pair_call(kernel, operands, out_shape, name, extra=(), **static):
        return pl.pallas_call(
            functools.partial(kernel, **static),
            in_specs=[vmem] * (len(operands) + 2 + len(extra)),
            out_specs=[vmem] * len(out_shape),
            out_shape=out_shape,
            compiler_params=params,
            name=name,
        )(near_by(masks), *[near_by(x) for x in operands], rates, *[near_by(x) for x in extra])

    total, ends = pair_call(pair_kernel, [own, got], [kept, sent], "pair_ends", rows=tok_rows, index=at.late)
    entering, near = [], None
    for m in range(levels):
        met = swap(ends, "ctx", 2 << m)
        if m < NEAR_PARTS:
            near = near_piece(m, near)
            met, near = lax.optimization_barrier((met, near))
        ends, enter, *total = pair_call(
            level_kernel,
            [total, met],
            [sent, kept] + [kept] * (m < levels - 1),
            "level_%d" % m,
            extra=entering,
            rows=tok_rows,
            level=m,
            lead=at.lead(m),
            later=at.later(m),
        )
        entering = [enter]
        total = total[0] if total else None
    on = (swap_across(ends, "ctx", 2 << levels), swap(ends, "ctx", 2 << levels))
    for m in range(levels, NEAR_PARTS):
        near = near_piece(m, near)
    q_short = query_piece(1, masks, q_short)[0]
    on, q_short, near = lax.optimization_barrier((on, q_short, near))
    mine, give_back = pair_call(
        enter_kernel,
        entering + [*on, own, got],
        [kept, kept],
        "pair_enter",
        rows=tok_rows,
        bit=2 << levels,
        lead=at.lead(levels),
        early_index=at.early,
    )
    got_back = swap(give_back, "ctx")

    alone = grp == 1
    resid = near_by(residual)

    def finish(own, enter, before):
        last = alone and not own
        out_specs = [hbm, vmem, vmem]
        out_shape = [
            jax.ShapeDtypeStruct((tok_rows, chans), bf16),
            pltpu.VMEM((chans // LANES, tok_rows, LANES), f32),
            pltpu.VMEM((tok_rows, LANES), f32),
        ]
        scratch = [
            pltpu.VMEM((tok_rows, chans // 2), bf16),
            copies(2),
            pltpu.VMEM((F_TILES, wide_rows, LANES), f32),
            pltpu.VMEM((F_TILES, modes, LANES), f32),
            pltpu.VMEM((F_TILES, SUBS * (modes + 1), LANES), f32),
        ]
        operands = [near_by(x) for x in (masks, states, enter, near, q_short)] + [resid, *rims, taps, rates, weights]
        if last:
            operands.append(near_by(norm_gain.reshape(1, chans)))
            out_specs.append(hbm)
            out_shape.append(jax.ShapeDtypeStruct((tok_rows, chans), bf16))
            scratch.append(pltpu.VMEM((tok_rows, chans), bf16))
        count = len(operands)
        in_specs = [vmem] * count
        if before:
            operands += [far_off(before[0]), near_by(before[1]), near_by(before[2])]
            in_specs += [hbm, vmem, vmem]
        return pl.pallas_call(
            functools.partial(
                final_kernel, span=span, modes=modes, channels=chans if alone else 0, most=F_TILES, chunk=chunk, own=own
            ),
            in_specs=in_specs,
            out_specs=out_specs,
            out_shape=out_shape,
            scratch_shapes=scratch,
            input_output_aliases={count + i: i for i in range(len(before))},
            compiler_params=params,
            cost_estimate=cost(450, 9 * tok_rows * chans),
            name="far_part_own" if own else "far_part_other",
        )(*operands)

    before = finish(True, mine, [])
    got_back, *before = lax.optimization_barrier((got_back, *before))
    outs = finish(False, got_back, before)
    if alone:
        return (outs[0], outs[3])
    hidden_out, whole, sums = outs
    hidden = whole.transpose(1, 0, 2).reshape(tok_rows, chans)
    square_sum = lax.psum(jnp.sum(sums, axis=1), "grp")
    inverse_rms = lax.rsqrt(square_sum / (chans * grp) + 1e-06)
    normed = (hidden * inverse_rms[:, None] * norm_gain[None, :]).astype(bf16)
    return (hidden_out, normed)


def solution(mesh):
    return jax.shard_map(
        shards,
        mesh=mesh,
        in_specs=(
            P("ctx", "grp"),
            P("ctx", "grp"),
            P("ctx", "grp"),
            P(None, None, "grp"),
            P(None, "grp"),
            P(None, "grp"),
            P(),
            P("ctx", "grp"),
            P("grp"),
        ),
        out_specs=(P("ctx", "grp"), P("ctx", "grp")),
        check_vma=False,
    )
```

```python
import functools
import math

import jax
import jax.numpy as jnp
from jax import lax
from jax.experimental import pallas as pl
from jax.experimental.pallas import tpu as pltpu
from jax.sharding import PartitionSpec as P

SUBS = 8
LANES = 128
MIB = 1024 * 1024
A_TILES, N_TILES, Q_TILES, F_TILES = 2, 2, 4, 4
NEAR_PARTS = 2
f32 = jnp.float32
bf16 = jnp.bfloat16


def from_behind(shard, axis, by):
    count = lax.axis_size(axis)
    return lax.ppermute(shard, axis, [(i, i + by) for i in range(count - by)])


def swap(shard, axis, bit=1):
    return lax.ppermute(shard, axis, [(i, i ^ bit) for i in range(lax.axis_size(axis))])


def swap_across(shard, axis, size):
    count = lax.axis_size(axis)
    pairs = [(i, i + size) for i in range(count - size) if (i // size) % 2 == 1]
    return lax.ppermute(shard, axis, pairs + [(j, i) for i, j in pairs])


def doc_start_rows(len_ref, base, span):
    rows = lax.broadcasted_iota(jnp.int32, (SUBS, LANES), 0) * span + base
    starts = [jnp.int32(0)]
    for d in range(len_ref.shape[0] - 1):
        starts.append(starts[-1] + len_ref[d])
    out = []
    for j in range(span):
        pos = rows + j
        best = jnp.zeros((SUBS, LANES), jnp.int32)
        for start in starts[1:]:
            best = jnp.where(pos >= start, start, best)
        out.append(best)
    return rows, out


def flag(cond):
    return jnp.where(cond, 1.0, 0.0).astype(f32)


def each_group(count, most, group):
    size = math.gcd(count, most)

    def step(i, carry):
        group([pl.multiple_of((i * size + m) * LANES, LANES) for m in range(size)])
        return carry

    lax.fori_loop(0, count // size, step, 0)


def each_chunk(chans, chunk, before, group, after, most):
    def step(c, carry):
        before(c)

        def inner(lanes):
            group([pl.multiple_of(c * chunk + lane, LANES) for lane in lanes])

        each_group(chunk // LANES, most, inner)
        after(c)
        return carry

    lax.fori_loop(0, chans // chunk, step, 0)


def cols_copy(src, dst, sem, c, chunk):
    cols = pl.ds(pl.multiple_of(c * chunk, chunk), chunk)
    return pltpu.make_async_copy(src.at[:, cols], dst.at[:, cols], sem.at[c])


def cols_of(lane):
    return pl.ds(lane, LANES)


def row_of(ref, index):
    return ref[pl.ds(index, SUBS, stride=0), :]


def spread(x, wide, span):
    x = x.astype(f32)
    for b in range(SUBS):
        wide[pl.ds(b * (span + 1), span), :] = x[b * span : (b + 1) * span]


class Conv:
    def __init__(self, wide, rim, taps, span):
        self.wide, self.span = wide, span
        self.taps = [jnp.broadcast_to(taps[m : m + 1], (SUBS, LANES)) for m in range(3)]
        top = lax.broadcasted_iota(jnp.int32, (SUBS, LANES), 0) == 0
        ahead = [0.0, 0.0] if rim is None else [jnp.broadcast_to(rim[m : m + 1], (SUBS, LANES)) for m in range(2)]
        self.behind = [jnp.where(top, ahead[m], pltpu.roll(self.row(span - 2 + m), 1, 0)) for m in range(2)]

    def row(self, j):
        return self.wide[pl.ds(j, SUBS, stride=self.span + 1), :]

    def step(self, j, keep_one, keep_two):
        here = self.row(j)
        two, one = self.behind
        self.behind = [one, here]
        return self.taps[0] * here + (self.taps[1] * one) * keep_one + (self.taps[2] * two) * keep_two


def half_start(chans, own):
    parity = lax.rem(lax.axis_index("ctx"), 2)
    return pl.multiple_of((parity if own else 1 - parity) * (chans // 2), LANES)


def twice(mask, modes):
    return jnp.concatenate([mask] * (modes // SUBS), axis=0)


def sub_state(state_ref, lane, b, modes):
    return state_ref[lax.div(lane, LANES), pl.ds(b * (modes + 1), modes), :]


def state_kernel(masks, key_ref, value_ref, rim_ref, taps_ref, rate_ref, *refs, span, modes, most, own):
    if own:
        _, _, gate_ref, state_ref, end_ref, wide_k, wide_v, tables, held = refs
    else:
        key_in, value_in, gate_ref, state_ref, end_ref, key_own, value_own, wide_k, wide_v, tables, held, sems = refs
    half = key_ref.shape[1]
    first = half_start(2 * half, own)
    if not own:
        fetches = half_copies(key_in, value_in, key_own, value_own, sems, True)
        for copy in fetches:
            copy.start()
    at = Masks(span)

    def group(lanes):
        for slot, lane in enumerate(lanes):
            spread(key_ref[:, cols_of(pl.multiple_of(lane - first, LANES))], wide_k.at[slot], span)
            spread(value_ref[:, cols_of(pl.multiple_of(lane - first, LANES))], wide_v.at[slot], span)
            rate = rate_ref[:, cols_of(lane)]
            tables[slot] = jnp.exp(-rate)
        convs = [
            [
                Conv(wide.at[slot], rim_ref[i, :, cols_of(lane)].astype(f32), taps_ref[i, :, cols_of(lane)], span)
                for i, wide in ((1, wide_k), (2, wide_v))
            ]
            for slot, lane in enumerate(lanes)
        ]
        last = [None] * len(lanes)
        for j in range(span):
            keep_one, keep_two = masks[at.one + j], masks[at.two + j]
            for slot, lane in enumerate(lanes):
                k_short, v_short = [conv.step(j, keep_one, keep_two) for conv in convs[slot]]
                if j % 2 == 0:
                    last[slot] = k_short * v_short
                    continue
                pair = jnp.concatenate([last[slot], k_short * v_short], axis=0).astype(bf16)
                gate_ref[pl.ds((j - 1) * SUBS, 2 * SUBS), cols_of(lane)] = pair
                pair = pair.astype(f32)
                held[slot, j - 1] = pair[:SUBS] * masks[at.last + j - 1]
                held[slot, j] = pair[SUBS:] * masks[at.last + j]
        for slot, lane in enumerate(lanes):
            decay = [row_of(tables.at[slot], n) for n in range(modes)]
            state = [held[slot, 0]] * modes
            for j in range(1, span):
                gate = held[slot, j]
                state = [decay[n] * state[n] + gate for n in range(modes)]
            for n in range(modes):
                state_ref[lax.div(lane, LANES), pl.ds(n, SUBS, stride=modes + 1), :] = state[n]
        for slot, lane in enumerate(lanes):
            leap = jnp.exp(-float(span) * rate_ref[:, cols_of(lane)])
            end = sub_state(state_ref, lane, 0, modes)
            for b in range(1, SUBS):
                end = (leap * twice(masks[at.passes + b], modes)) * end + sub_state(state_ref, lane, b, modes)
            end_ref[:, cols_of(pl.multiple_of(lane - first, LANES))] = end

    each_group(half // LANES, most, lambda lanes: group([pl.multiple_of(first + lane, LANES) for lane in lanes]))
    if not own:
        for copy in fetches:
            copy.wait()


def half_copies(key_in, value_in, key_half, value_half, sems, own):
    cols = pl.ds(half_start(key_in.shape[1], own), key_half.shape[1])
    return [
        pltpu.make_async_copy(key_in.at[:, cols], key_half, sems.at[0]),
        pltpu.make_async_copy(value_in.at[:, cols], value_half, sems.at[1]),
    ]


def first_kernel(
    base_ref, len_ref, key_in, value_in, taps_in, rate_in, masks, key_give, value_give, taps_ref, rate_ref, sems,
    *, span, levels,
):
    copies = half_copies(key_in, value_in, key_give, value_give, sems, False)
    copies.append(pltpu.make_async_copy(taps_in, taps_ref, sems.at[2]))
    copies.append(pltpu.make_async_copy(rate_in, rate_ref, sems.at[3]))
    for copy in copies:
        copy.start()
    write_masks(base_ref, len_ref, masks, span, levels)
    for copy in copies:
        copy.wait()


def tail_kernel(query_ref, key_ref, value_ref, tail_ref, bufs, sems):
    rows, count = query_ref.shape[0], bufs.shape[1]
    copies = [
        pltpu.make_async_copy(ref.at[pl.ds(rows - count, count)], bufs.at[i], sems.at[i])
        for i, ref in enumerate((query_ref, key_ref, value_ref))
    ]
    for copy in copies:
        copy.start()
    for i, copy in enumerate(copies):
        copy.wait()
        tail_ref[i] = bufs[i].astype(f32)[count - 2 :].astype(bf16)


def unbroken(len_ref, first, count):
    start = jnp.int32(0)
    whole = jnp.where((first <= 0) & (first + count > 0), 0.0, 1.0)
    for d in range(len_ref.shape[0] - 1):
        start = start + len_ref[d]
        whole = jnp.where((start >= first) & (start < first + count), 0.0, whole)
    return whole.astype(f32)


class Masks:
    def __init__(self, span):
        self.one, self.two, self.last, self.enter = 0, span, 2 * span, 3 * span
        self.passes = 4 * span
        self.edges = self.passes + SUBS
        self.late = self.edges + 3
        self.early = self.late + 1
        self.levels = self.late + 2

    def lead(self, level):
        return self.levels + 2 * level

    def later(self, level):
        return self.levels + 2 * level + 1

    def count(self, levels):
        return self.levels + 2 * levels + 1


def write_masks(base_ref, len_ref, masks, span, levels):
    at = Masks(span)
    rows, starts = doc_start_rows(len_ref, base_ref[0], span)
    for j in range(span):
        masks[at.one + j] = flag(starts[j] < rows + j)
        masks[at.two + j] = flag(starts[j] < rows + (j - 1))
        masks[at.last + j] = flag(starts[span - 1] <= rows + j)
        masks[at.enter + j] = flag(starts[j] < rows)
    top = flag(lax.broadcasted_iota(jnp.int32, (SUBS, LANES), 0) == 0)
    masks[at.edges] = top * masks[at.one]
    masks[at.edges + 1] = top * masks[at.two]
    masks[at.edges + 2] = top * masks[at.two + 1]
    size = SUBS * span
    parity = lax.rem(lax.div(base_ref[0], size), 2)
    pair_at = base_ref[0] - parity * size
    ranges = [(base_ref[0] + b * span, span) for b in range(SUBS)]
    flags = [at.passes + b for b in range(SUBS)]
    ranges += [(pair_at + size, size), (pair_at, size)]
    flags += [at.late, at.early]
    for m in range(levels + 1):
        group = 2 * size << m
        group_at = base_ref[0] - lax.rem(base_ref[0], group)
        ranges.append((group_at, pair_at - group_at))
        flags.append(at.lead(m))
        if m < levels:
            ranges.append((group_at + group * (1 - lax.rem(lax.div(base_ref[0], group), 2)), group))
            flags.append(at.later(m))
    for index, (first, count) in zip(flags, ranges):
        masks[index] = jnp.full((SUBS, LANES), unbroken(len_ref, first, count), f32)


def near_kernel(masks, gate_ref, rate_ref, weight_ref, *refs, span, modes, most, first, count):
    near_ref, sums, tap_rows = refs[-3:]
    at = Masks(span)

    def group(lanes):
        for slot, lane in enumerate(lanes):
            decay = jnp.exp(-rate_ref[:, cols_of(lane)])
            term = weight_ref[:, cols_of(lane)]
            for lag in range(span):
                part = term[:SUBS]
                for n in range(SUBS, modes, SUBS):
                    part = part + term[n : n + SUBS]
                sums[slot, pl.ds(lag * (SUBS + 1), SUBS), :] = part
                term = term * decay
        for slot in range(len(lanes)):
            for first_lag in range(0, span, SUBS):
                total = [
                    sums[slot, pl.ds(first_lag * (SUBS + 1) + m, SUBS, stride=SUBS + 1), :] for m in range(SUBS)
                ]
                while len(total) > 1:
                    total = [total[m] + total[m + 1] for m in range(0, len(total), 2)]
                tap_rows[slot, pl.ds(first_lag, SUBS), :] = total[0]
        taps = [[row_of(tap_rows.at[slot], lag) for lag in range(span)] for slot in range(len(lanes))]
        for parts, lane in zip(taps, lanes):
            live = []
            for j in range(span):
                if j % 2 == 0:
                    pair = gate_ref[pl.ds(j * SUBS, 2 * SUBS), cols_of(lane)].astype(f32)
                keep = masks[at.one + j]
                live = [g * keep for g in live]
                live.append(pair[(j % 2) * SUBS : (j % 2 + 1) * SUBS])
                total = parts[0] * live[j]
                for lag in range(1, j + 1):
                    total = total + parts[lag] * live[j - lag]
                near_ref[pl.ds(j * SUBS, SUBS), cols_of(lane)] = total

    each_group(count // LANES, most, lambda lanes: group([pl.multiple_of(first + lane, LANES) for lane in lanes]))


def query_kernel(masks, query_ref, taps_ref, *refs, span, most, chunk, first, count):
    short_ref, query_buf, sems, wide_q = refs[-4:]

    def fetch(c):
        there = pl.ds(first + c * chunk if isinstance(c, int) else pl.multiple_of(first + c * chunk, chunk), chunk)
        here = pl.ds(c * chunk if isinstance(c, int) else pl.multiple_of(c * chunk, chunk), chunk)
        return pltpu.make_async_copy(query_ref.at[:, there], query_buf.at[:, here], sems.at[c])

    for c in range(count // chunk):
        fetch(c).start()
    at = Masks(span)

    def group(lanes):
        for slot, lane in enumerate(lanes):
            spread(query_buf[:, cols_of(lane)], wide_q.at[slot], span)
        convs = [
            Conv(wide_q.at[slot], None, taps_ref[0, :, cols_of(pl.multiple_of(first + lane, LANES))], span)
            for slot, lane in enumerate(lanes)
        ]
        for j in range(span):
            keep_one, keep_two = masks[at.one + j], masks[at.two + j]
            for slot, lane in enumerate(lanes):
                short_ref[pl.ds(j * SUBS, SUBS), cols_of(pl.multiple_of(first + lane, LANES))] = convs[slot].step(j, keep_one, keep_two)

    each_chunk(count, chunk, lambda c: fetch(c).wait(), group, lambda c: None, most)


def pair_rates(rate_ref, count):
    parity = lax.rem(lax.axis_index("ctx"), 2)
    return parity, rate_ref[:, pl.ds(pl.multiple_of(parity * count, LANES), count)]


def early_late(parity, own, got):
    odd = jnp.full(own.shape, parity, jnp.int32) == 1
    return jnp.where(odd, got, own), jnp.where(odd, own, got)


def leap(masks, index, rate, rows):
    return jnp.exp(-float(rows) * rate) * masks[index][0:1, 0:1]


def pair_kernel(masks, own_ref, got_ref, rate_ref, total_ref, sent_ref, *, rows, index):
    parity, rate = pair_rates(rate_ref, own_ref.shape[1])
    early, late = early_late(parity, own_ref[...], got_ref[...])
    total = late + leap(masks, index, rate, rows) * early
    total_ref[...] = total
    sent_ref[...] = total.astype(bf16)


def lead_leap(masks, index, rate, rows, bit):
    me = lax.axis_index("ctx")
    lead = (lax.rem(me, bit) - lax.rem(me, 2)) * rows
    return jnp.exp(rate * -lead.astype(f32)) * masks[index][0:1, 0:1]


def level_kernel(masks, total_ref, got_ref, rate_ref, *refs, rows, level, lead, later):
    before_ref = refs[0] if level else None
    sent_ref, enter_ref, *new_ref = refs[1 if level else 0 :]
    _, rate = pair_rates(rate_ref, total_ref.shape[1])
    bit = 2 << level
    after = lax.rem(lax.div(lax.axis_index("ctx"), bit), 2)
    got = got_ref[...].astype(f32)
    early, late = early_late(after, total_ref[...], got)
    total = late + leap(masks, later, rate, bit * rows) * early
    for ref in new_ref:
        ref[...] = total
    sent_ref[...] = total.astype(bf16)
    entering = jnp.where(jnp.full(got.shape, after, jnp.int32) == 1, got, 0.0) * lead_leap(masks, lead, rate, rows, bit)
    enter_ref[...] = entering if before_ref is None else before_ref[...] + entering


def enter_kernel(
    masks, before_ref, even_ref, odd_ref, own_ref, other_ref, rate_ref, mine_ref, give_ref, *, rows, bit, lead, early_index
):
    parity, rate = pair_rates(rate_ref, own_ref.shape[1])
    group = jnp.full(own_ref.shape, lax.div(lax.axis_index("ctx"), bit), jnp.int32)
    got = jnp.where(lax.rem(group, 2) == 1, odd_ref[...].astype(f32), even_ref[...].astype(f32))
    got = jnp.where(group == 0, 0.0, got)
    first = before_ref[...] + lead_leap(masks, lead, rate, rows, bit) * got
    early, _ = early_late(parity, own_ref[...], other_ref[...])
    second = early + leap(masks, early_index, rate, rows) * first
    give, mine = early_late(parity, second, first)
    mine_ref[...] = mine
    give_ref[...] = give


def final_kernel(
    masks, state_ref, enter_ref, near_ref, short_ref, resid_ref, rim_ref, taps_ref, rate_ref, weight_ref, *refs,
    span, modes, channels, most, chunk, own,
):
    if own:
        hidden_out, whole, sums, hidden_ref, sems, wide, tables, starts_at = refs
    elif channels:
        gain_ref, _, _, _, hidden_out, whole, sums, normed_out, hidden_ref, sems, wide, tables, starts_at, normed_ref = refs
    else:
        _, _, _, hidden_out, whole, sums, hidden_ref, sems, wide, tables, starts_at = refs
    chans = resid_ref.shape[1]
    half = chans // 2
    first = half_start(chans, own)
    at = Masks(span)

    def store(c):
        here = pl.ds(pl.multiple_of(c * chunk, chunk), chunk)
        there = pl.ds(pl.multiple_of(first + c * chunk, chunk), chunk)
        return pltpu.make_async_copy(hidden_ref.at[:, here], hidden_out.at[:, there], sems.at[0, c])

    def store_normed(c):
        return cols_copy(normed_ref, normed_out, sems.at[1], c, chunk)

    if own:
        sums[...] = jnp.zeros(sums.shape, f32)

    def group(lanes):
        for slot, lane in enumerate(lanes):
            state = enter_ref[:, cols_of(pl.multiple_of(lane - first, LANES))]
            rate = rate_ref[:, cols_of(lane)]
            weight = weight_ref[:, cols_of(lane)]
            tables[slot] = jnp.exp(-rate)
            leap = jnp.exp(-float(span) * rate)
            for b in range(SUBS):
                starts_at[slot, pl.ds(b * (modes + 1), modes), :] = weight * state
                if b < SUBS - 1:
                    state = (leap * twice(masks[at.passes + b], modes)) * state + sub_state(state_ref, lane, b, modes)
        for slot, lane in enumerate(lanes):
            part = [starts_at[slot, pl.ds(n, SUBS, stride=modes + 1), :] for n in range(modes)]
            decay = [row_of(tables.at[slot], n) for n in range(modes)]
            rim = rim_ref[0, :, cols_of(lane)].astype(f32)
            tap = taps_ref[0, :, cols_of(lane)]
            edge = [
                (tap[1:2] * rim[1:2]) * masks[at.edges] + (tap[2:3] * rim[0:1]) * masks[at.edges + 1],
                (tap[2:3] * rim[1:2]) * masks[at.edges + 2],
            ]
            for j in range(span):
                part = [part[n] * decay[n] for n in range(modes)]
                total = part
                while len(total) > 1:
                    total = [total[m] + total[m + 1] for m in range(0, len(total), 2)]
                conv = near_ref[pl.ds(j * SUBS, SUBS), cols_of(lane)] + total[0] * masks[at.enter + j]
                conv = conv.astype(bf16).astype(f32)
                short = short_ref[pl.ds(j * SUBS, SUBS), cols_of(lane)]
                if j < 2:
                    short = short + edge[j]
                wide[slot, pl.ds(j, SUBS, stride=span + 1), :] = short * conv
        for b in range(SUBS):
            rows = pl.ds(b * span, span)
            squares = sums[rows, :]
            for slot, lane in enumerate(lanes):
                hidden = wide[slot, pl.ds(b * (span + 1), span), :] + resid_ref[rows, cols_of(lane)].astype(f32)
                whole[lax.div(lane, LANES), rows, :] = hidden
                hidden_ref[rows, cols_of(pl.multiple_of(lane - first, LANES))] = hidden.astype(bf16)
                squares = squares + hidden * hidden
            sums[rows, :] = squares

    each_chunk(
        half,
        chunk,
        lambda c: None,
        lambda lanes: group([pl.multiple_of(first + lane, LANES) for lane in lanes]),
        lambda c: store(c).start(),
        most,
    )
    if channels and not own:
        inverse = lax.rsqrt(jnp.sum(sums[...], axis=1, keepdims=True) / channels + 1e-06)
        sums[...] = jnp.broadcast_to(inverse, sums.shape)

        def scale(lanes):
            for lane in lanes:
                normed = whole[lax.div(lane, LANES)] * sums[...] * gain_ref[:, cols_of(lane)]
                normed_ref[:, cols_of(lane)] = normed.astype(bf16)

        each_chunk(chans, chunk, lambda c: None, scale, lambda c: store_normed(c).start(), 4)
        for c in range(chans // chunk):
            store_normed(c).wait()
    for c in range(half // chunk):
        store(c).wait()


def shards(
    query_in, key_in, value_in, short_taps, decay_rate, residues, doc_lengths, residual, norm_gain
):
    tok_rows, chans = query_in.shape
    modes = decay_rate.shape[0]
    span = tok_rows // SUBS
    blocks = lax.axis_size("ctx")
    grp = lax.axis_size("grp")
    chunk = min(chans // 2, 1024)
    pieces = chans // chunk
    ctx_index = lax.axis_index("ctx")
    base = (ctx_index * tok_rows).astype(jnp.int32).reshape(1)
    weight = residues * jnp.sqrt(-jnp.expm1(-2.0 * decay_rate))

    smem = pl.BlockSpec(memory_space=pltpu.SMEM)
    vmem = pl.BlockSpec(memory_space=pltpu.VMEM)
    hbm = pl.BlockSpec(memory_space=pltpu.HBM)
    tile_shape = (SUBS, LANES)
    wide_rows = SUBS * (span + 1)
    params = pltpu.CompilerParams(vmem_limit_bytes=16 * MIB)

    lengths = pltpu.with_memory_space_constraint(doc_lengths, pltpu.HBM)

    def near_by(x):
        return pltpu.with_memory_space_constraint(x, pltpu.VMEM)

    def far_off(x):
        return pltpu.with_memory_space_constraint(x, pltpu.HBM)

    def copies(kinds):
        return pltpu.SemaphoreType.DMA((kinds, pieces))

    def cost(per_tile, moved):
        return pl.CostEstimate(flops=per_tile * (chans // LANES) * SUBS * LANES, bytes_accessed=moved, transcendentals=0)

    tails = pl.pallas_call(
        tail_kernel,
        in_specs=[hbm, hbm, hbm],
        out_specs=vmem,
        out_shape=pltpu.VMEM((3, 2, chans), bf16),
        scratch_shapes=[pltpu.VMEM((3, 16, chans), bf16), pltpu.SemaphoreType.DMA((3,))],
        compiler_params=params,
        name="tails",
    )(far_off(query_in), far_off(key_in), far_off(value_in))
    rim_rows = from_behind(tails, "ctx", 1)
    levels = max(1, (blocks // 4).bit_length() - 2)
    mask_shape = (Masks(span).count(levels),) + tile_shape

    def query_piece(part, masks, before):
        count = chans // 2
        scratch = [
            pltpu.VMEM((tok_rows, count), bf16),
            pltpu.SemaphoreType.DMA((count // chunk,)),
            pltpu.VMEM((Q_TILES, wide_rows, LANES), f32),
        ]
        operands = [near_by(masks), far_off(query_in), taps] + ([near_by(before)] if part else [])
        return pl.pallas_call(
            functools.partial(
                query_kernel, span=span, most=Q_TILES, chunk=chunk, first=part * count, count=count
            ),
            in_specs=[vmem, hbm, vmem] + [vmem] * (len(operands) - 3),
            out_specs=vmem,
            out_shape=pltpu.VMEM((tok_rows, chans), f32),
            scratch_shapes=scratch,
            input_output_aliases={3: 0} if part else {},
            compiler_params=params,
            cost_estimate=cost(100, 3 * tok_rows * chans),
            name="query_part_%d" % part,
        )(*operands)

    key_half = pltpu.VMEM((tok_rows, chans // 2), bf16)
    masks, key_give, value_give, taps, rates = pl.pallas_call(
        functools.partial(first_kernel, span=span, levels=levels),
        in_specs=[smem, smem, hbm, hbm, hbm, hbm],
        out_specs=[vmem] * 5,
        out_shape=[
            pltpu.VMEM(mask_shape, f32), key_half, key_half,
            pltpu.VMEM(short_taps.shape, f32), pltpu.VMEM(decay_rate.shape, f32),
        ],
        scratch_shapes=[pltpu.SemaphoreType.DMA((4,))],
        compiler_params=params,
        name="masks_and_fetch",
    )(base, lengths, far_off(key_in), far_off(value_in), far_off(short_taps), far_off(decay_rate))
    rim_rows, masks = lax.optimization_barrier((rim_rows, masks))
    rates, weights, taps, rims = near_by(rates), near_by(weight), near_by(taps), near_by(rim_rows)
    kept = pltpu.VMEM((modes, chans // 2), f32)
    sent = pltpu.VMEM((modes, chans // 2), bf16)

    def states_of(own, keys, values, before):
        operands = [near_by(x) for x in (masks, keys, values)] + [rims, taps, rates]
        in_specs = [vmem] * len(operands)
        out_shape = [
            pltpu.VMEM((tok_rows, chans), bf16),
            pltpu.VMEM((chans // LANES, SUBS * (modes + 1), LANES), f32),
            kept,
        ]
        scratch = [
            pltpu.VMEM((A_TILES, wide_rows, LANES), f32),
            pltpu.VMEM((A_TILES, wide_rows, LANES), f32),
            pltpu.VMEM((A_TILES, modes, LANES), f32),
            pltpu.VMEM((A_TILES, span) + tile_shape, f32),
        ]
        if own:
            operands += [near_by(x) for x in before]
            in_specs += [vmem] * len(before)
        else:
            operands += [far_off(key_in), far_off(value_in)]
            in_specs += [hbm, hbm]
            out_shape += [key_half, key_half]
            scratch.append(pltpu.SemaphoreType.DMA((2,)))
        return pl.pallas_call(
            functools.partial(state_kernel, span=span, modes=modes, most=A_TILES, own=own),
            in_specs=in_specs,
            out_specs=[vmem] * len(out_shape),
            out_shape=out_shape,
            scratch_shapes=scratch,
            input_output_aliases={6: 0, 7: 1} if own else {},
            compiler_params=params,
            cost_estimate=cost(500, 6 * tok_rows * chans),
            name="block_states_own" if own else "block_states_give",
        )(*operands)

    gates, states, give, key_own, value_own = states_of(False, key_give, value_give, [])
    got = swap(give, "ctx")
    gates, states, own = states_of(True, key_own, value_own, [gates, states])
    got, gates, states, own = lax.optimization_barrier((got, gates, states, own))

    def near_piece(part, near):
        count = chans // NEAR_PARTS
        before = [] if near is None else [near_by(near)]
        return pl.pallas_call(
            functools.partial(
                near_kernel, span=span, modes=modes, most=N_TILES, first=part * count, count=count
            ),
            in_specs=[vmem] * (4 + len(before)),
            out_specs=vmem,
            out_shape=pltpu.VMEM((tok_rows, chans), f32),
            scratch_shapes=[
                pltpu.VMEM((N_TILES, span * (SUBS + 1), LANES), f32),
                pltpu.VMEM((N_TILES, span, LANES), f32),
            ],
            compiler_params=params,
            input_output_aliases={4: 0} if before else {},
            cost_estimate=cost(600 // NEAR_PARTS, 7 * tok_rows * count),
            name="near_part_%d" % part,
        )(near_by(masks), near_by(gates), rates, weights, *before)

    got = swap(give, "ctx")

    at = Masks(span)

    def pair_call(kernel, operands, out_shape, name, extra=(), **static):
        return pl.pallas_call(
            functools.partial(kernel, **static),
            in_specs=[vmem] * (len(operands) + 2 + len(extra)),
            out_specs=[vmem] * len(out_shape),
            out_shape=out_shape,
            compiler_params=params,
            name=name,
        )(near_by(masks), *[near_by(x) for x in operands], rates, *[near_by(x) for x in extra])

    total, ends = pair_call(pair_kernel, [own, got], [kept, sent], "pair_ends", rows=tok_rows, index=at.late)
    entering, near = [], None
    for m in range(levels):
        met = swap(ends, "ctx", 2 << m)
        if m < NEAR_PARTS:
            near = near_piece(m, near)
            if m == 0:
                q_short = query_piece(0, masks, None)
                met, q_short = lax.optimization_barrier((met, q_short))
            met, near = lax.optimization_barrier((met, near))
        ends, enter, *total = pair_call(
            level_kernel,
            [total, met],
            [sent, kept] + [kept] * (m < levels - 1),
            "level_%d" % m,
            extra=entering,
            rows=tok_rows,
            level=m,
            lead=at.lead(m),
            later=at.later(m),
        )
        entering = [enter]
        total = total[0] if total else None
    on = (swap_across(ends, "ctx", 2 << levels), swap(ends, "ctx", 2 << levels))
    for m in range(levels, NEAR_PARTS):
        near = near_piece(m, near)
    q_short = query_piece(1, masks, q_short)
    on, q_short, near = lax.optimization_barrier((on, q_short, near))
    mine, give_back = pair_call(
        enter_kernel,
        entering + [*on, own, got],
        [kept, kept],
        "pair_enter",
        rows=tok_rows,
        bit=2 << levels,
        lead=at.lead(levels),
        early_index=at.early,
    )
    got_back = swap(give_back, "ctx")

    alone = grp == 1
    resid = near_by(residual)

    def finish(own, enter, before):
        last = alone and not own
        out_specs = [hbm, vmem, vmem]
        out_shape = [
            jax.ShapeDtypeStruct((tok_rows, chans), bf16),
            pltpu.VMEM((chans // LANES, tok_rows, LANES), f32),
            pltpu.VMEM((tok_rows, LANES), f32),
        ]
        scratch = [
            pltpu.VMEM((tok_rows, chans // 2), bf16),
            copies(2),
            pltpu.VMEM((F_TILES, wide_rows, LANES), f32),
            pltpu.VMEM((F_TILES, modes, LANES), f32),
            pltpu.VMEM((F_TILES, SUBS * (modes + 1), LANES), f32),
        ]
        operands = [near_by(x) for x in (masks, states, enter, near, q_short)] + [resid, rims, taps, rates, weights]
        if last:
            operands.append(near_by(norm_gain.reshape(1, chans)))
            out_specs.append(hbm)
            out_shape.append(jax.ShapeDtypeStruct((tok_rows, chans), bf16))
            scratch.append(pltpu.VMEM((tok_rows, chans), bf16))
        count = len(operands)
        in_specs = [vmem] * count
        if before:
            operands += [far_off(before[0]), near_by(before[1]), near_by(before[2])]
            in_specs += [hbm, vmem, vmem]
        return pl.pallas_call(
            functools.partial(
                final_kernel, span=span, modes=modes, channels=chans if alone else 0, most=F_TILES, chunk=chunk, own=own
            ),
            in_specs=in_specs,
            out_specs=out_specs,
            out_shape=out_shape,
            scratch_shapes=scratch,
            input_output_aliases={count + i: i for i in range(len(before))},
            compiler_params=params,
            cost_estimate=cost(450, 9 * tok_rows * chans),
            name="far_part_own" if own else "far_part_other",
        )(*operands)

    before = finish(True, mine, [])
    got_back, *before = lax.optimization_barrier((got_back, *before))
    outs = finish(False, got_back, before)
    if alone:
        return (outs[0], outs[3])
    hidden_out, whole, sums = outs
    hidden = whole.transpose(1, 0, 2).reshape(tok_rows, chans)
    square_sum = lax.psum(jnp.sum(sums, axis=1), "grp")
    inverse_rms = lax.rsqrt(square_sum / (chans * grp) + 1e-06)
    normed = (hidden * inverse_rms[:, None] * norm_gain[None, :]).astype(bf16)
    return (hidden_out, normed)


def solution(mesh):
    return jax.shard_map(
        shards,
        mesh=mesh,
        in_specs=(
            P("ctx", "grp"),
            P("ctx", "grp"),
            P("ctx", "grp"),
            P(None, None, "grp"),
            P(None, "grp"),
            P(None, "grp"),
            P(),
            P("ctx", "grp"),
            P("grp"),
        ),
        out_specs=(P("ctx", "grp"), P("ctx", "grp")),
        check_vma=False,
    )
```

```python
import functools
import math

import jax
import jax.numpy as jnp
from jax import lax
from jax.experimental import pallas as pl
from jax.experimental.pallas import tpu as pltpu
from jax.sharding import PartitionSpec as P

SUBS = 8
LANES = 128
MIB = 1024 * 1024
A_TILES, N_TILES, Q_TILES, F_TILES = 2, 2, 4, 4
NEAR_PARTS = 2
f32 = jnp.float32
bf16 = jnp.bfloat16


def from_behind(shard, axis, by):
    count = lax.axis_size(axis)
    return lax.ppermute(shard, axis, [(i, i + by) for i in range(count - by)])


def swap(shard, axis, bit=1):
    return lax.ppermute(shard, axis, [(i, i ^ bit) for i in range(lax.axis_size(axis))])


def doc_start_rows(len_ref, base, span):
    rows = lax.broadcasted_iota(jnp.int32, (SUBS, LANES), 0) * span + base
    starts = [jnp.int32(0)]
    for d in range(len_ref.shape[0] - 1):
        starts.append(starts[-1] + len_ref[d])
    out = []
    for j in range(span):
        pos = rows + j
        best = jnp.zeros((SUBS, LANES), jnp.int32)
        for start in starts[1:]:
            best = jnp.where(pos >= start, start, best)
        out.append(best)
    return rows, out


def flag(cond):
    return jnp.where(cond, 1.0, 0.0).astype(f32)


def each_group(count, most, group):
    size = math.gcd(count, most)

    def step(i, carry):
        group([pl.multiple_of((i * size + m) * LANES, LANES) for m in range(size)])
        return carry

    lax.fori_loop(0, count // size, step, 0)


def each_chunk(chans, chunk, before, group, after, most):
    def step(c, carry):
        before(c)

        def inner(lanes):
            group([pl.multiple_of(c * chunk + lane, LANES) for lane in lanes])

        each_group(chunk // LANES, most, inner)
        after(c)
        return carry

    lax.fori_loop(0, chans // chunk, step, 0)


def cols_copy(src, dst, sem, c, chunk):
    cols = pl.ds(pl.multiple_of(c * chunk, chunk), chunk)
    return pltpu.make_async_copy(src.at[:, cols], dst.at[:, cols], sem.at[c])


def cols_of(lane):
    return pl.ds(lane, LANES)


def row_of(ref, index):
    return ref[pl.ds(index, SUBS, stride=0), :]


def spread(x, wide, span):
    x = x.astype(f32)
    for b in range(SUBS):
        wide[pl.ds(b * (span + 1), span), :] = x[b * span : (b + 1) * span]


class Conv:
    def __init__(self, wide, rim, taps, span):
        self.wide, self.span = wide, span
        self.taps = [jnp.broadcast_to(taps[m : m + 1], (SUBS, LANES)) for m in range(3)]
        top = lax.broadcasted_iota(jnp.int32, (SUBS, LANES), 0) == 0
        ahead = [0.0, 0.0] if rim is None else [jnp.broadcast_to(rim[m : m + 1], (SUBS, LANES)) for m in range(2)]
        self.behind = [jnp.where(top, ahead[m], pltpu.roll(self.row(span - 2 + m), 1, 0)) for m in range(2)]

    def row(self, j):
        return self.wide[pl.ds(j, SUBS, stride=self.span + 1), :]

    def step(self, j, keep_one, keep_two):
        here = self.row(j)
        two, one = self.behind
        self.behind = [one, here]
        return self.taps[0] * here + (self.taps[1] * one) * keep_one + (self.taps[2] * two) * keep_two


def half_start(chans, own):
    parity = lax.rem(lax.axis_index("ctx"), 2)
    return pl.multiple_of((parity if own else 1 - parity) * (chans // 2), LANES)


def twice(mask, modes):
    return jnp.concatenate([mask] * (modes // SUBS), axis=0)


def sub_state(state_ref, lane, b, modes):
    return state_ref[lax.div(lane, LANES), pl.ds(b * (modes + 1), modes), :]


def state_kernel(masks, *refs, span, modes, most, own, chunk):
    if own:
        key_ref, value_ref, rim_ref, taps_ref, rate_ref, _, _, gate_ref, state_ref, end_ref, wide_k, wide_v, tables, held = refs
    else:
        (key_in, value_in, taps_ref, rate_ref, gate_ref, state_ref, end_ref, key_own, value_own, heads,
         key_ref, value_ref, wide_k, wide_v, tables, held, sems) = refs
    half = key_ref.shape[1]
    first = half_start(2 * half, own)
    if not own:
        def fetch(c):
            there = pl.ds(pl.multiple_of(first + c * chunk, chunk), chunk)
            here = pl.ds(pl.multiple_of(c * chunk, chunk), chunk)
            return [
                pltpu.make_async_copy(key_in.at[:, there], key_ref.at[:, here], sems.at[0, c]),
                pltpu.make_async_copy(value_in.at[:, there], value_ref.at[:, here], sems.at[1, c]),
            ]

        cols = pl.ds(half_start(2 * half, True), half)
        others = [
            pltpu.make_async_copy(key_in.at[:, cols], key_own, sems.at[0, half // chunk]),
            pltpu.make_async_copy(value_in.at[:, cols], value_own, sems.at[1, half // chunk]),
        ]
        for c in range(half // chunk):
            for copy in fetch(c):
                copy.start()
        for copy in others:
            copy.start()
    at = Masks(span)

    def group(lanes):
        for slot, lane in enumerate(lanes):
            spread(key_ref[:, cols_of(pl.multiple_of(lane - first, LANES))], wide_k.at[slot], span)
            spread(value_ref[:, cols_of(pl.multiple_of(lane - first, LANES))], wide_v.at[slot], span)
            rate = rate_ref[:, cols_of(lane)]
            tables[slot] = jnp.exp(-rate)
        convs = [
            [
                Conv(wide.at[slot], rim_ref[i, :, cols_of(lane)].astype(f32) if own else None, taps_ref[i, :, cols_of(lane)], span)
                for i, wide in ((1, wide_k), (2, wide_v))
            ]
            for slot, lane in enumerate(lanes)
        ]
        last = [None] * len(lanes)
        for j in range(span):
            keep_one, keep_two = masks[at.one + j], masks[at.two + j]
            for slot, lane in enumerate(lanes):
                k_short, v_short = [conv.step(j, keep_one, keep_two) for conv in convs[slot]]
                if j % 2 == 0:
                    last[slot] = k_short * v_short
                    continue
                pair = jnp.concatenate([last[slot], k_short * v_short], axis=0).astype(bf16)
                gate_ref[pl.ds((j - 1) * SUBS, 2 * SUBS), cols_of(lane)] = pair
                pair = pair.astype(f32)
                used = at.inner if j == 1 and not own else at.last + j - 1
                held[slot, j - 1] = pair[:SUBS] * masks[used]
                held[slot, j] = pair[SUBS:] * masks[used + 1]
        for slot, lane in enumerate(lanes):
            decay = [row_of(tables.at[slot], n) for n in range(modes)]
            state = [held[slot, 0]] * modes
            for j in range(1, span):
                gate = held[slot, j]
                state = [decay[n] * state[n] + gate for n in range(modes)]
            for n in range(modes):
                state_ref[lax.div(lane, LANES), pl.ds(n, SUBS, stride=modes + 1), :] = state[n]
        for slot, lane in enumerate(lanes):
            leap = jnp.exp(-float(span) * rate_ref[:, cols_of(lane)])
            end = sub_state(state_ref, lane, 0, modes)
            for b in range(1, SUBS):
                end = (leap * twice(masks[at.passes + b], modes)) * end + sub_state(state_ref, lane, b, modes)
            end_ref[:, cols_of(pl.multiple_of(lane - first, LANES))] = end

    def shifted(lanes):
        group([pl.multiple_of(first + lane, LANES) for lane in lanes])

    if own:
        each_group(half // LANES, most, shifted)
    else:
        def before(c):
            for copy in fetch(c):
                copy.wait()

        each_chunk(half, chunk, before, shifted, lambda c: None, most)
        heads[0] = key_ref[pl.ds(0, heads.shape[1]), :]
        heads[1] = value_ref[pl.ds(0, heads.shape[1]), :]
        for copy in others:
            copy.wait()


def patch_kernel(
    masks, heads, rim_ref, taps_ref, rate_ref, gate_in, state_in, end_in, gate_ref, state_ref, end_ref, *, span, modes
):
    half = end_ref.shape[1]
    first = half_start(2 * half, False)
    at = Masks(span)
    rows = lax.broadcasted_iota(jnp.int32, (2 * SUBS, LANES), 0)

    def one(index):
        return masks[index][0:1]

    def group(lanes):
        for lane in lanes:
            there = cols_of(pl.multiple_of(first + lane, LANES))
            shorts = []
            for i in (1, 2):
                here = heads[i - 1, :, cols_of(lane)].astype(f32)
                rim = rim_ref[i, :, there].astype(f32)
                tap = taps_ref[i, :, there]
                shorts.append([
                    tap[0:1] * here[0:1] + (tap[1:2] * rim[1:2]) * one(at.one) + (tap[2:3] * rim[0:1]) * one(at.two),
                    tap[0:1] * here[1:2] + (tap[1:2] * here[0:1]) * one(at.one + 1) + (tap[2:3] * rim[1:2]) * one(at.two + 1),
                ])
            gates = [(k * v).astype(bf16).astype(f32) for k, v in zip(*shorts)]
            old = gate_in[pl.ds(0, 2 * SUBS), there].astype(f32)
            new = jnp.where(rows == 0, gates[0], jnp.where(rows == SUBS, gates[1], old))
            gate_ref[pl.ds(0, 2 * SUBS), there] = new.astype(bf16)
            rate = rate_ref[:, there]
            added = jnp.exp(-float(span - 1) * rate) * (gates[0] * one(at.last)) + jnp.exp(-float(span - 2) * rate) * (
                gates[1] * one(at.last + 1)
            )
            tile = lax.div(first + lane, LANES)
            state_ref[tile, pl.ds(0, modes), :] = state_in[tile, pl.ds(0, modes), :] + added
            reach = jnp.exp(-float((SUBS - 1) * span) * rate) * one(at.rest)
            end_ref[:, cols_of(lane)] = end_in[:, cols_of(lane)] + reach * added

    each_group(half // LANES, 4, group)


def tail_kernel(base_ref, len_ref, query_ref, key_ref, value_ref, tail_ref, masks, bufs, sems, *, span, levels):
    rows, count = query_ref.shape[0], bufs.shape[1]
    copies = [
        pltpu.make_async_copy(ref.at[pl.ds(rows - count, count)], bufs.at[i], sems.at[i])
        for i, ref in enumerate((query_ref, key_ref, value_ref))
    ]
    for copy in copies:
        copy.start()
    write_masks(base_ref, len_ref, masks, span, levels)
    for i, copy in enumerate(copies):
        copy.wait()
        tail_ref[i] = bufs[i].astype(f32)[count - 2 :].astype(bf16)


def unbroken(len_ref, first, count):
    start = jnp.int32(0)
    whole = jnp.where((first <= 0) & (first + count > 0), 0.0, 1.0)
    for d in range(len_ref.shape[0] - 1):
        start = start + len_ref[d]
        whole = jnp.where((start >= first) & (start < first + count), 0.0, whole)
    return whole.astype(f32)


class Masks:
    def __init__(self, span):
        self.one, self.two, self.last, self.enter = 0, span, 2 * span, 3 * span
        self.passes = 4 * span
        self.edges = self.passes + SUBS
        self.late = self.edges + 3
        self.early = self.late + 1
        self.rest = self.late + 2
        self.inner = self.late + 3
        self.levels = self.late + 5

    def lead(self, level):
        return self.levels + 2 * level

    def later(self, level):
        return self.levels + 2 * level + 1

    def count(self, levels):
        return self.levels + 2 * levels + 1


def write_masks(base_ref, len_ref, masks, span, levels):
    at = Masks(span)
    rows, starts = doc_start_rows(len_ref, base_ref[0], span)
    for j in range(span):
        masks[at.one + j] = flag(starts[j] < rows + j)
        masks[at.two + j] = flag(starts[j] < rows + (j - 1))
        masks[at.last + j] = flag(starts[span - 1] <= rows + j)
        masks[at.enter + j] = flag(starts[j] < rows)
    top = flag(lax.broadcasted_iota(jnp.int32, (SUBS, LANES), 0) == 0)
    for j in range(2):
        masks[at.inner + j] = (1.0 - top) * masks[at.last + j]
    masks[at.edges] = top * masks[at.one]
    masks[at.edges + 1] = top * masks[at.two]
    masks[at.edges + 2] = top * masks[at.two + 1]
    size = SUBS * span
    parity = lax.rem(lax.div(base_ref[0], size), 2)
    pair_at = base_ref[0] - parity * size
    ranges = [(base_ref[0] + b * span, span) for b in range(SUBS)]
    flags = [at.passes + b for b in range(SUBS)]
    ranges += [(pair_at + size, size), (pair_at, size), (base_ref[0] + span, size - span)]
    flags += [at.late, at.early, at.rest]
    for m in range(levels + 1):
        group = 2 * size << m
        group_at = base_ref[0] - lax.rem(base_ref[0], group)
        ranges.append((group_at, pair_at - group_at))
        flags.append(at.lead(m))
        if m < levels:
            ranges.append((group_at + group * (1 - lax.rem(lax.div(base_ref[0], group), 2)), group))
            flags.append(at.later(m))
    for index, (first, count) in zip(flags, ranges):
        masks[index] = jnp.full((SUBS, LANES), unbroken(len_ref, first, count), f32)


def near_kernel(masks, gate_ref, rate_ref, weight_ref, *refs, span, modes, most, first, count):
    near_ref, sums, tap_rows = refs[-3:]
    at = Masks(span)

    def group(lanes):
        for slot, lane in enumerate(lanes):
            decay = jnp.exp(-rate_ref[:, cols_of(lane)])
            term = weight_ref[:, cols_of(lane)]
            for lag in range(span):
                part = term[:SUBS]
                for n in range(SUBS, modes, SUBS):
                    part = part + term[n : n + SUBS]
                sums[slot, pl.ds(lag * (SUBS + 1), SUBS), :] = part
                term = term * decay
        for slot in range(len(lanes)):
            for first_lag in range(0, span, SUBS):
                total = [
                    sums[slot, pl.ds(first_lag * (SUBS + 1) + m, SUBS, stride=SUBS + 1), :] for m in range(SUBS)
                ]
                while len(total) > 1:
                    total = [total[m] + total[m + 1] for m in range(0, len(total), 2)]
                tap_rows[slot, pl.ds(first_lag, SUBS), :] = total[0]
        taps = [[row_of(tap_rows.at[slot], lag) for lag in range(span)] for slot in range(len(lanes))]
        for parts, lane in zip(taps, lanes):
            live = []
            for j in range(span):
                if j % 2 == 0:
                    pair = gate_ref[pl.ds(j * SUBS, 2 * SUBS), cols_of(lane)].astype(f32)
                keep = masks[at.one + j]
                live = [g * keep for g in live]
                live.append(pair[(j % 2) * SUBS : (j % 2 + 1) * SUBS])
                total = parts[0] * live[j]
                for lag in range(1, j + 1):
                    total = total + parts[lag] * live[j - lag]
                near_ref[pl.ds(j * SUBS, SUBS), cols_of(lane)] = total

    each_group(count // LANES, most, lambda lanes: group([pl.multiple_of(first + lane, LANES) for lane in lanes]))


def query_kernel(masks, query_ref, taps_ref, *refs, span, most, chunk, first, count):
    short_ref, query_buf, sems, wide_q = refs[-4:]

    def fetch(c):
        there = pl.ds(first + c * chunk if isinstance(c, int) else pl.multiple_of(first + c * chunk, chunk), chunk)
        here = pl.ds(c * chunk if isinstance(c, int) else pl.multiple_of(c * chunk, chunk), chunk)
        return pltpu.make_async_copy(query_ref.at[:, there], query_buf.at[:, here], sems.at[c])

    for c in range(count // chunk):
        fetch(c).start()
    at = Masks(span)

    def group(lanes):
        for slot, lane in enumerate(lanes):
            spread(query_buf[:, cols_of(lane)], wide_q.at[slot], span)
        convs = [
            Conv(wide_q.at[slot], None, taps_ref[0, :, cols_of(pl.multiple_of(first + lane, LANES))], span)
            for slot, lane in enumerate(lanes)
        ]
        for j in range(span):
            keep_one, keep_two = masks[at.one + j], masks[at.two + j]
            for slot, lane in enumerate(lanes):
                short_ref[pl.ds(j * SUBS, SUBS), cols_of(pl.multiple_of(first + lane, LANES))] = convs[slot].step(j, keep_one, keep_two)

    each_chunk(count, chunk, lambda c: fetch(c).wait(), group, lambda c: None, most)


def pair_rates(rate_ref, count):
    parity = lax.rem(lax.axis_index("ctx"), 2)
    return parity, rate_ref[:, pl.ds(pl.multiple_of(parity * count, LANES), count)]


def early_late(parity, own, got):
    odd = jnp.full(own.shape, parity, jnp.int32) == 1
    return jnp.where(odd, got, own), jnp.where(odd, own, got)


def leap(masks, index, rate, rows):
    return jnp.exp(-float(rows) * rate) * masks[index][0:1, 0:1]


def pair_kernel(masks, own_ref, got_ref, rate_ref, total_ref, sent_ref, *, rows, index):
    parity, rate = pair_rates(rate_ref, own_ref.shape[1])
    early, late = early_late(parity, own_ref[...], got_ref[...])
    total = late + leap(masks, index, rate, rows) * early
    total_ref[...] = total
    sent_ref[...] = total.astype(bf16)


def lead_leap(masks, index, rate, rows, bit):
    me = lax.axis_index("ctx")
    lead = (lax.rem(me, bit) - lax.rem(me, 2)) * rows
    return jnp.exp(rate * -lead.astype(f32)) * masks[index][0:1, 0:1]


def level_kernel(masks, total_ref, got_ref, rate_ref, *refs, rows, level, lead, later):
    before_ref = refs[0] if level else None
    sent_ref, enter_ref, *new_ref = refs[1 if level else 0 :]
    _, rate = pair_rates(rate_ref, total_ref.shape[1])
    bit = 2 << level
    after = lax.rem(lax.div(lax.axis_index("ctx"), bit), 2)
    got = got_ref[...].astype(f32)
    early, late = early_late(after, total_ref[...], got)
    total = late + leap(masks, later, rate, bit * rows) * early
    for ref in new_ref:
        ref[...] = total
    sent_ref[...] = total.astype(bf16)
    entering = jnp.where(jnp.full(got.shape, after, jnp.int32) == 1, got, 0.0) * lead_leap(masks, lead, rate, rows, bit)
    enter_ref[...] = entering if before_ref is None else before_ref[...] + entering


def enter_kernel(
    masks, before_ref, got_ref, own_ref, other_ref, rate_ref, mine_ref, give_ref, *, rows, bit, lead, early_index
):
    parity, rate = pair_rates(rate_ref, own_ref.shape[1])
    first = before_ref[...] + lead_leap(masks, lead, rate, rows, bit) * got_ref[...].astype(f32)
    early, _ = early_late(parity, own_ref[...], other_ref[...])
    second = early + leap(masks, early_index, rate, rows) * first
    give, mine = early_late(parity, second, first)
    mine_ref[...] = mine
    give_ref[...] = give


def final_kernel(
    masks, state_ref, enter_ref, near_ref, short_ref, resid_ref, rim_ref, taps_ref, rate_ref, weight_ref, *refs,
    span, modes, channels, most, chunk, own,
):
    if own:
        hidden_out, whole, sums, hidden_ref, sems, wide, tables, starts_at = refs
    elif channels:
        gain_ref, _, _, _, hidden_out, whole, sums, normed_out, hidden_ref, sems, wide, tables, starts_at, normed_ref = refs
    else:
        _, _, _, hidden_out, whole, sums, hidden_ref, sems, wide, tables, starts_at = refs
    chans = resid_ref.shape[1]
    half = chans // 2
    first = half_start(chans, own)
    at = Masks(span)

    def store(c):
        here = pl.ds(pl.multiple_of(c * chunk, chunk), chunk)
        there = pl.ds(pl.multiple_of(first + c * chunk, chunk), chunk)
        return pltpu.make_async_copy(hidden_ref.at[:, here], hidden_out.at[:, there], sems.at[0, c])

    def store_normed(c):
        return cols_copy(normed_ref, normed_out, sems.at[1], c, chunk)

    if own:
        sums[...] = jnp.zeros(sums.shape, f32)

    def group(lanes):
        for slot, lane in enumerate(lanes):
            state = enter_ref[:, cols_of(pl.multiple_of(lane - first, LANES))]
            rate = rate_ref[:, cols_of(lane)]
            weight = weight_ref[:, cols_of(lane)]
            tables[slot] = jnp.exp(-rate)
            leap = jnp.exp(-float(span) * rate)
            for b in range(SUBS):
                starts_at[slot, pl.ds(b * (modes + 1), modes), :] = weight * state
                if b < SUBS - 1:
                    state = (leap * twice(masks[at.passes + b], modes)) * state + sub_state(state_ref, lane, b, modes)
        for slot, lane in enumerate(lanes):
            part = [starts_at[slot, pl.ds(n, SUBS, stride=modes + 1), :] for n in range(modes)]
            decay = [row_of(tables.at[slot], n) for n in range(modes)]
            rim = rim_ref[0, :, cols_of(lane)].astype(f32)
            tap = taps_ref[0, :, cols_of(lane)]
            edge = [
                (tap[1:2] * rim[1:2]) * masks[at.edges] + (tap[2:3] * rim[0:1]) * masks[at.edges + 1],
                (tap[2:3] * rim[1:2]) * masks[at.edges + 2],
            ]
            for j in range(span):
                part = [part[n] * decay[n] for n in range(modes)]
                total = part
                while len(total) > 1:
                    total = [total[m] + total[m + 1] for m in range(0, len(total), 2)]
                conv = near_ref[pl.ds(j * SUBS, SUBS), cols_of(lane)] + total[0] * masks[at.enter + j]
                conv = conv.astype(bf16).astype(f32)
                short = short_ref[pl.ds(j * SUBS, SUBS), cols_of(lane)]
                if j < 2:
                    short = short + edge[j]
                wide[slot, pl.ds(j, SUBS, stride=span + 1), :] = short * conv
        for b in range(SUBS):
            rows = pl.ds(b * span, span)
            squares = sums[rows, :]
            for slot, lane in enumerate(lanes):
                hidden = wide[slot, pl.ds(b * (span + 1), span), :] + resid_ref[rows, cols_of(lane)].astype(f32)
                whole[lax.div(lane, LANES), rows, :] = hidden
                hidden_ref[rows, cols_of(pl.multiple_of(lane - first, LANES))] = hidden.astype(bf16)
                squares = squares + hidden * hidden
            sums[rows, :] = squares

    each_chunk(
        half,
        chunk,
        lambda c: None,
        lambda lanes: group([pl.multiple_of(first + lane, LANES) for lane in lanes]),
        lambda c: store(c).start(),
        most,
    )
    if channels and not own:
        inverse = lax.rsqrt(jnp.sum(sums[...], axis=1, keepdims=True) / channels + 1e-06)
        sums[...] = jnp.broadcast_to(inverse, sums.shape)

        def scale(lanes):
            for lane in lanes:
                normed = whole[lax.div(lane, LANES)] * sums[...] * gain_ref[:, cols_of(lane)]
                normed_ref[:, cols_of(lane)] = normed.astype(bf16)

        each_chunk(chans, chunk, lambda c: None, scale, lambda c: store_normed(c).start(), 4)
        for c in range(chans // chunk):
            store_normed(c).wait()
    for c in range(half // chunk):
        store(c).wait()


def shards(
    query_in, key_in, value_in, short_taps, decay_rate, residues, doc_lengths, residual, norm_gain
):
    tok_rows, chans = query_in.shape
    modes = decay_rate.shape[0]
    span = tok_rows // SUBS
    blocks = lax.axis_size("ctx")
    grp = lax.axis_size("grp")
    chunk = min(chans // 2, 1024)
    pieces = chans // chunk
    ctx_index = lax.axis_index("ctx")
    base = (ctx_index * tok_rows).astype(jnp.int32).reshape(1)
    weight = residues * jnp.sqrt(-jnp.expm1(-2.0 * decay_rate))

    smem = pl.BlockSpec(memory_space=pltpu.SMEM)
    vmem = pl.BlockSpec(memory_space=pltpu.VMEM)
    hbm = pl.BlockSpec(memory_space=pltpu.HBM)
    tile_shape = (SUBS, LANES)
    wide_rows = SUBS * (span + 1)
    params = pltpu.CompilerParams(vmem_limit_bytes=16 * MIB)

    lengths = pltpu.with_memory_space_constraint(doc_lengths, pltpu.HBM)

    def near_by(x):
        return pltpu.with_memory_space_constraint(x, pltpu.VMEM)

    def far_off(x):
        return pltpu.with_memory_space_constraint(x, pltpu.HBM)

    def copies(kinds):
        return pltpu.SemaphoreType.DMA((kinds, pieces))

    def cost(per_tile, moved):
        return pl.CostEstimate(flops=per_tile * (chans // LANES) * SUBS * LANES, bytes_accessed=moved, transcendentals=0)

    levels = max(1, (blocks // 4).bit_length() - 2)
    mask_shape = (Masks(span).count(levels),) + tile_shape
    tails, masks = pl.pallas_call(
        functools.partial(tail_kernel, span=span, levels=levels),
        in_specs=[smem, smem, hbm, hbm, hbm],
        out_specs=[vmem, vmem],
        out_shape=[pltpu.VMEM((3, 2, chans), bf16), pltpu.VMEM(mask_shape, f32)],
        scratch_shapes=[pltpu.VMEM((3, 16, chans), bf16), pltpu.SemaphoreType.DMA((3,))],
        compiler_params=params,
        name="tails",
    )(base, lengths, far_off(query_in), far_off(key_in), far_off(value_in))
    rim_rows = from_behind(tails, "ctx", 1)
    def query_piece(part, masks, before):
        count = chans // 2
        scratch = [
            pltpu.VMEM((tok_rows, count), bf16),
            pltpu.SemaphoreType.DMA((count // chunk,)),
            pltpu.VMEM((Q_TILES, wide_rows, LANES), f32),
        ]
        operands = [near_by(masks), far_off(query_in), taps] + ([near_by(before)] if part else [])
        return pl.pallas_call(
            functools.partial(
                query_kernel, span=span, most=Q_TILES, chunk=chunk, first=part * count, count=count
            ),
            in_specs=[vmem, hbm, vmem] + [vmem] * (len(operands) - 3),
            out_specs=vmem,
            out_shape=pltpu.VMEM((tok_rows, chans), f32),
            scratch_shapes=scratch,
            input_output_aliases={3: 0} if part else {},
            compiler_params=params,
            cost_estimate=cost(100, 3 * tok_rows * chans),
            name="query_part_%d" % part,
        )(*operands)

    key_half = pltpu.VMEM((tok_rows, chans // 2), bf16)
    rates, weights, taps, rims = near_by(decay_rate), near_by(weight), near_by(short_taps), near_by(rim_rows)
    kept = pltpu.VMEM((modes, chans // 2), f32)
    sent = pltpu.VMEM((modes, chans // 2), bf16)

    small = min(chans // 2, 512)
    gate_shape = pltpu.VMEM((tok_rows, chans), bf16)
    state_shape = pltpu.VMEM((chans // LANES, SUBS * (modes + 1), LANES), f32)

    def states_of(own, operands, in_specs, out_shape, scratch, aliases):
        return pl.pallas_call(
            functools.partial(state_kernel, span=span, modes=modes, most=A_TILES, own=own, chunk=small),
            in_specs=[vmem] + in_specs,
            out_specs=[vmem] * (3 + len(out_shape)),
            out_shape=[gate_shape, state_shape, kept] + out_shape,
            scratch_shapes=scratch[:-1]
            + [
                pltpu.VMEM((A_TILES, wide_rows, LANES), f32),
                pltpu.VMEM((A_TILES, wide_rows, LANES), f32),
                pltpu.VMEM((A_TILES, modes, LANES), f32),
                pltpu.VMEM((A_TILES, span) + tile_shape, f32),
            ]
            + scratch[-1:],
            input_output_aliases=aliases,
            compiler_params=params,
            cost_estimate=cost(500, 6 * tok_rows * chans),
            name="block_states_own" if own else "block_states_give",
        )(near_by(masks), *operands)

    gates, states, give, key_own, value_own, heads = states_of(
        False,
        [far_off(key_in), far_off(value_in), taps, rates],
        [hbm, hbm, vmem, vmem],
        [key_half, key_half, pltpu.VMEM((2, 16, chans // 2), bf16)],
        [
            pltpu.VMEM((tok_rows, chans // 2), bf16),
            pltpu.VMEM((tok_rows, chans // 2), bf16),
            pltpu.SemaphoreType.DMA((2, chans // 2 // small + 1)),
        ],
        {},
    )
    gates, states, give = pl.pallas_call(
        functools.partial(patch_kernel, span=span, modes=modes),
        in_specs=[vmem] * 8,
        out_specs=[vmem] * 3,
        out_shape=[gate_shape, state_shape, kept],
        input_output_aliases={5: 0, 6: 1, 7: 2},
        compiler_params=params,
        name="first_rows",
    )(near_by(masks), near_by(heads), rims, taps, rates, near_by(gates), near_by(states), near_by(give))
    got = swap(give, "ctx")
    gates, states, own = states_of(
        True,
        [near_by(key_own), near_by(value_own), rims, taps, rates, near_by(gates), near_by(states)],
        [vmem] * 7,
        [],
        [],
        {6: 0, 7: 1},
    )
    got, gates, states, own = lax.optimization_barrier((got, gates, states, own))

    def near_piece(part, near):
        count = chans // NEAR_PARTS
        before = [] if near is None else [near_by(near)]
        return pl.pallas_call(
            functools.partial(
                near_kernel, span=span, modes=modes, most=N_TILES, first=part * count, count=count
            ),
            in_specs=[vmem] * (4 + len(before)),
            out_specs=vmem,
            out_shape=pltpu.VMEM((tok_rows, chans), f32),
            scratch_shapes=[
                pltpu.VMEM((N_TILES, span * (SUBS + 1), LANES), f32),
                pltpu.VMEM((N_TILES, span, LANES), f32),
            ],
            compiler_params=params,
            input_output_aliases={4: 0} if before else {},
            cost_estimate=cost(600 // NEAR_PARTS, 7 * tok_rows * count),
            name="near_part_%d" % part,
        )(near_by(masks), near_by(gates), rates, weights, *before)

    got = swap(give, "ctx")

    at = Masks(span)

    def pair_call(kernel, operands, out_shape, name, extra=(), **static):
        return pl.pallas_call(
            functools.partial(kernel, **static),
            in_specs=[vmem] * (len(operands) + 2 + len(extra)),
            out_specs=[vmem] * len(out_shape),
            out_shape=out_shape,
            compiler_params=params,
            name=name,
        )(near_by(masks), *[near_by(x) for x in operands], rates, *[near_by(x) for x in extra])

    total, ends = pair_call(pair_kernel, [own, got], [kept, sent], "pair_ends", rows=tok_rows, index=at.late)
    entering, near = [], None
    for m in range(levels):
        met = swap(ends, "ctx", 2 << m)
        if m < NEAR_PARTS:
            near = near_piece(m, near)
            if m == 0:
                q_short = query_piece(0, masks, None)
                met, q_short = lax.optimization_barrier((met, q_short))
            met, near = lax.optimization_barrier((met, near))
        ends, enter, *total = pair_call(
            level_kernel,
            [total, met],
            [sent, kept] + [kept] * (m < levels - 1),
            "level_%d" % m,
            extra=entering,
            rows=tok_rows,
            level=m,
            lead=at.lead(m),
            later=at.later(m),
        )
        entering = [enter]
        total = total[0] if total else None
    on = from_behind(ends, "ctx", 2 << levels)
    for m in range(levels, NEAR_PARTS):
        near = near_piece(m, near)
    q_short = query_piece(1, masks, q_short)
    on, q_short, near = lax.optimization_barrier((on, q_short, near))
    mine, give_back = pair_call(
        enter_kernel,
        entering + [on, own, got],
        [kept, kept],
        "pair_enter",
        rows=tok_rows,
        bit=2 << levels,
        lead=at.lead(levels),
        early_index=at.early,
    )
    got_back = swap(give_back, "ctx")

    alone = grp == 1
    resid = near_by(residual)

    def finish(own, enter, before):
        last = alone and not own
        out_specs = [hbm, vmem, vmem]
        out_shape = [
            jax.ShapeDtypeStruct((tok_rows, chans), bf16),
            pltpu.VMEM((chans // LANES, tok_rows, LANES), f32),
            pltpu.VMEM((tok_rows, LANES), f32),
        ]
        scratch = [
            pltpu.VMEM((tok_rows, chans // 2), bf16),
            copies(2),
            pltpu.VMEM((F_TILES, wide_rows, LANES), f32),
            pltpu.VMEM((F_TILES, modes, LANES), f32),
            pltpu.VMEM((F_TILES, SUBS * (modes + 1), LANES), f32),
        ]
        operands = [near_by(x) for x in (masks, states, enter, near, q_short)] + [resid, rims, taps, rates, weights]
        if last:
            operands.append(near_by(norm_gain.reshape(1, chans)))
            out_specs.append(hbm)
            out_shape.append(jax.ShapeDtypeStruct((tok_rows, chans), bf16))
            scratch.append(pltpu.VMEM((tok_rows, chans), bf16))
        count = len(operands)
        in_specs = [vmem] * count
        if before:
            operands += [far_off(before[0]), near_by(before[1]), near_by(before[2])]
            in_specs += [hbm, vmem, vmem]
        return pl.pallas_call(
            functools.partial(
                final_kernel, span=span, modes=modes, channels=chans if alone else 0, most=F_TILES, chunk=chunk, own=own
            ),
            in_specs=in_specs,
            out_specs=out_specs,
            out_shape=out_shape,
            scratch_shapes=scratch,
            input_output_aliases={count + i: i for i in range(len(before))},
            compiler_params=params,
            cost_estimate=cost(450, 9 * tok_rows * chans),
            name="far_part_own" if own else "far_part_other",
        )(*operands)

    before = finish(True, mine, [])
    got_back, *before = lax.optimization_barrier((got_back, *before))
    outs = finish(False, got_back, before)
    if alone:
        return (outs[0], outs[3])
    hidden_out, whole, sums = outs
    hidden = whole.transpose(1, 0, 2).reshape(tok_rows, chans)
    square_sum = lax.psum(jnp.sum(sums, axis=1), "grp")
    inverse_rms = lax.rsqrt(square_sum / (chans * grp) + 1e-06)
    normed = (hidden * inverse_rms[:, None] * norm_gain[None, :]).astype(bf16)
    return (hidden_out, normed)


def solution(mesh):
    return jax.shard_map(
        shards,
        mesh=mesh,
        in_specs=(
            P("ctx", "grp"),
            P("ctx", "grp"),
            P("ctx", "grp"),
            P(None, None, "grp"),
            P(None, "grp"),
            P(None, "grp"),
            P(),
            P("ctx", "grp"),
            P("grp"),
        ),
        out_specs=(P("ctx", "grp"), P("ctx", "grp")),
        check_vma=False,
    )
```

```python
import functools
import math

import jax
import jax.numpy as jnp
from jax import lax
from jax.experimental import pallas as pl
from jax.experimental.pallas import tpu as pltpu
from jax.sharding import PartitionSpec as P

SUBS = 8
LANES = 128
MIB = 1024 * 1024
A_TILES, N_TILES, Q_TILES, F_TILES = 2, 2, 4, 4
NEAR_PARTS = 2
f32 = jnp.float32
bf16 = jnp.bfloat16


def from_behind(shard, axis, by):
    count = lax.axis_size(axis)
    return lax.ppermute(shard, axis, [(i, i + by) for i in range(count - by)])


def swap(shard, axis, bit=1):
    return lax.ppermute(shard, axis, [(i, i ^ bit) for i in range(lax.axis_size(axis))])


def doc_start_rows(len_ref, base, span):
    rows = lax.broadcasted_iota(jnp.int32, (SUBS, LANES), 0) * span + base
    starts = [jnp.int32(0)]
    for d in range(len_ref.shape[0] - 1):
        starts.append(starts[-1] + len_ref[d])
    out = []
    for j in range(span):
        pos = rows + j
        best = jnp.zeros((SUBS, LANES), jnp.int32)
        for start in starts[1:]:
            best = jnp.where(pos >= start, start, best)
        out.append(best)
    return rows, out


def flag(cond):
    return jnp.where(cond, 1.0, 0.0).astype(f32)


def each_group(count, most, group):
    size = math.gcd(count, most)

    def step(i, carry):
        group([pl.multiple_of((i * size + m) * LANES, LANES) for m in range(size)])
        return carry

    lax.fori_loop(0, count // size, step, 0)


def each_chunk(chans, chunk, before, group, after, most, start=0):
    def step(c, carry):
        before(c)

        def inner(lanes):
            group([pl.multiple_of(c * chunk + lane, LANES) for lane in lanes])

        each_group(chunk // LANES, most, inner)
        after(c)
        return carry

    lax.fori_loop(start, chans // chunk, step, 0)


def cols_copy(src, dst, sem, c, chunk):
    cols = pl.ds(pl.multiple_of(c * chunk, chunk), chunk)
    return pltpu.make_async_copy(src.at[:, cols], dst.at[:, cols], sem.at[c])


def cols_of(lane):
    return pl.ds(lane, LANES)


def row_of(ref, index):
    return ref[pl.ds(index, SUBS, stride=0), :]


def spread(x, wide, span):
    x = x.astype(f32)
    for b in range(SUBS):
        wide[pl.ds(b * (span + 1), span), :] = x[b * span : (b + 1) * span]


class Conv:
    def __init__(self, wide, rim, taps, span):
        self.wide, self.span = wide, span
        self.taps = [jnp.broadcast_to(taps[m : m + 1], (SUBS, LANES)) for m in range(3)]
        top = lax.broadcasted_iota(jnp.int32, (SUBS, LANES), 0) == 0
        ahead = [0.0, 0.0] if rim is None else [jnp.broadcast_to(rim[m : m + 1], (SUBS, LANES)) for m in range(2)]
        self.behind = [jnp.where(top, ahead[m], pltpu.roll(self.row(span - 2 + m), 1, 0)) for m in range(2)]

    def row(self, j):
        return self.wide[pl.ds(j, SUBS, stride=self.span + 1), :]

    def step(self, j, keep_one, keep_two):
        here = self.row(j)
        two, one = self.behind
        self.behind = [one, here]
        return self.taps[0] * here + (self.taps[1] * one) * keep_one + (self.taps[2] * two) * keep_two


def half_start(chans, own):
    parity = lax.rem(lax.axis_index("ctx"), 2)
    return pl.multiple_of((parity if own else 1 - parity) * (chans // 2), LANES)


def twice(mask, modes):
    return jnp.concatenate([mask] * (modes // SUBS), axis=0)


def sub_state(state_ref, lane, b, modes):
    return state_ref[lax.div(lane, LANES), pl.ds(b * (modes + 1), modes), :]


def state_kernel(masks, *refs, span, modes, most, own, chunk):
    if own:
        key_ref, value_ref, rim_ref, taps_ref, rate_ref, _, _, gate_ref, state_ref, end_ref, wide_k, wide_v, tables, held = refs
    else:
        (ahead_ref, key_in, value_in, taps_ref, rate_ref, gate_ref, state_ref, end_ref, key_own, value_own, heads,
         key_ref, value_ref, wide_k, wide_v, tables, held, sems) = refs
    half = key_ref.shape[1]
    first = half_start(2 * half, own)
    if not own:
        def fetch(c):
            there = pl.ds(pl.multiple_of(first + c * chunk, chunk), chunk)
            here = pl.ds(pl.multiple_of(c * chunk, chunk), chunk)
            return [
                pltpu.make_async_copy(key_in.at[:, there], key_ref.at[:, here], sems.at[0, c]),
                pltpu.make_async_copy(value_in.at[:, there], value_ref.at[:, here], sems.at[1, c]),
            ]

        cols = pl.ds(half_start(2 * half, True), half)
        others = [
            pltpu.make_async_copy(key_in.at[:, cols], key_own, sems.at[0, half // chunk]),
            pltpu.make_async_copy(value_in.at[:, cols], value_own, sems.at[1, half // chunk]),
        ]
        for c in range(1, half // chunk):
            for copy in fetch(c):
                copy.start()
    at = Masks(span)

    def group(lanes, keys=key_ref, values=value_ref):
        for slot, lane in enumerate(lanes):
            spread(keys[:, cols_of(pl.multiple_of(lane - first, LANES))], wide_k.at[slot], span)
            spread(values[:, cols_of(pl.multiple_of(lane - first, LANES))], wide_v.at[slot], span)
            rate = rate_ref[:, cols_of(lane)]
            tables[slot] = jnp.exp(-rate)
        convs = [
            [
                Conv(wide.at[slot], rim_ref[i, :, cols_of(lane)].astype(f32) if own else None, taps_ref[i, :, cols_of(lane)], span)
                for i, wide in ((1, wide_k), (2, wide_v))
            ]
            for slot, lane in enumerate(lanes)
        ]
        last = [None] * len(lanes)
        for j in range(span):
            keep_one, keep_two = masks[at.one + j], masks[at.two + j]
            for slot, lane in enumerate(lanes):
                k_short, v_short = [conv.step(j, keep_one, keep_two) for conv in convs[slot]]
                if j % 2 == 0:
                    last[slot] = k_short * v_short
                    continue
                pair = jnp.concatenate([last[slot], k_short * v_short], axis=0).astype(bf16)
                gate_ref[pl.ds((j - 1) * SUBS, 2 * SUBS), cols_of(lane)] = pair
                pair = pair.astype(f32)
                used = at.inner if j == 1 and not own else at.last + j - 1
                held[slot, j - 1] = pair[:SUBS] * masks[used]
                held[slot, j] = pair[SUBS:] * masks[used + 1]
        for slot, lane in enumerate(lanes):
            decay = [row_of(tables.at[slot], n) for n in range(modes)]
            state = [held[slot, 0]] * modes
            for j in range(1, span):
                gate = held[slot, j]
                state = [decay[n] * state[n] + gate for n in range(modes)]
            for n in range(modes):
                state_ref[lax.div(lane, LANES), pl.ds(n, SUBS, stride=modes + 1), :] = state[n]
        for slot, lane in enumerate(lanes):
            leap = jnp.exp(-float(span) * rate_ref[:, cols_of(lane)])
            end = sub_state(state_ref, lane, 0, modes)
            for b in range(1, SUBS):
                end = (leap * twice(masks[at.passes + b], modes)) * end + sub_state(state_ref, lane, b, modes)
            end_ref[:, cols_of(pl.multiple_of(lane - first, LANES))] = end

    def shifted(lanes, *sources):
        group([pl.multiple_of(first + lane, LANES) for lane in lanes], *sources)

    if own:
        each_group(half // LANES, most, shifted)
    else:
        def before(c):
            for copy in fetch(c):
                copy.wait()

        each_group(chunk // LANES, most, lambda lanes: shifted(lanes, ahead_ref.at[0], ahead_ref.at[1]))
        for copy in others:
            copy.start()
        each_chunk(half, chunk, before, shifted, lambda c: None, most, 1)
        rows = pl.ds(0, heads.shape[1])
        for i, ref in enumerate((key_ref, value_ref)):
            heads[i, :, pl.ds(0, chunk)] = ahead_ref[i, rows, :]
            if half > chunk:
                heads[i, :, pl.ds(chunk, half - chunk)] = ref[rows, pl.ds(chunk, half - chunk)]
        for copy in others:
            copy.wait()


def patch_kernel(
    masks, heads, rim_ref, taps_ref, rate_ref, gate_in, state_in, end_in, gate_ref, state_ref, end_ref, *, span, modes
):
    half = end_ref.shape[1]
    first = half_start(2 * half, False)
    at = Masks(span)
    rows = lax.broadcasted_iota(jnp.int32, (2 * SUBS, LANES), 0)

    def one(index):
        return masks[index][0:1]

    def group(lanes):
        for lane in lanes:
            there = cols_of(pl.multiple_of(first + lane, LANES))
            shorts = []
            for i in (1, 2):
                here = heads[i - 1, :, cols_of(lane)].astype(f32)
                rim = rim_ref[i, :, there].astype(f32)
                tap = taps_ref[i, :, there]
                shorts.append([
                    tap[0:1] * here[0:1] + (tap[1:2] * rim[1:2]) * one(at.one) + (tap[2:3] * rim[0:1]) * one(at.two),
                    tap[0:1] * here[1:2] + (tap[1:2] * here[0:1]) * one(at.one + 1) + (tap[2:3] * rim[1:2]) * one(at.two + 1),
                ])
            gates = [(k * v).astype(bf16).astype(f32) for k, v in zip(*shorts)]
            old = gate_in[pl.ds(0, 2 * SUBS), there].astype(f32)
            new = jnp.where(rows == 0, gates[0], jnp.where(rows == SUBS, gates[1], old))
            gate_ref[pl.ds(0, 2 * SUBS), there] = new.astype(bf16)
            rate = rate_ref[:, there]
            added = jnp.exp(-float(span - 1) * rate) * (gates[0] * one(at.last)) + jnp.exp(-float(span - 2) * rate) * (
                gates[1] * one(at.last + 1)
            )
            tile = lax.div(first + lane, LANES)
            state_ref[tile, pl.ds(0, modes), :] = state_in[tile, pl.ds(0, modes), :] + added
            reach = jnp.exp(-float((SUBS - 1) * span) * rate) * one(at.rest)
            end_ref[:, cols_of(lane)] = end_in[:, cols_of(lane)] + reach * added

    each_group(half // LANES, 4, group)


def tail_kernel(
    base_ref, len_ref, query_ref, key_ref, value_ref, tail_ref, masks, ahead_ref, bufs, rows_of, sems, *, span, levels
):
    rows, count = query_ref.shape[0], bufs.shape[1]
    copies = [
        pltpu.make_async_copy(ref.at[pl.ds(rows - count, count)], bufs.at[i], sems.at[i])
        for i, ref in enumerate((query_ref, key_ref, value_ref))
    ]
    cols = pl.ds(half_start(query_ref.shape[1], False), ahead_ref.shape[2])
    aheads = [
        pltpu.make_async_copy(ref.at[:, cols], ahead_ref.at[i], sems.at[3 + i])
        for i, ref in enumerate((key_ref, value_ref))
    ]
    for copy in copies + aheads:
        copy.start()
    write_masks(base_ref, len_ref, masks, rows_of, span, levels)
    for i, copy in enumerate(copies):
        copy.wait()
        tail_ref[i] = bufs[i].astype(f32)[count - 2 :].astype(bf16)
    for copy in aheads:
        copy.wait()


def unbroken(len_ref, first, count):
    start = jnp.int32(0)
    whole = jnp.where((first <= 0) & (first + count > 0), 0.0, 1.0)
    for d in range(len_ref.shape[0] - 1):
        start = start + len_ref[d]
        whole = jnp.where((start >= first) & (start < first + count), 0.0, whole)
    return whole.astype(f32)


class Masks:
    def __init__(self, span):
        self.one, self.two, self.last, self.enter = 0, span, 2 * span, 3 * span
        self.passes = 4 * span
        self.edges = self.passes + SUBS
        self.late = self.edges + 3
        self.early = self.late + 1
        self.rest = self.late + 2
        self.inner = self.late + 3
        self.levels = self.late + 5

    def lead(self, level):
        return self.levels + 2 * level

    def later(self, level):
        return self.levels + 2 * level + 1

    def count(self, levels):
        return self.levels + 2 * levels + 1


def write_masks(base_ref, len_ref, masks, rows_of, span, levels):
    at = Masks(span)
    rows, starts = doc_start_rows(len_ref, base_ref[0], span)
    for j in range(span):
        masks[at.one + j] = flag(starts[j] < rows + j)
        masks[at.two + j] = flag(starts[j] < rows + (j - 1))
        masks[at.last + j] = flag(starts[span - 1] <= rows + j)
        masks[at.enter + j] = flag(starts[j] < rows)
    top = flag(lax.broadcasted_iota(jnp.int32, (SUBS, LANES), 0) == 0)
    for j in range(2):
        masks[at.inner + j] = (1.0 - top) * masks[at.last + j]
    masks[at.edges] = top * masks[at.one]
    masks[at.edges + 1] = top * masks[at.two]
    masks[at.edges + 2] = top * masks[at.two + 1]
    size = SUBS * span
    parity = lax.rem(lax.div(base_ref[0], size), 2)
    pair_at = base_ref[0] - parity * size
    rows_of[...] = flag(starts[span - 1] < rows)
    for b in range(SUBS):
        masks[at.passes + b] = row_of(rows_of, b)
    ranges = []
    flags = []
    ranges += [(pair_at + size, size), (pair_at, size), (base_ref[0] + span, size - span)]
    flags += [at.late, at.early, at.rest]
    for m in range(levels + 1):
        group = 2 * size << m
        group_at = base_ref[0] - lax.rem(base_ref[0], group)
        ranges.append((group_at, pair_at - group_at))
        flags.append(at.lead(m))
        if m < levels:
            ranges.append((group_at + group * (1 - lax.rem(lax.div(base_ref[0], group), 2)), group))
            flags.append(at.later(m))
    for index, (first, count) in zip(flags, ranges):
        masks[index] = jnp.full((SUBS, LANES), unbroken(len_ref, first, count), f32)


def near_kernel(masks, gate_ref, rate_ref, weight_ref, *refs, span, modes, most, first, count):
    near_ref, sums, tap_rows = refs[-3:]
    at = Masks(span)

    def group(lanes):
        for slot, lane in enumerate(lanes):
            decay = jnp.exp(-rate_ref[:, cols_of(lane)])
            term = weight_ref[:, cols_of(lane)]
            for lag in range(span):
                part = term[:SUBS]
                for n in range(SUBS, modes, SUBS):
                    part = part + term[n : n + SUBS]
                sums[slot, pl.ds(lag * (SUBS + 1), SUBS), :] = part
                term = term * decay
        for slot in range(len(lanes)):
            for first_lag in range(0, span, SUBS):
                total = [
                    sums[slot, pl.ds(first_lag * (SUBS + 1) + m, SUBS, stride=SUBS + 1), :] for m in range(SUBS)
                ]
                while len(total) > 1:
                    total = [total[m] + total[m + 1] for m in range(0, len(total), 2)]
                tap_rows[slot, pl.ds(first_lag, SUBS), :] = total[0]
        taps = [[row_of(tap_rows.at[slot], lag) for lag in range(span)] for slot in range(len(lanes))]
        for parts, lane in zip(taps, lanes):
            live = []
            for j in range(span):
                if j % 2 == 0:
                    pair = gate_ref[pl.ds(j * SUBS, 2 * SUBS), cols_of(lane)].astype(f32)
                keep = masks[at.one + j]
                live = [g * keep for g in live]
                live.append(pair[(j % 2) * SUBS : (j % 2 + 1) * SUBS])
                total = parts[0] * live[j]
                for lag in range(1, j + 1):
                    total = total + parts[lag] * live[j - lag]
                near_ref[pl.ds(j * SUBS, SUBS), cols_of(lane)] = total

    each_group(count // LANES, most, lambda lanes: group([pl.multiple_of(first + lane, LANES) for lane in lanes]))


def query_kernel(masks, query_ref, taps_ref, *refs, span, most, chunk, first, count):
    short_ref, query_buf, sems, wide_q = refs[-4:]

    def fetch(c):
        there = pl.ds(first + c * chunk if isinstance(c, int) else pl.multiple_of(first + c * chunk, chunk), chunk)
        here = pl.ds(c * chunk if isinstance(c, int) else pl.multiple_of(c * chunk, chunk), chunk)
        return pltpu.make_async_copy(query_ref.at[:, there], query_buf.at[:, here], sems.at[c])

    for c in range(count // chunk):
        fetch(c).start()
    at = Masks(span)

    def group(lanes):
        for slot, lane in enumerate(lanes):
            spread(query_buf[:, cols_of(lane)], wide_q.at[slot], span)
        convs = [
            Conv(wide_q.at[slot], None, taps_ref[0, :, cols_of(pl.multiple_of(first + lane, LANES))], span)
            for slot, lane in enumerate(lanes)
        ]
        for j in range(span):
            keep_one, keep_two = masks[at.one + j], masks[at.two + j]
            for slot, lane in enumerate(lanes):
                short_ref[pl.ds(j * SUBS, SUBS), cols_of(pl.multiple_of(first + lane, LANES))] = convs[slot].step(j, keep_one, keep_two)

    each_chunk(count, chunk, lambda c: fetch(c).wait(), group, lambda c: None, most)


def pair_rates(rate_ref, count):
    parity = lax.rem(lax.axis_index("ctx"), 2)
    return parity, rate_ref[:, pl.ds(pl.multiple_of(parity * count, LANES), count)]


def early_late(parity, own, got):
    odd = jnp.full(own.shape, parity, jnp.int32) == 1
    return jnp.where(odd, got, own), jnp.where(odd, own, got)


def leap(masks, index, rate, rows):
    return jnp.exp(-float(rows) * rate) * masks[index][0:1, 0:1]


def pair_kernel(masks, own_ref, got_ref, rate_ref, total_ref, sent_ref, *, rows, index):
    parity, rate = pair_rates(rate_ref, own_ref.shape[1])
    early, late = early_late(parity, own_ref[...], got_ref[...])
    total = late + leap(masks, index, rate, rows) * early
    total_ref[...] = total
    sent_ref[...] = total.astype(bf16)


def lead_leap(masks, index, rate, rows, bit):
    me = lax.axis_index("ctx")
    lead = (lax.rem(me, bit) - lax.rem(me, 2)) * rows
    return jnp.exp(rate * -lead.astype(f32)) * masks[index][0:1, 0:1]


def level_kernel(masks, total_ref, got_ref, rate_ref, *refs, rows, level, lead, later):
    before_ref = refs[0] if level else None
    sent_ref, enter_ref, *new_ref = refs[1 if level else 0 :]
    _, rate = pair_rates(rate_ref, total_ref.shape[1])
    bit = 2 << level
    after = lax.rem(lax.div(lax.axis_index("ctx"), bit), 2)
    got = got_ref[...].astype(f32)
    early, late = early_late(after, total_ref[...], got)
    total = late + leap(masks, later, rate, bit * rows) * early
    for ref in new_ref:
        ref[...] = total
    sent_ref[...] = total.astype(bf16)
    entering = jnp.where(jnp.full(got.shape, after, jnp.int32) == 1, got, 0.0) * lead_leap(masks, lead, rate, rows, bit)
    enter_ref[...] = entering if before_ref is None else before_ref[...] + entering


def enter_kernel(
    masks, before_ref, got_ref, own_ref, other_ref, rate_ref, mine_ref, give_ref, *, rows, bit, lead, early_index
):
    parity, rate = pair_rates(rate_ref, own_ref.shape[1])
    first = before_ref[...] + lead_leap(masks, lead, rate, rows, bit) * got_ref[...].astype(f32)
    early, _ = early_late(parity, own_ref[...], other_ref[...])
    second = early + leap(masks, early_index, rate, rows) * first
    give, mine = early_late(parity, second, first)
    mine_ref[...] = mine
    give_ref[...] = give


def final_kernel(
    masks, state_ref, enter_ref, near_ref, short_ref, resid_ref, rim_ref, taps_ref, rate_ref, weight_ref, *refs,
    span, modes, channels, most, chunk, own,
):
    if own:
        hidden_out, whole, sums, hidden_ref, sems, wide, tables, starts_at = refs
    elif channels:
        gain_ref, _, _, _, hidden_out, whole, sums, normed_out, hidden_ref, sems, wide, tables, starts_at, normed_ref = refs
    else:
        _, _, _, hidden_out, whole, sums, hidden_ref, sems, wide, tables, starts_at = refs
    chans = resid_ref.shape[1]
    half = chans // 2
    first = half_start(chans, own)
    at = Masks(span)

    def store(c):
        here = pl.ds(pl.multiple_of(c * chunk, chunk), chunk)
        there = pl.ds(pl.multiple_of(first + c * chunk, chunk), chunk)
        return pltpu.make_async_copy(hidden_ref.at[:, here], hidden_out.at[:, there], sems.at[0, c])

    def store_normed(c):
        return cols_copy(normed_ref, normed_out, sems.at[1], c, chunk)

    if own:
        sums[...] = jnp.zeros(sums.shape, f32)

    def group(lanes):
        for slot, lane in enumerate(lanes):
            state = enter_ref[:, cols_of(pl.multiple_of(lane - first, LANES))]
            rate = rate_ref[:, cols_of(lane)]
            weight = weight_ref[:, cols_of(lane)]
            tables[slot] = jnp.exp(-rate)
            leap = jnp.exp(-float(span) * rate)
            for b in range(SUBS):
                starts_at[slot, pl.ds(b * (modes + 1), modes), :] = weight * state
                if b < SUBS - 1:
                    state = (leap * twice(masks[at.passes + b], modes)) * state + sub_state(state_ref, lane, b, modes)
        for slot, lane in enumerate(lanes):
            part = [starts_at[slot, pl.ds(n, SUBS, stride=modes + 1), :] for n in range(modes)]
            decay = [row_of(tables.at[slot], n) for n in range(modes)]
            rim = rim_ref[0, :, cols_of(lane)].astype(f32)
            tap = taps_ref[0, :, cols_of(lane)]
            edge = [
                (tap[1:2] * rim[1:2]) * masks[at.edges] + (tap[2:3] * rim[0:1]) * masks[at.edges + 1],
                (tap[2:3] * rim[1:2]) * masks[at.edges + 2],
            ]
            for j in range(span):
                part = [part[n] * decay[n] for n in range(modes)]
                total = part
                while len(total) > 1:
                    total = [total[m] + total[m + 1] for m in range(0, len(total), 2)]
                conv = near_ref[pl.ds(j * SUBS, SUBS), cols_of(lane)] + total[0] * masks[at.enter + j]
                conv = conv.astype(bf16).astype(f32)
                short = short_ref[pl.ds(j * SUBS, SUBS), cols_of(lane)]
                if j < 2:
                    short = short + edge[j]
                wide[slot, pl.ds(j, SUBS, stride=span + 1), :] = short * conv
        for b in range(SUBS):
            rows = pl.ds(b * span, span)
            squares = sums[rows, :]
            for slot, lane in enumerate(lanes):
                hidden = wide[slot, pl.ds(b * (span + 1), span), :] + resid_ref[rows, cols_of(lane)].astype(f32)
                whole[lax.div(lane, LANES), rows, :] = hidden
                hidden_ref[rows, cols_of(pl.multiple_of(lane - first, LANES))] = hidden.astype(bf16)
                squares = squares + hidden * hidden
            sums[rows, :] = squares

    each_chunk(
        half,
        chunk,
        lambda c: None,
        lambda lanes: group([pl.multiple_of(first + lane, LANES) for lane in lanes]),
        lambda c: store(c).start(),
        most,
    )
    if channels and not own:
        inverse = lax.rsqrt(jnp.sum(sums[...], axis=1, keepdims=True) / channels + 1e-06)
        sums[...] = jnp.broadcast_to(inverse, sums.shape)

        def scale(lanes):
            for lane in lanes:
                normed = whole[lax.div(lane, LANES)] * sums[...] * gain_ref[:, cols_of(lane)]
                normed_ref[:, cols_of(lane)] = normed.astype(bf16)

        each_chunk(chans, chunk, lambda c: None, scale, lambda c: store_normed(c).start(), 4)
        for c in range(chans // chunk):
            store_normed(c).wait()
    for c in range(half // chunk):
        store(c).wait()


def shards(
    query_in, key_in, value_in, short_taps, decay_rate, residues, doc_lengths, residual, norm_gain
):
    tok_rows, chans = query_in.shape
    modes = decay_rate.shape[0]
    span = tok_rows // SUBS
    blocks = lax.axis_size("ctx")
    grp = lax.axis_size("grp")
    chunk = min(chans // 2, 512)
    pieces = chans // chunk
    ctx_index = lax.axis_index("ctx")
    base = (ctx_index * tok_rows).astype(jnp.int32).reshape(1)
    weight = residues * jnp.sqrt(-jnp.expm1(-2.0 * decay_rate))

    smem = pl.BlockSpec(memory_space=pltpu.SMEM)
    vmem = pl.BlockSpec(memory_space=pltpu.VMEM)
    hbm = pl.BlockSpec(memory_space=pltpu.HBM)
    tile_shape = (SUBS, LANES)
    wide_rows = SUBS * (span + 1)
    params = pltpu.CompilerParams(vmem_limit_bytes=16 * MIB)

    lengths = pltpu.with_memory_space_constraint(doc_lengths, pltpu.HBM)

    def near_by(x):
        return pltpu.with_memory_space_constraint(x, pltpu.VMEM)

    def far_off(x):
        return pltpu.with_memory_space_constraint(x, pltpu.HBM)

    def copies(kinds):
        return pltpu.SemaphoreType.DMA((kinds, pieces))

    def cost(per_tile, moved):
        return pl.CostEstimate(flops=per_tile * (chans // LANES) * SUBS * LANES, bytes_accessed=moved, transcendentals=0)

    levels = max(1, (blocks // 4).bit_length() - 2)
    mask_shape = (Masks(span).count(levels),) + tile_shape
    small = min(chans // 2, 512)
    tails, masks, ahead = pl.pallas_call(
        functools.partial(tail_kernel, span=span, levels=levels),
        in_specs=[smem, smem, hbm, hbm, hbm],
        out_specs=[vmem, vmem, vmem],
        out_shape=[
            pltpu.VMEM((3, 2, chans), bf16), pltpu.VMEM(mask_shape, f32), pltpu.VMEM((2, tok_rows, small), bf16)
        ],
        scratch_shapes=[
            pltpu.VMEM((3, 16, chans), bf16), pltpu.VMEM(tile_shape, f32), pltpu.SemaphoreType.DMA((5,))
        ],
        compiler_params=params,
        name="tails",
    )(base, lengths, far_off(query_in), far_off(key_in), far_off(value_in))
    rim_rows = from_behind(tails, "ctx", 1)
    def query_piece(part, masks, before):
        count = chans // 2
        scratch = [
            pltpu.VMEM((tok_rows, count), bf16),
            pltpu.SemaphoreType.DMA((count // chunk,)),
            pltpu.VMEM((Q_TILES, wide_rows, LANES), f32),
        ]
        operands = [near_by(masks), far_off(query_in), taps] + ([near_by(before)] if part else [])
        return pl.pallas_call(
            functools.partial(
                query_kernel, span=span, most=Q_TILES, chunk=chunk, first=part * count, count=count
            ),
            in_specs=[vmem, hbm, vmem] + [vmem] * (len(operands) - 3),
            out_specs=vmem,
            out_shape=pltpu.VMEM((tok_rows, chans), f32),
            scratch_shapes=scratch,
            input_output_aliases={3: 0} if part else {},
            compiler_params=params,
            cost_estimate=cost(100, 3 * tok_rows * chans),
            name="query_part_%d" % part,
        )(*operands)

    key_half = pltpu.VMEM((tok_rows, chans // 2), bf16)
    rates, weights, taps, rims = near_by(decay_rate), near_by(weight), near_by(short_taps), near_by(rim_rows)
    kept = pltpu.VMEM((modes, chans // 2), f32)
    sent = pltpu.VMEM((modes, chans // 2), bf16)

    gate_shape = pltpu.VMEM((tok_rows, chans), bf16)
    state_shape = pltpu.VMEM((chans // LANES, SUBS * (modes + 1), LANES), f32)

    def states_of(own, operands, in_specs, out_shape, scratch, aliases):
        return pl.pallas_call(
            functools.partial(state_kernel, span=span, modes=modes, most=A_TILES, own=own, chunk=small),
            in_specs=[vmem] + in_specs,
            out_specs=[vmem] * (3 + len(out_shape)),
            out_shape=[gate_shape, state_shape, kept] + out_shape,
            scratch_shapes=scratch[:-1]
            + [
                pltpu.VMEM((A_TILES, wide_rows, LANES), f32),
                pltpu.VMEM((A_TILES, wide_rows, LANES), f32),
                pltpu.VMEM((A_TILES, modes, LANES), f32),
                pltpu.VMEM((A_TILES, span) + tile_shape, f32),
            ]
            + scratch[-1:],
            input_output_aliases=aliases,
            compiler_params=params,
            cost_estimate=cost(500, 6 * tok_rows * chans),
            name="block_states_own" if own else "block_states_give",
        )(near_by(masks), *operands)

    gates, states, give, key_own, value_own, heads = states_of(
        False,
        [near_by(ahead), far_off(key_in), far_off(value_in), taps, rates],
        [vmem, hbm, hbm, vmem, vmem],
        [key_half, key_half, pltpu.VMEM((2, 16, chans // 2), bf16)],
        [
            pltpu.VMEM((tok_rows, chans // 2), bf16),
            pltpu.VMEM((tok_rows, chans // 2), bf16),
            pltpu.SemaphoreType.DMA((2, chans // 2 // small + 1)),
        ],
        {},
    )
    gates, states, give = pl.pallas_call(
        functools.partial(patch_kernel, span=span, modes=modes),
        in_specs=[vmem] * 8,
        out_specs=[vmem] * 3,
        out_shape=[gate_shape, state_shape, kept],
        input_output_aliases={5: 0, 6: 1, 7: 2},
        compiler_params=params,
        name="first_rows",
    )(near_by(masks), near_by(heads), rims, taps, rates, near_by(gates), near_by(states), near_by(give))
    got = swap(give, "ctx")
    gates, states, own = states_of(
        True,
        [near_by(key_own), near_by(value_own), rims, taps, rates, near_by(gates), near_by(states)],
        [vmem] * 7,
        [],
        [],
        {6: 0, 7: 1},
    )
    got, gates, states, own = lax.optimization_barrier((got, gates, states, own))

    def near_piece(part, near):
        count = chans // NEAR_PARTS
        before = [] if near is None else [near_by(near)]
        return pl.pallas_call(
            functools.partial(
                near_kernel, span=span, modes=modes, most=N_TILES, first=part * count, count=count
            ),
            in_specs=[vmem] * (4 + len(before)),
            out_specs=vmem,
            out_shape=pltpu.VMEM((tok_rows, chans), f32),
            scratch_shapes=[
                pltpu.VMEM((N_TILES, span * (SUBS + 1), LANES), f32),
                pltpu.VMEM((N_TILES, span, LANES), f32),
            ],
            compiler_params=params,
            input_output_aliases={4: 0} if before else {},
            cost_estimate=cost(600 // NEAR_PARTS, 7 * tok_rows * count),
            name="near_part_%d" % part,
        )(near_by(masks), near_by(gates), rates, weights, *before)

    got = swap(give, "ctx")

    at = Masks(span)

    def pair_call(kernel, operands, out_shape, name, extra=(), **static):
        return pl.pallas_call(
            functools.partial(kernel, **static),
            in_specs=[vmem] * (len(operands) + 2 + len(extra)),
            out_specs=[vmem] * len(out_shape),
            out_shape=out_shape,
            compiler_params=params,
            name=name,
        )(near_by(masks), *[near_by(x) for x in operands], rates, *[near_by(x) for x in extra])

    total, ends = pair_call(pair_kernel, [own, got], [kept, sent], "pair_ends", rows=tok_rows, index=at.late)
    entering, near = [], None
    for m in range(levels):
        met = swap(ends, "ctx", 2 << m)
        if m < NEAR_PARTS:
            near = near_piece(m, near)
            if m == 0:
                q_short = query_piece(0, masks, None)
                met, q_short = lax.optimization_barrier((met, q_short))
            met, near = lax.optimization_barrier((met, near))
        ends, enter, *total = pair_call(
            level_kernel,
            [total, met],
            [sent, kept] + [kept] * (m < levels - 1),
            "level_%d" % m,
            extra=entering,
            rows=tok_rows,
            level=m,
            lead=at.lead(m),
            later=at.later(m),
        )
        entering = [enter]
        total = total[0] if total else None
    on = from_behind(ends, "ctx", 2 << levels)
    for m in range(levels, NEAR_PARTS):
        near = near_piece(m, near)
    q_short = query_piece(1, masks, q_short)
    on, q_short, near = lax.optimization_barrier((on, q_short, near))
    mine, give_back = pair_call(
        enter_kernel,
        entering + [on, own, got],
        [kept, kept],
        "pair_enter",
        rows=tok_rows,
        bit=2 << levels,
        lead=at.lead(levels),
        early_index=at.early,
    )
    got_back = swap(give_back, "ctx")

    alone = grp == 1
    resid = near_by(residual)

    def finish(own, enter, before):
        last = alone and not own
        out_specs = [hbm, vmem, vmem]
        out_shape = [
            jax.ShapeDtypeStruct((tok_rows, chans), bf16),
            pltpu.VMEM((chans // LANES, tok_rows, LANES), f32),
            pltpu.VMEM((tok_rows, LANES), f32),
        ]
        scratch = [
            pltpu.VMEM((tok_rows, chans // 2), bf16),
            copies(2),
            pltpu.VMEM((F_TILES, wide_rows, LANES), f32),
            pltpu.VMEM((F_TILES, modes, LANES), f32),
            pltpu.VMEM((F_TILES, SUBS * (modes + 1), LANES), f32),
        ]
        operands = [near_by(x) for x in (masks, states, enter, near, q_short)] + [resid, rims, taps, rates, weights]
        if last:
            operands.append(near_by(norm_gain.reshape(1, chans)))
            out_specs.append(hbm)
            out_shape.append(jax.ShapeDtypeStruct((tok_rows, chans), bf16))
            scratch.append(pltpu.VMEM((tok_rows, chans), bf16))
        count = len(operands)
        in_specs = [vmem] * count
        if before:
            operands += [far_off(before[0]), near_by(before[1]), near_by(before[2])]
            in_specs += [hbm, vmem, vmem]
        return pl.pallas_call(
            functools.partial(
                final_kernel, span=span, modes=modes, channels=chans if alone else 0, most=F_TILES, chunk=chunk, own=own
            ),
            in_specs=in_specs,
            out_specs=out_specs,
            out_shape=out_shape,
            scratch_shapes=scratch,
            input_output_aliases={count + i: i for i in range(len(before))},
            compiler_params=params,
            cost_estimate=cost(450, 9 * tok_rows * chans),
            name="far_part_own" if own else "far_part_other",
        )(*operands)

    before = finish(True, mine, [])
    got_back, *before = lax.optimization_barrier((got_back, *before))
    outs = finish(False, got_back, before)
    if alone:
        return (outs[0], outs[3])
    hidden_out, whole, sums = outs
    hidden = whole.transpose(1, 0, 2).reshape(tok_rows, chans)
    square_sum = lax.psum(jnp.sum(sums, axis=1), "grp")
    inverse_rms = lax.rsqrt(square_sum / (chans * grp) + 1e-06)
    normed = (hidden * inverse_rms[:, None] * norm_gain[None, :]).astype(bf16)
    return (hidden_out, normed)


def solution(mesh):
    return jax.shard_map(
        shards,
        mesh=mesh,
        in_specs=(
            P("ctx", "grp"),
            P("ctx", "grp"),
            P("ctx", "grp"),
            P(None, None, "grp"),
            P(None, "grp"),
            P(None, "grp"),
            P(),
            P("ctx", "grp"),
            P("grp"),
        ),
        out_specs=(P("ctx", "grp"), P("ctx", "grp")),
        check_vma=False,
    )
```

```python
import functools
import math

import jax
import jax.numpy as jnp
from jax import lax
from jax.experimental import pallas as pl
from jax.experimental.pallas import tpu as pltpu
from jax.sharding import PartitionSpec as P

SUBS = 8
LANES = 128
MIB = 1024 * 1024
A_TILES, N_TILES, Q_TILES, F_TILES = 2, 2, 4, 4
NEAR_PARTS = 2
f32 = jnp.float32
bf16 = jnp.bfloat16


def from_behind(shard, axis, by):
    count = lax.axis_size(axis)
    return lax.ppermute(shard, axis, [(i, i + by) for i in range(count - by)])


def swap(shard, axis, bit=1):
    return lax.ppermute(shard, axis, [(i, i ^ bit) for i in range(lax.axis_size(axis))])


def doc_start_rows(len_ref, base, span):
    rows = lax.broadcasted_iota(jnp.int32, (SUBS, LANES), 0) * span + base
    starts = [jnp.int32(0)]
    for d in range(len_ref.shape[0] - 1):
        starts.append(starts[-1] + len_ref[d])
    out = []
    for j in range(span):
        pos = rows + j
        best = jnp.zeros((SUBS, LANES), jnp.int32)
        for start in starts[1:]:
            best = jnp.where(pos >= start, start, best)
        out.append(best)
    return rows, out


def flag(cond):
    return jnp.where(cond, 1.0, 0.0).astype(f32)


def each_group(count, most, group):
    size = math.gcd(count, most)

    def step(i, carry):
        group([pl.multiple_of((i * size + m) * LANES, LANES) for m in range(size)])
        return carry

    lax.fori_loop(0, count // size, step, 0)


def each_chunk(chans, chunk, before, group, after, most, start=0):
    def step(c, carry):
        before(c)

        def inner(lanes):
            group([pl.multiple_of(c * chunk + lane, LANES) for lane in lanes])

        each_group(chunk // LANES, most, inner)
        after(c)
        return carry

    lax.fori_loop(start, chans // chunk, step, 0)


def cols_copy(src, dst, sem, c, chunk):
    cols = pl.ds(pl.multiple_of(c * chunk, chunk), chunk)
    return pltpu.make_async_copy(src.at[:, cols], dst.at[:, cols], sem.at[c])


def cols_of(lane):
    return pl.ds(lane, LANES)


def row_of(ref, index):
    return ref[pl.ds(index, SUBS, stride=0), :]


def spread(x, wide, span):
    x = x.astype(f32)
    for b in range(SUBS):
        wide[pl.ds(b * (span + 1), span), :] = x[b * span : (b + 1) * span]


class Conv:
    def __init__(self, wide, rim, taps, span):
        self.wide, self.span = wide, span
        self.taps = [jnp.broadcast_to(taps[m : m + 1], (SUBS, LANES)) for m in range(3)]
        top = lax.broadcasted_iota(jnp.int32, (SUBS, LANES), 0) == 0
        ahead = [0.0, 0.0] if rim is None else [jnp.broadcast_to(rim[m : m + 1], (SUBS, LANES)) for m in range(2)]
        self.behind = [jnp.where(top, ahead[m], pltpu.roll(self.row(span - 2 + m), 1, 0)) for m in range(2)]

    def row(self, j):
        return self.wide[pl.ds(j, SUBS, stride=self.span + 1), :]

    def step(self, j, keep_one, keep_two):
        here = self.row(j)
        two, one = self.behind
        self.behind = [one, here]
        return self.taps[0] * here + (self.taps[1] * one) * keep_one + (self.taps[2] * two) * keep_two


def half_start(chans, own):
    parity = lax.rem(lax.axis_index("ctx"), 2)
    return pl.multiple_of((parity if own else 1 - parity) * (chans // 2), LANES)


def twice(mask, modes):
    return jnp.concatenate([mask] * (modes // SUBS), axis=0)


def sub_state(state_ref, lane, b, modes):
    return state_ref[lax.div(lane, LANES), pl.ds(b * (modes + 1), modes), :]


def state_kernel(*refs, span, modes, most, own, chunk, levels):
    if own:
        masks, key_ref, value_ref, rim_ref, taps_ref, rate_ref, _, _, gate_ref, state_ref, end_ref, wide_k, wide_v, tables, held = refs
    else:
        (base_ref, len_ref, ahead_ref, key_in, value_in, taps_ref, rate_ref,
         gate_ref, state_ref, end_ref, masks, key_own, value_own, heads,
         key_ref, value_ref, rows_of, wide_k, wide_v, tables, held, sems) = refs
    half = key_ref.shape[1]
    first = half_start(2 * half, own)
    if not own:
        def fetch(c):
            there = pl.ds(pl.multiple_of(first + c * chunk, chunk), chunk)
            here = pl.ds(pl.multiple_of(c * chunk, chunk), chunk)
            return [
                pltpu.make_async_copy(key_in.at[:, there], key_ref.at[:, here], sems.at[0, c]),
                pltpu.make_async_copy(value_in.at[:, there], value_ref.at[:, here], sems.at[1, c]),
            ]

        cols = pl.ds(half_start(2 * half, True), half)
        others = [
            pltpu.make_async_copy(key_in.at[:, cols], key_own, sems.at[0, half // chunk]),
            pltpu.make_async_copy(value_in.at[:, cols], value_own, sems.at[1, half // chunk]),
        ]
        for c in range(1, half // chunk):
            for copy in fetch(c):
                copy.start()
        write_masks(base_ref, len_ref, masks, rows_of, span, levels)
    at = Masks(span)

    def group(lanes, keys=key_ref, values=value_ref):
        for slot, lane in enumerate(lanes):
            spread(keys[:, cols_of(pl.multiple_of(lane - first, LANES))], wide_k.at[slot], span)
            spread(values[:, cols_of(pl.multiple_of(lane - first, LANES))], wide_v.at[slot], span)
            rate = rate_ref[:, cols_of(lane)]
            tables[slot] = jnp.exp(-rate)
        convs = [
            [
                Conv(wide.at[slot], rim_ref[i, :, cols_of(lane)].astype(f32) if own else None, taps_ref[i, :, cols_of(lane)], span)
                for i, wide in ((1, wide_k), (2, wide_v))
            ]
            for slot, lane in enumerate(lanes)
        ]
        last = [None] * len(lanes)
        for j in range(span):
            keep_one, keep_two = masks[at.one + j], masks[at.two + j]
            for slot, lane in enumerate(lanes):
                k_short, v_short = [conv.step(j, keep_one, keep_two) for conv in convs[slot]]
                if j % 2 == 0:
                    last[slot] = k_short * v_short
                    continue
                pair = jnp.concatenate([last[slot], k_short * v_short], axis=0).astype(bf16)
                gate_ref[pl.ds((j - 1) * SUBS, 2 * SUBS), cols_of(lane)] = pair
                pair = pair.astype(f32)
                used = at.inner if j == 1 and not own else at.last + j - 1
                held[slot, j - 1] = pair[:SUBS] * masks[used]
                held[slot, j] = pair[SUBS:] * masks[used + 1]
        for slot, lane in enumerate(lanes):
            decay = [row_of(tables.at[slot], n) for n in range(modes)]
            state = [held[slot, 0]] * modes
            for j in range(1, span):
                gate = held[slot, j]
                state = [decay[n] * state[n] + gate for n in range(modes)]
            for n in range(modes):
                state_ref[lax.div(lane, LANES), pl.ds(n, SUBS, stride=modes + 1), :] = state[n]
        for slot, lane in enumerate(lanes):
            leap = jnp.exp(-float(span) * rate_ref[:, cols_of(lane)])
            end = sub_state(state_ref, lane, 0, modes)
            for b in range(1, SUBS):
                end = (leap * twice(masks[at.passes + b], modes)) * end + sub_state(state_ref, lane, b, modes)
            end_ref[:, cols_of(pl.multiple_of(lane - first, LANES))] = end

    def shifted(lanes, *sources):
        group([pl.multiple_of(first + lane, LANES) for lane in lanes], *sources)

    if own:
        each_group(half // LANES, most, shifted)
    else:
        def before(c):
            for copy in fetch(c):
                copy.wait()

        each_group(chunk // LANES, most, lambda lanes: shifted(lanes, ahead_ref.at[0], ahead_ref.at[1]))
        for copy in others:
            copy.start()
        each_chunk(half, chunk, before, shifted, lambda c: None, most, 1)
        rows = pl.ds(0, heads.shape[1])
        for i, ref in enumerate((key_ref, value_ref)):
            heads[i, :, pl.ds(0, chunk)] = ahead_ref[i, rows, :]
            if half > chunk:
                heads[i, :, pl.ds(chunk, half - chunk)] = ref[rows, pl.ds(chunk, half - chunk)]
        for copy in others:
            copy.wait()


def patch_kernel(
    masks, heads, rim_ref, taps_ref, rate_ref, gate_in, state_in, end_in, gate_ref, state_ref, end_ref, *, span, modes
):
    half = end_ref.shape[1]
    first = half_start(2 * half, False)
    at = Masks(span)
    rows = lax.broadcasted_iota(jnp.int32, (2 * SUBS, LANES), 0)

    def one(index):
        return masks[index][0:1]

    def group(lanes):
        for lane in lanes:
            there = cols_of(pl.multiple_of(first + lane, LANES))
            shorts = []
            for i in (1, 2):
                here = heads[i - 1, :, cols_of(lane)].astype(f32)
                rim = rim_ref[i, :, there].astype(f32)
                tap = taps_ref[i, :, there]
                shorts.append([
                    tap[0:1] * here[0:1] + (tap[1:2] * rim[1:2]) * one(at.one) + (tap[2:3] * rim[0:1]) * one(at.two),
                    tap[0:1] * here[1:2] + (tap[1:2] * here[0:1]) * one(at.one + 1) + (tap[2:3] * rim[1:2]) * one(at.two + 1),
                ])
            gates = [(k * v).astype(bf16).astype(f32) for k, v in zip(*shorts)]
            old = gate_in[pl.ds(0, 2 * SUBS), there].astype(f32)
            new = jnp.where(rows == 0, gates[0], jnp.where(rows == SUBS, gates[1], old))
            gate_ref[pl.ds(0, 2 * SUBS), there] = new.astype(bf16)
            rate = rate_ref[:, there]
            added = jnp.exp(-float(span - 1) * rate) * (gates[0] * one(at.last)) + jnp.exp(-float(span - 2) * rate) * (
                gates[1] * one(at.last + 1)
            )
            tile = lax.div(first + lane, LANES)
            state_ref[tile, pl.ds(0, modes), :] = state_in[tile, pl.ds(0, modes), :] + added
            reach = jnp.exp(-float((SUBS - 1) * span) * rate) * one(at.rest)
            end_ref[:, cols_of(lane)] = end_in[:, cols_of(lane)] + reach * added

    each_group(half // LANES, 4, group)


def tail_kernel(
    query_ref, key_ref, value_ref, tail_ref, ahead_ref, bufs, sems
):
    rows, count = query_ref.shape[0], bufs.shape[1]
    copies = [
        pltpu.make_async_copy(ref.at[pl.ds(rows - count, count)], bufs.at[i], sems.at[i])
        for i, ref in enumerate((query_ref, key_ref, value_ref))
    ]
    cols = pl.ds(half_start(query_ref.shape[1], False), ahead_ref.shape[2])
    aheads = [
        pltpu.make_async_copy(ref.at[:, cols], ahead_ref.at[i], sems.at[3 + i])
        for i, ref in enumerate((key_ref, value_ref))
    ]
    for copy in copies + aheads:
        copy.start()
    for i, copy in enumerate(copies):
        copy.wait()
        tail_ref[i] = bufs[i].astype(f32)[count - 2 :].astype(bf16)
    for copy in aheads:
        copy.wait()


def unbroken(len_ref, first, count):
    start = jnp.int32(0)
    whole = jnp.where((first <= 0) & (first + count > 0), 0.0, 1.0)
    for d in range(len_ref.shape[0] - 1):
        start = start + len_ref[d]
        whole = jnp.where((start >= first) & (start < first + count), 0.0, whole)
    return whole.astype(f32)


class Masks:
    def __init__(self, span):
        self.one, self.two, self.last, self.enter = 0, span, 2 * span, 3 * span
        self.passes = 4 * span
        self.edges = self.passes + SUBS
        self.late = self.edges + 3
        self.early = self.late + 1
        self.rest = self.late + 2
        self.inner = self.late + 3
        self.levels = self.late + 5

    def lead(self, level):
        return self.levels + 2 * level

    def later(self, level):
        return self.levels + 2 * level + 1

    def count(self, levels):
        return self.levels + 2 * levels + 1


def write_masks(base_ref, len_ref, masks, rows_of, span, levels):
    at = Masks(span)
    rows, starts = doc_start_rows(len_ref, base_ref[0], span)
    for j in range(span):
        masks[at.one + j] = flag(starts[j] < rows + j)
        masks[at.two + j] = flag(starts[j] < rows + (j - 1))
        masks[at.last + j] = flag(starts[span - 1] <= rows + j)
        masks[at.enter + j] = flag(starts[j] < rows)
    top = flag(lax.broadcasted_iota(jnp.int32, (SUBS, LANES), 0) == 0)
    for j in range(2):
        masks[at.inner + j] = (1.0 - top) * masks[at.last + j]
    masks[at.edges] = top * masks[at.one]
    masks[at.edges + 1] = top * masks[at.two]
    masks[at.edges + 2] = top * masks[at.two + 1]
    size = SUBS * span
    parity = lax.rem(lax.div(base_ref[0], size), 2)
    pair_at = base_ref[0] - parity * size
    rows_of[...] = flag(starts[span - 1] < rows)
    for b in range(SUBS):
        masks[at.passes + b] = row_of(rows_of, b)
    ranges = []
    flags = []
    ranges += [(pair_at + size, size), (pair_at, size), (base_ref[0] + span, size - span)]
    flags += [at.late, at.early, at.rest]
    for m in range(levels + 1):
        group = 2 * size << m
        group_at = base_ref[0] - lax.rem(base_ref[0], group)
        ranges.append((group_at, pair_at - group_at))
        flags.append(at.lead(m))
        if m < levels:
            ranges.append((group_at + group * (1 - lax.rem(lax.div(base_ref[0], group), 2)), group))
            flags.append(at.later(m))
    for index, (first, count) in zip(flags, ranges):
        masks[index] = jnp.full((SUBS, LANES), unbroken(len_ref, first, count), f32)


def near_kernel(masks, gate_ref, rate_ref, weight_ref, *refs, span, modes, most, first, count):
    near_ref, sums, tap_rows = refs[-3:]
    at = Masks(span)

    def group(lanes):
        for slot, lane in enumerate(lanes):
            decay = jnp.exp(-rate_ref[:, cols_of(lane)])
            term = weight_ref[:, cols_of(lane)]
            for lag in range(span):
                part = term[:SUBS]
                for n in range(SUBS, modes, SUBS):
                    part = part + term[n : n + SUBS]
                sums[slot, pl.ds(lag * (SUBS + 1), SUBS), :] = part
                term = term * decay
        for slot in range(len(lanes)):
            for first_lag in range(0, span, SUBS):
                total = [
                    sums[slot, pl.ds(first_lag * (SUBS + 1) + m, SUBS, stride=SUBS + 1), :] for m in range(SUBS)
                ]
                while len(total) > 1:
                    total = [total[m] + total[m + 1] for m in range(0, len(total), 2)]
                tap_rows[slot, pl.ds(first_lag, SUBS), :] = total[0]
        taps = [[row_of(tap_rows.at[slot], lag) for lag in range(span)] for slot in range(len(lanes))]
        for parts, lane in zip(taps, lanes):
            live = []
            for j in range(span):
                if j % 2 == 0:
                    pair = gate_ref[pl.ds(j * SUBS, 2 * SUBS), cols_of(lane)].astype(f32)
                keep = masks[at.one + j]
                live = [g * keep for g in live]
                live.append(pair[(j % 2) * SUBS : (j % 2 + 1) * SUBS])
                total = parts[0] * live[j]
                for lag in range(1, j + 1):
                    total = total + parts[lag] * live[j - lag]
                near_ref[pl.ds(j * SUBS, SUBS), cols_of(lane)] = total

    each_group(count // LANES, most, lambda lanes: group([pl.multiple_of(first + lane, LANES) for lane in lanes]))


def query_kernel(masks, query_ref, taps_ref, *refs, span, most, chunk, first, count):
    short_ref, query_buf, sems, wide_q = refs[-4:]

    def fetch(c):
        there = pl.ds(first + c * chunk if isinstance(c, int) else pl.multiple_of(first + c * chunk, chunk), chunk)
        here = pl.ds(c * chunk if isinstance(c, int) else pl.multiple_of(c * chunk, chunk), chunk)
        return pltpu.make_async_copy(query_ref.at[:, there], query_buf.at[:, here], sems.at[c])

    for c in range(count // chunk):
        fetch(c).start()
    at = Masks(span)

    def group(lanes):
        for slot, lane in enumerate(lanes):
            spread(query_buf[:, cols_of(lane)], wide_q.at[slot], span)
        convs = [
            Conv(wide_q.at[slot], None, taps_ref[0, :, cols_of(pl.multiple_of(first + lane, LANES))], span)
            for slot, lane in enumerate(lanes)
        ]
        for j in range(span):
            keep_one, keep_two = masks[at.one + j], masks[at.two + j]
            for slot, lane in enumerate(lanes):
                short_ref[pl.ds(j * SUBS, SUBS), cols_of(pl.multiple_of(first + lane, LANES))] = convs[slot].step(j, keep_one, keep_two)

    each_chunk(count, chunk, lambda c: fetch(c).wait(), group, lambda c: None, most)


def pair_rates(rate_ref, count):
    parity = lax.rem(lax.axis_index("ctx"), 2)
    return parity, rate_ref[:, pl.ds(pl.multiple_of(parity * count, LANES), count)]


def early_late(parity, own, got):
    odd = jnp.full(own.shape, parity, jnp.int32) == 1
    return jnp.where(odd, got, own), jnp.where(odd, own, got)


def leap(masks, index, rate, rows):
    return jnp.exp(-float(rows) * rate) * masks[index][0:1, 0:1]


def pair_kernel(masks, own_ref, got_ref, rate_ref, total_ref, sent_ref, *, rows, index):
    parity, rate = pair_rates(rate_ref, own_ref.shape[1])
    early, late = early_late(parity, own_ref[...], got_ref[...])
    total = late + leap(masks, index, rate, rows) * early
    total_ref[...] = total
    sent_ref[...] = total.astype(bf16)


def lead_leap(masks, index, rate, rows, bit):
    me = lax.axis_index("ctx")
    lead = (lax.rem(me, bit) - lax.rem(me, 2)) * rows
    return jnp.exp(rate * -lead.astype(f32)) * masks[index][0:1, 0:1]


def level_kernel(masks, total_ref, got_ref, rate_ref, *refs, rows, level, lead, later):
    before_ref = refs[0] if level else None
    sent_ref, enter_ref, *new_ref = refs[1 if level else 0 :]
    _, rate = pair_rates(rate_ref, total_ref.shape[1])
    bit = 2 << level
    after = lax.rem(lax.div(lax.axis_index("ctx"), bit), 2)
    got = got_ref[...].astype(f32)
    early, late = early_late(after, total_ref[...], got)
    total = late + leap(masks, later, rate, bit * rows) * early
    for ref in new_ref:
        ref[...] = total
    sent_ref[...] = total.astype(bf16)
    entering = jnp.where(jnp.full(got.shape, after, jnp.int32) == 1, got, 0.0) * lead_leap(masks, lead, rate, rows, bit)
    enter_ref[...] = entering if before_ref is None else before_ref[...] + entering


def enter_kernel(
    masks, before_ref, got_ref, own_ref, other_ref, rate_ref, mine_ref, give_ref, *, rows, bit, lead, early_index
):
    parity, rate = pair_rates(rate_ref, own_ref.shape[1])
    first = before_ref[...] + lead_leap(masks, lead, rate, rows, bit) * got_ref[...].astype(f32)
    early, _ = early_late(parity, own_ref[...], other_ref[...])
    second = early + leap(masks, early_index, rate, rows) * first
    give, mine = early_late(parity, second, first)
    mine_ref[...] = mine
    give_ref[...] = give


def final_kernel(
    masks, state_ref, enter_ref, near_ref, short_ref, resid_ref, rim_ref, taps_ref, rate_ref, weight_ref, *refs,
    span, modes, channels, most, chunk, own,
):
    if own:
        hidden_out, whole, sums, hidden_ref, sems, wide, tables, starts_at = refs
    elif channels:
        gain_ref, _, _, _, hidden_out, whole, sums, normed_out, hidden_ref, sems, wide, tables, starts_at, normed_ref = refs
    else:
        _, _, _, hidden_out, whole, sums, hidden_ref, sems, wide, tables, starts_at = refs
    chans = resid_ref.shape[1]
    half = chans // 2
    first = half_start(chans, own)
    at = Masks(span)

    def store(c):
        here = pl.ds(pl.multiple_of(c * chunk, chunk), chunk)
        there = pl.ds(pl.multiple_of(first + c * chunk, chunk), chunk)
        return pltpu.make_async_copy(hidden_ref.at[:, here], hidden_out.at[:, there], sems.at[0, c])

    def store_normed(c):
        return cols_copy(normed_ref, normed_out, sems.at[1], c, chunk)

    if own:
        sums[...] = jnp.zeros(sums.shape, f32)

    def group(lanes):
        for slot, lane in enumerate(lanes):
            state = enter_ref[:, cols_of(pl.multiple_of(lane - first, LANES))]
            rate = rate_ref[:, cols_of(lane)]
            weight = weight_ref[:, cols_of(lane)]
            tables[slot] = jnp.exp(-rate)
            leap = jnp.exp(-float(span) * rate)
            for b in range(SUBS):
                starts_at[slot, pl.ds(b * (modes + 1), modes), :] = weight * state
                if b < SUBS - 1:
                    state = (leap * twice(masks[at.passes + b], modes)) * state + sub_state(state_ref, lane, b, modes)
        for slot, lane in enumerate(lanes):
            part = [starts_at[slot, pl.ds(n, SUBS, stride=modes + 1), :] for n in range(modes)]
            decay = [row_of(tables.at[slot], n) for n in range(modes)]
            rim = rim_ref[0, :, cols_of(lane)].astype(f32)
            tap = taps_ref[0, :, cols_of(lane)]
            edge = [
                (tap[1:2] * rim[1:2]) * masks[at.edges] + (tap[2:3] * rim[0:1]) * masks[at.edges + 1],
                (tap[2:3] * rim[1:2]) * masks[at.edges + 2],
            ]
            for j in range(span):
                part = [part[n] * decay[n] for n in range(modes)]
                total = part
                while len(total) > 1:
                    total = [total[m] + total[m + 1] for m in range(0, len(total), 2)]
                conv = near_ref[pl.ds(j * SUBS, SUBS), cols_of(lane)] + total[0] * masks[at.enter + j]
                conv = conv.astype(bf16).astype(f32)
                short = short_ref[pl.ds(j * SUBS, SUBS), cols_of(lane)]
                if j < 2:
                    short = short + edge[j]
                wide[slot, pl.ds(j, SUBS, stride=span + 1), :] = short * conv
        for b in range(SUBS):
            rows = pl.ds(b * span, span)
            squares = sums[rows, :]
            for slot, lane in enumerate(lanes):
                hidden = wide[slot, pl.ds(b * (span + 1), span), :] + resid_ref[rows, cols_of(lane)].astype(f32)
                whole[lax.div(lane, LANES), rows, :] = hidden
                hidden_ref[rows, cols_of(pl.multiple_of(lane - first, LANES))] = hidden.astype(bf16)
                squares = squares + hidden * hidden
            sums[rows, :] = squares

    each_chunk(
        half,
        chunk,
        lambda c: None,
        lambda lanes: group([pl.multiple_of(first + lane, LANES) for lane in lanes]),
        lambda c: store(c).start(),
        most,
    )
    if channels and not own:
        inverse = lax.rsqrt(jnp.sum(sums[...], axis=1, keepdims=True) / channels + 1e-06)
        sums[...] = jnp.broadcast_to(inverse, sums.shape)

        def scale(lanes):
            for lane in lanes:
                normed = whole[lax.div(lane, LANES)] * sums[...] * gain_ref[:, cols_of(lane)]
                normed_ref[:, cols_of(lane)] = normed.astype(bf16)

        each_chunk(chans, chunk, lambda c: None, scale, lambda c: store_normed(c).start(), 4)
        for c in range(chans // chunk):
            store_normed(c).wait()
    for c in range(half // chunk):
        store(c).wait()


def shards(
    query_in, key_in, value_in, short_taps, decay_rate, residues, doc_lengths, residual, norm_gain
):
    tok_rows, chans = query_in.shape
    modes = decay_rate.shape[0]
    span = tok_rows // SUBS
    blocks = lax.axis_size("ctx")
    grp = lax.axis_size("grp")
    chunk = min(chans // 2, 512)
    pieces = chans // chunk
    ctx_index = lax.axis_index("ctx")
    base = (ctx_index * tok_rows).astype(jnp.int32).reshape(1)
    weight = residues * jnp.sqrt(-jnp.expm1(-2.0 * decay_rate))

    smem = pl.BlockSpec(memory_space=pltpu.SMEM)
    vmem = pl.BlockSpec(memory_space=pltpu.VMEM)
    hbm = pl.BlockSpec(memory_space=pltpu.HBM)
    tile_shape = (SUBS, LANES)
    wide_rows = SUBS * (span + 1)
    params = pltpu.CompilerParams(vmem_limit_bytes=16 * MIB)

    lengths = pltpu.with_memory_space_constraint(doc_lengths, pltpu.HBM)

    def near_by(x):
        return pltpu.with_memory_space_constraint(x, pltpu.VMEM)

    def far_off(x):
        return pltpu.with_memory_space_constraint(x, pltpu.HBM)

    def copies(kinds):
        return pltpu.SemaphoreType.DMA((kinds, pieces))

    def cost(per_tile, moved):
        return pl.CostEstimate(flops=per_tile * (chans // LANES) * SUBS * LANES, bytes_accessed=moved, transcendentals=0)

    levels = max(1, (blocks // 4).bit_length() - 2)
    mask_shape = (Masks(span).count(levels),) + tile_shape
    small = min(chans // 2, 512)
    tails, ahead = pl.pallas_call(
        tail_kernel,
        in_specs=[hbm, hbm, hbm],
        out_specs=[vmem, vmem],
        out_shape=[pltpu.VMEM((3, 2, chans), bf16), pltpu.VMEM((2, tok_rows, small), bf16)],
        scratch_shapes=[pltpu.VMEM((3, 16, chans), bf16), pltpu.SemaphoreType.DMA((5,))],
        compiler_params=params,
        name="tails",
    )(far_off(query_in), far_off(key_in), far_off(value_in))
    rim_rows = from_behind(tails, "ctx", 1)
    def query_piece(part, masks, before):
        count = chans // 2
        scratch = [
            pltpu.VMEM((tok_rows, count), bf16),
            pltpu.SemaphoreType.DMA((count // chunk,)),
            pltpu.VMEM((Q_TILES, wide_rows, LANES), f32),
        ]
        operands = [near_by(masks), far_off(query_in), taps] + ([near_by(before)] if part else [])
        return pl.pallas_call(
            functools.partial(
                query_kernel, span=span, most=Q_TILES, chunk=chunk, first=part * count, count=count
            ),
            in_specs=[vmem, hbm, vmem] + [vmem] * (len(operands) - 3),
            out_specs=vmem,
            out_shape=pltpu.VMEM((tok_rows, chans), f32),
            scratch_shapes=scratch,
            input_output_aliases={3: 0} if part else {},
            compiler_params=params,
            cost_estimate=cost(100, 3 * tok_rows * chans),
            name="query_part_%d" % part,
        )(*operands)

    key_half = pltpu.VMEM((tok_rows, chans // 2), bf16)
    rates, weights, taps, rims = near_by(decay_rate), near_by(weight), near_by(short_taps), near_by(rim_rows)
    kept = pltpu.VMEM((modes, chans // 2), f32)
    sent = pltpu.VMEM((modes, chans // 2), bf16)

    gate_shape = pltpu.VMEM((tok_rows, chans), bf16)
    state_shape = pltpu.VMEM((chans // LANES, SUBS * (modes + 1), LANES), f32)

    def states_of(own, operands, in_specs, out_shape, scratch, aliases):
        return pl.pallas_call(
            functools.partial(
                state_kernel, span=span, modes=modes, most=A_TILES, own=own, chunk=small, levels=levels
            ),
            in_specs=in_specs,
            out_specs=[vmem] * (3 + len(out_shape)),
            out_shape=[gate_shape, state_shape, kept] + out_shape,
            scratch_shapes=scratch[:-1]
            + [
                pltpu.VMEM((A_TILES, wide_rows, LANES), f32),
                pltpu.VMEM((A_TILES, wide_rows, LANES), f32),
                pltpu.VMEM((A_TILES, modes, LANES), f32),
                pltpu.VMEM((A_TILES, span) + tile_shape, f32),
            ]
            + scratch[-1:],
            input_output_aliases=aliases,
            compiler_params=params,
            cost_estimate=cost(500, 6 * tok_rows * chans),
            name="block_states_own" if own else "block_states_give",
        )(*operands)

    gates, states, give, masks, key_own, value_own, heads = states_of(
        False,
        [base, lengths, near_by(ahead), far_off(key_in), far_off(value_in), taps, rates],
        [smem, smem, vmem, hbm, hbm, vmem, vmem],
        [pltpu.VMEM(mask_shape, f32), key_half, key_half, pltpu.VMEM((2, 16, chans // 2), bf16)],
        [
            pltpu.VMEM((tok_rows, chans // 2), bf16),
            pltpu.VMEM((tok_rows, chans // 2), bf16),
            pltpu.VMEM(tile_shape, f32),
            pltpu.SemaphoreType.DMA((2, chans // 2 // small + 1)),
        ],
        {},
    )
    gates, states, give = pl.pallas_call(
        functools.partial(patch_kernel, span=span, modes=modes),
        in_specs=[vmem] * 8,
        out_specs=[vmem] * 3,
        out_shape=[gate_shape, state_shape, kept],
        input_output_aliases={5: 0, 6: 1, 7: 2},
        compiler_params=params,
        name="first_rows",
    )(near_by(masks), near_by(heads), rims, taps, rates, near_by(gates), near_by(states), near_by(give))
    got = swap(give, "ctx")
    gates, states, own = states_of(
        True,
        [near_by(masks), near_by(key_own), near_by(value_own), rims, taps, rates, near_by(gates), near_by(states)],
        [vmem] * 8,
        [],
        [],
        {6: 0, 7: 1},
    )
    got, gates, states, own = lax.optimization_barrier((got, gates, states, own))

    def near_piece(part, near):
        count = chans // NEAR_PARTS
        before = [] if near is None else [near_by(near)]
        return pl.pallas_call(
            functools.partial(
                near_kernel, span=span, modes=modes, most=N_TILES, first=part * count, count=count
            ),
            in_specs=[vmem] * (4 + len(before)),
            out_specs=vmem,
            out_shape=pltpu.VMEM((tok_rows, chans), f32),
            scratch_shapes=[
                pltpu.VMEM((N_TILES, span * (SUBS + 1), LANES), f32),
                pltpu.VMEM((N_TILES, span, LANES), f32),
            ],
            compiler_params=params,
            input_output_aliases={4: 0} if before else {},
            cost_estimate=cost(600 // NEAR_PARTS, 7 * tok_rows * count),
            name="near_part_%d" % part,
        )(near_by(masks), near_by(gates), rates, weights, *before)

    got = swap(give, "ctx")

    at = Masks(span)

    def pair_call(kernel, operands, out_shape, name, extra=(), **static):
        return pl.pallas_call(
            functools.partial(kernel, **static),
            in_specs=[vmem] * (len(operands) + 2 + len(extra)),
            out_specs=[vmem] * len(out_shape),
            out_shape=out_shape,
            compiler_params=params,
            name=name,
        )(near_by(masks), *[near_by(x) for x in operands], rates, *[near_by(x) for x in extra])

    total, ends = pair_call(pair_kernel, [own, got], [kept, sent], "pair_ends", rows=tok_rows, index=at.late)
    entering, near = [], None
    for m in range(levels):
        met = swap(ends, "ctx", 2 << m)
        if m < NEAR_PARTS:
            near = near_piece(m, near)
            if m == 0:
                q_short = query_piece(0, masks, None)
                met, q_short = lax.optimization_barrier((met, q_short))
            met, near = lax.optimization_barrier((met, near))
        ends, enter, *total = pair_call(
            level_kernel,
            [total, met],
            [sent, kept] + [kept] * (m < levels - 1),
            "level_%d" % m,
            extra=entering,
            rows=tok_rows,
            level=m,
            lead=at.lead(m),
            later=at.later(m),
        )
        entering = [enter]
        total = total[0] if total else None
    on = from_behind(ends, "ctx", 2 << levels)
    for m in range(levels, NEAR_PARTS):
        near = near_piece(m, near)
    q_short = query_piece(1, masks, q_short)
    on, q_short, near = lax.optimization_barrier((on, q_short, near))
    mine, give_back = pair_call(
        enter_kernel,
        entering + [on, own, got],
        [kept, kept],
        "pair_enter",
        rows=tok_rows,
        bit=2 << levels,
        lead=at.lead(levels),
        early_index=at.early,
    )
    got_back = swap(give_back, "ctx")

    alone = grp == 1
    resid = near_by(residual)

    def finish(own, enter, before):
        last = alone and not own
        out_specs = [hbm, vmem, vmem]
        out_shape = [
            jax.ShapeDtypeStruct((tok_rows, chans), bf16),
            pltpu.VMEM((chans // LANES, tok_rows, LANES), f32),
            pltpu.VMEM((tok_rows, LANES), f32),
        ]
        scratch = [
            pltpu.VMEM((tok_rows, chans // 2), bf16),
            copies(2),
            pltpu.VMEM((F_TILES, wide_rows, LANES), f32),
            pltpu.VMEM((F_TILES, modes, LANES), f32),
            pltpu.VMEM((F_TILES, SUBS * (modes + 1), LANES), f32),
        ]
        operands = [near_by(x) for x in (masks, states, enter, near, q_short)] + [resid, rims, taps, rates, weights]
        if last:
            operands.append(near_by(norm_gain.reshape(1, chans)))
            out_specs.append(hbm)
            out_shape.append(jax.ShapeDtypeStruct((tok_rows, chans), bf16))
            scratch.append(pltpu.VMEM((tok_rows, chans), bf16))
        count = len(operands)
        in_specs = [vmem] * count
        if before:
            operands += [far_off(before[0]), near_by(before[1]), near_by(before[2])]
            in_specs += [hbm, vmem, vmem]
        return pl.pallas_call(
            functools.partial(
                final_kernel, span=span, modes=modes, channels=chans if alone else 0, most=F_TILES, chunk=chunk, own=own
            ),
            in_specs=in_specs,
            out_specs=out_specs,
            out_shape=out_shape,
            scratch_shapes=scratch,
            input_output_aliases={count + i: i for i in range(len(before))},
            compiler_params=params,
            cost_estimate=cost(450, 9 * tok_rows * chans),
            name="far_part_own" if own else "far_part_other",
        )(*operands)

    before = finish(True, mine, [])
    got_back, *before = lax.optimization_barrier((got_back, *before))
    outs = finish(False, got_back, before)
    if alone:
        return (outs[0], outs[3])
    hidden_out, whole, sums = outs
    hidden = whole.transpose(1, 0, 2).reshape(tok_rows, chans)
    square_sum = lax.psum(jnp.sum(sums, axis=1), "grp")
    inverse_rms = lax.rsqrt(square_sum / (chans * grp) + 1e-06)
    normed = (hidden * inverse_rms[:, None] * norm_gain[None, :]).astype(bf16)
    return (hidden_out, normed)


def solution(mesh):
    return jax.shard_map(
        shards,
        mesh=mesh,
        in_specs=(
            P("ctx", "grp"),
            P("ctx", "grp"),
            P("ctx", "grp"),
            P(None, None, "grp"),
            P(None, "grp"),
            P(None, "grp"),
            P(),
            P("ctx", "grp"),
            P("grp"),
        ),
        out_specs=(P("ctx", "grp"), P("ctx", "grp")),
        check_vma=False,
    )
```

```python
import functools
import math

import jax
import jax.numpy as jnp
from jax import lax
from jax.experimental import pallas as pl
from jax.experimental.pallas import tpu as pltpu
from jax.sharding import PartitionSpec as P

SUBS = 8
LANES = 128
MIB = 1024 * 1024
A_TILES, N_TILES, Q_TILES, F_TILES = 1, 1, 2, 2
NEAR_PARTS = 2
f32 = jnp.float32
bf16 = jnp.bfloat16


def from_behind(shard, axis, by):
    count = lax.axis_size(axis)
    return lax.ppermute(shard, axis, [(i, i + by) for i in range(count - by)])


def swap(shard, axis, bit=1):
    return lax.ppermute(shard, axis, [(i, i ^ bit) for i in range(lax.axis_size(axis))])


def doc_start_rows(len_ref, base, span):
    rows = lax.broadcasted_iota(jnp.int32, (SUBS, LANES), 0) * span + base
    starts = [jnp.int32(0)]
    for d in range(len_ref.shape[0] - 1):
        starts.append(starts[-1] + len_ref[d])
    out = []
    for j in range(span):
        pos = rows + j
        best = jnp.zeros((SUBS, LANES), jnp.int32)
        for start in starts[1:]:
            best = jnp.where(pos >= start, start, best)
        out.append(best)
    return rows, out


def flag(cond):
    return jnp.where(cond, 1.0, 0.0).astype(f32)


def each_group(count, most, group):
    size = math.gcd(count, most)

    def step(i, carry):
        group([pl.multiple_of((i * size + m) * LANES, LANES) for m in range(size)])
        return carry

    lax.fori_loop(0, count // size, step, 0)


def each_chunk(chans, chunk, before, group, after, most, start=0):
    def step(c, carry):
        before(c)

        def inner(lanes):
            group([pl.multiple_of(c * chunk + lane, LANES) for lane in lanes])

        each_group(chunk // LANES, most, inner)
        after(c)
        return carry

    lax.fori_loop(start, chans // chunk, step, 0)


def cols_copy(src, dst, sem, c, chunk):
    cols = pl.ds(pl.multiple_of(c * chunk, chunk), chunk)
    return pltpu.make_async_copy(src.at[:, cols], dst.at[:, cols], sem.at[c])


def cols_of(lane):
    return pl.ds(lane, LANES)


def row_of(ref, index):
    return ref[pl.ds(index, SUBS, stride=0), :]


def spread(x, wide, span):
    x = x.astype(f32)
    for b in range(SUBS):
        wide[pl.ds(b * (span + 1), span), :] = x[b * span : (b + 1) * span]


class Conv:
    def __init__(self, wide, rim, taps, span):
        self.wide, self.span = wide, span
        self.taps = [jnp.broadcast_to(taps[m : m + 1], (SUBS, LANES)) for m in range(3)]
        top = lax.broadcasted_iota(jnp.int32, (SUBS, LANES), 0) == 0
        ahead = [0.0, 0.0] if rim is None else [jnp.broadcast_to(rim[m : m + 1], (SUBS, LANES)) for m in range(2)]
        self.behind = [jnp.where(top, ahead[m], pltpu.roll(self.row(span - 2 + m), 1, 0)) for m in range(2)]

    def row(self, j):
        return self.wide[pl.ds(j, SUBS, stride=self.span + 1), :]

    def step(self, j, keep_one, keep_two):
        here = self.row(j)
        two, one = self.behind
        self.behind = [one, here]
        return self.taps[0] * here + (self.taps[1] * one) * keep_one + (self.taps[2] * two) * keep_two


def half_start(chans, own):
    parity = lax.rem(lax.axis_index("ctx"), 2)
    return pl.multiple_of((parity if own else 1 - parity) * (chans // 2), LANES)


def twice(mask, modes):
    return jnp.concatenate([mask] * (modes // SUBS), axis=0)


def sub_state(state_ref, lane, b, modes):
    return state_ref[lax.div(lane, LANES), pl.ds(b * (modes + 1), modes), :]


def state_kernel(*refs, span, modes, most, own, chunk, levels):
    if own:
        masks, key_ref, value_ref, rim_ref, taps_ref, rate_ref, _, _, gate_ref, state_ref, end_ref, wide_k, wide_v, tables, held = refs
    else:
        (base_ref, len_ref, ahead_ref, key_in, value_in, taps_ref, rate_ref,
         gate_ref, state_ref, end_ref, masks, key_own, value_own, heads,
         key_ref, value_ref, rows_of, wide_k, wide_v, tables, held, sems) = refs
    half = key_ref.shape[1]
    first = half_start(2 * half, own)
    if not own:
        def fetch(c):
            there = pl.ds(pl.multiple_of(first + c * chunk, chunk), chunk)
            here = pl.ds(pl.multiple_of(c * chunk, chunk), chunk)
            return [
                pltpu.make_async_copy(key_in.at[:, there], key_ref.at[:, here], sems.at[0, c]),
                pltpu.make_async_copy(value_in.at[:, there], value_ref.at[:, here], sems.at[1, c]),
            ]

        cols = pl.ds(half_start(2 * half, True), half)
        others = [
            pltpu.make_async_copy(key_in.at[:, cols], key_own, sems.at[0, half // chunk]),
            pltpu.make_async_copy(value_in.at[:, cols], value_own, sems.at[1, half // chunk]),
        ]
        for c in range(1, half // chunk):
            for copy in fetch(c):
                copy.start()
        write_masks(base_ref, len_ref, masks, rows_of, span, levels)
    at = Masks(span)

    def group(lanes, keys=key_ref, values=value_ref):
        for slot, lane in enumerate(lanes):
            spread(keys[:, cols_of(pl.multiple_of(lane - first, LANES))], wide_k.at[slot], span)
            spread(values[:, cols_of(pl.multiple_of(lane - first, LANES))], wide_v.at[slot], span)
            rate = rate_ref[:, cols_of(lane)]
            tables[slot] = jnp.exp(-rate)
        convs = [
            [
                Conv(wide.at[slot], rim_ref[i, :, cols_of(lane)].astype(f32) if own else None, taps_ref[i, :, cols_of(lane)], span)
                for i, wide in ((1, wide_k), (2, wide_v))
            ]
            for slot, lane in enumerate(lanes)
        ]
        last = [None] * len(lanes)
        for j in range(span):
            keep_one, keep_two = masks[at.one + j], masks[at.two + j]
            for slot, lane in enumerate(lanes):
                k_short, v_short = [conv.step(j, keep_one, keep_two) for conv in convs[slot]]
                if j % 2 == 0:
                    last[slot] = k_short * v_short
                    continue
                pair = jnp.concatenate([last[slot], k_short * v_short], axis=0).astype(bf16)
                gate_ref[pl.ds((j - 1) * SUBS, 2 * SUBS), cols_of(lane)] = pair
                pair = pair.astype(f32)
                used = at.inner if j == 1 and not own else at.last + j - 1
                held[slot, j - 1] = pair[:SUBS] * masks[used]
                held[slot, j] = pair[SUBS:] * masks[used + 1]
        for slot, lane in enumerate(lanes):
            decay = [row_of(tables.at[slot], n) for n in range(modes)]
            state = [held[slot, 0]] * modes
            for j in range(1, span):
                gate = held[slot, j]
                state = [decay[n] * state[n] + gate for n in range(modes)]
            for n in range(modes):
                state_ref[lax.div(lane, LANES), pl.ds(n, SUBS, stride=modes + 1), :] = state[n]
        for slot, lane in enumerate(lanes):
            leap = jnp.exp(-float(span) * rate_ref[:, cols_of(lane)])
            end = sub_state(state_ref, lane, 0, modes)
            for b in range(1, SUBS):
                end = (leap * twice(masks[at.passes + b], modes)) * end + sub_state(state_ref, lane, b, modes)
            end_ref[:, cols_of(pl.multiple_of(lane - first, LANES))] = end

    def shifted(lanes, *sources):
        group([pl.multiple_of(first + lane, LANES) for lane in lanes], *sources)

    if own:
        each_group(half // LANES, most, shifted)
    else:
        def before(c):
            for copy in fetch(c):
                copy.wait()

        each_group(chunk // LANES, most, lambda lanes: shifted(lanes, ahead_ref.at[0], ahead_ref.at[1]))
        for copy in others:
            copy.start()
        each_chunk(half, chunk, before, shifted, lambda c: None, most, 1)
        rows = pl.ds(0, heads.shape[1])
        for i, ref in enumerate((key_ref, value_ref)):
            heads[i, :, pl.ds(0, chunk)] = ahead_ref[i, rows, :]
            if half > chunk:
                heads[i, :, pl.ds(chunk, half - chunk)] = ref[rows, pl.ds(chunk, half - chunk)]
        for copy in others:
            copy.wait()


def patch_kernel(
    masks, heads, rim_ref, taps_ref, rate_ref, gate_in, state_in, end_in, gate_ref, state_ref, end_ref, *, span, modes
):
    half = end_ref.shape[1]
    first = half_start(2 * half, False)
    at = Masks(span)
    rows = lax.broadcasted_iota(jnp.int32, (2 * SUBS, LANES), 0)

    def one(index):
        return masks[index][0:1]

    def group(lanes):
        for lane in lanes:
            there = cols_of(pl.multiple_of(first + lane, LANES))
            shorts = []
            for i in (1, 2):
                here = heads[i - 1, :, cols_of(lane)].astype(f32)
                rim = rim_ref[i, :, there].astype(f32)
                tap = taps_ref[i, :, there]
                shorts.append([
                    tap[0:1] * here[0:1] + (tap[1:2] * rim[1:2]) * one(at.one) + (tap[2:3] * rim[0:1]) * one(at.two),
                    tap[0:1] * here[1:2] + (tap[1:2] * here[0:1]) * one(at.one + 1) + (tap[2:3] * rim[1:2]) * one(at.two + 1),
                ])
            gates = [(k * v).astype(bf16).astype(f32) for k, v in zip(*shorts)]
            old = gate_in[pl.ds(0, 2 * SUBS), there].astype(f32)
            new = jnp.where(rows == 0, gates[0], jnp.where(rows == SUBS, gates[1], old))
            gate_ref[pl.ds(0, 2 * SUBS), there] = new.astype(bf16)
            rate = rate_ref[:, there]
            added = jnp.exp(-float(span - 1) * rate) * (gates[0] * one(at.last)) + jnp.exp(-float(span - 2) * rate) * (
                gates[1] * one(at.last + 1)
            )
            tile = lax.div(first + lane, LANES)
            state_ref[tile, pl.ds(0, modes), :] = state_in[tile, pl.ds(0, modes), :] + added
            reach = jnp.exp(-float((SUBS - 1) * span) * rate) * one(at.rest)
            end_ref[:, cols_of(lane)] = end_in[:, cols_of(lane)] + reach * added

    each_group(half // LANES, 4, group)


def tail_kernel(
    query_ref, key_ref, value_ref, tail_ref, ahead_ref, bufs, sems
):
    rows, count = query_ref.shape[0], bufs.shape[1]
    copies = [
        pltpu.make_async_copy(ref.at[pl.ds(rows - count, count)], bufs.at[i], sems.at[i])
        for i, ref in enumerate((query_ref, key_ref, value_ref))
    ]
    cols = pl.ds(half_start(query_ref.shape[1], False), ahead_ref.shape[2])
    aheads = [
        pltpu.make_async_copy(ref.at[:, cols], ahead_ref.at[i], sems.at[3 + i])
        for i, ref in enumerate((key_ref, value_ref))
    ]
    for copy in copies + aheads:
        copy.start()
    for i, copy in enumerate(copies):
        copy.wait()
        tail_ref[i] = bufs[i].astype(f32)[count - 2 :].astype(bf16)
    for copy in aheads:
        copy.wait()


def unbroken(len_ref, first, count):
    start = jnp.int32(0)
    whole = jnp.where((first <= 0) & (first + count > 0), 0.0, 1.0)
    for d in range(len_ref.shape[0] - 1):
        start = start + len_ref[d]
        whole = jnp.where((start >= first) & (start < first + count), 0.0, whole)
    return whole.astype(f32)


class Masks:
    def __init__(self, span):
        self.one, self.two, self.last, self.enter = 0, span, 2 * span, 3 * span
        self.passes = 4 * span
        self.edges = self.passes + SUBS
        self.late = self.edges + 3
        self.early = self.late + 1
        self.rest = self.late + 2
        self.inner = self.late + 3
        self.levels = self.late + 5

    def lead(self, level):
        return self.levels + 2 * level

    def later(self, level):
        return self.levels + 2 * level + 1

    def count(self, levels):
        return self.levels + 2 * levels + 1


def write_masks(base_ref, len_ref, masks, rows_of, span, levels):
    at = Masks(span)
    rows, starts = doc_start_rows(len_ref, base_ref[0], span)
    for j in range(span):
        masks[at.one + j] = flag(starts[j] < rows + j)
        masks[at.two + j] = flag(starts[j] < rows + (j - 1))
        masks[at.last + j] = flag(starts[span - 1] <= rows + j)
        masks[at.enter + j] = flag(starts[j] < rows)
    top = flag(lax.broadcasted_iota(jnp.int32, (SUBS, LANES), 0) == 0)
    for j in range(2):
        masks[at.inner + j] = (1.0 - top) * masks[at.last + j]
    masks[at.edges] = top * masks[at.one]
    masks[at.edges + 1] = top * masks[at.two]
    masks[at.edges + 2] = top * masks[at.two + 1]
    size = SUBS * span
    parity = lax.rem(lax.div(base_ref[0], size), 2)
    pair_at = base_ref[0] - parity * size
    rows_of[...] = flag(starts[span - 1] < rows)
    for b in range(SUBS):
        masks[at.passes + b] = row_of(rows_of, b)
    ranges = []
    flags = []
    ranges += [(pair_at + size, size), (pair_at, size), (base_ref[0] + span, size - span)]
    flags += [at.late, at.early, at.rest]
    for m in range(levels + 1):
        group = 2 * size << m
        group_at = base_ref[0] - lax.rem(base_ref[0], group)
        ranges.append((group_at, pair_at - group_at))
        flags.append(at.lead(m))
        if m < levels:
            ranges.append((group_at + group * (1 - lax.rem(lax.div(base_ref[0], group), 2)), group))
            flags.append(at.later(m))
    for index, (first, count) in zip(flags, ranges):
        masks[index] = jnp.full((SUBS, LANES), unbroken(len_ref, first, count), f32)


def near_kernel(masks, gate_ref, rate_ref, weight_ref, *refs, span, modes, most, first, count):
    near_ref, sums, tap_rows = refs[-3:]
    at = Masks(span)

    def group(lanes):
        for slot, lane in enumerate(lanes):
            decay = jnp.exp(-rate_ref[:, cols_of(lane)])
            term = weight_ref[:, cols_of(lane)]
            for lag in range(span):
                part = term[:SUBS]
                for n in range(SUBS, modes, SUBS):
                    part = part + term[n : n + SUBS]
                sums[slot, pl.ds(lag * (SUBS + 1), SUBS), :] = part
                term = term * decay
        for slot in range(len(lanes)):
            for first_lag in range(0, span, SUBS):
                total = [
                    sums[slot, pl.ds(first_lag * (SUBS + 1) + m, SUBS, stride=SUBS + 1), :] for m in range(SUBS)
                ]
                while len(total) > 1:
                    total = [total[m] + total[m + 1] for m in range(0, len(total), 2)]
                tap_rows[slot, pl.ds(first_lag, SUBS), :] = total[0]
        taps = [[row_of(tap_rows.at[slot], lag) for lag in range(span)] for slot in range(len(lanes))]
        for parts, lane in zip(taps, lanes):
            live = []
            for j in range(span):
                if j % 2 == 0:
                    pair = gate_ref[pl.ds(j * SUBS, 2 * SUBS), cols_of(lane)].astype(f32)
                keep = masks[at.one + j]
                live = [g * keep for g in live]
                live.append(pair[(j % 2) * SUBS : (j % 2 + 1) * SUBS])
                total = parts[0] * live[j]
                for lag in range(1, j + 1):
                    total = total + parts[lag] * live[j - lag]
                near_ref[pl.ds(j * SUBS, SUBS), cols_of(lane)] = total

    each_group(count // LANES, most, lambda lanes: group([pl.multiple_of(first + lane, LANES) for lane in lanes]))


def query_kernel(masks, query_ref, taps_ref, *refs, span, most, chunk, first, count):
    short_ref, query_buf, sems, wide_q = refs[-4:]

    def fetch(c):
        there = pl.ds(first + c * chunk if isinstance(c, int) else pl.multiple_of(first + c * chunk, chunk), chunk)
        here = pl.ds(c * chunk if isinstance(c, int) else pl.multiple_of(c * chunk, chunk), chunk)
        return pltpu.make_async_copy(query_ref.at[:, there], query_buf.at[:, here], sems.at[c])

    for c in range(count // chunk):
        fetch(c).start()
    at = Masks(span)

    def group(lanes):
        for slot, lane in enumerate(lanes):
            spread(query_buf[:, cols_of(lane)], wide_q.at[slot], span)
        convs = [
            Conv(wide_q.at[slot], None, taps_ref[0, :, cols_of(pl.multiple_of(first + lane, LANES))], span)
            for slot, lane in enumerate(lanes)
        ]
        for j in range(span):
            keep_one, keep_two = masks[at.one + j], masks[at.two + j]
            for slot, lane in enumerate(lanes):
                short_ref[pl.ds(j * SUBS, SUBS), cols_of(pl.multiple_of(first + lane, LANES))] = convs[slot].step(j, keep_one, keep_two)

    each_chunk(count, chunk, lambda c: fetch(c).wait(), group, lambda c: None, most)


def pair_rates(rate_ref, count):
    parity = lax.rem(lax.axis_index("ctx"), 2)
    return parity, rate_ref[:, pl.ds(pl.multiple_of(parity * count, LANES), count)]


def early_late(parity, own, got):
    odd = jnp.full(own.shape, parity, jnp.int32) == 1
    return jnp.where(odd, got, own), jnp.where(odd, own, got)


def leap(masks, index, rate, rows):
    return jnp.exp(-float(rows) * rate) * masks[index][0:1, 0:1]


def pair_kernel(masks, own_ref, got_ref, rate_ref, total_ref, sent_ref, *, rows, index):
    parity, rate = pair_rates(rate_ref, own_ref.shape[1])
    early, late = early_late(parity, own_ref[...], got_ref[...])
    total = late + leap(masks, index, rate, rows) * early
    total_ref[...] = total
    sent_ref[...] = total.astype(bf16)


def lead_leap(masks, index, rate, rows, bit):
    me = lax.axis_index("ctx")
    lead = (lax.rem(me, bit) - lax.rem(me, 2)) * rows
    return jnp.exp(rate * -lead.astype(f32)) * masks[index][0:1, 0:1]


def level_kernel(masks, total_ref, got_ref, rate_ref, *refs, rows, level, lead, later):
    before_ref = refs[0] if level else None
    sent_ref, enter_ref, *new_ref = refs[1 if level else 0 :]
    _, rate = pair_rates(rate_ref, total_ref.shape[1])
    bit = 2 << level
    after = lax.rem(lax.div(lax.axis_index("ctx"), bit), 2)
    got = got_ref[...].astype(f32)
    early, late = early_late(after, total_ref[...], got)
    total = late + leap(masks, later, rate, bit * rows) * early
    for ref in new_ref:
        ref[...] = total
    sent_ref[...] = total.astype(bf16)
    entering = jnp.where(jnp.full(got.shape, after, jnp.int32) == 1, got, 0.0) * lead_leap(masks, lead, rate, rows, bit)
    enter_ref[...] = entering if before_ref is None else before_ref[...] + entering


def enter_kernel(
    masks, before_ref, got_ref, own_ref, other_ref, rate_ref, mine_ref, give_ref, *, rows, bit, lead, early_index
):
    parity, rate = pair_rates(rate_ref, own_ref.shape[1])
    first = before_ref[...] + lead_leap(masks, lead, rate, rows, bit) * got_ref[...].astype(f32)
    early, _ = early_late(parity, own_ref[...], other_ref[...])
    second = early + leap(masks, early_index, rate, rows) * first
    give, mine = early_late(parity, second, first)
    mine_ref[...] = mine
    give_ref[...] = give


def final_kernel(
    masks, state_ref, enter_ref, near_ref, short_ref, resid_ref, rim_ref, taps_ref, rate_ref, weight_ref, *refs,
    span, modes, channels, most, chunk, own,
):
    if own:
        hidden_out, whole, sums, hidden_ref, sems, wide, tables, starts_at = refs
    elif channels:
        gain_ref, _, _, _, hidden_out, whole, sums, normed_out, hidden_ref, sems, wide, tables, starts_at, normed_ref = refs
    else:
        _, _, _, hidden_out, whole, sums, hidden_ref, sems, wide, tables, starts_at = refs
    chans = resid_ref.shape[1]
    half = chans // 2
    first = half_start(chans, own)
    at = Masks(span)

    def store(c):
        here = pl.ds(pl.multiple_of(c * chunk, chunk), chunk)
        there = pl.ds(pl.multiple_of(first + c * chunk, chunk), chunk)
        return pltpu.make_async_copy(hidden_ref.at[:, here], hidden_out.at[:, there], sems.at[0, c])

    def store_normed(c):
        return cols_copy(normed_ref, normed_out, sems.at[1], c, chunk)

    if own:
        sums[...] = jnp.zeros(sums.shape, f32)

    def group(lanes):
        for slot, lane in enumerate(lanes):
            state = enter_ref[:, cols_of(pl.multiple_of(lane - first, LANES))]
            rate = rate_ref[:, cols_of(lane)]
            weight = weight_ref[:, cols_of(lane)]
            tables[slot] = jnp.exp(-rate)
            leap = jnp.exp(-float(span) * rate)
            for b in range(SUBS):
                starts_at[slot, pl.ds(b * (modes + 1), modes), :] = weight * state
                if b < SUBS - 1:
                    state = (leap * twice(masks[at.passes + b], modes)) * state + sub_state(state_ref, lane, b, modes)
        for slot, lane in enumerate(lanes):
            part = [starts_at[slot, pl.ds(n, SUBS, stride=modes + 1), :] for n in range(modes)]
            decay = [row_of(tables.at[slot], n) for n in range(modes)]
            rim = rim_ref[0, :, cols_of(lane)].astype(f32)
            tap = taps_ref[0, :, cols_of(lane)]
            edge = [
                (tap[1:2] * rim[1:2]) * masks[at.edges] + (tap[2:3] * rim[0:1]) * masks[at.edges + 1],
                (tap[2:3] * rim[1:2]) * masks[at.edges + 2],
            ]
            for j in range(span):
                part = [part[n] * decay[n] for n in range(modes)]
                total = part
                while len(total) > 1:
                    total = [total[m] + total[m + 1] for m in range(0, len(total), 2)]
                conv = near_ref[pl.ds(j * SUBS, SUBS), cols_of(lane)] + total[0] * masks[at.enter + j]
                conv = conv.astype(bf16).astype(f32)
                short = short_ref[pl.ds(j * SUBS, SUBS), cols_of(lane)]
                if j < 2:
                    short = short + edge[j]
                wide[slot, pl.ds(j, SUBS, stride=span + 1), :] = short * conv
        for b in range(SUBS):
            rows = pl.ds(b * span, span)
            squares = sums[rows, :]
            for slot, lane in enumerate(lanes):
                hidden = wide[slot, pl.ds(b * (span + 1), span), :] + resid_ref[rows, cols_of(lane)].astype(f32)
                whole[lax.div(lane, LANES), rows, :] = hidden
                hidden_ref[rows, cols_of(pl.multiple_of(lane - first, LANES))] = hidden.astype(bf16)
                squares = squares + hidden * hidden
            sums[rows, :] = squares

    each_chunk(
        half,
        chunk,
        lambda c: None,
        lambda lanes: group([pl.multiple_of(first + lane, LANES) for lane in lanes]),
        lambda c: store(c).start(),
        most,
    )
    if channels and not own:
        inverse = lax.rsqrt(jnp.sum(sums[...], axis=1, keepdims=True) / channels + 1e-06)
        sums[...] = jnp.broadcast_to(inverse, sums.shape)

        def scale(lanes):
            for lane in lanes:
                normed = whole[lax.div(lane, LANES)] * sums[...] * gain_ref[:, cols_of(lane)]
                normed_ref[:, cols_of(lane)] = normed.astype(bf16)

        each_chunk(chans, chunk, lambda c: None, scale, lambda c: store_normed(c).start(), 4)
        for c in range(chans // chunk):
            store_normed(c).wait()
    for c in range(half // chunk):
        store(c).wait()


def shards(
    query_in, key_in, value_in, short_taps, decay_rate, residues, doc_lengths, residual, norm_gain
):
    tok_rows, chans = query_in.shape
    modes = decay_rate.shape[0]
    span = tok_rows // SUBS
    blocks = lax.axis_size("ctx")
    grp = lax.axis_size("grp")
    chunk = min(chans // 2, 512)
    pieces = chans // chunk
    ctx_index = lax.axis_index("ctx")
    base = (ctx_index * tok_rows).astype(jnp.int32).reshape(1)
    weight = residues * jnp.sqrt(-jnp.expm1(-2.0 * decay_rate))

    smem = pl.BlockSpec(memory_space=pltpu.SMEM)
    vmem = pl.BlockSpec(memory_space=pltpu.VMEM)
    hbm = pl.BlockSpec(memory_space=pltpu.HBM)
    tile_shape = (SUBS, LANES)
    wide_rows = SUBS * (span + 1)
    params = pltpu.CompilerParams(vmem_limit_bytes=16 * MIB)

    lengths = pltpu.with_memory_space_constraint(doc_lengths, pltpu.HBM)

    def near_by(x):
        return pltpu.with_memory_space_constraint(x, pltpu.VMEM)

    def far_off(x):
        return pltpu.with_memory_space_constraint(x, pltpu.HBM)

    def copies(kinds):
        return pltpu.SemaphoreType.DMA((kinds, pieces))

    def cost(per_tile, moved):
        return pl.CostEstimate(flops=per_tile * (chans // LANES) * SUBS * LANES, bytes_accessed=moved, transcendentals=0)

    levels = max(1, (blocks // 4).bit_length() - 2)
    mask_shape = (Masks(span).count(levels),) + tile_shape
    small = min(chans // 2, 512)
    tails, ahead = pl.pallas_call(
        tail_kernel,
        in_specs=[hbm, hbm, hbm],
        out_specs=[vmem, vmem],
        out_shape=[pltpu.VMEM((3, 2, chans), bf16), pltpu.VMEM((2, tok_rows, small), bf16)],
        scratch_shapes=[pltpu.VMEM((3, 16, chans), bf16), pltpu.SemaphoreType.DMA((5,))],
        compiler_params=params,
        name="tails",
    )(far_off(query_in), far_off(key_in), far_off(value_in))
    rim_rows = from_behind(tails, "ctx", 1)
    def query_piece(part, masks, before):
        count = chans // 2
        scratch = [
            pltpu.VMEM((tok_rows, count), bf16),
            pltpu.SemaphoreType.DMA((count // chunk,)),
            pltpu.VMEM((Q_TILES, wide_rows, LANES), f32),
        ]
        operands = [near_by(masks), far_off(query_in), taps] + ([near_by(before)] if part else [])
        return pl.pallas_call(
            functools.partial(
                query_kernel, span=span, most=Q_TILES, chunk=chunk, first=part * count, count=count
            ),
            in_specs=[vmem, hbm, vmem] + [vmem] * (len(operands) - 3),
            out_specs=vmem,
            out_shape=pltpu.VMEM((tok_rows, chans), f32),
            scratch_shapes=scratch,
            input_output_aliases={3: 0} if part else {},
            compiler_params=params,
            cost_estimate=cost(100, 3 * tok_rows * chans),
            name="query_part_%d" % part,
        )(*operands)

    key_half = pltpu.VMEM((tok_rows, chans // 2), bf16)
    rates, weights, taps, rims = near_by(decay_rate), near_by(weight), near_by(short_taps), near_by(rim_rows)
    kept = pltpu.VMEM((modes, chans // 2), f32)
    sent = pltpu.VMEM((modes, chans // 2), bf16)

    gate_shape = pltpu.VMEM((tok_rows, chans), bf16)
    state_shape = pltpu.VMEM((chans // LANES, SUBS * (modes + 1), LANES), f32)

    def states_of(own, operands, in_specs, out_shape, scratch, aliases):
        return pl.pallas_call(
            functools.partial(
                state_kernel, span=span, modes=modes, most=A_TILES, own=own, chunk=small, levels=levels
            ),
            in_specs=in_specs,
            out_specs=[vmem] * (3 + len(out_shape)),
            out_shape=[gate_shape, state_shape, kept] + out_shape,
            scratch_shapes=scratch[:-1]
            + [
                pltpu.VMEM((A_TILES, wide_rows, LANES), f32),
                pltpu.VMEM((A_TILES, wide_rows, LANES), f32),
                pltpu.VMEM((A_TILES, modes, LANES), f32),
                pltpu.VMEM((A_TILES, span) + tile_shape, f32),
            ]
            + scratch[-1:],
            input_output_aliases=aliases,
            compiler_params=params,
            cost_estimate=cost(500, 6 * tok_rows * chans),
            name="block_states_own" if own else "block_states_give",
        )(*operands)

    gates, states, give, masks, key_own, value_own, heads = states_of(
        False,
        [base, lengths, near_by(ahead), far_off(key_in), far_off(value_in), taps, rates],
        [smem, smem, vmem, hbm, hbm, vmem, vmem],
        [pltpu.VMEM(mask_shape, f32), key_half, key_half, pltpu.VMEM((2, 16, chans // 2), bf16)],
        [
            pltpu.VMEM((tok_rows, chans // 2), bf16),
            pltpu.VMEM((tok_rows, chans // 2), bf16),
            pltpu.VMEM(tile_shape, f32),
            pltpu.SemaphoreType.DMA((2, chans // 2 // small + 1)),
        ],
        {},
    )
    gates, states, give = pl.pallas_call(
        functools.partial(patch_kernel, span=span, modes=modes),
        in_specs=[vmem] * 8,
        out_specs=[vmem] * 3,
        out_shape=[gate_shape, state_shape, kept],
        input_output_aliases={5: 0, 6: 1, 7: 2},
        compiler_params=params,
        name="first_rows",
    )(near_by(masks), near_by(heads), rims, taps, rates, near_by(gates), near_by(states), near_by(give))
    got = swap(give, "ctx")
    gates, states, own = states_of(
        True,
        [near_by(masks), near_by(key_own), near_by(value_own), rims, taps, rates, near_by(gates), near_by(states)],
        [vmem] * 8,
        [],
        [],
        {6: 0, 7: 1},
    )
    got, gates, states, own = lax.optimization_barrier((got, gates, states, own))

    def near_piece(part, near):
        count = chans // NEAR_PARTS
        before = [] if near is None else [near_by(near)]
        return pl.pallas_call(
            functools.partial(
                near_kernel, span=span, modes=modes, most=N_TILES, first=part * count, count=count
            ),
            in_specs=[vmem] * (4 + len(before)),
            out_specs=vmem,
            out_shape=pltpu.VMEM((tok_rows, chans), f32),
            scratch_shapes=[
                pltpu.VMEM((N_TILES, span * (SUBS + 1), LANES), f32),
                pltpu.VMEM((N_TILES, span, LANES), f32),
            ],
            compiler_params=params,
            input_output_aliases={4: 0} if before else {},
            cost_estimate=cost(600 // NEAR_PARTS, 7 * tok_rows * count),
            name="near_part_%d" % part,
        )(near_by(masks), near_by(gates), rates, weights, *before)

    got = swap(give, "ctx")

    at = Masks(span)

    def pair_call(kernel, operands, out_shape, name, extra=(), **static):
        return pl.pallas_call(
            functools.partial(kernel, **static),
            in_specs=[vmem] * (len(operands) + 2 + len(extra)),
            out_specs=[vmem] * len(out_shape),
            out_shape=out_shape,
            compiler_params=params,
            name=name,
        )(near_by(masks), *[near_by(x) for x in operands], rates, *[near_by(x) for x in extra])

    total, ends = pair_call(pair_kernel, [own, got], [kept, sent], "pair_ends", rows=tok_rows, index=at.late)
    entering, near = [], None
    for m in range(levels):
        met = swap(ends, "ctx", 2 << m)
        if m < NEAR_PARTS:
            near = near_piece(m, near)
            if m == 0:
                q_short = query_piece(0, masks, None)
                met, q_short = lax.optimization_barrier((met, q_short))
            met, near = lax.optimization_barrier((met, near))
        ends, enter, *total = pair_call(
            level_kernel,
            [total, met],
            [sent, kept] + [kept] * (m < levels - 1),
            "level_%d" % m,
            extra=entering,
            rows=tok_rows,
            level=m,
            lead=at.lead(m),
            later=at.later(m),
        )
        entering = [enter]
        total = total[0] if total else None
    on = from_behind(ends, "ctx", 2 << levels)
    for m in range(levels, NEAR_PARTS):
        near = near_piece(m, near)
    q_short = query_piece(1, masks, q_short)
    on, q_short, near = lax.optimization_barrier((on, q_short, near))
    mine, give_back = pair_call(
        enter_kernel,
        entering + [on, own, got],
        [kept, kept],
        "pair_enter",
        rows=tok_rows,
        bit=2 << levels,
        lead=at.lead(levels),
        early_index=at.early,
    )
    got_back = swap(give_back, "ctx")

    alone = grp == 1
    resid = near_by(residual)

    def finish(own, enter, before):
        last = alone and not own
        out_specs = [hbm, vmem, vmem]
        out_shape = [
            jax.ShapeDtypeStruct((tok_rows, chans), bf16),
            pltpu.VMEM((chans // LANES, tok_rows, LANES), f32),
            pltpu.VMEM((tok_rows, LANES), f32),
        ]
        scratch = [
            pltpu.VMEM((tok_rows, chans // 2), bf16),
            copies(2),
            pltpu.VMEM((F_TILES, wide_rows, LANES), f32),
            pltpu.VMEM((F_TILES, modes, LANES), f32),
            pltpu.VMEM((F_TILES, SUBS * (modes + 1), LANES), f32),
        ]
        operands = [near_by(x) for x in (masks, states, enter, near, q_short)] + [resid, rims, taps, rates, weights]
        if last:
            operands.append(near_by(norm_gain.reshape(1, chans)))
            out_specs.append(hbm)
            out_shape.append(jax.ShapeDtypeStruct((tok_rows, chans), bf16))
            scratch.append(pltpu.VMEM((tok_rows, chans), bf16))
        count = len(operands)
        in_specs = [vmem] * count
        if before:
            operands += [far_off(before[0]), near_by(before[1]), near_by(before[2])]
            in_specs += [hbm, vmem, vmem]
        return pl.pallas_call(
            functools.partial(
                final_kernel, span=span, modes=modes, channels=chans if alone else 0, most=F_TILES, chunk=chunk, own=own
            ),
            in_specs=in_specs,
            out_specs=out_specs,
            out_shape=out_shape,
            scratch_shapes=scratch,
            input_output_aliases={count + i: i for i in range(len(before))},
            compiler_params=params,
            cost_estimate=cost(450, 9 * tok_rows * chans),
            name="far_part_own" if own else "far_part_other",
        )(*operands)

    before = finish(True, mine, [])
    got_back, *before = lax.optimization_barrier((got_back, *before))
    outs = finish(False, got_back, before)
    if alone:
        return (outs[0], outs[3])
    hidden_out, whole, sums = outs
    hidden = whole.transpose(1, 0, 2).reshape(tok_rows, chans)
    square_sum = lax.psum(jnp.sum(sums, axis=1), "grp")
    inverse_rms = lax.rsqrt(square_sum / (chans * grp) + 1e-06)
    normed = (hidden * inverse_rms[:, None] * norm_gain[None, :]).astype(bf16)
    return (hidden_out, normed)


def solution(mesh):
    return jax.shard_map(
        shards,
        mesh=mesh,
        in_specs=(
            P("ctx", "grp"),
            P("ctx", "grp"),
            P("ctx", "grp"),
            P(None, None, "grp"),
            P(None, "grp"),
            P(None, "grp"),
            P(),
            P("ctx", "grp"),
            P("grp"),
        ),
        out_specs=(P("ctx", "grp"), P("ctx", "grp")),
        check_vma=False,
    )
```

```python
import functools
import math

import jax
import jax.numpy as jnp
from jax import lax
from jax.experimental import pallas as pl
from jax.experimental.pallas import tpu as pltpu
from jax.sharding import PartitionSpec as P

SUBS = 8
LANES = 128
MIB = 1024 * 1024
A_TILES, N_TILES, Q_TILES, F_TILES = 4, 4, 8, 8
NEAR_PARTS = 2
f32 = jnp.float32
bf16 = jnp.bfloat16


def from_behind(shard, axis, by):
    count = lax.axis_size(axis)
    return lax.ppermute(shard, axis, [(i, i + by) for i in range(count - by)])


def swap(shard, axis, bit=1):
    return lax.ppermute(shard, axis, [(i, i ^ bit) for i in range(lax.axis_size(axis))])


def doc_start_rows(len_ref, base, span):
    rows = lax.broadcasted_iota(jnp.int32, (SUBS, LANES), 0) * span + base
    starts = [jnp.int32(0)]
    for d in range(len_ref.shape[0] - 1):
        starts.append(starts[-1] + len_ref[d])
    out = []
    for j in range(span):
        pos = rows + j
        best = jnp.zeros((SUBS, LANES), jnp.int32)
        for start in starts[1:]:
            best = jnp.where(pos >= start, start, best)
        out.append(best)
    return rows, out


def flag(cond):
    return jnp.where(cond, 1.0, 0.0).astype(f32)


def each_group(count, most, group):
    size = math.gcd(count, most)

    def step(i, carry):
        group([pl.multiple_of((i * size + m) * LANES, LANES) for m in range(size)])
        return carry

    lax.fori_loop(0, count // size, step, 0)


def each_chunk(chans, chunk, before, group, after, most, start=0):
    def step(c, carry):
        before(c)

        def inner(lanes):
            group([pl.multiple_of(c * chunk + lane, LANES) for lane in lanes])

        each_group(chunk // LANES, most, inner)
        after(c)
        return carry

    lax.fori_loop(start, chans // chunk, step, 0)


def cols_copy(src, dst, sem, c, chunk):
    cols = pl.ds(pl.multiple_of(c * chunk, chunk), chunk)
    return pltpu.make_async_copy(src.at[:, cols], dst.at[:, cols], sem.at[c])


def cols_of(lane):
    return pl.ds(lane, LANES)


def row_of(ref, index):
    return ref[pl.ds(index, SUBS, stride=0), :]


def spread(x, wide, span):
    x = x.astype(f32)
    for b in range(SUBS):
        wide[pl.ds(b * (span + 1), span), :] = x[b * span : (b + 1) * span]


class Conv:
    def __init__(self, wide, rim, taps, span):
        self.wide, self.span = wide, span
        self.taps = [jnp.broadcast_to(taps[m : m + 1], (SUBS, LANES)) for m in range(3)]
        top = lax.broadcasted_iota(jnp.int32, (SUBS, LANES), 0) == 0
        ahead = [0.0, 0.0] if rim is None else [jnp.broadcast_to(rim[m : m + 1], (SUBS, LANES)) for m in range(2)]
        self.behind = [jnp.where(top, ahead[m], pltpu.roll(self.row(span - 2 + m), 1, 0)) for m in range(2)]

    def row(self, j):
        return self.wide[pl.ds(j, SUBS, stride=self.span + 1), :]

    def step(self, j, keep_one, keep_two):
        here = self.row(j)
        two, one = self.behind
        self.behind = [one, here]
        return self.taps[0] * here + (self.taps[1] * one) * keep_one + (self.taps[2] * two) * keep_two


def half_start(chans, own):
    parity = lax.rem(lax.axis_index("ctx"), 2)
    return pl.multiple_of((parity if own else 1 - parity) * (chans // 2), LANES)


def twice(mask, modes):
    return jnp.concatenate([mask] * (modes // SUBS), axis=0)


def sub_state(state_ref, lane, b, modes):
    return state_ref[lax.div(lane, LANES), pl.ds(b * (modes + 1), modes), :]


def state_kernel(*refs, span, modes, most, own, chunk, levels):
    if own:
        masks, key_ref, value_ref, rim_ref, taps_ref, rate_ref, _, _, gate_ref, state_ref, end_ref, wide_k, wide_v, tables, held = refs
    else:
        (base_ref, len_ref, ahead_ref, key_in, value_in, taps_ref, rate_ref,
         gate_ref, state_ref, end_ref, masks, key_own, value_own, heads,
         key_ref, value_ref, rows_of, wide_k, wide_v, tables, held, sems) = refs
    half = key_ref.shape[1]
    first = half_start(2 * half, own)
    if not own:
        def fetch(c):
            there = pl.ds(pl.multiple_of(first + c * chunk, chunk), chunk)
            here = pl.ds(pl.multiple_of(c * chunk, chunk), chunk)
            return [
                pltpu.make_async_copy(key_in.at[:, there], key_ref.at[:, here], sems.at[0, c]),
                pltpu.make_async_copy(value_in.at[:, there], value_ref.at[:, here], sems.at[1, c]),
            ]

        cols = pl.ds(half_start(2 * half, True), half)
        others = [
            pltpu.make_async_copy(key_in.at[:, cols], key_own, sems.at[0, half // chunk]),
            pltpu.make_async_copy(value_in.at[:, cols], value_own, sems.at[1, half // chunk]),
        ]
        for c in range(1, half // chunk):
            for copy in fetch(c):
                copy.start()
        write_masks(base_ref, len_ref, masks, rows_of, span, levels)
    at = Masks(span)

    def group(lanes, keys=key_ref, values=value_ref):
        for slot, lane in enumerate(lanes):
            spread(keys[:, cols_of(pl.multiple_of(lane - first, LANES))], wide_k.at[slot], span)
            spread(values[:, cols_of(pl.multiple_of(lane - first, LANES))], wide_v.at[slot], span)
            rate = rate_ref[:, cols_of(lane)]
            tables[slot] = jnp.exp(-rate)
        convs = [
            [
                Conv(wide.at[slot], rim_ref[i, :, cols_of(lane)].astype(f32) if own else None, taps_ref[i, :, cols_of(lane)], span)
                for i, wide in ((1, wide_k), (2, wide_v))
            ]
            for slot, lane in enumerate(lanes)
        ]
        last = [None] * len(lanes)
        for j in range(span):
            keep_one, keep_two = masks[at.one + j], masks[at.two + j]
            for slot, lane in enumerate(lanes):
                k_short, v_short = [conv.step(j, keep_one, keep_two) for conv in convs[slot]]
                if j % 2 == 0:
                    last[slot] = k_short * v_short
                    continue
                pair = jnp.concatenate([last[slot], k_short * v_short], axis=0).astype(bf16)
                gate_ref[pl.ds((j - 1) * SUBS, 2 * SUBS), cols_of(lane)] = pair
                pair = pair.astype(f32)
                used = at.inner if j == 1 and not own else at.last + j - 1
                held[slot, j - 1] = pair[:SUBS] * masks[used]
                held[slot, j] = pair[SUBS:] * masks[used + 1]
        for slot, lane in enumerate(lanes):
            decay = [row_of(tables.at[slot], n) for n in range(modes)]
            state = [held[slot, 0]] * modes
            for j in range(1, span):
                gate = held[slot, j]
                state = [decay[n] * state[n] + gate for n in range(modes)]
            for n in range(modes):
                state_ref[lax.div(lane, LANES), pl.ds(n, SUBS, stride=modes + 1), :] = state[n]
        for slot, lane in enumerate(lanes):
            leap = jnp.exp(-float(span) * rate_ref[:, cols_of(lane)])
            end = sub_state(state_ref, lane, 0, modes)
            for b in range(1, SUBS):
                end = (leap * twice(masks[at.passes + b], modes)) * end + sub_state(state_ref, lane, b, modes)
            end_ref[:, cols_of(pl.multiple_of(lane - first, LANES))] = end

    def shifted(lanes, *sources):
        group([pl.multiple_of(first + lane, LANES) for lane in lanes], *sources)

    if own:
        each_group(half // LANES, most, shifted)
    else:
        def before(c):
            for copy in fetch(c):
                copy.wait()

        each_group(chunk // LANES, most, lambda lanes: shifted(lanes, ahead_ref.at[0], ahead_ref.at[1]))
        for copy in others:
            copy.start()
        each_chunk(half, chunk, before, shifted, lambda c: None, most, 1)
        rows = pl.ds(0, heads.shape[1])
        for i, ref in enumerate((key_ref, value_ref)):
            heads[i, :, pl.ds(0, chunk)] = ahead_ref[i, rows, :]
            if half > chunk:
                heads[i, :, pl.ds(chunk, half - chunk)] = ref[rows, pl.ds(chunk, half - chunk)]
        for copy in others:
            copy.wait()


def patch_kernel(
    masks, heads, rim_ref, taps_ref, rate_ref, gate_in, state_in, end_in, gate_ref, state_ref, end_ref, *, span, modes
):
    half = end_ref.shape[1]
    first = half_start(2 * half, False)
    at = Masks(span)
    rows = lax.broadcasted_iota(jnp.int32, (2 * SUBS, LANES), 0)

    def one(index):
        return masks[index][0:1]

    def group(lanes):
        for lane in lanes:
            there = cols_of(pl.multiple_of(first + lane, LANES))
            shorts = []
            for i in (1, 2):
                here = heads[i - 1, :, cols_of(lane)].astype(f32)
                rim = rim_ref[i, :, there].astype(f32)
                tap = taps_ref[i, :, there]
                shorts.append([
                    tap[0:1] * here[0:1] + (tap[1:2] * rim[1:2]) * one(at.one) + (tap[2:3] * rim[0:1]) * one(at.two),
                    tap[0:1] * here[1:2] + (tap[1:2] * here[0:1]) * one(at.one + 1) + (tap[2:3] * rim[1:2]) * one(at.two + 1),
                ])
            gates = [(k * v).astype(bf16).astype(f32) for k, v in zip(*shorts)]
            old = gate_in[pl.ds(0, 2 * SUBS), there].astype(f32)
            new = jnp.where(rows == 0, gates[0], jnp.where(rows == SUBS, gates[1], old))
            gate_ref[pl.ds(0, 2 * SUBS), there] = new.astype(bf16)
            rate = rate_ref[:, there]
            added = jnp.exp(-float(span - 1) * rate) * (gates[0] * one(at.last)) + jnp.exp(-float(span - 2) * rate) * (
                gates[1] * one(at.last + 1)
            )
            tile = lax.div(first + lane, LANES)
            state_ref[tile, pl.ds(0, modes), :] = state_in[tile, pl.ds(0, modes), :] + added
            reach = jnp.exp(-float((SUBS - 1) * span) * rate) * one(at.rest)
            end_ref[:, cols_of(lane)] = end_in[:, cols_of(lane)] + reach * added

    each_group(half // LANES, 4, group)


def tail_kernel(
    query_ref, key_ref, value_ref, tail_ref, ahead_ref, bufs, sems
):
    rows, count = query_ref.shape[0], bufs.shape[1]
    copies = [
        pltpu.make_async_copy(ref.at[pl.ds(rows - count, count)], bufs.at[i], sems.at[i])
        for i, ref in enumerate((query_ref, key_ref, value_ref))
    ]
    cols = pl.ds(half_start(query_ref.shape[1], False), ahead_ref.shape[2])
    aheads = [
        pltpu.make_async_copy(ref.at[:, cols], ahead_ref.at[i], sems.at[3 + i])
        for i, ref in enumerate((key_ref, value_ref))
    ]
    for copy in copies + aheads:
        copy.start()
    for i, copy in enumerate(copies):
        copy.wait()
        tail_ref[i] = bufs[i].astype(f32)[count - 2 :].astype(bf16)
    for copy in aheads:
        copy.wait()


def unbroken(len_ref, first, count):
    start = jnp.int32(0)
    whole = jnp.where((first <= 0) & (first + count > 0), 0.0, 1.0)
    for d in range(len_ref.shape[0] - 1):
        start = start + len_ref[d]
        whole = jnp.where((start >= first) & (start < first + count), 0.0, whole)
    return whole.astype(f32)


class Masks:
    def __init__(self, span):
        self.one, self.two, self.last, self.enter = 0, span, 2 * span, 3 * span
        self.passes = 4 * span
        self.edges = self.passes + SUBS
        self.late = self.edges + 3
        self.early = self.late + 1
        self.rest = self.late + 2
        self.inner = self.late + 3
        self.levels = self.late + 5

    def lead(self, level):
        return self.levels + 2 * level

    def later(self, level):
        return self.levels + 2 * level + 1

    def count(self, levels):
        return self.levels + 2 * levels + 1


def write_masks(base_ref, len_ref, masks, rows_of, span, levels):
    at = Masks(span)
    rows, starts = doc_start_rows(len_ref, base_ref[0], span)
    for j in range(span):
        masks[at.one + j] = flag(starts[j] < rows + j)
        masks[at.two + j] = flag(starts[j] < rows + (j - 1))
        masks[at.last + j] = flag(starts[span - 1] <= rows + j)
        masks[at.enter + j] = flag(starts[j] < rows)
    top = flag(lax.broadcasted_iota(jnp.int32, (SUBS, LANES), 0) == 0)
    for j in range(2):
        masks[at.inner + j] = (1.0 - top) * masks[at.last + j]
    masks[at.edges] = top * masks[at.one]
    masks[at.edges + 1] = top * masks[at.two]
    masks[at.edges + 2] = top * masks[at.two + 1]
    size = SUBS * span
    parity = lax.rem(lax.div(base_ref[0], size), 2)
    pair_at = base_ref[0] - parity * size
    rows_of[...] = flag(starts[span - 1] < rows)
    for b in range(SUBS):
        masks[at.passes + b] = row_of(rows_of, b)
    ranges = []
    flags = []
    ranges += [(pair_at + size, size), (pair_at, size), (base_ref[0] + span, size - span)]
    flags += [at.late, at.early, at.rest]
    for m in range(levels + 1):
        group = 2 * size << m
        group_at = base_ref[0] - lax.rem(base_ref[0], group)
        ranges.append((group_at, pair_at - group_at))
        flags.append(at.lead(m))
        if m < levels:
            ranges.append((group_at + group * (1 - lax.rem(lax.div(base_ref[0], group), 2)), group))
            flags.append(at.later(m))
    for index, (first, count) in zip(flags, ranges):
        masks[index] = jnp.full((SUBS, LANES), unbroken(len_ref, first, count), f32)


def near_kernel(masks, gate_ref, rate_ref, weight_ref, *refs, span, modes, most, first, count):
    near_ref, sums, tap_rows = refs[-3:]
    at = Masks(span)

    def group(lanes):
        for slot, lane in enumerate(lanes):
            decay = jnp.exp(-rate_ref[:, cols_of(lane)])
            term = weight_ref[:, cols_of(lane)]
            for lag in range(span):
                part = term[:SUBS]
                for n in range(SUBS, modes, SUBS):
                    part = part + term[n : n + SUBS]
                sums[slot, pl.ds(lag * (SUBS + 1), SUBS), :] = part
                term = term * decay
        for slot in range(len(lanes)):
            for first_lag in range(0, span, SUBS):
                total = [
                    sums[slot, pl.ds(first_lag * (SUBS + 1) + m, SUBS, stride=SUBS + 1), :] for m in range(SUBS)
                ]
                while len(total) > 1:
                    total = [total[m] + total[m + 1] for m in range(0, len(total), 2)]
                tap_rows[slot, pl.ds(first_lag, SUBS), :] = total[0]
        taps = [[row_of(tap_rows.at[slot], lag) for lag in range(span)] for slot in range(len(lanes))]
        for parts, lane in zip(taps, lanes):
            live = []
            for j in range(span):
                if j % 2 == 0:
                    pair = gate_ref[pl.ds(j * SUBS, 2 * SUBS), cols_of(lane)].astype(f32)
                keep = masks[at.one + j]
                live = [g * keep for g in live]
                live.append(pair[(j % 2) * SUBS : (j % 2 + 1) * SUBS])
                total = parts[0] * live[j]
                for lag in range(1, j + 1):
                    total = total + parts[lag] * live[j - lag]
                near_ref[pl.ds(j * SUBS, SUBS), cols_of(lane)] = total

    each_group(count // LANES, most, lambda lanes: group([pl.multiple_of(first + lane, LANES) for lane in lanes]))


def query_kernel(masks, query_ref, taps_ref, *refs, span, most, chunk, first, count):
    short_ref, query_buf, sems, wide_q = refs[-4:]

    def fetch(c):
        there = pl.ds(first + c * chunk if isinstance(c, int) else pl.multiple_of(first + c * chunk, chunk), chunk)
        here = pl.ds(c * chunk if isinstance(c, int) else pl.multiple_of(c * chunk, chunk), chunk)
        return pltpu.make_async_copy(query_ref.at[:, there], query_buf.at[:, here], sems.at[c])

    for c in range(count // chunk):
        fetch(c).start()
    at = Masks(span)

    def group(lanes):
        for slot, lane in enumerate(lanes):
            spread(query_buf[:, cols_of(lane)], wide_q.at[slot], span)
        convs = [
            Conv(wide_q.at[slot], None, taps_ref[0, :, cols_of(pl.multiple_of(first + lane, LANES))], span)
            for slot, lane in enumerate(lanes)
        ]
        for j in range(span):
            keep_one, keep_two = masks[at.one + j], masks[at.two + j]
            for slot, lane in enumerate(lanes):
                short_ref[pl.ds(j * SUBS, SUBS), cols_of(pl.multiple_of(first + lane, LANES))] = convs[slot].step(j, keep_one, keep_two)

    each_chunk(count, chunk, lambda c: fetch(c).wait(), group, lambda c: None, most)


def pair_rates(rate_ref, count):
    parity = lax.rem(lax.axis_index("ctx"), 2)
    return parity, rate_ref[:, pl.ds(pl.multiple_of(parity * count, LANES), count)]


def early_late(parity, own, got):
    odd = jnp.full(own.shape, parity, jnp.int32) == 1
    return jnp.where(odd, got, own), jnp.where(odd, own, got)


def leap(masks, index, rate, rows):
    return jnp.exp(-float(rows) * rate) * masks[index][0:1, 0:1]


def pair_kernel(masks, own_ref, got_ref, rate_ref, total_ref, sent_ref, *, rows, index):
    parity, rate = pair_rates(rate_ref, own_ref.shape[1])
    early, late = early_late(parity, own_ref[...], got_ref[...])
    total = late + leap(masks, index, rate, rows) * early
    total_ref[...] = total
    sent_ref[...] = total.astype(bf16)


def lead_leap(masks, index, rate, rows, bit):
    me = lax.axis_index("ctx")
    lead = (lax.rem(me, bit) - lax.rem(me, 2)) * rows
    return jnp.exp(rate * -lead.astype(f32)) * masks[index][0:1, 0:1]


def level_kernel(masks, total_ref, got_ref, rate_ref, *refs, rows, level, lead, later):
    before_ref = refs[0] if level else None
    sent_ref, enter_ref, *new_ref = refs[1 if level else 0 :]
    _, rate = pair_rates(rate_ref, total_ref.shape[1])
    bit = 2 << level
    after = lax.rem(lax.div(lax.axis_index("ctx"), bit), 2)
    got = got_ref[...].astype(f32)
    early, late = early_late(after, total_ref[...], got)
    total = late + leap(masks, later, rate, bit * rows) * early
    for ref in new_ref:
        ref[...] = total
    sent_ref[...] = total.astype(bf16)
    entering = jnp.where(jnp.full(got.shape, after, jnp.int32) == 1, got, 0.0) * lead_leap(masks, lead, rate, rows, bit)
    enter_ref[...] = entering if before_ref is None else before_ref[...] + entering


def enter_kernel(
    masks, before_ref, got_ref, own_ref, other_ref, rate_ref, mine_ref, give_ref, *, rows, bit, lead, early_index
):
    parity, rate = pair_rates(rate_ref, own_ref.shape[1])
    first = before_ref[...] + lead_leap(masks, lead, rate, rows, bit) * got_ref[...].astype(f32)
    early, _ = early_late(parity, own_ref[...], other_ref[...])
    second = early + leap(masks, early_index, rate, rows) * first
    give, mine = early_late(parity, second, first)
    mine_ref[...] = mine
    give_ref[...] = give


def final_kernel(
    masks, state_ref, enter_ref, near_ref, short_ref, resid_ref, rim_ref, taps_ref, rate_ref, weight_ref, *refs,
    span, modes, channels, most, chunk, own,
):
    if own:
        hidden_out, whole, sums, hidden_ref, sems, wide, tables, starts_at = refs
    elif channels:
        gain_ref, _, _, _, hidden_out, whole, sums, normed_out, hidden_ref, sems, wide, tables, starts_at, normed_ref = refs
    else:
        _, _, _, hidden_out, whole, sums, hidden_ref, sems, wide, tables, starts_at = refs
    chans = resid_ref.shape[1]
    half = chans // 2
    first = half_start(chans, own)
    at = Masks(span)

    def store(c):
        here = pl.ds(pl.multiple_of(c * chunk, chunk), chunk)
        there = pl.ds(pl.multiple_of(first + c * chunk, chunk), chunk)
        return pltpu.make_async_copy(hidden_ref.at[:, here], hidden_out.at[:, there], sems.at[0, c])

    def store_normed(c):
        return cols_copy(normed_ref, normed_out, sems.at[1], c, chunk)

    if own:
        sums[...] = jnp.zeros(sums.shape, f32)

    def group(lanes):
        for slot, lane in enumerate(lanes):
            state = enter_ref[:, cols_of(pl.multiple_of(lane - first, LANES))]
            rate = rate_ref[:, cols_of(lane)]
            weight = weight_ref[:, cols_of(lane)]
            tables[slot] = jnp.exp(-rate)
            leap = jnp.exp(-float(span) * rate)
            for b in range(SUBS):
                starts_at[slot, pl.ds(b * (modes + 1), modes), :] = weight * state
                if b < SUBS - 1:
                    state = (leap * twice(masks[at.passes + b], modes)) * state + sub_state(state_ref, lane, b, modes)
        for slot, lane in enumerate(lanes):
            part = [starts_at[slot, pl.ds(n, SUBS, stride=modes + 1), :] for n in range(modes)]
            decay = [row_of(tables.at[slot], n) for n in range(modes)]
            rim = rim_ref[0, :, cols_of(lane)].astype(f32)
            tap = taps_ref[0, :, cols_of(lane)]
            edge = [
                (tap[1:2] * rim[1:2]) * masks[at.edges] + (tap[2:3] * rim[0:1]) * masks[at.edges + 1],
                (tap[2:3] * rim[1:2]) * masks[at.edges + 2],
            ]
            for j in range(span):
                part = [part[n] * decay[n] for n in range(modes)]
                total = part
                while len(total) > 1:
                    total = [total[m] + total[m + 1] for m in range(0, len(total), 2)]
                conv = near_ref[pl.ds(j * SUBS, SUBS), cols_of(lane)] + total[0] * masks[at.enter + j]
                conv = conv.astype(bf16).astype(f32)
                short = short_ref[pl.ds(j * SUBS, SUBS), cols_of(lane)]
                if j < 2:
                    short = short + edge[j]
                wide[slot, pl.ds(j, SUBS, stride=span + 1), :] = short * conv
        for b in range(SUBS):
            rows = pl.ds(b * span, span)
            squares = sums[rows, :]
            for slot, lane in enumerate(lanes):
                hidden = wide[slot, pl.ds(b * (span + 1), span), :] + resid_ref[rows, cols_of(lane)].astype(f32)
                whole[lax.div(lane, LANES), rows, :] = hidden
                hidden_ref[rows, cols_of(pl.multiple_of(lane - first, LANES))] = hidden.astype(bf16)
                squares = squares + hidden * hidden
            sums[rows, :] = squares

    each_chunk(
        half,
        chunk,
        lambda c: None,
        lambda lanes: group([pl.multiple_of(first + lane, LANES) for lane in lanes]),
        lambda c: store(c).start(),
        most,
    )
    if channels and not own:
        inverse = lax.rsqrt(jnp.sum(sums[...], axis=1, keepdims=True) / channels + 1e-06)
        sums[...] = jnp.broadcast_to(inverse, sums.shape)

        def scale(lanes):
            for lane in lanes:
                normed = whole[lax.div(lane, LANES)] * sums[...] * gain_ref[:, cols_of(lane)]
                normed_ref[:, cols_of(lane)] = normed.astype(bf16)

        each_chunk(chans, chunk, lambda c: None, scale, lambda c: store_normed(c).start(), 4)
        for c in range(chans // chunk):
            store_normed(c).wait()
    for c in range(half // chunk):
        store(c).wait()


def shards(
    query_in, key_in, value_in, short_taps, decay_rate, residues, doc_lengths, residual, norm_gain
):
    tok_rows, chans = query_in.shape
    modes = decay_rate.shape[0]
    span = tok_rows // SUBS
    blocks = lax.axis_size("ctx")
    grp = lax.axis_size("grp")
    chunk = min(chans // 2, 1024)
    pieces = chans // chunk
    ctx_index = lax.axis_index("ctx")
    base = (ctx_index * tok_rows).astype(jnp.int32).reshape(1)
    weight = residues * jnp.sqrt(-jnp.expm1(-2.0 * decay_rate))

    smem = pl.BlockSpec(memory_space=pltpu.SMEM)
    vmem = pl.BlockSpec(memory_space=pltpu.VMEM)
    hbm = pl.BlockSpec(memory_space=pltpu.HBM)
    tile_shape = (SUBS, LANES)
    wide_rows = SUBS * (span + 1)
    params = pltpu.CompilerParams(vmem_limit_bytes=16 * MIB)

    lengths = pltpu.with_memory_space_constraint(doc_lengths, pltpu.HBM)

    def near_by(x):
        return pltpu.with_memory_space_constraint(x, pltpu.VMEM)

    def far_off(x):
        return pltpu.with_memory_space_constraint(x, pltpu.HBM)

    def copies(kinds):
        return pltpu.SemaphoreType.DMA((kinds, pieces))

    def cost(per_tile, moved):
        return pl.CostEstimate(flops=per_tile * (chans // LANES) * SUBS * LANES, bytes_accessed=moved, transcendentals=0)

    levels = max(1, (blocks // 4).bit_length() - 2)
    mask_shape = (Masks(span).count(levels),) + tile_shape
    small = min(chans // 2, 512)
    tails, ahead = pl.pallas_call(
        tail_kernel,
        in_specs=[hbm, hbm, hbm],
        out_specs=[vmem, vmem],
        out_shape=[pltpu.VMEM((3, 2, chans), bf16), pltpu.VMEM((2, tok_rows, small), bf16)],
        scratch_shapes=[pltpu.VMEM((3, 16, chans), bf16), pltpu.SemaphoreType.DMA((5,))],
        compiler_params=params,
        name="tails",
    )(far_off(query_in), far_off(key_in), far_off(value_in))
    rim_rows = from_behind(tails, "ctx", 1)
    def query_piece(part, masks, before):
        count = chans // 2
        scratch = [
            pltpu.VMEM((tok_rows, count), bf16),
            pltpu.SemaphoreType.DMA((count // chunk,)),
            pltpu.VMEM((Q_TILES, wide_rows, LANES), f32),
        ]
        operands = [near_by(masks), far_off(query_in), taps] + ([near_by(before)] if part else [])
        return pl.pallas_call(
            functools.partial(
                query_kernel, span=span, most=Q_TILES, chunk=chunk, first=part * count, count=count
            ),
            in_specs=[vmem, hbm, vmem] + [vmem] * (len(operands) - 3),
            out_specs=vmem,
            out_shape=pltpu.VMEM((tok_rows, chans), f32),
            scratch_shapes=scratch,
            input_output_aliases={3: 0} if part else {},
            compiler_params=params,
            cost_estimate=cost(100, 3 * tok_rows * chans),
            name="query_part_%d" % part,
        )(*operands)

    key_half = pltpu.VMEM((tok_rows, chans // 2), bf16)
    rates, weights, taps, rims = near_by(decay_rate), near_by(weight), near_by(short_taps), near_by(rim_rows)
    kept = pltpu.VMEM((modes, chans // 2), f32)
    sent = pltpu.VMEM((modes, chans // 2), bf16)

    gate_shape = pltpu.VMEM((tok_rows, chans), bf16)
    state_shape = pltpu.VMEM((chans // LANES, SUBS * (modes + 1), LANES), f32)

    def states_of(own, operands, in_specs, out_shape, scratch, aliases):
        return pl.pallas_call(
            functools.partial(
                state_kernel, span=span, modes=modes, most=A_TILES, own=own, chunk=small, levels=levels
            ),
            in_specs=in_specs,
            out_specs=[vmem] * (3 + len(out_shape)),
            out_shape=[gate_shape, state_shape, kept] + out_shape,
            scratch_shapes=scratch[:-1]
            + [
                pltpu.VMEM((A_TILES, wide_rows, LANES), f32),
                pltpu.VMEM((A_TILES, wide_rows, LANES), f32),
                pltpu.VMEM((A_TILES, modes, LANES), f32),
                pltpu.VMEM((A_TILES, span) + tile_shape, f32),
            ]
            + scratch[-1:],
            input_output_aliases=aliases,
            compiler_params=params,
            cost_estimate=cost(500, 6 * tok_rows * chans),
            name="block_states_own" if own else "block_states_give",
        )(*operands)

    gates, states, give, masks, key_own, value_own, heads = states_of(
        False,
        [base, lengths, near_by(ahead), far_off(key_in), far_off(value_in), taps, rates],
        [smem, smem, vmem, hbm, hbm, vmem, vmem],
        [pltpu.VMEM(mask_shape, f32), key_half, key_half, pltpu.VMEM((2, 16, chans // 2), bf16)],
        [
            pltpu.VMEM((tok_rows, chans // 2), bf16),
            pltpu.VMEM((tok_rows, chans // 2), bf16),
            pltpu.VMEM(tile_shape, f32),
            pltpu.SemaphoreType.DMA((2, chans // 2 // small + 1)),
        ],
        {},
    )
    gates, states, give = pl.pallas_call(
        functools.partial(patch_kernel, span=span, modes=modes),
        in_specs=[vmem] * 8,
        out_specs=[vmem] * 3,
        out_shape=[gate_shape, state_shape, kept],
        input_output_aliases={5: 0, 6: 1, 7: 2},
        compiler_params=params,
        name="first_rows",
    )(near_by(masks), near_by(heads), rims, taps, rates, near_by(gates), near_by(states), near_by(give))
    got = swap(give, "ctx")
    gates, states, own = states_of(
        True,
        [near_by(masks), near_by(key_own), near_by(value_own), rims, taps, rates, near_by(gates), near_by(states)],
        [vmem] * 8,
        [],
        [],
        {6: 0, 7: 1},
    )
    got, gates, states, own = lax.optimization_barrier((got, gates, states, own))

    def near_piece(part, near):
        count = chans // NEAR_PARTS
        before = [] if near is None else [near_by(near)]
        return pl.pallas_call(
            functools.partial(
                near_kernel, span=span, modes=modes, most=N_TILES, first=part * count, count=count
            ),
            in_specs=[vmem] * (4 + len(before)),
            out_specs=vmem,
            out_shape=pltpu.VMEM((tok_rows, chans), f32),
            scratch_shapes=[
                pltpu.VMEM((N_TILES, span * (SUBS + 1), LANES), f32),
                pltpu.VMEM((N_TILES, span, LANES), f32),
            ],
            compiler_params=params,
            input_output_aliases={4: 0} if before else {},
            cost_estimate=cost(600 // NEAR_PARTS, 7 * tok_rows * count),
            name="near_part_%d" % part,
        )(near_by(masks), near_by(gates), rates, weights, *before)

    got = swap(give, "ctx")

    at = Masks(span)

    def pair_call(kernel, operands, out_shape, name, extra=(), **static):
        return pl.pallas_call(
            functools.partial(kernel, **static),
            in_specs=[vmem] * (len(operands) + 2 + len(extra)),
            out_specs=[vmem] * len(out_shape),
            out_shape=out_shape,
            compiler_params=params,
            name=name,
        )(near_by(masks), *[near_by(x) for x in operands], rates, *[near_by(x) for x in extra])

    total, ends = pair_call(pair_kernel, [own, got], [kept, sent], "pair_ends", rows=tok_rows, index=at.late)
    entering, near = [], None
    for m in range(levels):
        met = swap(ends, "ctx", 2 << m)
        if m < NEAR_PARTS:
            near = near_piece(m, near)
            if m == 0:
                q_short = query_piece(0, masks, None)
                met, q_short = lax.optimization_barrier((met, q_short))
            met, near = lax.optimization_barrier((met, near))
        ends, enter, *total = pair_call(
            level_kernel,
            [total, met],
            [sent, kept] + [kept] * (m < levels - 1),
            "level_%d" % m,
            extra=entering,
            rows=tok_rows,
            level=m,
            lead=at.lead(m),
            later=at.later(m),
        )
        entering = [enter]
        total = total[0] if total else None
    on = from_behind(ends, "ctx", 2 << levels)
    for m in range(levels, NEAR_PARTS):
        near = near_piece(m, near)
    q_short = query_piece(1, masks, q_short)
    on, q_short, near = lax.optimization_barrier((on, q_short, near))
    mine, give_back = pair_call(
        enter_kernel,
        entering + [on, own, got],
        [kept, kept],
        "pair_enter",
        rows=tok_rows,
        bit=2 << levels,
        lead=at.lead(levels),
        early_index=at.early,
    )
    got_back = swap(give_back, "ctx")

    alone = grp == 1
    resid = near_by(residual)

    def finish(own, enter, before):
        last = alone and not own
        out_specs = [hbm, vmem, vmem]
        out_shape = [
            jax.ShapeDtypeStruct((tok_rows, chans), bf16),
            pltpu.VMEM((chans // LANES, tok_rows, LANES), f32),
            pltpu.VMEM((tok_rows, LANES), f32),
        ]
        scratch = [
            pltpu.VMEM((tok_rows, chans // 2), bf16),
            copies(2),
            pltpu.VMEM((F_TILES, wide_rows, LANES), f32),
            pltpu.VMEM((F_TILES, modes, LANES), f32),
            pltpu.VMEM((F_TILES, SUBS * (modes + 1), LANES), f32),
        ]
        operands = [near_by(x) for x in (masks, states, enter, near, q_short)] + [resid, rims, taps, rates, weights]
        if last:
            operands.append(near_by(norm_gain.reshape(1, chans)))
            out_specs.append(hbm)
            out_shape.append(jax.ShapeDtypeStruct((tok_rows, chans), bf16))
            scratch.append(pltpu.VMEM((tok_rows, chans), bf16))
        count = len(operands)
        in_specs = [vmem] * count
        if before:
            operands += [far_off(before[0]), near_by(before[1]), near_by(before[2])]
            in_specs += [hbm, vmem, vmem]
        return pl.pallas_call(
            functools.partial(
                final_kernel, span=span, modes=modes, channels=chans if alone else 0, most=F_TILES, chunk=chunk, own=own
            ),
            in_specs=in_specs,
            out_specs=out_specs,
            out_shape=out_shape,
            scratch_shapes=scratch,
            input_output_aliases={count + i: i for i in range(len(before))},
            compiler_params=params,
            cost_estimate=cost(450, 9 * tok_rows * chans),
            name="far_part_own" if own else "far_part_other",
        )(*operands)

    before = finish(True, mine, [])
    got_back, *before = lax.optimization_barrier((got_back, *before))
    outs = finish(False, got_back, before)
    if alone:
        return (outs[0], outs[3])
    hidden_out, whole, sums = outs
    hidden = whole.transpose(1, 0, 2).reshape(tok_rows, chans)
    square_sum = lax.psum(jnp.sum(sums, axis=1), "grp")
    inverse_rms = lax.rsqrt(square_sum / (chans * grp) + 1e-06)
    normed = (hidden * inverse_rms[:, None] * norm_gain[None, :]).astype(bf16)
    return (hidden_out, normed)


def solution(mesh):
    return jax.shard_map(
        shards,
        mesh=mesh,
        in_specs=(
            P("ctx", "grp"),
            P("ctx", "grp"),
            P("ctx", "grp"),
            P(None, None, "grp"),
            P(None, "grp"),
            P(None, "grp"),
            P(),
            P("ctx", "grp"),
            P("grp"),
        ),
        out_specs=(P("ctx", "grp"), P("ctx", "grp")),
        check_vma=False,
    )
```

```python
import functools
import math

import jax
import jax.numpy as jnp
from jax import lax
from jax.experimental import pallas as pl
from jax.experimental.pallas import tpu as pltpu
from jax.sharding import PartitionSpec as P

SUBS = 8
LANES = 128
MIB = 1024 * 1024
A_TILES, N_TILES, Q_TILES, F_TILES = 4, 8, 8, 8
NEAR_PARTS = 2
f32 = jnp.float32
bf16 = jnp.bfloat16


def from_behind(shard, axis, by):
    count = lax.axis_size(axis)
    return lax.ppermute(shard, axis, [(i, i + by) for i in range(count - by)])


def swap(shard, axis, bit=1):
    return lax.ppermute(shard, axis, [(i, i ^ bit) for i in range(lax.axis_size(axis))])


def doc_start_rows(len_ref, base, span):
    rows = lax.broadcasted_iota(jnp.int32, (SUBS, LANES), 0) * span + base
    starts = [jnp.int32(0)]
    for d in range(len_ref.shape[0] - 1):
        starts.append(starts[-1] + len_ref[d])
    out = []
    for j in range(span):
        pos = rows + j
        best = jnp.zeros((SUBS, LANES), jnp.int32)
        for start in starts[1:]:
            best = jnp.where(pos >= start, start, best)
        out.append(best)
    return rows, out


def flag(cond):
    return jnp.where(cond, 1.0, 0.0).astype(f32)


def each_group(count, most, group):
    size = math.gcd(count, most)

    def step(i, carry):
        group([pl.multiple_of((i * size + m) * LANES, LANES) for m in range(size)])
        return carry

    lax.fori_loop(0, count // size, step, 0)


def each_chunk(chans, chunk, before, group, after, most, start=0):
    def step(c, carry):
        before(c)

        def inner(lanes):
            group([pl.multiple_of(c * chunk + lane, LANES) for lane in lanes])

        each_group(chunk // LANES, most, inner)
        after(c)
        return carry

    lax.fori_loop(start, chans // chunk, step, 0)


def cols_copy(src, dst, sem, c, chunk):
    cols = pl.ds(pl.multiple_of(c * chunk, chunk), chunk)
    return pltpu.make_async_copy(src.at[:, cols], dst.at[:, cols], sem.at[c])


def cols_of(lane):
    return pl.ds(lane, LANES)


def row_of(ref, index):
    return ref[pl.ds(index, SUBS, stride=0), :]


def spread(x, wide, span):
    x = x.astype(f32)
    for b in range(SUBS):
        wide[pl.ds(b * (span + 1), span), :] = x[b * span : (b + 1) * span]


class Conv:
    def __init__(self, wide, rim, taps, span):
        self.wide, self.span = wide, span
        self.taps = [jnp.broadcast_to(taps[m : m + 1], (SUBS, LANES)) for m in range(3)]
        top = lax.broadcasted_iota(jnp.int32, (SUBS, LANES), 0) == 0
        ahead = [0.0, 0.0] if rim is None else [jnp.broadcast_to(rim[m : m + 1], (SUBS, LANES)) for m in range(2)]
        self.behind = [jnp.where(top, ahead[m], pltpu.roll(self.row(span - 2 + m), 1, 0)) for m in range(2)]

    def row(self, j):
        return self.wide[pl.ds(j, SUBS, stride=self.span + 1), :]

    def step(self, j, keep_one, keep_two):
        here = self.row(j)
        two, one = self.behind
        self.behind = [one, here]
        return self.taps[0] * here + (self.taps[1] * one) * keep_one + (self.taps[2] * two) * keep_two


def half_start(chans, own):
    parity = lax.rem(lax.axis_index("ctx"), 2)
    return pl.multiple_of((parity if own else 1 - parity) * (chans // 2), LANES)


def twice(mask, modes):
    return jnp.concatenate([mask] * (modes // SUBS), axis=0)


def sub_state(state_ref, lane, b, modes):
    return state_ref[lax.div(lane, LANES), pl.ds(b * (modes + 1), modes), :]


def state_kernel(*refs, span, modes, most, own, chunk, levels):
    if own:
        masks, key_ref, value_ref, rim_ref, taps_ref, rate_ref, _, _, gate_ref, state_ref, end_ref, wide_k, wide_v, tables, held = refs
    else:
        (base_ref, len_ref, ahead_ref, key_in, value_in, taps_ref, rate_ref,
         gate_ref, state_ref, end_ref, masks, key_own, value_own, heads,
         key_ref, value_ref, rows_of, wide_k, wide_v, tables, held, sems) = refs
    half = key_ref.shape[1]
    first = half_start(2 * half, own)
    if not own:
        def fetch(c):
            there = pl.ds(pl.multiple_of(first + c * chunk, chunk), chunk)
            here = pl.ds(pl.multiple_of(c * chunk, chunk), chunk)
            return [
                pltpu.make_async_copy(key_in.at[:, there], key_ref.at[:, here], sems.at[0, c]),
                pltpu.make_async_copy(value_in.at[:, there], value_ref.at[:, here], sems.at[1, c]),
            ]

        cols = pl.ds(half_start(2 * half, True), half)
        others = [
            pltpu.make_async_copy(key_in.at[:, cols], key_own, sems.at[0, half // chunk]),
            pltpu.make_async_copy(value_in.at[:, cols], value_own, sems.at[1, half // chunk]),
        ]
        for c in range(1, half // chunk):
            for copy in fetch(c):
                copy.start()
        write_masks(base_ref, len_ref, masks, rows_of, span, levels)
    at = Masks(span)

    def group(lanes, keys=key_ref, values=value_ref):
        for slot, lane in enumerate(lanes):
            spread(keys[:, cols_of(pl.multiple_of(lane - first, LANES))], wide_k.at[slot], span)
            spread(values[:, cols_of(pl.multiple_of(lane - first, LANES))], wide_v.at[slot], span)
            rate = rate_ref[:, cols_of(lane)]
            tables[slot, pl.ds(0, modes), :] = jnp.exp(-rate)
        convs = [
            [
                Conv(wide.at[slot], rim_ref[i, :, cols_of(lane)].astype(f32) if own else None, taps_ref[i, :, cols_of(lane)], span)
                for i, wide in ((1, wide_k), (2, wide_v))
            ]
            for slot, lane in enumerate(lanes)
        ]
        last = [None] * len(lanes)
        for j in range(span):
            keep_one, keep_two = masks[at.one + j], masks[at.two + j]
            for slot, lane in enumerate(lanes):
                k_short, v_short = [conv.step(j, keep_one, keep_two) for conv in convs[slot]]
                if j % 2 == 0:
                    last[slot] = k_short * v_short
                    continue
                pair = jnp.concatenate([last[slot], k_short * v_short], axis=0).astype(bf16)
                gate_ref[pl.ds((j - 1) * SUBS, 2 * SUBS), cols_of(lane)] = pair
                pair = pair.astype(f32)
                used = at.inner if j == 1 and not own else at.last + j - 1
                held[slot, j - 1] = pair[:SUBS] * masks[used]
                held[slot, j] = pair[SUBS:] * masks[used + 1]
        for slot, lane in enumerate(lanes):
            decay = [row_of(tables.at[slot], n) for n in range(modes)]
            state = [held[slot, 0]] * modes
            for j in range(1, span):
                gate = held[slot, j]
                state = [decay[n] * state[n] + gate for n in range(modes)]
            for n in range(modes):
                state_ref[lax.div(lane, LANES), pl.ds(n, SUBS, stride=modes + 1), :] = state[n]
        for slot, lane in enumerate(lanes):
            leap = jnp.exp(-float(span) * rate_ref[:, cols_of(lane)])
            end = sub_state(state_ref, lane, 0, modes)
            for b in range(1, SUBS):
                end = (leap * twice(masks[at.passes + b], modes)) * end + sub_state(state_ref, lane, b, modes)
            end_ref[:, cols_of(pl.multiple_of(lane - first, LANES))] = end

    def shifted(lanes, *sources):
        group([pl.multiple_of(first + lane, LANES) for lane in lanes], *sources)

    if own:
        each_group(half // LANES, most, shifted)
    else:
        def before(c):
            for copy in fetch(c):
                copy.wait()

        each_group(chunk // LANES, most, lambda lanes: shifted(lanes, ahead_ref.at[0], ahead_ref.at[1]))
        for copy in others:
            copy.start()
        each_chunk(half, chunk, before, shifted, lambda c: None, most, 1)
        rows = pl.ds(0, heads.shape[1])
        for i, ref in enumerate((key_ref, value_ref)):
            heads[i, :, pl.ds(0, chunk)] = ahead_ref[i, rows, :]
            if half > chunk:
                heads[i, :, pl.ds(chunk, half - chunk)] = ref[rows, pl.ds(chunk, half - chunk)]
        for copy in others:
            copy.wait()


def patch_kernel(
    masks, heads, rim_ref, taps_ref, rate_ref, gate_in, state_in, end_in, gate_ref, state_ref, end_ref, *, span, modes
):
    half = end_ref.shape[1]
    first = half_start(2 * half, False)
    at = Masks(span)
    rows = lax.broadcasted_iota(jnp.int32, (2 * SUBS, LANES), 0)

    def one(index):
        return masks[index][0:1]

    def group(lanes):
        for lane in lanes:
            there = cols_of(pl.multiple_of(first + lane, LANES))
            shorts = []
            for i in (1, 2):
                here = heads[i - 1, :, cols_of(lane)].astype(f32)
                rim = rim_ref[i, :, there].astype(f32)
                tap = taps_ref[i, :, there]
                shorts.append([
                    tap[0:1] * here[0:1] + (tap[1:2] * rim[1:2]) * one(at.one) + (tap[2:3] * rim[0:1]) * one(at.two),
                    tap[0:1] * here[1:2] + (tap[1:2] * here[0:1]) * one(at.one + 1) + (tap[2:3] * rim[1:2]) * one(at.two + 1),
                ])
            gates = [(k * v).astype(bf16).astype(f32) for k, v in zip(*shorts)]
            old = gate_in[pl.ds(0, 2 * SUBS), there].astype(f32)
            new = jnp.where(rows == 0, gates[0], jnp.where(rows == SUBS, gates[1], old))
            gate_ref[pl.ds(0, 2 * SUBS), there] = new.astype(bf16)
            rate = rate_ref[:, there]
            added = jnp.exp(-float(span - 1) * rate) * (gates[0] * one(at.last)) + jnp.exp(-float(span - 2) * rate) * (
                gates[1] * one(at.last + 1)
            )
            tile = lax.div(first + lane, LANES)
            state_ref[tile, pl.ds(0, modes), :] = state_in[tile, pl.ds(0, modes), :] + added
            reach = jnp.exp(-float((SUBS - 1) * span) * rate) * one(at.rest)
            end_ref[:, cols_of(lane)] = end_in[:, cols_of(lane)] + reach * added

    each_group(half // LANES, 4, group)


def tail_kernel(
    query_ref, key_ref, value_ref, tail_ref, ahead_ref, bufs, sems
):
    rows, count = query_ref.shape[0], bufs.shape[1]
    copies = [
        pltpu.make_async_copy(ref.at[pl.ds(rows - count, count)], bufs.at[i], sems.at[i])
        for i, ref in enumerate((query_ref, key_ref, value_ref))
    ]
    cols = pl.ds(half_start(query_ref.shape[1], False), ahead_ref.shape[2])
    aheads = [
        pltpu.make_async_copy(ref.at[:, cols], ahead_ref.at[i], sems.at[3 + i])
        for i, ref in enumerate((key_ref, value_ref))
    ]
    for copy in copies + aheads:
        copy.start()
    for i, copy in enumerate(copies):
        copy.wait()
        tail_ref[i] = bufs[i].astype(f32)[count - 2 :].astype(bf16)
    for copy in aheads:
        copy.wait()


def unbroken(len_ref, first, count):
    start = jnp.int32(0)
    whole = jnp.where((first <= 0) & (first + count > 0), 0.0, 1.0)
    for d in range(len_ref.shape[0] - 1):
        start = start + len_ref[d]
        whole = jnp.where((start >= first) & (start < first + count), 0.0, whole)
    return whole.astype(f32)


class Masks:
    def __init__(self, span):
        self.one, self.two, self.last, self.enter = 0, span, 2 * span, 3 * span
        self.passes = 4 * span
        self.edges = self.passes + SUBS
        self.late = self.edges + 3
        self.early = self.late + 1
        self.rest = self.late + 2
        self.inner = self.late + 3
        self.levels = self.late + 5

    def lead(self, level):
        return self.levels + 2 * level

    def later(self, level):
        return self.levels + 2 * level + 1

    def count(self, levels):
        return self.levels + 2 * levels + 1


def write_masks(base_ref, len_ref, masks, rows_of, span, levels):
    at = Masks(span)
    rows, starts = doc_start_rows(len_ref, base_ref[0], span)
    for j in range(span):
        masks[at.one + j] = flag(starts[j] < rows + j)
        masks[at.two + j] = flag(starts[j] < rows + (j - 1))
        masks[at.last + j] = flag(starts[span - 1] <= rows + j)
        masks[at.enter + j] = flag(starts[j] < rows)
    top = flag(lax.broadcasted_iota(jnp.int32, (SUBS, LANES), 0) == 0)
    for j in range(2):
        masks[at.inner + j] = (1.0 - top) * masks[at.last + j]
    masks[at.edges] = top * masks[at.one]
    masks[at.edges + 1] = top * masks[at.two]
    masks[at.edges + 2] = top * masks[at.two + 1]
    size = SUBS * span
    parity = lax.rem(lax.div(base_ref[0], size), 2)
    pair_at = base_ref[0] - parity * size
    rows_of[pl.ds(0, SUBS), :] = flag(starts[span - 1] < rows)
    for b in range(SUBS):
        masks[at.passes + b] = row_of(rows_of, b)
    ranges = []
    flags = []
    ranges += [(pair_at + size, size), (pair_at, size), (base_ref[0] + span, size - span)]
    flags += [at.late, at.early, at.rest]
    for m in range(levels + 1):
        group = 2 * size << m
        group_at = base_ref[0] - lax.rem(base_ref[0], group)
        ranges.append((group_at, pair_at - group_at))
        flags.append(at.lead(m))
        if m < levels:
            ranges.append((group_at + group * (1 - lax.rem(lax.div(base_ref[0], group), 2)), group))
            flags.append(at.later(m))
    for index, (first, count) in zip(flags, ranges):
        masks[index] = jnp.full((SUBS, LANES), unbroken(len_ref, first, count), f32)


def near_kernel(masks, gate_ref, rate_ref, weight_ref, *refs, span, modes, most, first, count):
    near_ref, sums, tap_rows = refs[-3:]
    at = Masks(span)

    def group(lanes):
        for slot, lane in enumerate(lanes):
            decay = jnp.exp(-rate_ref[:, cols_of(lane)])
            term = weight_ref[:, cols_of(lane)]
            for lag in range(span):
                part = term[:SUBS]
                for n in range(SUBS, modes, SUBS):
                    part = part + term[n : n + SUBS]
                sums[slot, pl.ds(lag * (SUBS + 1), SUBS), :] = part
                term = term * decay
        for slot in range(len(lanes)):
            for first_lag in range(0, span, SUBS):
                total = [
                    sums[slot, pl.ds(first_lag * (SUBS + 1) + m, SUBS, stride=SUBS + 1), :] for m in range(SUBS)
                ]
                while len(total) > 1:
                    total = [total[m] + total[m + 1] for m in range(0, len(total), 2)]
                tap_rows[slot, pl.ds(first_lag, SUBS), :] = total[0]
        taps = [[row_of(tap_rows.at[slot], lag) for lag in range(span)] for slot in range(len(lanes))]
        for parts, lane in zip(taps, lanes):
            live = []
            for j in range(span):
                if j % 2 == 0:
                    pair = gate_ref[pl.ds(j * SUBS, 2 * SUBS), cols_of(lane)].astype(f32)
                keep = masks[at.one + j]
                live = [g * keep for g in live]
                live.append(pair[(j % 2) * SUBS : (j % 2 + 1) * SUBS])
                total = parts[0] * live[j]
                for lag in range(1, j + 1):
                    total = total + parts[lag] * live[j - lag]
                near_ref[pl.ds(j * SUBS, SUBS), cols_of(lane)] = total

    each_group(count // LANES, most, lambda lanes: group([pl.multiple_of(first + lane, LANES) for lane in lanes]))


def query_kernel(masks, query_ref, taps_ref, *refs, span, most, chunk, first, count):
    short_ref, query_buf, sems, wide_q = refs[-4:]

    def fetch(c):
        there = pl.ds(first + c * chunk if isinstance(c, int) else pl.multiple_of(first + c * chunk, chunk), chunk)
        here = pl.ds(c * chunk if isinstance(c, int) else pl.multiple_of(c * chunk, chunk), chunk)
        return pltpu.make_async_copy(query_ref.at[:, there], query_buf.at[:, here], sems.at[c])

    for c in range(count // chunk):
        fetch(c).start()
    at = Masks(span)

    def group(lanes):
        for slot, lane in enumerate(lanes):
            spread(query_buf[:, cols_of(lane)], wide_q.at[slot], span)
        convs = [
            Conv(wide_q.at[slot], None, taps_ref[0, :, cols_of(pl.multiple_of(first + lane, LANES))], span)
            for slot, lane in enumerate(lanes)
        ]
        for j in range(span):
            keep_one, keep_two = masks[at.one + j], masks[at.two + j]
            for slot, lane in enumerate(lanes):
                short_ref[pl.ds(j * SUBS, SUBS), cols_of(pl.multiple_of(first + lane, LANES))] = convs[slot].step(j, keep_one, keep_two)

    each_chunk(count, chunk, lambda c: fetch(c).wait(), group, lambda c: None, most)


def pair_rates(rate_ref, count):
    parity = lax.rem(lax.axis_index("ctx"), 2)
    return parity, rate_ref[:, pl.ds(pl.multiple_of(parity * count, LANES), count)]


def early_late(parity, own, got):
    odd = jnp.full(own.shape, parity, jnp.int32) == 1
    return jnp.where(odd, got, own), jnp.where(odd, own, got)


def leap(masks, index, rate, rows):
    return jnp.exp(-float(rows) * rate) * masks[index][0:1, 0:1]


def pair_kernel(masks, own_ref, got_ref, rate_ref, total_ref, sent_ref, *, rows, index):
    parity, rate = pair_rates(rate_ref, own_ref.shape[1])
    early, late = early_late(parity, own_ref[...], got_ref[...])
    total = late + leap(masks, index, rate, rows) * early
    total_ref[...] = total
    sent_ref[...] = total.astype(bf16)


def lead_leap(masks, index, rate, rows, bit):
    me = lax.axis_index("ctx")
    lead = (lax.rem(me, bit) - lax.rem(me, 2)) * rows
    return jnp.exp(rate * -lead.astype(f32)) * masks[index][0:1, 0:1]


def level_kernel(masks, total_ref, got_ref, rate_ref, *refs, rows, level, lead, later):
    before_ref = refs[0] if level else None
    sent_ref, enter_ref, *new_ref = refs[1 if level else 0 :]
    _, rate = pair_rates(rate_ref, total_ref.shape[1])
    bit = 2 << level
    after = lax.rem(lax.div(lax.axis_index("ctx"), bit), 2)
    got = got_ref[...].astype(f32)
    early, late = early_late(after, total_ref[...], got)
    total = late + leap(masks, later, rate, bit * rows) * early
    for ref in new_ref:
        ref[...] = total
    sent_ref[...] = total.astype(bf16)
    entering = jnp.where(jnp.full(got.shape, after, jnp.int32) == 1, got, 0.0) * lead_leap(masks, lead, rate, rows, bit)
    enter_ref[...] = entering if before_ref is None else before_ref[...] + entering


def enter_kernel(
    masks, before_ref, got_ref, own_ref, other_ref, rate_ref, mine_ref, give_ref, *, rows, bit, lead, early_index
):
    parity, rate = pair_rates(rate_ref, own_ref.shape[1])
    first = before_ref[...] + lead_leap(masks, lead, rate, rows, bit) * got_ref[...].astype(f32)
    early, _ = early_late(parity, own_ref[...], other_ref[...])
    second = early + leap(masks, early_index, rate, rows) * first
    give, mine = early_late(parity, second, first)
    mine_ref[...] = mine
    give_ref[...] = give


def final_kernel(
    masks, state_ref, enter_ref, near_ref, short_ref, resid_ref, rim_ref, taps_ref, rate_ref, weight_ref, *refs,
    span, modes, channels, most, chunk, own,
):
    if own:
        hidden_out, whole, sums, hidden_ref, sems, wide, tables, starts_at = refs
    elif channels:
        gain_ref, _, _, _, hidden_out, whole, sums, normed_out, hidden_ref, sems, wide, tables, starts_at, normed_ref = refs
    else:
        _, _, _, hidden_out, whole, sums, hidden_ref, sems, wide, tables, starts_at = refs
    chans = resid_ref.shape[1]
    half = chans // 2
    first = half_start(chans, own)
    at = Masks(span)

    def store(c):
        here = pl.ds(pl.multiple_of(c * chunk, chunk), chunk)
        there = pl.ds(pl.multiple_of(first + c * chunk, chunk), chunk)
        return pltpu.make_async_copy(hidden_ref.at[:, here], hidden_out.at[:, there], sems.at[0, c])

    def store_normed(c):
        return cols_copy(normed_ref, normed_out, sems.at[1], c, chunk)

    if own:
        sums[...] = jnp.zeros(sums.shape, f32)

    def group(lanes):
        for slot, lane in enumerate(lanes):
            state = enter_ref[:, cols_of(pl.multiple_of(lane - first, LANES))]
            rate = rate_ref[:, cols_of(lane)]
            weight = weight_ref[:, cols_of(lane)]
            tables[slot, pl.ds(0, modes), :] = jnp.exp(-rate)
            leap = jnp.exp(-float(span) * rate)
            for b in range(SUBS):
                starts_at[slot, pl.ds(b * (modes + 1), modes), :] = weight * state
                if b < SUBS - 1:
                    state = (leap * twice(masks[at.passes + b], modes)) * state + sub_state(state_ref, lane, b, modes)
        for slot, lane in enumerate(lanes):
            part = [starts_at[slot, pl.ds(n, SUBS, stride=modes + 1), :] for n in range(modes)]
            decay = [row_of(tables.at[slot], n) for n in range(modes)]
            rim = rim_ref[0, :, cols_of(lane)].astype(f32)
            tap = taps_ref[0, :, cols_of(lane)]
            edge = [
                (tap[1:2] * rim[1:2]) * masks[at.edges] + (tap[2:3] * rim[0:1]) * masks[at.edges + 1],
                (tap[2:3] * rim[1:2]) * masks[at.edges + 2],
            ]
            for j in range(span):
                part = [part[n] * decay[n] for n in range(modes)]
                total = part
                while len(total) > 1:
                    total = [total[m] + total[m + 1] for m in range(0, len(total), 2)]
                conv = near_ref[pl.ds(j * SUBS, SUBS), cols_of(lane)] + total[0] * masks[at.enter + j]
                conv = conv.astype(bf16).astype(f32)
                short = short_ref[pl.ds(j * SUBS, SUBS), cols_of(lane)]
                if j < 2:
                    short = short + edge[j]
                wide[slot, pl.ds(j, SUBS, stride=span + 1), :] = short * conv
        for b in range(SUBS):
            rows = pl.ds(b * span, span)
            squares = sums[rows, :]
            for slot, lane in enumerate(lanes):
                hidden = wide[slot, pl.ds(b * (span + 1), span), :] + resid_ref[rows, cols_of(lane)].astype(f32)
                whole[lax.div(lane, LANES), rows, :] = hidden
                hidden_ref[rows, cols_of(pl.multiple_of(lane - first, LANES))] = hidden.astype(bf16)
                squares = squares + hidden * hidden
            sums[rows, :] = squares

    each_chunk(
        half,
        chunk,
        lambda c: None,
        lambda lanes: group([pl.multiple_of(first + lane, LANES) for lane in lanes]),
        lambda c: store(c).start(),
        most,
    )
    if channels and not own:
        inverse = lax.rsqrt(jnp.sum(sums[...], axis=1, keepdims=True) / channels + 1e-06)
        sums[...] = jnp.broadcast_to(inverse, sums.shape)

        def scale(lanes):
            for lane in lanes:
                normed = whole[lax.div(lane, LANES)] * sums[...] * gain_ref[:, cols_of(lane)]
                normed_ref[:, cols_of(lane)] = normed.astype(bf16)

        each_chunk(chans, chunk, lambda c: None, scale, lambda c: store_normed(c).start(), 4)
        for c in range(chans // chunk):
            store_normed(c).wait()
    for c in range(half // chunk):
        store(c).wait()


def shards(
    query_in, key_in, value_in, short_taps, decay_rate, residues, doc_lengths, residual, norm_gain
):
    tok_rows, chans = query_in.shape
    modes = decay_rate.shape[0]
    span = tok_rows // SUBS
    blocks = lax.axis_size("ctx")
    grp = lax.axis_size("grp")
    chunk = min(chans // 2, 1024)
    pieces = chans // chunk
    ctx_index = lax.axis_index("ctx")
    base = (ctx_index * tok_rows).astype(jnp.int32).reshape(1)
    weight = residues * jnp.sqrt(-jnp.expm1(-2.0 * decay_rate))

    smem = pl.BlockSpec(memory_space=pltpu.SMEM)
    vmem = pl.BlockSpec(memory_space=pltpu.VMEM)
    hbm = pl.BlockSpec(memory_space=pltpu.HBM)
    tile_shape = (SUBS, LANES)
    wide_rows = SUBS * (span + 3)
    params = pltpu.CompilerParams(vmem_limit_bytes=16 * MIB)

    lengths = pltpu.with_memory_space_constraint(doc_lengths, pltpu.HBM)

    def near_by(x):
        return pltpu.with_memory_space_constraint(x, pltpu.VMEM)

    def far_off(x):
        return pltpu.with_memory_space_constraint(x, pltpu.HBM)

    def copies(kinds):
        return pltpu.SemaphoreType.DMA((kinds, pieces))

    def cost(per_tile, moved):
        return pl.CostEstimate(flops=per_tile * (chans // LANES) * SUBS * LANES, bytes_accessed=moved, transcendentals=0)

    levels = max(1, (blocks // 4).bit_length() - 2)
    mask_shape = (Masks(span).count(levels),) + tile_shape
    small = min(chans // 2, 512)
    tails, ahead = pl.pallas_call(
        tail_kernel,
        in_specs=[hbm, hbm, hbm],
        out_specs=[vmem, vmem],
        out_shape=[pltpu.VMEM((3, 2, chans), bf16), pltpu.VMEM((2, tok_rows, small), bf16)],
        scratch_shapes=[pltpu.VMEM((3, 16, chans), bf16), pltpu.SemaphoreType.DMA((5,))],
        compiler_params=params,
        name="tails",
    )(far_off(query_in), far_off(key_in), far_off(value_in))
    rim_rows = from_behind(tails, "ctx", 1)
    def query_piece(part, masks, before):
        count = chans // 2
        scratch = [
            pltpu.VMEM((tok_rows, count), bf16),
            pltpu.SemaphoreType.DMA((count // chunk,)),
            pltpu.VMEM((Q_TILES, wide_rows, LANES), f32),
        ]
        operands = [near_by(masks), far_off(query_in), taps] + ([near_by(before)] if part else [])
        return pl.pallas_call(
            functools.partial(
                query_kernel, span=span, most=Q_TILES, chunk=chunk, first=part * count, count=count
            ),
            in_specs=[vmem, hbm, vmem] + [vmem] * (len(operands) - 3),
            out_specs=vmem,
            out_shape=pltpu.VMEM((tok_rows, chans), f32),
            scratch_shapes=scratch,
            input_output_aliases={3: 0} if part else {},
            compiler_params=params,
            cost_estimate=cost(100, 3 * tok_rows * chans),
            name="query_part_%d" % part,
        )(*operands)

    key_half = pltpu.VMEM((tok_rows, chans // 2), bf16)
    rates, weights, taps, rims = near_by(decay_rate), near_by(weight), near_by(short_taps), near_by(rim_rows)
    kept = pltpu.VMEM((modes, chans // 2), f32)
    sent = pltpu.VMEM((modes, chans // 2), bf16)

    gate_shape = pltpu.VMEM((tok_rows, chans), bf16)
    state_shape = pltpu.VMEM((chans // LANES, SUBS * (modes + 3), LANES), f32)

    def states_of(own, operands, in_specs, out_shape, scratch, aliases):
        return pl.pallas_call(
            functools.partial(
                state_kernel, span=span, modes=modes, most=A_TILES, own=own, chunk=small, levels=levels
            ),
            in_specs=in_specs,
            out_specs=[vmem] * (3 + len(out_shape)),
            out_shape=[gate_shape, state_shape, kept] + out_shape,
            scratch_shapes=scratch[:-1]
            + [
                pltpu.VMEM((A_TILES, wide_rows, LANES), f32),
                pltpu.VMEM((A_TILES, wide_rows, LANES), f32),
                pltpu.VMEM((A_TILES, modes + SUBS, LANES), f32),
                pltpu.VMEM((A_TILES, span) + tile_shape, f32),
            ]
            + scratch[-1:],
            input_output_aliases=aliases,
            compiler_params=params,
            cost_estimate=cost(500, 6 * tok_rows * chans),
            name="block_states_own" if own else "block_states_give",
        )(*operands)

    gates, states, give, masks, key_own, value_own, heads = states_of(
        False,
        [base, lengths, near_by(ahead), far_off(key_in), far_off(value_in), taps, rates],
        [smem, smem, vmem, hbm, hbm, vmem, vmem],
        [pltpu.VMEM(mask_shape, f32), key_half, key_half, pltpu.VMEM((2, 16, chans // 2), bf16)],
        [
            pltpu.VMEM((tok_rows, chans // 2), bf16),
            pltpu.VMEM((tok_rows, chans // 2), bf16),
            pltpu.VMEM((2 * SUBS, LANES), f32),
            pltpu.SemaphoreType.DMA((2, chans // 2 // small + 1)),
        ],
        {},
    )
    gates, states, give = pl.pallas_call(
        functools.partial(patch_kernel, span=span, modes=modes),
        in_specs=[vmem] * 8,
        out_specs=[vmem] * 3,
        out_shape=[gate_shape, state_shape, kept],
        input_output_aliases={5: 0, 6: 1, 7: 2},
        compiler_params=params,
        name="first_rows",
    )(near_by(masks), near_by(heads), rims, taps, rates, near_by(gates), near_by(states), near_by(give))
    got = swap(give, "ctx")
    gates, states, own = states_of(
        True,
        [near_by(masks), near_by(key_own), near_by(value_own), rims, taps, rates, near_by(gates), near_by(states)],
        [vmem] * 8,
        [],
        [],
        {6: 0, 7: 1},
    )
    got, gates, states, own = lax.optimization_barrier((got, gates, states, own))

    def near_piece(part, near):
        count = chans // NEAR_PARTS
        before = [] if near is None else [near_by(near)]
        return pl.pallas_call(
            functools.partial(
                near_kernel, span=span, modes=modes, most=N_TILES, first=part * count, count=count
            ),
            in_specs=[vmem] * (4 + len(before)),
            out_specs=vmem,
            out_shape=pltpu.VMEM((tok_rows, chans), f32),
            scratch_shapes=[
                pltpu.VMEM((N_TILES, span * (SUBS + 2), LANES), f32),
                pltpu.VMEM((N_TILES, span + SUBS, LANES), f32),
            ],
            compiler_params=params,
            input_output_aliases={4: 0} if before else {},
            cost_estimate=cost(600 // NEAR_PARTS, 7 * tok_rows * count),
            name="near_part_%d" % part,
        )(near_by(masks), near_by(gates), rates, weights, *before)

    got = swap(give, "ctx")

    at = Masks(span)

    def pair_call(kernel, operands, out_shape, name, extra=(), **static):
        return pl.pallas_call(
            functools.partial(kernel, **static),
            in_specs=[vmem] * (len(operands) + 2 + len(extra)),
            out_specs=[vmem] * len(out_shape),
            out_shape=out_shape,
            compiler_params=params,
            name=name,
        )(near_by(masks), *[near_by(x) for x in operands], rates, *[near_by(x) for x in extra])

    total, ends = pair_call(pair_kernel, [own, got], [kept, sent], "pair_ends", rows=tok_rows, index=at.late)
    entering, near = [], None
    for m in range(levels):
        met = swap(ends, "ctx", 2 << m)
        if m < NEAR_PARTS:
            near = near_piece(m, near)
            if m == 0:
                q_short = query_piece(0, masks, None)
                met, q_short = lax.optimization_barrier((met, q_short))
            met, near = lax.optimization_barrier((met, near))
        ends, enter, *total = pair_call(
            level_kernel,
            [total, met],
            [sent, kept] + [kept] * (m < levels - 1),
            "level_%d" % m,
            extra=entering,
            rows=tok_rows,
            level=m,
            lead=at.lead(m),
            later=at.later(m),
        )
        entering = [enter]
        total = total[0] if total else None
    on = from_behind(ends, "ctx", 2 << levels)
    for m in range(levels, NEAR_PARTS):
        near = near_piece(m, near)
    q_short = query_piece(1, masks, q_short)
    on, q_short, near = lax.optimization_barrier((on, q_short, near))
    mine, give_back = pair_call(
        enter_kernel,
        entering + [on, own, got],
        [kept, kept],
        "pair_enter",
        rows=tok_rows,
        bit=2 << levels,
        lead=at.lead(levels),
        early_index=at.early,
    )
    got_back = swap(give_back, "ctx")

    alone = grp == 1
    resid = near_by(residual)

    def finish(own, enter, before):
        last = alone and not own
        out_specs = [hbm, vmem, vmem]
        out_shape = [
            jax.ShapeDtypeStruct((tok_rows, chans), bf16),
            pltpu.VMEM((chans // LANES, tok_rows, LANES), f32),
            pltpu.VMEM((tok_rows, LANES), f32),
        ]
        scratch = [
            pltpu.VMEM((tok_rows, chans // 2), bf16),
            copies(2),
            pltpu.VMEM((F_TILES, wide_rows, LANES), f32),
            pltpu.VMEM((F_TILES, modes + SUBS, LANES), f32),
            pltpu.VMEM((F_TILES, SUBS * (modes + 3), LANES), f32),
        ]
        operands = [near_by(x) for x in (masks, states, enter, near, q_short)] + [resid, rims, taps, rates, weights]
        if last:
            operands.append(near_by(norm_gain.reshape(1, chans)))
            out_specs.append(hbm)
            out_shape.append(jax.ShapeDtypeStruct((tok_rows, chans), bf16))
            scratch.append(pltpu.VMEM((tok_rows, chans), bf16))
        count = len(operands)
        in_specs = [vmem] * count
        if before:
            operands += [far_off(before[0]), near_by(before[1]), near_by(before[2])]
            in_specs += [hbm, vmem, vmem]
        return pl.pallas_call(
            functools.partial(
                final_kernel, span=span, modes=modes, channels=chans if alone else 0, most=F_TILES, chunk=chunk, own=own
            ),
            in_specs=in_specs,
            out_specs=out_specs,
            out_shape=out_shape,
            scratch_shapes=scratch,
            input_output_aliases={count + i: i for i in range(len(before))},
            compiler_params=params,
            cost_estimate=cost(450, 9 * tok_rows * chans),
            name="far_part_own" if own else "far_part_other",
        )(*operands)

    before = finish(True, mine, [])
    got_back, *before = lax.optimization_barrier((got_back, *before))
    outs = finish(False, got_back, before)
    if alone:
        return (outs[0], outs[3])
    hidden_out, whole, sums = outs
    hidden = whole.transpose(1, 0, 2).reshape(tok_rows, chans)
    square_sum = lax.psum(jnp.sum(sums, axis=1), "grp")
    inverse_rms = lax.rsqrt(square_sum / (chans * grp) + 1e-06)
    normed = (hidden * inverse_rms[:, None] * norm_gain[None, :]).astype(bf16)
    return (hidden_out, normed)


def solution(mesh):
    return jax.shard_map(
        shards,
        mesh=mesh,
        in_specs=(
            P("ctx", "grp"),
            P("ctx", "grp"),
            P("ctx", "grp"),
            P(None, None, "grp"),
            P(None, "grp"),
            P(None, "grp"),
            P(),
            P("ctx", "grp"),
            P("grp"),
        ),
        out_specs=(P("ctx", "grp"), P("ctx", "grp")),
        check_vma=False,
    )
```
